128 devices in a mesh: dp: 8 (over x, core), blk: 16 (over y, z).
Axes of the slice: x: 4, y: 4, z: 4, core: 2. Of those that a mesh axis runs over, the one named last changes fastest.
Arguments:
- inputs: bfloat16 [8, 2048, 768], P('dp', 'blk'), may hold values from -6 to 6
- aug_source: int32 [8, 2048], P('dp', 'blk'), may hold values from 0 to 127
- aug_flags: int32 [8, 2048], P('dp', 'blk'), may hold values 0 or 1
- lengths: int32 [8], P('dp'), may hold values from 1921 to 2048, as said below
- head_flags: int32 [6], replicated, may hold values from 0 to 1, as said below
- cotangent: bfloat16 [8, 2048, 768], P('dp', 'blk'), may hold values from -6 to 6
- qkv_teacher: bfloat16 [768, 2304], replicated, may hold values from -0.21875 to 0.21875
- qv_bias_teacher: float32 [1536], replicated, may hold values from -1.5 to 1.5
- out_teacher: bfloat16 [768, 768], replicated, may hold values from -2.5 to 2.5
- up_teacher: bfloat16 [768, 3072], replicated, may hold values from -0.21875 to 0.21875
- down_teacher: bfloat16 [3072, 768], replicated, may hold values from -0.109375 to 0.109375
- up_bias_teacher: float32 [3072], replicated, may hold values from -1.5 to 1.5
- vectors_teacher: float32 [6, 768], replicated, may hold values from -1.5 to 1.5, as said below
- qkv_student: bfloat16 [768, 1152], replicated, may hold values from -0.21875 to 0.21875
- qv_bias_student: float32 [768], replicated, may hold values from -1.5 to 1.5
- out_student: bfloat16 [384, 768], replicated, may hold values from -3.5 to 3.5
- up_student: bfloat16 [768, 1536], replicated, may hold values from -0.21875 to 0.21875
- down_student: bfloat16 [1536, 768], replicated, may hold values from -0.15625 to 0.15625
- up_bias_student: float32 [1536], replicated, may hold values from -1.5 to 1.5
- vectors_student: float32 [6, 768], replicated, may hold values from -1.5 to 1.5, as said below
Outputs:
- output: float32 [8, 2048, 768], P('dp', 'blk')
- grad_inputs: float32 [8, 2048, 768], P('dp', 'blk')
- grad_qkv_teacher: float32 [768, 2304], P(('dp', 'blk'))
- grad_qv_bias_teacher: float32 [1536], P(('dp', 'blk'))
- grad_out_teacher: float32 [768, 768], P(None, ('dp', 'blk'))
- grad_up_teacher: float32 [768, 3072], P(('dp', 'blk'))
- grad_down_teacher: float32 [3072, 768], P(None, ('dp', 'blk'))
- grad_up_bias_teacher: float32 [3072], P(('dp', 'blk'))
- grad_vectors_teacher: float32 [6, 768], P(None, ('dp', 'blk'))
- grad_qkv_student: float32 [768, 1152], P(('dp', 'blk'))
- grad_qv_bias_student: float32 [768], P(('dp', 'blk'))
- grad_out_student: float32 [384, 768], P(None, ('dp', 'blk'))
- grad_up_student: float32 [768, 1536], P(('dp', 'blk'))
- grad_down_student: float32 [1536, 768], P(None, ('dp', 'blk'))
- grad_up_bias_student: float32 [1536], P(('dp', 'blk'))
- grad_vectors_student: float32 [6, 768], P(None, ('dp', 'blk'))
The draws below stay inside these ranges and needn't reach their ends.
Inputs may be any that keep to these rules, and one draw needn't show every extreme that they name: `lengths`: among the 1 sequence of each index of dp, one has more than 1920 tokens valid; some sequence has all 2048 tokens valid. `head_flags`: at least one head has flag 1 and at least one has flag 0. `vectors_teacher`: rows 1 and 4 lie in 0.5 to 1.5. `vectors_student`: rows 1 and 4 lie in 0.5 to 1.5.
All inputs are finite; a program needn't handle non-finite values. No bound on the sum of `aug_flags` on one device may be relied on, other than what follows from the above.
Results may differ from the reference program's by a relative error of at most 0.035.
Values may be sent and summed in bfloat16 or wider, within the bound.
A program may use at most 192 MiB of HBM per device.

```python
import jax
import jax.numpy as jnp
from jax import lax

D = 768
HEADS_T = 12
HEADS_S = 6
HDIM = 64
FF = 3072
FF_S = 1536
TB = 128
NSEQ = 1
SEQS = 8
SEQ_LEN = 2048
N_BLK = 16


def vector_rows(key):
    first, second = jax.random.split(key)
    gains = jax.random.uniform(first, (6, D), jnp.float32, 0.5, 1.5)
    shifts = jnp.clip(0.3 * jax.random.normal(second, (6, D), jnp.float32), -1.5, 1.5)
    row_ids = jnp.arange(6)[:, None]
    return jnp.where((row_ids == 1) | (row_ids == 4), gains, shifts)


def draw_lengths(key, part):
    key = jax.random.fold_in(key, 11)
    first, second, third, fourth = jax.random.split(key, 4)
    drawn = jax.random.randint(first, (SEQS,), SEQ_LEN // 2, SEQ_LEN + 1)
    reaching_len = jax.random.randint(fourth, (SEQS,), SEQ_LEN - TB + 1, SEQ_LEN - TB // 2 + 1)
    chosen = jax.random.randint(second, (SEQS // NSEQ,), 0, NSEQ)
    full_seq = jax.random.randint(third, (), 0, SEQS)
    seq_ids = jnp.arange(SEQS)
    reaching = seq_ids % NSEQ == chosen[seq_ids // NSEQ]
    picked = jnp.where(reaching, reaching_len, drawn)
    return jnp.where(seq_ids == full_seq, SEQ_LEN, picked).astype(jnp.int32)


def draw_head_flags(key, part):
    key = jax.random.fold_in(key, 23)
    first, second, third = jax.random.split(key, 3)
    drawn = jax.random.randint(first, (HEADS_S,), 0, 2)
    forced_one = jax.random.randint(second, (), 0, HEADS_S)
    forced_zero = (forced_one + 1 + jax.random.randint(third, (), 0, HEADS_S - 1)) % HEADS_S
    head_ids = jnp.arange(HEADS_S)
    flags = jnp.where(head_ids == forced_one, 1, drawn)
    return jnp.where(head_ids == forced_zero, 0, flags).astype(jnp.int32)


def draw_vectors_teacher(key, part):
    key = jax.random.fold_in(key, 31)
    return vector_rows(key)


def draw_vectors_student(key, part):
    key = jax.random.fold_in(key, 37)
    return vector_rows(key)


def place_ends(entries, key, low, top_value):
    longest = entries.shape.index(max(entries.shape))
    spots = []
    for shift in (0, 1):
        where = [jax.random.randint(jax.random.fold_in(key, axis), (), 0, length) for axis, length in enumerate(entries.shape)]
        where[longest] = (where[longest] + shift) % entries.shape[longest]
        spots.append(tuple(where))
    return entries.at[spots[0]].set(low).at[spots[1]].set(top_value)


def level_of(key, extent, pieces, least, top_value):
    def one(dim, blocks):
        steps = jax.random.uniform(jax.random.fold_in(jax.random.fold_in(key, 6), dim), (blocks,), jnp.float32, least / len(pieces), top_value / len(pieces))
        return jnp.repeat(jnp.exp(steps), extent[dim] // blocks).reshape((-1,) + (1,) * (len(extent) - dim - 1))

    factor_of = one(*pieces[0])
    for cut in pieces[1:]:
        factor_of = factor_of * one(*cut)
    return factor_of


def normal_values(own_key, extent, deviation, limit, shards=(), dtype=jnp.bfloat16):
    result = deviation * jax.random.normal(own_key, extent, jnp.float32)
    if shards:
        result = result * level_of(own_key, extent, shards, -0.22, 0.18)
    return jnp.clip(result, -limit, limit).astype(dtype)


def setup_inputs(seed: int = 0) -> dict:
    arg_keys = jax.random.split(jax.random.key(seed), 21)
    return {
        "inputs": normal_values(arg_keys[0], (SEQS, SEQ_LEN, D), 1.0, 6.0, ((0, 8), (1, 16))),
        "aug_source": place_ends(jax.random.randint(arg_keys[1], (SEQS, SEQ_LEN), 0, TB), jax.random.fold_in(arg_keys[1], 1), 0, TB - 1).astype(jnp.int32),
        "aug_flags": place_ends((jax.random.randint(arg_keys[2], (SEQS, SEQ_LEN), 0, 6) < 1).astype(jnp.int32), jax.random.fold_in(arg_keys[2], 1), 0, 1),
        "lengths": draw_lengths(jax.random.fold_in(arg_keys[20], 71), 0),
        "head_flags": draw_head_flags(jax.random.fold_in(arg_keys[20], 71), 0),
        "cotangent": normal_values(arg_keys[5], (SEQS, SEQ_LEN, D), 1.0, 6.0, ((0, 8), (1, 16))),
        "qkv_teacher": normal_values(arg_keys[6], (D, 3 * HEADS_T * HDIM), D ** -0.5, 0.21875),
        "qv_bias_teacher": normal_values(arg_keys[7], (2 * HEADS_T * HDIM,), 0.3, 1.5, (), jnp.float32),
        "out_teacher": normal_values(arg_keys[8], (HEADS_T * HDIM, D), (max(1, HEADS_T * HDIM // 128)) ** -0.5, 2.5),
        "up_teacher": normal_values(arg_keys[9], (D, FF), D ** -0.5, 0.21875),
        "down_teacher": normal_values(arg_keys[10], (FF, D), FF ** -0.5, 0.109375),
        "up_bias_teacher": normal_values(arg_keys[11], (FF,), 0.3, 1.5, (), jnp.float32),
        "vectors_teacher": draw_vectors_teacher(jax.random.fold_in(arg_keys[20], 71), 0),
        "qkv_student": normal_values(arg_keys[13], (D, 3 * HEADS_S * HDIM), D ** -0.5, 0.21875),
        "qv_bias_student": normal_values(arg_keys[14], (2 * HEADS_S * HDIM,), 0.3, 1.5, (), jnp.float32),
        "out_student": normal_values(arg_keys[15], (HEADS_S * HDIM, D), (max(1, HEADS_S * HDIM // 128)) ** -0.5, 3.5),
        "up_student": normal_values(arg_keys[16], (D, FF_S), D ** -0.5, 0.21875),
        "down_student": normal_values(arg_keys[17], (FF_S, D), FF_S ** -0.5, 0.15625),
        "up_bias_student": normal_values(arg_keys[18], (FF_S,), 0.3, 1.5, (), jnp.float32),
        "vectors_student": draw_vectors_student(jax.random.fold_in(arg_keys[20], 71), 0),
    }


MASK_FILL = -1e+30
HIGH_PRECISION = lax.Precision.HIGHEST

@jax.custom_vjp
def low(v):
    return lax.optimization_barrier(v.astype(jnp.bfloat16)).astype(jnp.float32)

@jax.custom_vjp
def low_back(v):
    return v

def low_keep(v):
    return (low(v), None)

def low_pass(kept, grad):
    return (grad,)

def back_keep(v):
    return (v, None)

def back_low(kept, grad):
    return (low(grad),)
low.defvjp(low_keep, low_pass)
low_back.defvjp(back_keep, back_low)

def matmul(left_side, right_side):
    return jnp.dot(left_side, right_side, precision=HIGH_PRECISION, preferred_element_type=jnp.float32)

def layer_norm(values, norm_gain, norm_shift):
    center = values - lax.optimization_barrier(jnp.mean(values, axis=-1, keepdims=True))
    spread = lax.optimization_barrier(jnp.mean(center * center, axis=-1, keepdims=True))
    return center * lax.rsqrt(spread + 1e-06) * norm_gain + norm_shift

def gelu_exact(values):
    return jax.nn.gelu(values, approximate=False)

def split_heads(matrix, head_count):
    return matrix.reshape(matrix.shape[0], head_count, HDIM).transpose(1, 0, 2)

def attention_inputs(hidden, weight, bias_pair, head_count):
    head_span = head_count * HDIM
    joined = matmul(low(hidden), weight)
    queries = low_back(low(joined[:, :head_span] + bias_pair[:head_span]))
    keys_flat = low_back(low(joined[:, head_span:2 * head_span]))
    values = low_back(low(joined[:, 2 * head_span:] + bias_pair[head_span:]))
    return (split_heads(queries, head_count), split_heads(keys_flat, head_count), split_heads(values, head_count))

def masked_scores(queries, keys_all, key_valid):
    scores = low_back(jnp.einsum('hqd,hkd->hqk', queries, keys_all, precision=HIGH_PRECISION) * 0.125)
    return jnp.where(key_valid[None, None, :], scores, MASK_FILL)

def query_blocks(tensor):
    rows_per = min(512, SEQ_LEN)
    return tensor.reshape(tensor.shape[0], SEQ_LEN // rows_per, rows_per, tensor.shape[2]).transpose(1, 0, 2, 3)

def merge_blocks(tensor):
    return tensor.transpose(1, 0, 2, 3).reshape(tensor.shape[1], SEQ_LEN, tensor.shape[3])

def teacher_attention(queries, keys_all, values_all, key_valid):

    def one_block(query_rows):
        scores = masked_scores(query_rows, keys_all, key_valid)
        probabilities = jax.nn.softmax(scores, axis=-1)
        attended = jnp.einsum('hqk,hkd->hqd', low(probabilities), values_all, precision=HIGH_PRECISION)
        return (attended, scores[:HEADS_S])
    attended, teacher_scores = lax.map(jax.checkpoint(one_block), query_blocks(queries))
    return (merge_blocks(attended), teacher_scores)

def student_attention(queries, keys_all, values_all, teacher_scores, key_valid, flag_weights):
    rows_per = min(512, SEQ_LEN)
    valid_blocks = key_valid.astype(jnp.float32).reshape(SEQ_LEN // rows_per, rows_per)

    def one_block(packed):
        query_rows, teacher_rows, valid_rows = packed
        scores = masked_scores(query_rows, keys_all, key_valid)
        probabilities = jax.nn.softmax(scores, axis=-1)
        teacher_probs = jax.nn.softmax(teacher_rows, axis=-1)
        attended = jnp.einsum('hqk,hkd->hqd', low(probabilities), values_all, precision=HIGH_PRECISION)
        prob_gap = probabilities - teacher_probs
        map_loss = SEQ_LEN * jnp.sum(flag_weights[:, None, None] * valid_rows[None, :, None] * prob_gap * prob_gap)
        return (attended, map_loss)
    attended, map_loss = lax.map(jax.checkpoint(one_block), (query_blocks(queries), teacher_scores, valid_blocks))
    return (merge_blocks(attended), jnp.sum(map_loss))

def dense_layer(residual, attended, out_weight, up_weight, down_weight, up_bias, vectors):
    joined = attended.transpose(1, 0, 2).reshape(SEQ_LEN, -1)
    mixed = low_back(low(joined))
    projected = low_back(matmul(mixed, out_weight)) + vectors[0]
    normed = layer_norm(residual + projected, vectors[1], vectors[2])
    upward = low_back(matmul(low(normed), up_weight)) + up_bias
    downward = low_back(matmul(low(gelu_exact(upward)), down_weight)) + vectors[3]
    return layer_norm(normed + downward, vectors[4], vectors[5])

def sequence_forward(weights, initial, source, replace, length, flag_weights):
    qkv_t, bias_t, out_t, up_t, down_t, upb_t, vec_t, qkv_s, bias_s, out_s, up_s, down_s, upb_s, vec_s = weights
    blocks = initial.reshape(N_BLK, TB, D)
    taken_rows = jnp.take_along_axis(blocks, source.reshape(N_BLK, TB, 1), axis=1).reshape(SEQ_LEN, D)
    augmented = jnp.where(replace[:, None] == 1, taken_rows, initial)
    key_valid = jnp.arange(SEQ_LEN) < length
    teacher_q, teacher_k, teacher_v = attention_inputs(augmented, qkv_t, bias_t, HEADS_T)
    teacher_att, teacher_scores = teacher_attention(teacher_q, teacher_k, teacher_v, key_valid)
    hidden = dense_layer(augmented, teacher_att, out_t, up_t, down_t, upb_t, vec_t)
    student_q, student_k, student_v = attention_inputs(hidden, qkv_s, bias_s, HEADS_S)
    student_att, map_loss = student_attention(student_q, student_k, student_v, teacher_scores, key_valid, flag_weights)
    output = dense_layer(hidden, student_att, out_s, up_s, down_s, upb_s, vec_s)
    return (output, map_loss)

def reference(inputs, aug_source, aug_flags, lengths, head_flags, cotangent, qkv_teacher, qv_bias_teacher, out_teacher, up_teacher, down_teacher, up_bias_teacher, vectors_teacher, qkv_student, qv_bias_student, out_student, up_student, down_student, up_bias_student, vectors_student):
    params = tuple((weight.astype(jnp.float32) for weight in (qkv_teacher, qv_bias_teacher, out_teacher, up_teacher, down_teacher, up_bias_teacher, vectors_teacher, qkv_student, qv_bias_student, out_student, up_student, down_student, up_bias_student, vectors_student)))
    flag_weights = head_flags.astype(jnp.float32)

    def one_sequence(totals, packed):
        seq_inputs, seq_source, seq_flags, seq_length, seq_cot = packed

        def objective(weights, initial):
            output, map_loss = sequence_forward(weights, initial, seq_source, seq_flags, seq_length, flag_weights)
            return (jnp.sum(output * seq_cot.astype(jnp.float32)) + map_loss, output)
        value, backward, output = jax.vjp(objective, params, seq_inputs.astype(jnp.float32), has_aux=True)
        grad_weights, grad_initial = backward(jnp.ones_like(value))
        totals = jax.tree.map(jnp.add, totals, grad_weights)
        return (totals, (output, grad_initial))
    zeros = jax.tree.map(jnp.zeros_like, params)
    totals, (outputs, grad_inputs) = lax.scan(one_sequence, zeros, (inputs, aug_source, aug_flags, lengths, cotangent))
    return (outputs, grad_inputs, totals[0], totals[1], totals[2], totals[3], totals[4], totals[5], totals[6], totals[7], totals[8], totals[9], totals[10], totals[11], totals[12], totals[13])
```

```python
import jax
import jax.numpy as jnp
from jax import lax
from jax.experimental import pallas as pl
from jax.experimental.pallas import tpu as pltpu
from jax.sharding import PartitionSpec as P

MESH = pl.DeviceIdType.MESH
LOG2E = 1.4426950408889634
C2 = 0.125 * LOG2E
SEQ = 2048
QC = 256
KT = 256
NKT = SEQ // KT
MIB = 1 << 20


def dot(a, b):
    return jnp.dot(a, b, preferred_element_type=jnp.float32)


def place():
    b = lax.axis_index("blk")
    r = lax.rem(lax.rem(b, 4) - b // 4 + 7, 4)
    return b, 3 * (b // 4) + r, r < 3


def owner_of(hh):
    y = hh // 3
    return 4 * y + lax.rem(y + lax.rem(hh, 3) + 1, 4)


def greet_group():
    b = lax.axis_index("blk")
    sem = pltpu.get_barrier_semaphore()

    def hello(i, carry):
        pl.semaphore_signal(
            sem, inc=1, device_id={"blk": lax.rem(b + i, 16)}, device_id_type=MESH
        )
        return carry

    lax.fori_loop(1, 16, hello, 0)
    pl.semaphore_wait(sem, 15)


def copy_to(src, dst, send_sem, recv_sem, d):
    return pltpu.make_async_remote_copy(
        src_ref=src,
        dst_ref=dst,
        send_sem=send_sem,
        recv_sem=recv_sem,
        device_id={"blk": d},
        device_id_type=MESH,
    )


def start_to(src, dst, send_sem, recv_sem, d, b):
    @pl.when(d != b)
    def _():
        copy_to(src, dst, send_sem, recv_sem, d).start()

    @pl.when(d == b)
    def _():
        pltpu.make_async_copy(src, dst, recv_sem).start()


def sent_to(src, dst, send_sem, recv_sem, d, b):
    @pl.when(d != b)
    def _():
        copy_to(src, dst, send_sem, recv_sem, d).wait_send()


def got(dst, recv_sem):
    pltpu.make_async_copy(dst, dst, recv_sem).wait()


def lanes(start, size):
    return pl.ds(pl.multiple_of(start, 128), size)


def fold(v):
    return jnp.sum(v.reshape(v.shape[0] // 8, 8, v.shape[1]), axis=0)


def key_ok(length):
    rows = lax.broadcasted_iota(jnp.int32, (KT, QC), 0) + (SEQ - KT)
    return rows < length


def attn_forward(q_at, kn, vt, s_ref, p_ref, length):
    q = q_at
    m8 = jnp.full((8, QC), -3e38, jnp.float32)
    for t in range(NKT):
        s = dot(kn[t * KT : (t + 1) * KT, :], q)
        if t == NKT - 1:
            s = jnp.where(key_ok(length), s, -1e30)
        s_ref[t * KT : (t + 1) * KT, :] = s
        m8 = jnp.maximum(m8, jnp.max(s.reshape(KT // 8, 8, QC), axis=0))
    mc = jnp.max(m8, axis=0, keepdims=True) * C2
    l8 = jnp.zeros((8, QC), jnp.float32)
    for t in range(NKT):
        p = jnp.exp2(s_ref[t * KT : (t + 1) * KT, :] * C2 - mc)
        l8 = l8 + fold(p)
        p_ref[t * KT : (t + 1) * KT, :] = p.astype(jnp.bfloat16)
    total = jnp.sum(l8, axis=0, keepdims=True)
    o = dot(vt, p_ref[...]) / total
    return o, mc + jnp.log2(total)


def attn_backward(
    q, q2, do, lse, lse2, weight, kn, k2n, vn, kt, length, pf, gf, x_ref, acc
):
    d8 = jnp.zeros((8, QC), jnp.float32)
    ok = key_ok(length)
    for t in range(NKT):
        rows = slice(t * KT, (t + 1) * KT)
        p = jnp.exp2(dot(kn[rows, :], q) * C2 - lse)
        p2 = jnp.exp2(dot(k2n[rows, :], q2) * C2 - lse2)
        if t == NKT - 1:
            p = jnp.where(ok, p, 0.0)
            p2 = jnp.where(ok, p2, 0.0)
        g = dot(vn[rows, :], do) + weight * (p - p2)
        d8 = d8 + fold(p * g)
        pf[rows, :] = p
        gf[rows, :] = g
        x_ref[rows, QC:] = p.astype(jnp.bfloat16)
    delta = jnp.sum(d8, axis=0, keepdims=True)
    for t in range(NKT):
        rows = slice(t * KT, (t + 1) * KT)
        x_ref[rows, :QC] = (pf[rows, :] * (gf[rows, :] - delta)).astype(jnp.bfloat16)
    both = jnp.concatenate([q, do], axis=0).astype(jnp.float32).T
    col = lax.broadcasted_iota(jnp.int32, (QC, 128), 1)
    rhs = jnp.concatenate(
        [jnp.where(col < 64, both, 0.0), jnp.where(col < 64, 0.0, both)], axis=0
    ).astype(jnp.bfloat16)
    for t in range(NKT):
        rows = slice(t * KT, (t + 1) * KT)
        acc[rows, :] += dot(x_ref[rows, :], rhs)
    return dot(kt, x_ref[:, :QC]) * 0.125


def natural(x):
    return x.astype(jnp.float32).T.astype(jnp.bfloat16)


def teacher_forward_kernel(
    len_ref, src, buf, dist, att, lse, lse_d,
    o_buf, kn, s_ref, p_ref,
    send1, recv1, send2, recv2, send3, recv3, lse_sem,
):
    b, hh, owner = place()
    greet_group()

    def out1(j, carry):
        h = lax.rem(j + b, 12)
        start_to(src.at[h], buf.at[:, lanes(b * 128, 128)], send1.at[h], recv1.at[b], owner_of(h), b)
        return carry

    lax.fori_loop(0, 12, out1, 0)

    def out2(j, carry):
        h = lax.rem(j + b, 6)
        start_to(
            src.at[h, 0:128], dist.at[:, lanes(b * 128, 128)], send2.at[h], recv2.at[b], owner_of(h + 6), b
        )
        return carry

    lax.fori_loop(0, 6, out2, 0)

    @pl.when(owner)
    def _():
        def arrive(i, carry):
            got(buf.at[:, lanes(i * 128, 128)], recv1.at[i])
            return carry

        lax.fori_loop(0, 16, arrive, 0)
        kn[...] = natural(buf[64:128, :])
        length = len_ref[0]

        def chunk(c, carry):
            here = lanes(c * QC, QC)
            o, stat = attn_forward(buf[0:64, here], kn, buf[128:192, :], s_ref, p_ref, length)
            o_buf[:, here] = o.astype(jnp.bfloat16)
            lse[:, here] = jnp.broadcast_to(stat, (8, QC))
            for i in range(2):
                d = 2 * c + i
                start_to(
                    o_buf.at[:, lanes(d * 128, 128)], att.at[hh], send3.at[d], recv3.at[hh], d, b
                )
            return carry

        lax.fori_loop(0, SEQ // QC, chunk, 0)

        def done3(d, carry):
            sent_to(o_buf.at[:, lanes(d * 128, 128)], att.at[hh], send3.at[d], recv3.at[hh], d, b)
            return carry

        lax.fori_loop(0, 16, done3, 0)

    @pl.when(owner & (hh < 6))
    def _():
        lse_d[:, 0:1024] = lse[:, 0:1024]
        far = copy_to(
            lse.at[:, 1024:2048], lse_d.at[:, 1024:2048], lse_sem.at[0], lse_sem.at[1], owner_of(hh + 6)
        )
        far.start()
        pltpu.make_async_copy(buf.at[0:128], dist, lse_sem.at[2]).start()
        pltpu.make_async_copy(buf.at[0:128], dist, lse_sem.at[2]).wait()
        far.wait_send()

    @pl.when(owner & (hh >= 6))
    def _():
        def arrive(i, carry):
            got(dist.at[:, lanes(i * 128, 128)], recv2.at[i])
            return carry

        lax.fori_loop(0, 16, arrive, 0)
        got(lse_d.at[:, 1024:2048], lse_sem.at[1])

    def back(h, carry):
        got(att.at[h], recv3.at[h])
        return carry

    lax.fori_loop(0, 12, back, 0)

    def done1(h, carry):
        sent_to(src.at[h], buf.at[:, lanes(b * 128, 128)], send1.at[h], recv1.at[b], owner_of(h), b)
        return carry

    lax.fori_loop(0, 12, done1, 0)

    def done2(h, carry):
        sent_to(
            src.at[h, 0:128], dist.at[:, lanes(b * 128, 128)], send2.at[h], recv2.at[b], owner_of(h + 6), b
        )
        return carry

    lax.fori_loop(0, 6, done2, 0)


def student_forward_kernel(
    len_ref, src, buf, att, lse,
    o_buf, kn, s_ref, p_ref,
    send1, recv1, send3, recv3, lse_sem,
):
    b, hh, owner = place()
    half = hh // 6
    head = lax.rem(hh, 6)
    greet_group()

    def out1(j, carry):
        h = lax.rem(j + b, 12)
        start_to(
            src.at[lax.rem(h, 6)], buf.at[:, lanes(b * 128, 128)], send1.at[h], recv1.at[b], owner_of(h), b
        )
        return carry

    lax.fori_loop(0, 12, out1, 0)

    @pl.when(owner)
    def _():
        def arrive(i, carry):
            got(buf.at[:, lanes(i * 128, 128)], recv1.at[i])
            return carry

        lse[:, 0:1024] = jnp.full((8, 1024), 1e30, jnp.float32)
        lax.fori_loop(0, 16, arrive, 0)
        kn[...] = natural(buf[64:128, :])
        length = len_ref[0]

        def chunk(c, carry):
            here = lanes(half * 1024 + c * QC, QC)
            o, stat = attn_forward(buf[0:64, here], kn, buf[128:192, :], s_ref, p_ref, length)
            o_buf[:, lanes(c * QC, QC)] = o.astype(jnp.bfloat16)
            lse[:, here] = jnp.broadcast_to(stat, (8, QC))
            for i in range(2):
                j = 2 * c + i
                d = 8 * half + j
                start_to(
                    o_buf.at[:, lanes(j * 128, 128)], att.at[head], send3.at[j], recv3.at[head], d, b
                )
            return carry

        lax.fori_loop(0, 1024 // QC, chunk, 0)

        def done3(j, carry):
            d = 8 * half + j
            sent_to(o_buf.at[:, lanes(j * 128, 128)], att.at[head], send3.at[j], recv3.at[head], d, b)
            return carry

        lax.fori_loop(0, 8, done3, 0)

    @pl.when(owner & (hh >= 6))
    def _():
        far = copy_to(
            lse.at[:, 1024:2048], lse.at[:, 1024:2048], lse_sem.at[0], lse_sem.at[1], owner_of(hh - 6)
        )
        far.start()
        far.wait_send()

    @pl.when(owner & (hh < 6))
    def _():
        got(lse.at[:, 1024:2048], lse_sem.at[1])

    def back(h, carry):
        got(att.at[h], recv3.at[h])
        return carry

    lax.fori_loop(0, 6, back, 0)

    def done1(h, carry):
        sent_to(
            src.at[lax.rem(h, 6)], buf.at[:, lanes(b * 128, 128)], send1.at[h], recv1.at[b], owner_of(h), b
        )
        return carry

    lax.fori_loop(0, 12, done1, 0)


def weight_row(len_ref, flag_ref, head, first, use):
    q = lax.broadcasted_iota(jnp.int32, (1, QC), 1) + first
    factor = jnp.where(use, flag_ref[head].astype(jnp.float32) * (2.0 * SEQ), 0.0)
    return jnp.where(q < len_ref[0], factor, 0.0)


def student_backward_kernel(
    len_ref, flag_ref, src, buf, dist, lse, lse_d, dq, dkv,
    do_buf, kn, k2n, vn, pf, gf, x_ref, acc, dq_buf, dkv_buf,
    send1, recv1, send2, recv2, send3, recv3,
):
    b, hh, owner = place()
    half = hh // 6
    head = lax.rem(hh, 6)
    greet_group()

    def out1(j, carry):
        h = lax.rem(j + b, 6)
        start_to(
            src.at[h], do_buf.at[:, lanes(lax.rem(b, 8) * 128, 128)],
            send1.at[h], recv1.at[lax.rem(b, 8)], owner_of(h + 6 * (b // 8)), b,
        )
        return carry

    lax.fori_loop(0, 6, out1, 0)

    @pl.when(owner)
    def _():
        kn[...] = natural(buf[64:128, :])
        vn[...] = natural(buf[128:192, :])
        k2n[...] = natural(dist[64:128, :])
        acc[...] = jnp.zeros_like(acc)

        def arrive(i, carry):
            got(do_buf.at[:, lanes(i * 128, 128)], recv1.at[i])
            return carry

        lax.fori_loop(0, 8, arrive, 0)

        def chunk(c, carry):
            first = half * 1024 + c * QC
            here = lanes(first, QC)
            g = attn_backward(
                buf[0:64, here], dist[0:64, here], do_buf[:, lanes(c * QC, QC)],
                lse[0:1, here], lse_d[0:1, here],
                weight_row(len_ref, flag_ref, head, first, True),
                kn, k2n, vn, buf[64:128, :], len_ref[0], pf, gf, x_ref, acc,
            )
            dq_buf[:, lanes(c * QC, QC)] = g.astype(jnp.bfloat16)
            for i in range(2):
                j = 2 * c + i
                start_to(
                    dq_buf.at[:, lanes(j * 128, 128)], dq.at[head], send2.at[j], recv2.at[head], 8 * half + j, b
                )
            return carry

        lax.fori_loop(0, 1024 // QC, chunk, 0)
        row = lax.broadcasted_iota(jnp.int32, (128, SEQ), 0)
        total = acc[...].T
        dkv_buf[...] = jnp.where(row < 64, total * 0.125, total).astype(jnp.bfloat16)

        def out3(i, carry):
            d = lax.rem(b + i, 16)
            start_to(dkv_buf.at[:, lanes(d * 128, 128)], dkv.at[hh], send3.at[d], recv3.at[hh], d, b)
            return carry

        lax.fori_loop(0, 16, out3, 0)

        def done2(j, carry):
            sent_to(
                dq_buf.at[:, lanes(j * 128, 128)], dq.at[head], send2.at[j], recv2.at[head], 8 * half + j, b
            )
            return carry

        lax.fori_loop(0, 8, done2, 0)

        def done3(d, carry):
            sent_to(dkv_buf.at[:, lanes(d * 128, 128)], dkv.at[hh], send3.at[d], recv3.at[hh], d, b)
            return carry

        lax.fori_loop(0, 16, done3, 0)

    def back2(h, carry):
        got(dq.at[h], recv2.at[h])
        return carry

    lax.fori_loop(0, 6, back2, 0)

    def back3(h, carry):
        got(dkv.at[h], recv3.at[h])
        return carry

    lax.fori_loop(0, 12, back3, 0)

    def done1(h, carry):
        sent_to(
            src.at[h], do_buf.at[:, lanes(lax.rem(b, 8) * 128, 128)],
            send1.at[h], recv1.at[lax.rem(b, 8)], owner_of(h + 6 * (b // 8)), b,
        )
        return carry

    lax.fori_loop(0, 6, done1, 0)


def teacher_backward_kernel(
    len_ref, flag_ref, src, buf, other, lse, lse_s, dqkv,
    do_buf, kn, k2n, vn, pf, gf, x_ref, acc, dq_buf, dkv_buf,
    send1, recv1, send2, recv2, send3, recv3,
):
    b, hh, owner = place()
    greet_group()

    def out1(j, carry):
        h = lax.rem(j + b, 12)
        start_to(src.at[h], do_buf.at[:, lanes(b * 128, 128)], send1.at[h], recv1.at[b], owner_of(h), b)
        return carry

    lax.fori_loop(0, 12, out1, 0)

    @pl.when(owner)
    def _():
        kn[...] = natural(buf[64:128, :])
        vn[...] = natural(buf[128:192, :])
        k2n[...] = natural(other[64:128, :])
        acc[...] = jnp.zeros_like(acc)

        def arrive(i, carry):
            got(do_buf.at[:, lanes(i * 128, 128)], recv1.at[i])
            return carry

        lax.fori_loop(0, 16, arrive, 0)

        def chunk(c, carry):
            first = c * QC
            here = lanes(first, QC)
            g = attn_backward(
                buf[0:64, here], other[0:64, here], do_buf[:, here],
                lse[0:1, here], lse_s[0:1, here],
                weight_row(len_ref, flag_ref, lax.rem(hh, 6), first, hh < 6),
                kn, k2n, vn, buf[64:128, :], len_ref[0], pf, gf, x_ref, acc,
            )
            dq_buf[:, here] = g.astype(jnp.bfloat16)
            for i in range(2):
                d = 2 * c + i
                start_to(
                    dq_buf.at[:, lanes(d * 128, 128)], dqkv.at[hh, 0:64], send2.at[d], recv2.at[hh], d, b
                )
            return carry

        lax.fori_loop(0, SEQ // QC, chunk, 0)
        row = lax.broadcasted_iota(jnp.int32, (128, SEQ), 0)
        total = acc[...].T
        dkv_buf[...] = jnp.where(row < 64, total * 0.125, total).astype(jnp.bfloat16)

        def out3(i, carry):
            d = lax.rem(b + i, 16)
            start_to(
                dkv_buf.at[:, lanes(d * 128, 128)], dqkv.at[hh, 64:192], send3.at[d], recv3.at[hh], d, b
            )
            return carry

        lax.fori_loop(0, 16, out3, 0)

        def done2(d, carry):
            sent_to(
                dq_buf.at[:, lanes(d * 128, 128)], dqkv.at[hh, 0:64], send2.at[d], recv2.at[hh], d, b
            )
            return carry

        lax.fori_loop(0, 16, done2, 0)

        def done3(d, carry):
            sent_to(
                dkv_buf.at[:, lanes(d * 128, 128)], dqkv.at[hh, 64:192], send3.at[d], recv3.at[hh], d, b
            )
            return carry

        lax.fori_loop(0, 16, done3, 0)

    def back(h, carry):
        got(dqkv.at[h, 0:64], recv2.at[h])
        got(dqkv.at[h, 64:192], recv3.at[h])
        return carry

    lax.fori_loop(0, 12, back, 0)

    def done1(h, carry):
        sent_to(src.at[h], do_buf.at[:, lanes(b * 128, 128)], send1.at[h], recv1.at[b], owner_of(h), b)
        return carry

    lax.fori_loop(0, 12, done1, 0)


SMEM = pl.BlockSpec(memory_space=pltpu.SMEM)
VMEM = pl.BlockSpec(memory_space=pltpu.VMEM)
DMA = pltpu.SemaphoreType.DMA
BF = jnp.bfloat16
F32 = jnp.float32


def remote_call(kernel, ident, outs, scratch, n_smem, args):
    return pl.pallas_call(
        kernel,
        out_shape=tuple(jax.ShapeDtypeStruct(s, t) for s, t in outs),
        in_specs=[SMEM] * n_smem + [VMEM] * (len(args) - n_smem),
        out_specs=tuple(VMEM for _ in outs),
        scratch_shapes=scratch,
        compiler_params=pltpu.CompilerParams(
            collective_id=ident, has_side_effects=True, vmem_limit_bytes=40 * MIB
        ),
    )(*args)


def attn_teacher_fwd(lengths, src):
    return remote_call(
        teacher_forward_kernel, 1,
        [((192, SEQ), BF), ((128, SEQ), BF), ((12, 64, 128), BF), ((8, SEQ), F32), ((8, SEQ), F32)],
        [
            pltpu.VMEM((64, SEQ), BF), pltpu.VMEM((SEQ, 64), BF),
            pltpu.VMEM((SEQ, QC), F32), pltpu.VMEM((SEQ, QC), BF),
            DMA((12,)), DMA((16,)), DMA((6,)), DMA((16,)), DMA((16,)), DMA((12,)), DMA((3,)),
        ],
        1, (lengths, src),
    )


def attn_student_fwd(lengths, src):
    return remote_call(
        student_forward_kernel, 2,
        [((192, SEQ), BF), ((6, 64, 128), BF), ((8, SEQ), F32)],
        [
            pltpu.VMEM((64, 1024), BF), pltpu.VMEM((SEQ, 64), BF),
            pltpu.VMEM((SEQ, QC), F32), pltpu.VMEM((SEQ, QC), BF),
            DMA((12,)), DMA((16,)), DMA((8,)), DMA((6,)), DMA((2,)),
        ],
        1, (lengths, src),
    )


def backward_scratch(nq, n1, r1, n2, r2):
    return [
        pltpu.VMEM((64, nq), BF),
        pltpu.VMEM((SEQ, 64), BF), pltpu.VMEM((SEQ, 64), BF), pltpu.VMEM((SEQ, 64), BF),
        pltpu.VMEM((SEQ, QC), F32), pltpu.VMEM((SEQ, QC), F32), pltpu.VMEM((SEQ, 2 * QC), BF),
        pltpu.VMEM((SEQ, 128), F32), pltpu.VMEM((64, nq), BF), pltpu.VMEM((128, SEQ), BF),
        DMA((n1,)), DMA((r1,)), DMA((n2,)), DMA((r2,)), DMA((16,)), DMA((12,)),
    ]


def attn_student_bwd(lengths, flags, src, buf, dist, lse, lse_d):
    return remote_call(
        student_backward_kernel, 3,
        [((6, 64, 128), BF), ((12, 128, 128), BF)],
        backward_scratch(1024, 6, 8, 8, 6),
        2, (lengths, flags, src, buf, dist, lse, lse_d),
    )


def attn_teacher_bwd(lengths, flags, src, buf, other, lse, lse_s):
    return remote_call(
        teacher_backward_kernel, 4,
        [((12, 192, 128), BF)],
        backward_scratch(SEQ, 12, 16, 16, 12),
        2, (lengths, flags, src, buf, other, lse, lse_s),
    )[0]


def layer_norm(values, norm_gain, norm_shift):
    center = values - jnp.mean(values, axis=-1, keepdims=True)
    spread = jnp.mean(center * center, axis=-1, keepdims=True)
    return center * lax.rsqrt(spread + 1e-06) * norm_gain + norm_shift


def gelu_exact(values):
    return jax.nn.gelu(values, approximate=False)


def outer_rows(left_side, right_side):
    return lax.dot_general(
        left_side, right_side, (((0,), (0,)), ((), ())), preferred_element_type=jnp.float32
    )


def times_transpose(left_side, right_side):
    return lax.dot_general(
        left_side, right_side, (((1,), (1,)), ((), ())), preferred_element_type=jnp.float32
    )


def qkv_forward(hidden_low, weight, bias_pair, head_span):
    joined = jnp.dot(hidden_low, weight, preferred_element_type=jnp.float32)
    bias = jnp.concatenate(
        [bias_pair[:head_span], jnp.zeros((head_span,), F32), bias_pair[head_span:]]
    )
    return (joined + bias).astype(BF)


def by_heads(flat, heads):
    return flat.reshape(128, -1, heads, 64).transpose(2, 1, 3, 0).reshape(heads, -1, 128)


def from_heads(blocks, parts):
    heads = blocks.shape[0]
    return blocks.reshape(heads, parts, 64, 128).transpose(3, 1, 0, 2).reshape(128, -1)


def dense_forward(residual, attended_low, out_weight, up_weight, down_weight, up_bias, vectors):
    first_sum = residual + (
        jnp.dot(attended_low, out_weight, preferred_element_type=jnp.float32) + vectors[0]
    )
    normed, first_back = jax.vjp(layer_norm, first_sum, vectors[1], vectors[2])
    normed_low = normed.astype(jnp.bfloat16)
    upward = jnp.dot(normed_low, up_weight, preferred_element_type=jnp.float32) + up_bias
    activated, gelu_back = jax.vjp(gelu_exact, upward)
    activated_low = activated.astype(jnp.bfloat16)
    second_sum = normed + (
        jnp.dot(activated_low, down_weight, preferred_element_type=jnp.float32) + vectors[3]
    )
    result, second_back = jax.vjp(layer_norm, second_sum, vectors[4], vectors[5])
    return (result, (attended_low, normed_low, activated_low, first_back, gelu_back, second_back))


def dense_backward(grad_result, kept, out_weight, up_weight, down_weight):
    attended_low, normed_low, activated_low, first_back, gelu_back, second_back = kept
    grad_second, grad_gain_two, grad_shift_two = second_back(grad_result)
    down_low = grad_second.astype(jnp.bfloat16)
    grad_down = outer_rows(down_low, activated_low)
    (grad_upward,) = gelu_back(times_transpose(down_low, down_weight))
    upward_low = grad_upward.astype(jnp.bfloat16)
    grad_up = outer_rows(normed_low, upward_low)
    grad_first, grad_gain_one, grad_shift_one = first_back(
        grad_second + times_transpose(upward_low, up_weight)
    )
    first_low = grad_first.astype(jnp.bfloat16)
    grad_out = outer_rows(first_low, attended_low)
    grad_attended = times_transpose(first_low, out_weight).astype(jnp.bfloat16)
    grad_vectors = jnp.stack(
        [
            jnp.sum(grad_first, axis=0),
            grad_gain_one,
            grad_shift_one,
            jnp.sum(grad_second, axis=0),
            grad_gain_two,
            grad_shift_two,
        ]
    )
    return (
        grad_first,
        grad_attended,
        (grad_out, grad_up, grad_down, jnp.sum(grad_upward, axis=0), grad_vectors),
    )


def qkv_backward(hidden_low, weight, joined):
    span = weight.shape[1] // 3
    low_sums = jnp.sum(joined.astype(jnp.float32), axis=0)
    grad_bias = jnp.concatenate([low_sums[:span], low_sums[2 * span :]])
    return (outer_rows(hidden_low, joined), grad_bias, times_transpose(joined, weight))


def per_device(
    inputs, aug_source, aug_flags, lengths, head_flags, cotangent,
    qkv_teacher, qv_bias_teacher, out_teacher, up_teacher, down_teacher, up_bias_teacher, vectors_teacher,
    qkv_student, qv_bias_student, out_student, up_student, down_student, up_bias_student, vectors_student,
):
    x_in = inputs[0]
    replaced = aug_flags[0] == 1
    chooser = jnp.logical_and(
        aug_source[0][:, None] == jnp.arange(128)[None, :], replaced[:, None]
    )
    taken = jnp.dot(chooser.astype(BF), x_in, preferred_element_type=F32)
    x0 = jnp.where(replaced[:, None], taken, x_in.astype(F32))
    x0_low = x0.astype(BF)
    qkv_t = qkv_forward(x0_low, qkv_teacher, qv_bias_teacher, 768)
    buf_t, dist, att_t, _, lse_d = (res_t := attn_teacher_fwd(lengths, by_heads(qkv_t, 12)))
    lse_t = res_t[3]
    hidden, kept_t = dense_forward(
        x0, from_heads(att_t, 1), out_teacher, up_teacher, down_teacher, up_bias_teacher, vectors_teacher
    )
    hidden_low = hidden.astype(BF)
    qkv_s = qkv_forward(hidden_low, qkv_student, qv_bias_student, 384)
    buf_s, att_s, lse_s = attn_student_fwd(lengths, by_heads(qkv_s, 6))
    output, kept_s = dense_forward(
        hidden, from_heads(att_s, 1), out_student, up_student, down_student, up_bias_student, vectors_student
    )
    grad_hidden, d_att_s, dense_s = dense_backward(
        cotangent[0].astype(F32), kept_s, out_student, up_student, down_student
    )
    dq_s, dkv_s = attn_student_bwd(lengths, head_flags, by_heads(d_att_s, 6), buf_s, dist, lse_s, lse_d)
    dkv_s = (dkv_s[:6].astype(F32) + dkv_s[6:].astype(F32)).astype(BF)
    joined_s = from_heads(jnp.concatenate([dq_s, dkv_s], axis=1), 3)
    g_qkv_s, g_bias_s, more = qkv_backward(hidden_low, qkv_student, joined_s)
    grad_x0, d_att_t, dense_t = dense_backward(
        grad_hidden + more, kept_t, out_teacher, up_teacher, down_teacher
    )
    dqkv_t = attn_teacher_bwd(lengths, head_flags, by_heads(d_att_t, 12), buf_t, buf_s, lse_t, lse_s)
    joined_t = from_heads(dqkv_t, 3)
    g_qkv_t, g_bias_t, more = qkv_backward(x0_low, qkv_teacher, joined_t)
    grad_aug = grad_x0 + more
    copied = lax.dot_general(
        chooser.astype(F32), grad_aug, (((0,), (0,)), ((), ())),
        precision=lax.Precision.HIGHEST, preferred_element_type=F32,
    )
    grad_inputs = jnp.where(replaced[:, None], 0.0, grad_aug) + copied
    small = jnp.concatenate(
        [
            g_bias_t.reshape(768, 2), dense_t[3].reshape(768, 4), dense_t[4].T,
            g_bias_s.reshape(768, 1), dense_s[3].reshape(768, 2), dense_s[4].T,
        ],
        axis=1,
    )
    wide = [g_qkv_t, dense_t[0], dense_t[1], dense_t[2], g_qkv_s, dense_s[0], dense_s[1], dense_s[2], small]
    cuts = [sum(w.shape[1] for w in wide[:i]) for i in range(10)]
    whole = jnp.concatenate([w.astype(BF) for w in wide], axis=1)
    mine = lax.psum_scatter(whole, ("dp", "blk"), scatter_dimension=0, tiled=True).astype(F32)
    parts = [mine[:, cuts[i] : cuts[i + 1]] for i in range(9)]
    tiny = parts[8]
    return (
        output[None], grad_inputs[None],
        parts[0], tiny[:, 0:2].reshape(12), parts[1].T, parts[2], parts[3].T,
        tiny[:, 2:6].reshape(24), tiny[:, 6:12].T,
        parts[4], tiny[:, 12:13].reshape(6), parts[5].T, parts[6], parts[7].T,
        tiny[:, 13:15].reshape(12), tiny[:, 15:21].T,
    )


def solution(mesh):
    both = ("dp", "blk")
    row, flat, col = P(both, None), P(both), P(None, both)
    tokens, marks = P("dp", "blk", None), P("dp", "blk")
    return jax.shard_map(
        per_device,
        mesh=mesh,
        in_specs=(tokens, marks, marks, P("dp"), P(), tokens) + (P(),) * 14,
        out_specs=(tokens, tokens) + (row, flat, col, row, col, flat, col) * 2,
        check_vma=False,
    )
```

```python
import jax
import jax.numpy as jnp
from jax import lax
from jax.experimental import pallas as pl
from jax.experimental.pallas import tpu as pltpu
from jax.sharding import PartitionSpec as P

MESH = pl.DeviceIdType.MESH
LOG2E = 1.4426950408889634
C2 = 0.125 * LOG2E
SEQ = 2048
QC = 256
KT = 256
NKT = SEQ // KT
MIB = 1 << 20


def dot(a, b):
    return jnp.dot(a, b, preferred_element_type=jnp.float32)


def place():
    b = lax.axis_index("blk")
    r = lax.rem(lax.rem(b, 4) - b // 4 + 7, 4)
    return b, 3 * (b // 4) + r, r < 3


def owner_of(hh):
    y = hh // 3
    return 4 * y + lax.rem(y + lax.rem(hh, 3) + 1, 4)


def greet_group():
    b = lax.axis_index("blk")
    sem = pltpu.get_barrier_semaphore()

    def hello(i, carry):
        pl.semaphore_signal(
            sem, inc=1, device_id={"blk": lax.rem(b + i, 16)}, device_id_type=MESH
        )
        return carry

    lax.fori_loop(1, 16, hello, 0)
    pl.semaphore_wait(sem, 15)


def copy_to(src, dst, send_sem, recv_sem, d):
    return pltpu.make_async_remote_copy(
        src_ref=src,
        dst_ref=dst,
        send_sem=send_sem,
        recv_sem=recv_sem,
        device_id={"blk": d},
        device_id_type=MESH,
    )


def start_to(src, dst, send_sem, recv_sem, d, b):
    @pl.when(d != b)
    def _():
        copy_to(src, dst, send_sem, recv_sem, d).start()

    @pl.when(d == b)
    def _():
        pltpu.make_async_copy(src, dst, recv_sem).start()


def sent_to(src, dst, send_sem, recv_sem, d, b):
    @pl.when(d != b)
    def _():
        copy_to(src, dst, send_sem, recv_sem, d).wait_send()


def got(dst, recv_sem):
    pltpu.make_async_copy(dst, dst, recv_sem).wait()


def lanes(start, size):
    return pl.ds(pl.multiple_of(start, 128), size)


def fold(v):
    return jnp.sum(v.reshape(v.shape[0] // 8, 8, v.shape[1]), axis=0)


def key_ok(length):
    rows = lax.broadcasted_iota(jnp.int32, (KT, QC), 0) + (SEQ - KT)
    return rows < length


def attn_forward(q_at, kn, vt, s_ref, p_ref, length):
    q = q_at
    m8 = jnp.full((8, QC), -3e38, jnp.float32)
    for t in range(NKT):
        s = dot(kn[t * KT : (t + 1) * KT, :], q)
        if t == NKT - 1:
            s = jnp.where(key_ok(length), s, -1e30)
        s_ref[t * KT : (t + 1) * KT, :] = s
        m8 = jnp.maximum(m8, jnp.max(s.reshape(KT // 8, 8, QC), axis=0))
    mc = jnp.max(m8, axis=0, keepdims=True) * C2
    l8 = jnp.zeros((8, QC), jnp.float32)
    for t in range(NKT):
        p = jnp.exp2(s_ref[t * KT : (t + 1) * KT, :] * C2 - mc)
        l8 = l8 + fold(p)
        p_ref[t * KT : (t + 1) * KT, :] = p.astype(jnp.bfloat16)
    total = jnp.sum(l8, axis=0, keepdims=True)
    o = dot(vt, p_ref[...]) / total
    return o, mc + jnp.log2(total)


def attn_backward(
    q, q2, do, lse, lse2, weight, kn, k2n, vn, kt, length, pf, gf, x_ref, acc
):
    d8 = jnp.zeros((8, QC), jnp.float32)
    ok = key_ok(length)
    for t in range(NKT):
        rows = slice(t * KT, (t + 1) * KT)
        p = jnp.exp2(dot(kn[rows, :], q) * C2 - lse)
        p2 = jnp.exp2(dot(k2n[rows, :], q2) * C2 - lse2)
        if t == NKT - 1:
            p = jnp.where(ok, p, 0.0)
            p2 = jnp.where(ok, p2, 0.0)
        g = dot(vn[rows, :], do) + weight * (p - p2)
        d8 = d8 + fold(p * g)
        pf[rows, :] = p
        gf[rows, :] = g
        x_ref[rows, QC:] = p.astype(jnp.bfloat16)
    delta = jnp.sum(d8, axis=0, keepdims=True)
    for t in range(NKT):
        rows = slice(t * KT, (t + 1) * KT)
        x_ref[rows, :QC] = (pf[rows, :] * (gf[rows, :] - delta)).astype(jnp.bfloat16)
    both = jnp.concatenate([q, do], axis=0).astype(jnp.float32).T
    col = lax.broadcasted_iota(jnp.int32, (QC, 128), 1)
    rhs = jnp.concatenate(
        [jnp.where(col < 64, both, 0.0), jnp.where(col < 64, 0.0, both)], axis=0
    ).astype(jnp.bfloat16)
    for t in range(NKT):
        rows = slice(t * KT, (t + 1) * KT)
        acc[rows, :] += dot(x_ref[rows, :], rhs)
    return dot(kt, x_ref[:, :QC]) * 0.125


def natural(x):
    return x.astype(jnp.float32).T.astype(jnp.bfloat16)


def teacher_forward_kernel(
    len_ref, src, buf, dist, att, lse, lse_d,
    o_buf, kn, s_ref, p_ref,
    send1, recv1, send2, recv2, send3, recv3, lse_sem,
):
    b, hh, owner = place()
    greet_group()

    def out1(j, carry):
        h = lax.rem(j + b, 12)
        start_to(src.at[h], buf.at[:, lanes(b * 128, 128)], send1.at[h], recv1.at[b], owner_of(h), b)
        return carry

    lax.fori_loop(0, 12, out1, 0)

    def out2(j, carry):
        h = lax.rem(j + b, 6)
        start_to(
            src.at[h, 0:128], dist.at[:, lanes(b * 128, 128)], send2.at[h], recv2.at[b], owner_of(h + 6), b
        )
        return carry

    lax.fori_loop(0, 6, out2, 0)

    @pl.when(owner)
    def _():
        def arrive(i, carry):
            got(buf.at[:, lanes(i * 128, 128)], recv1.at[i])
            return carry

        lax.fori_loop(0, 16, arrive, 0)
        kn[...] = natural(buf[64:128, :])
        length = len_ref[0]

        def chunk(c, carry):
            here = lanes(c * QC, QC)
            o, stat = attn_forward(buf[0:64, here], kn, buf[128:192, :], s_ref, p_ref, length)
            o_buf[:, here] = o.astype(jnp.bfloat16)
            lse[:, here] = jnp.broadcast_to(stat, (8, QC))
            for i in range(2):
                d = 2 * c + i
                start_to(
                    o_buf.at[:, lanes(d * 128, 128)], att.at[hh], send3.at[d], recv3.at[hh], d, b
                )
            return carry

        lax.fori_loop(0, SEQ // QC, chunk, 0)

        def done3(d, carry):
            sent_to(o_buf.at[:, lanes(d * 128, 128)], att.at[hh], send3.at[d], recv3.at[hh], d, b)
            return carry

        lax.fori_loop(0, 16, done3, 0)

    @pl.when(owner & (hh < 6))
    def _():
        lse_d[:, 0:1024] = lse[:, 0:1024]
        far = copy_to(
            lse.at[:, 1024:2048], lse_d.at[:, 1024:2048], lse_sem.at[0], lse_sem.at[1], owner_of(hh + 6)
        )
        far.start()
        pltpu.make_async_copy(buf.at[0:128], dist, lse_sem.at[2]).start()
        pltpu.make_async_copy(buf.at[0:128], dist, lse_sem.at[2]).wait()
        far.wait_send()

    @pl.when(owner & (hh >= 6))
    def _():
        def arrive(i, carry):
            got(dist.at[:, lanes(i * 128, 128)], recv2.at[i])
            return carry

        lax.fori_loop(0, 16, arrive, 0)
        got(lse_d.at[:, 1024:2048], lse_sem.at[1])

    def back(h, carry):
        got(att.at[h], recv3.at[h])
        return carry

    lax.fori_loop(0, 12, back, 0)

    def done1(h, carry):
        sent_to(src.at[h], buf.at[:, lanes(b * 128, 128)], send1.at[h], recv1.at[b], owner_of(h), b)
        return carry

    lax.fori_loop(0, 12, done1, 0)

    def done2(h, carry):
        sent_to(
            src.at[h, 0:128], dist.at[:, lanes(b * 128, 128)], send2.at[h], recv2.at[b], owner_of(h + 6), b
        )
        return carry

    lax.fori_loop(0, 6, done2, 0)


def student_forward_kernel(
    len_ref, src, buf, att, lse,
    o_buf, kn, s_ref, p_ref,
    send1, recv1, send3, recv3, lse_sem,
):
    b, hh, owner = place()
    half = hh // 6
    head = lax.rem(hh, 6)
    greet_group()

    def out1(j, carry):
        h = lax.rem(j + b, 12)
        start_to(
            src.at[lax.rem(h, 6)], buf.at[:, lanes(b * 128, 128)], send1.at[h], recv1.at[b], owner_of(h), b
        )
        return carry

    lax.fori_loop(0, 12, out1, 0)

    @pl.when(owner)
    def _():
        def arrive(i, carry):
            got(buf.at[:, lanes(i * 128, 128)], recv1.at[i])
            return carry

        lse[:, 0:1024] = jnp.full((8, 1024), 1e30, jnp.float32)
        lax.fori_loop(0, 16, arrive, 0)
        kn[...] = natural(buf[64:128, :])
        length = len_ref[0]

        def chunk(c, carry):
            here = lanes(half * 1024 + c * QC, QC)
            o, stat = attn_forward(buf[0:64, here], kn, buf[128:192, :], s_ref, p_ref, length)
            o_buf[:, lanes(c * QC, QC)] = o.astype(jnp.bfloat16)
            lse[:, here] = jnp.broadcast_to(stat, (8, QC))
            for i in range(2):
                j = 2 * c + i
                d = 8 * half + j
                start_to(
                    o_buf.at[:, lanes(j * 128, 128)], att.at[head], send3.at[j], recv3.at[head], d, b
                )
            return carry

        lax.fori_loop(0, 1024 // QC, chunk, 0)

        def done3(j, carry):
            d = 8 * half + j
            sent_to(o_buf.at[:, lanes(j * 128, 128)], att.at[head], send3.at[j], recv3.at[head], d, b)
            return carry

        lax.fori_loop(0, 8, done3, 0)

    @pl.when(owner & (hh >= 6))
    def _():
        far = copy_to(
            lse.at[:, 1024:2048], lse.at[:, 1024:2048], lse_sem.at[0], lse_sem.at[1], owner_of(hh - 6)
        )
        far.start()
        far.wait_send()

    @pl.when(owner & (hh < 6))
    def _():
        got(lse.at[:, 1024:2048], lse_sem.at[1])

    def back(h, carry):
        got(att.at[h], recv3.at[h])
        return carry

    lax.fori_loop(0, 6, back, 0)

    def done1(h, carry):
        sent_to(
            src.at[lax.rem(h, 6)], buf.at[:, lanes(b * 128, 128)], send1.at[h], recv1.at[b], owner_of(h), b
        )
        return carry

    lax.fori_loop(0, 12, done1, 0)


def weight_row(len_ref, flag_ref, head, first, use):
    q = lax.broadcasted_iota(jnp.int32, (1, QC), 1) + first
    factor = jnp.where(use, flag_ref[head].astype(jnp.float32) * (2.0 * SEQ), 0.0)
    return jnp.where(q < len_ref[0], factor, 0.0)


def student_backward_kernel(
    len_ref, flag_ref, src, buf, dist, lse, lse_d, dq, dkv,
    do_buf, kn, k2n, vn, pf, gf, x_ref, acc, dq_buf, dkv_buf,
    send1, recv1, send2, recv2, send3, recv3,
):
    b, hh, owner = place()
    half = hh // 6
    head = lax.rem(hh, 6)
    greet_group()

    def out1(j, carry):
        h = lax.rem(j + b, 6)
        start_to(
            src.at[h], do_buf.at[:, lanes(lax.rem(b, 8) * 128, 128)],
            send1.at[h], recv1.at[lax.rem(b, 8)], owner_of(h + 6 * (b // 8)), b,
        )
        return carry

    lax.fori_loop(0, 6, out1, 0)

    @pl.when(owner)
    def _():
        kn[...] = natural(buf[64:128, :])
        vn[...] = natural(buf[128:192, :])
        k2n[...] = natural(dist[64:128, :])
        acc[...] = jnp.zeros_like(acc)

        def arrive(i, carry):
            got(do_buf.at[:, lanes(i * 128, 128)], recv1.at[i])
            return carry

        lax.fori_loop(0, 8, arrive, 0)

        def chunk(c, carry):
            first = half * 1024 + c * QC
            here = lanes(first, QC)
            g = attn_backward(
                buf[0:64, here], dist[0:64, here], do_buf[:, lanes(c * QC, QC)],
                lse[0:1, here], lse_d[0:1, here],
                weight_row(len_ref, flag_ref, head, first, True),
                kn, k2n, vn, buf[64:128, :], len_ref[0], pf, gf, x_ref, acc,
            )
            dq_buf[:, lanes(c * QC, QC)] = g.astype(jnp.bfloat16)
            for i in range(2):
                j = 2 * c + i
                start_to(
                    dq_buf.at[:, lanes(j * 128, 128)], dq.at[head], send2.at[j], recv2.at[head], 8 * half + j, b
                )
            return carry

        lax.fori_loop(0, 1024 // QC, chunk, 0)
        row = lax.broadcasted_iota(jnp.int32, (128, SEQ), 0)
        total = acc[...].T
        dkv_buf[...] = jnp.where(row < 64, total * 0.125, total).astype(jnp.bfloat16)

        def out3(i, carry):
            d = lax.rem(b + i, 16)
            start_to(dkv_buf.at[:, lanes(d * 128, 128)], dkv.at[hh], send3.at[d], recv3.at[hh], d, b)
            return carry

        lax.fori_loop(0, 16, out3, 0)

        def done2(j, carry):
            sent_to(
                dq_buf.at[:, lanes(j * 128, 128)], dq.at[head], send2.at[j], recv2.at[head], 8 * half + j, b
            )
            return carry

        lax.fori_loop(0, 8, done2, 0)

        def done3(d, carry):
            sent_to(dkv_buf.at[:, lanes(d * 128, 128)], dkv.at[hh], send3.at[d], recv3.at[hh], d, b)
            return carry

        lax.fori_loop(0, 16, done3, 0)

    def back2(h, carry):
        got(dq.at[h], recv2.at[h])
        return carry

    lax.fori_loop(0, 6, back2, 0)

    def back3(h, carry):
        got(dkv.at[h], recv3.at[h])
        return carry

    lax.fori_loop(0, 12, back3, 0)

    def done1(h, carry):
        sent_to(
            src.at[h], do_buf.at[:, lanes(lax.rem(b, 8) * 128, 128)],
            send1.at[h], recv1.at[lax.rem(b, 8)], owner_of(h + 6 * (b // 8)), b,
        )
        return carry

    lax.fori_loop(0, 6, done1, 0)


def teacher_backward_kernel(
    len_ref, flag_ref, src, buf, other, lse, lse_s, dqkv,
    do_buf, kn, k2n, vn, pf, gf, x_ref, acc, dq_buf, dkv_buf,
    send1, recv1, send2, recv2, send3, recv3,
):
    b, hh, owner = place()
    greet_group()

    def out1(j, carry):
        h = lax.rem(j + b, 12)
        start_to(src.at[h], do_buf.at[:, lanes(b * 128, 128)], send1.at[h], recv1.at[b], owner_of(h), b)
        return carry

    lax.fori_loop(0, 12, out1, 0)

    @pl.when(owner)
    def _():
        kn[...] = natural(buf[64:128, :])
        vn[...] = natural(buf[128:192, :])
        k2n[...] = natural(other[64:128, :])
        acc[...] = jnp.zeros_like(acc)

        def arrive(i, carry):
            got(do_buf.at[:, lanes(i * 128, 128)], recv1.at[i])
            return carry

        lax.fori_loop(0, 16, arrive, 0)

        def chunk(c, carry):
            first = c * QC
            here = lanes(first, QC)
            g = attn_backward(
                buf[0:64, here], other[0:64, here], do_buf[:, here],
                lse[0:1, here], lse_s[0:1, here],
                weight_row(len_ref, flag_ref, lax.rem(hh, 6), first, hh < 6),
                kn, k2n, vn, buf[64:128, :], len_ref[0], pf, gf, x_ref, acc,
            )
            dq_buf[:, here] = g.astype(jnp.bfloat16)
            for i in range(2):
                d = 2 * c + i
                start_to(
                    dq_buf.at[:, lanes(d * 128, 128)], dqkv.at[hh, 0:64], send2.at[d], recv2.at[hh], d, b
                )
            return carry

        lax.fori_loop(0, SEQ // QC, chunk, 0)
        row = lax.broadcasted_iota(jnp.int32, (128, SEQ), 0)
        total = acc[...].T
        dkv_buf[...] = jnp.where(row < 64, total * 0.125, total).astype(jnp.bfloat16)

        def out3(i, carry):
            d = lax.rem(b + i, 16)
            start_to(
                dkv_buf.at[:, lanes(d * 128, 128)], dqkv.at[hh, 64:192], send3.at[d], recv3.at[hh], d, b
            )
            return carry

        lax.fori_loop(0, 16, out3, 0)

        def done2(d, carry):
            sent_to(
                dq_buf.at[:, lanes(d * 128, 128)], dqkv.at[hh, 0:64], send2.at[d], recv2.at[hh], d, b
            )
            return carry

        lax.fori_loop(0, 16, done2, 0)

        def done3(d, carry):
            sent_to(
                dkv_buf.at[:, lanes(d * 128, 128)], dqkv.at[hh, 64:192], send3.at[d], recv3.at[hh], d, b
            )
            return carry

        lax.fori_loop(0, 16, done3, 0)

    def back(h, carry):
        got(dqkv.at[h, 0:64], recv2.at[h])
        got(dqkv.at[h, 64:192], recv3.at[h])
        return carry

    lax.fori_loop(0, 12, back, 0)

    def done1(h, carry):
        sent_to(src.at[h], do_buf.at[:, lanes(b * 128, 128)], send1.at[h], recv1.at[b], owner_of(h), b)
        return carry

    lax.fori_loop(0, 12, done1, 0)


SMEM = pl.BlockSpec(memory_space=pltpu.SMEM)
VMEM = pl.BlockSpec(memory_space=pltpu.VMEM)
DMA = pltpu.SemaphoreType.DMA
BF = jnp.bfloat16
F32 = jnp.float32


def remote_call(kernel, ident, outs, scratch, n_smem, args):
    return pl.pallas_call(
        kernel,
        out_shape=tuple(jax.ShapeDtypeStruct(s, t) for s, t in outs),
        in_specs=[SMEM] * n_smem + [VMEM] * (len(args) - n_smem),
        out_specs=tuple(VMEM for _ in outs),
        scratch_shapes=scratch,
        compiler_params=pltpu.CompilerParams(
            collective_id=ident, has_side_effects=True, vmem_limit_bytes=40 * MIB
        ),
    )(*args)


def attn_teacher_fwd(lengths, src):
    return remote_call(
        teacher_forward_kernel, 1,
        [((192, SEQ), BF), ((128, SEQ), BF), ((12, 64, 128), BF), ((8, SEQ), F32), ((8, SEQ), F32)],
        [
            pltpu.VMEM((64, SEQ), BF), pltpu.VMEM((SEQ, 64), BF),
            pltpu.VMEM((SEQ, QC), F32), pltpu.VMEM((SEQ, QC), BF),
            DMA((12,)), DMA((16,)), DMA((6,)), DMA((16,)), DMA((16,)), DMA((12,)), DMA((3,)),
        ],
        1, (lengths, src),
    )


def attn_student_fwd(lengths, src):
    return remote_call(
        student_forward_kernel, 2,
        [((192, SEQ), BF), ((6, 64, 128), BF), ((8, SEQ), F32)],
        [
            pltpu.VMEM((64, 1024), BF), pltpu.VMEM((SEQ, 64), BF),
            pltpu.VMEM((SEQ, QC), F32), pltpu.VMEM((SEQ, QC), BF),
            DMA((12,)), DMA((16,)), DMA((8,)), DMA((6,)), DMA((2,)),
        ],
        1, (lengths, src),
    )


def backward_scratch(nq, n1, r1, n2, r2):
    return [
        pltpu.VMEM((64, nq), BF),
        pltpu.VMEM((SEQ, 64), BF), pltpu.VMEM((SEQ, 64), BF), pltpu.VMEM((SEQ, 64), BF),
        pltpu.VMEM((SEQ, QC), F32), pltpu.VMEM((SEQ, QC), F32), pltpu.VMEM((SEQ, 2 * QC), BF),
        pltpu.VMEM((SEQ, 128), F32), pltpu.VMEM((64, nq), BF), pltpu.VMEM((128, SEQ), BF),
        DMA((n1,)), DMA((r1,)), DMA((n2,)), DMA((r2,)), DMA((16,)), DMA((12,)),
    ]


def attn_student_bwd(lengths, flags, src, buf, dist, lse, lse_d):
    return remote_call(
        student_backward_kernel, 3,
        [((6, 64, 128), BF), ((12, 128, 128), BF)],
        backward_scratch(1024, 6, 8, 8, 6),
        2, (lengths, flags, src, buf, dist, lse, lse_d),
    )


def attn_teacher_bwd(lengths, flags, src, buf, other, lse, lse_s):
    return remote_call(
        teacher_backward_kernel, 4,
        [((12, 192, 128), BF)],
        backward_scratch(SEQ, 12, 16, 16, 12),
        2, (lengths, flags, src, buf, other, lse, lse_s),
    )[0]

CUTS = ((0, 12, 12), (12, 6, 6), (18, 2, 1), (20, 12, 12), (32, 5, 4), (37, 3, 3), (40, 9, 9), (49, 6, 6))
PARTS = ((0, 20), (20, 20), (40, 16))
MEMBERS = ((0, 1, 2), (3, 4, 5), (6, 7))
TILES = 56
WIDE = TILES * 128


def where_am_i():
    dp, blk = lax.axis_index("dp"), lax.axis_index("blk")
    return dp // 2, lax.rem(dp, 2), blk // 4, lax.rem(blk, 4)


def at_axis(axis, v):
    x, c, y, z = where_am_i()
    if axis == "x":
        return {"dp": 2 * v + c, "blk": 4 * y + z}
    if axis == "y":
        return {"dp": 2 * x + c, "blk": 4 * v + z}
    return {"dp": 2 * x + c, "blk": 4 * y + v}


def send_to(src, dst, send_sem, recv_sem, device):
    return pltpu.make_async_remote_copy(
        src_ref=src, dst_ref=dst, send_sem=send_sem, recv_sem=recv_sem,
        device_id=device, device_id_type=MESH,
    )


ORDERS = ("xyz", "yzx", "zxy")


def reduce_kernel(*refs):
    narrow, wide, small = refs[0:8], refs[8:16], refs[16]
    out = refs[17]
    (nt, cf, smp, pb, l1, a1, l2, a2, l3, a3,
     own_sem, n_send, n_recv, c_send, c_recv, s_sem,
     st_send, st_recv, f_send, f_recv) = refs[18:]
    x, c, y, z = where_am_i()
    here = {"x": x, "y": y, "z": z}
    dp, blk = 2 * x + c, 4 * y + z
    me = 16 * dp + blk
    partner = {"dp": 2 * x + 1 - c, "blk": blk}

    def holder(p, q, core):
        first, second = me // 32, lax.rem(me // 8, 4)
        at = dict(zip(ORDERS[p], (first, second, q)))
        return 2 * at["x"] + core, 4 * at["y"] + at["z"]

    def owner(p, k):
        i = 32 * here[ORDERS[p][0]] + 8 * here[ORDERS[p][1]] + k
        return i, {"dp": i // 16, "blk": lax.rem(i, 16)}

    barrier = pltpu.get_barrier_semaphore()
    pl.semaphore_signal(barrier, inc=1, device_id=partner, device_id_type=MESH)
    for axis in "xyz":
        for j in range(1, 4):
            pl.semaphore_signal(
                barrier, inc=1, device_id=at_axis(axis, lax.rem(here[axis] + j, 4)), device_id_type=MESH
            )
    for p in range(3):
        for q in range(4):
            for core in range(2):
                hd, hb = holder(p, q, core)

                pl.semaphore_signal(
                    barrier, inc=1, device_id={"dp": hd, "blk": hb}, device_id_type=MESH
                )
    pl.semaphore_wait(barrier, 34)

    small_copy = send_to(small, smp, s_sem.at[0], s_sem.at[1], partner)
    small_copy.start()
    n_copies, c_copies, own_copies = [], [], []
    for m, (first, count, step) in enumerate(CUTS):
        cols = slice(first * 128, (first + count) * 128)
        keep = pltpu.make_async_copy(
            wide[m].at[:, lanes(c * step * 128, count * 128)], cf.at[0:128, cols], own_sem.at[m]
        )
        keep.start()
        own_copies.append(keep)
        give = send_to(
            wide[m].at[:, lanes((1 - c) * step * 128, count * 128)], cf.at[128:256, cols],
            c_send.at[m], c_recv.at[m], partner,
        )
        give.start()
        c_copies.append(give)
        nt[m, :, 0:128] = narrow[m][...].T
        give = send_to(
            nt.at[m, :, 0:128], nt.at[m, :, 128:256], n_send.at[m], n_recv.at[m], partner
        )
        give.start()
        n_copies.append(give)

    def part_cols(p):
        return slice(PARTS[p][0] * 128, (PARTS[p][0] + PARTS[p][1]) * 128)

    def stage_copies(p, stage):
        axis = ORDERS[p][stage]
        copies = []
        for j in range(1, 4):
            v = lax.rem(here[axis] + j, 4)
            if stage == 0:
                src = pb.at[pl.ds(pl.multiple_of(192 * v, 16), 192), part_cols(p)]
                dst = l1.at[j - 1, :, part_cols(p)]
            elif stage == 1:
                src = a1.at[pl.ds(pl.multiple_of(48 * v, 16), 48), part_cols(p)]
                dst = l2.at[j - 1, :, part_cols(p)]
            else:
                q = PARTS[p][1] * 32
                src = a2.at[:, lanes(PARTS[p][0] * 128 + v * q, q)]
                dst = l3.at[j - 1, :, slice(PARTS[p][0] * 32, PARTS[p][0] * 32 + q)]
            n = 9 * stage + 3 * p + j - 1
            copies.append(send_to(src, dst, st_send.at[n], st_recv.at[n], at_axis(axis, v)))
        return copies

    copies = {}
    for p in range(3):
        for m in MEMBERS[p]:
            first, count, _ = CUTS[m]
            own_copies[m].wait()
            c_copies[m].wait_recv()
            n_copies[m].wait_recv()
            size = 3 if count % 3 == 0 else count

            def piece(i, carry, m=m, first=first, size=size):
                cols = lanes((first + i * size) * 128, size * 128)
                pb[:, cols] = dot(nt[m], cf[:, cols]).astype(BF)
                return carry

            lax.fori_loop(0, count // size, piece, 0)
        if p == 2:
            small_copy.wait_recv()
            pb[:, (TILES - 1) * 128 :] = (small[...].astype(F32) + smp[...].astype(F32)).astype(BF)
        copies[p, 0] = stage_copies(p, 0)
        for copy in copies[p, 0]:
            copy.start()

    for p in range(3):
        cols = part_cols(p)
        base = 192 * here[ORDERS[p][0]]
        for copy in copies[p, 0]:
            copy.wait_recv()

        def add1(r, carry, cols=cols, base=base):
            rows = pl.ds(pl.multiple_of(16 * r, 16), 16)
            own = pl.ds(pl.multiple_of(base + 16 * r, 16), 16)
            total = pb[own, cols].astype(F32)
            for j in range(3):
                total = total + l1[j, rows, cols].astype(F32)
            a1[rows, cols] = total.astype(BF)
            return carry

        lax.fori_loop(0, 12, add1, 0)
        copies[p, 1] = stage_copies(p, 1)
        for copy in copies[p, 1]:
            copy.start()

    for p in range(3):
        cols = part_cols(p)
        base = 48 * here[ORDERS[p][1]]
        for copy in copies[p, 1]:
            copy.wait_recv()

        def add2(r, carry, cols=cols, base=base):
            rows = pl.ds(pl.multiple_of(16 * r, 16), 16)
            own = pl.ds(pl.multiple_of(base + 16 * r, 16), 16)
            total = a1[own, cols].astype(F32)
            for j in range(3):
                total = total + l2[j, rows, cols].astype(F32)
            a2[rows, cols] = total.astype(BF)
            return carry

        lax.fori_loop(0, 3, add2, 0)
        copies[p, 2] = stage_copies(p, 2)
        for copy in copies[p, 2]:
            copy.start()

    for p in range(3):
        q = PARTS[p][1] * 32
        off = PARTS[p][0] * 32
        third = here[ORDERS[p][2]]
        for copy in copies[p, 2]:
            copy.wait_recv()
        total = a2[:, lanes(PARTS[p][0] * 128 + third * q, q)].astype(F32)
        for j in range(3):
            total = total + l3[j, :, off : off + q].astype(F32)
        for k in range(8):
            a3[k, 0:6, off : off + q] = total[6 * k : 6 * k + 6, :]

    def final(p, k):
        q = PARTS[p][1] * 32
        off = PARTS[p][0] * 32
        third = here[ORDERS[p][2]]
        i, device = owner(p, k)
        src = a3.at[k, :, slice(off, off + q)]
        dst = out.at[:, lanes((c * TILES + PARTS[p][0]) * 128 + third * q, q)]
        slot = f_recv.at[(c * 3 + p) * 4 + third]
        return i, src, dst, slot, send_to(src, dst, f_send.at[8 * p + k], slot, device)

    for p in range(3):
        for k in range(8):
            i, src, dst, slot, copy = final(p, k)

            @pl.when(i != me)
            def _():
                copy.start()

            @pl.when(i == me)
            def _():
                pltpu.make_async_copy(src, dst, slot).start()

    for core in range(2):
        for p in range(3):
            q = PARTS[p][1] * 32
            for third in range(4):
                start = (core * TILES + PARTS[p][0]) * 128 + third * q
                got(out.at[:, start : start + q], f_recv.at[(core * 3 + p) * 4 + third])
    for p in range(3):
        for k in range(8):
            i, src, dst, slot, copy = final(p, k)

            @pl.when(i != me)
            def _():
                copy.wait_send()
    small_copy.wait_send()
    for copy in n_copies + c_copies + sum(copies.values(), []):
        copy.wait_send()


def reduce_all(narrow, wide, small):
    return pl.pallas_call(
        reduce_kernel,
        out_shape=jax.ShapeDtypeStruct((8, 2 * WIDE), F32),
        in_specs=[VMEM] * 17,
        out_specs=VMEM,
        scratch_shapes=[
            pltpu.VMEM((8, 768, 256), BF), pltpu.VMEM((256, WIDE), BF), pltpu.VMEM((768, 128), BF),
            pltpu.VMEM((768, WIDE), BF), pltpu.VMEM((3, 192, WIDE), BF), pltpu.VMEM((192, WIDE), BF),
            pltpu.VMEM((3, 48, WIDE), BF), pltpu.VMEM((48, WIDE), BF),
            pltpu.VMEM((3, 48, WIDE // 4), BF), pltpu.VMEM((8, 8, WIDE // 4), F32),
            DMA((8,)), DMA((8,)), DMA((8,)), DMA((8,)), DMA((8,)), DMA((2,)),
            DMA((27,)), DMA((27,)), DMA((24,)), DMA((24,)),
        ],
        compiler_params=pltpu.CompilerParams(
            collective_id=5, has_side_effects=True, vmem_limit_bytes=56 * MIB
        ),
    )(*narrow, *wide, small)


def unpack_kernel(whole, *outs):
    def columns(m):
        first, count, step = CUTS[m]
        both = [whole[:, first * 128 : (first + count) * 128]]
        skip = count - step
        start = TILES + first + skip
        both.append(whole[:, start * 128 : (start + count - skip) * 128])
        return jnp.concatenate(both, axis=1)

    for m, o in ((6, 0), (0, 3), (4, 7), (1, 10)):
        outs[o][...] = columns(m)[0:6]
    for m, o in ((5, 2), (3, 4), (2, 9), (7, 11)):
        outs[o][...] = columns(m).T[:, 0:6]
    tiny = whole[:, (TILES - 1) * 128 : TILES * 128]
    outs[1][...] = tiny[0:6, 0:2]
    outs[5][...] = tiny[0:6, 2:6]
    outs[8][...] = tiny[0:6, 12:13]
    outs[12][...] = tiny[0:6, 13:15]
    turned = tiny.T
    outs[6][...] = turned[6:12, 0:6]
    outs[13][...] = turned[15:21, 0:6]


def unpack(whole):
    shapes = (
        (6, 2304), (6, 2), (768, 6), (6, 3072), (3072, 6), (6, 4), (6, 6),
        (6, 1152), (6, 1), (384, 6), (6, 1536), (1536, 6), (6, 2), (6, 6),
    )
    outs = list(
        pl.pallas_call(
            unpack_kernel,
            out_shape=tuple(jax.ShapeDtypeStruct(s, F32) for s in shapes),
            in_specs=[VMEM],
            out_specs=tuple(VMEM for _ in shapes),
            compiler_params=pltpu.CompilerParams(vmem_limit_bytes=40 * MIB),
        )(whole)
    )
    for i in (1, 5, 8, 12):
        outs[i] = outs[i].reshape(-1)
    return tuple(outs)


def layer_norm(values, norm_gain, norm_shift):
    center = values - jnp.mean(values, axis=-1, keepdims=True)
    spread = jnp.mean(center * center, axis=-1, keepdims=True)
    return center * lax.rsqrt(spread + 1e-06) * norm_gain + norm_shift


def gelu_exact(values):
    return jax.nn.gelu(values, approximate=False)


def outer_rows(left_side, right_side):
    return lax.dot_general(
        left_side, right_side, (((0,), (0,)), ((), ())), preferred_element_type=jnp.float32
    )


def times_transpose(left_side, right_side):
    return lax.dot_general(
        left_side, right_side, (((1,), (1,)), ((), ())), preferred_element_type=jnp.float32
    )


def qkv_forward(hidden_low, weight, bias_pair, head_span):
    joined = jnp.dot(hidden_low, weight, preferred_element_type=jnp.float32)
    bias = jnp.concatenate(
        [bias_pair[:head_span], jnp.zeros((head_span,), F32), bias_pair[head_span:]]
    )
    return (joined + bias).astype(BF)


def by_heads(flat, heads):
    return flat.reshape(128, -1, heads, 64).transpose(2, 1, 3, 0).reshape(heads, -1, 128)


def from_heads(blocks, parts):
    heads = blocks.shape[0]
    return blocks.reshape(heads, parts, 64, 128).transpose(3, 1, 0, 2).reshape(128, -1)


def dense_forward(residual, attended_low, out_weight, up_weight, down_weight, up_bias, vectors):
    first_sum = residual + (
        jnp.dot(attended_low, out_weight, preferred_element_type=jnp.float32) + vectors[0]
    )
    normed, first_back = jax.vjp(layer_norm, first_sum, vectors[1], vectors[2])
    normed_low = normed.astype(jnp.bfloat16)
    upward = jnp.dot(normed_low, up_weight, preferred_element_type=jnp.float32) + up_bias
    activated, gelu_back = jax.vjp(gelu_exact, upward)
    activated_low = activated.astype(jnp.bfloat16)
    second_sum = normed + (
        jnp.dot(activated_low, down_weight, preferred_element_type=jnp.float32) + vectors[3]
    )
    result, second_back = jax.vjp(layer_norm, second_sum, vectors[4], vectors[5])
    return (result, (attended_low, normed_low, activated_low, first_back, gelu_back, second_back))


def dense_backward(grad_result, kept, out_weight, up_weight, down_weight):
    attended_low, normed_low, activated_low, first_back, gelu_back, second_back = kept
    grad_second, grad_gain_two, grad_shift_two = second_back(grad_result)
    down_low = grad_second.astype(jnp.bfloat16)
    (grad_upward,) = gelu_back(times_transpose(down_low, down_weight))
    upward_low = grad_upward.astype(jnp.bfloat16)
    grad_first, grad_gain_one, grad_shift_one = first_back(
        grad_second + times_transpose(upward_low, up_weight)
    )
    first_low = grad_first.astype(jnp.bfloat16)
    grad_attended = times_transpose(first_low, out_weight).astype(jnp.bfloat16)
    grad_vectors = jnp.stack(
        [
            jnp.sum(grad_first, axis=0),
            grad_gain_one,
            grad_shift_one,
            jnp.sum(grad_second, axis=0),
            grad_gain_two,
            grad_shift_two,
        ]
    )
    return (
        grad_first,
        grad_attended,
        ((first_low, attended_low), (normed_low, upward_low), (down_low, activated_low), jnp.sum(grad_upward, axis=0), grad_vectors),
    )


def qkv_backward(hidden_low, weight, joined):
    span = weight.shape[1] // 3
    low_sums = jnp.sum(joined.astype(jnp.float32), axis=0)
    grad_bias = jnp.concatenate([low_sums[:span], low_sums[2 * span :]])
    return ((hidden_low, joined), grad_bias, times_transpose(joined, weight))


def per_device(
    inputs, aug_source, aug_flags, lengths, head_flags, cotangent,
    qkv_teacher, qv_bias_teacher, out_teacher, up_teacher, down_teacher, up_bias_teacher, vectors_teacher,
    qkv_student, qv_bias_student, out_student, up_student, down_student, up_bias_student, vectors_student,
):
    x_in = inputs[0]
    replaced = aug_flags[0] == 1
    chooser = jnp.logical_and(
        aug_source[0][:, None] == jnp.arange(128)[None, :], replaced[:, None]
    )
    taken = jnp.dot(chooser.astype(BF), x_in, preferred_element_type=F32)
    x0 = jnp.where(replaced[:, None], taken, x_in.astype(F32))
    x0_low = x0.astype(BF)
    qkv_t = qkv_forward(x0_low, qkv_teacher, qv_bias_teacher, 768)
    buf_t, dist, att_t, _, lse_d = (res_t := attn_teacher_fwd(lengths, by_heads(qkv_t, 12)))
    lse_t = res_t[3]
    hidden, kept_t = dense_forward(
        x0, from_heads(att_t, 1), out_teacher, up_teacher, down_teacher, up_bias_teacher, vectors_teacher
    )
    hidden_low = hidden.astype(BF)
    qkv_s = qkv_forward(hidden_low, qkv_student, qv_bias_student, 384)
    buf_s, att_s, lse_s = attn_student_fwd(lengths, by_heads(qkv_s, 6))
    output, kept_s = dense_forward(
        hidden, from_heads(att_s, 1), out_student, up_student, down_student, up_bias_student, vectors_student
    )
    grad_hidden, d_att_s, dense_s = dense_backward(
        cotangent[0].astype(F32), kept_s, out_student, up_student, down_student
    )
    dq_s, dkv_s = attn_student_bwd(lengths, head_flags, by_heads(d_att_s, 6), buf_s, dist, lse_s, lse_d)
    dkv_s = (dkv_s[:6].astype(F32) + dkv_s[6:].astype(F32)).astype(BF)
    joined_s = from_heads(jnp.concatenate([dq_s, dkv_s], axis=1), 3)
    g_qkv_s, g_bias_s, more = qkv_backward(hidden_low, qkv_student, joined_s)
    grad_x0, d_att_t, dense_t = dense_backward(
        grad_hidden + more, kept_t, out_teacher, up_teacher, down_teacher
    )
    dqkv_t = attn_teacher_bwd(lengths, head_flags, by_heads(d_att_t, 12), buf_t, buf_s, lse_t, lse_s)
    joined_t = from_heads(dqkv_t, 3)
    g_qkv_t, g_bias_t, more = qkv_backward(x0_low, qkv_teacher, joined_t)
    grad_aug = grad_x0 + more
    copied = lax.dot_general(
        chooser.astype(F32), grad_aug, (((0,), (0,)), ((), ())),
        precision=lax.Precision.HIGHEST, preferred_element_type=F32,
    )
    grad_inputs = jnp.where(replaced[:, None], 0.0, grad_aug) + copied
    small = jnp.concatenate(
        [
            g_bias_t.reshape(768, 2), dense_t[3].reshape(768, 4), dense_t[4].T,
            g_bias_s.reshape(768, 1), dense_s[3].reshape(768, 2), dense_s[4].T,
        ],
        axis=1,
    )
    small = jnp.pad(small, ((0, 0), (0, 107))).astype(BF)
    pairs = (dense_t[1], dense_s[1], dense_s[0], dense_t[2], g_qkv_s, dense_t[0], g_qkv_t, dense_s[2])
    whole = reduce_all([n for n, _ in pairs], [w for _, w in pairs], small)
    return (output[None], grad_inputs[None]) + unpack(whole)


def solution(mesh):
    both = ("dp", "blk")
    row, flat, col = P(both, None), P(both), P(None, both)
    tokens, marks = P("dp", "blk", None), P("dp", "blk")
    return jax.shard_map(
        per_device,
        mesh=mesh,
        in_specs=(tokens, marks, marks, P("dp"), P(), tokens) + (P(),) * 14,
        out_specs=(tokens, tokens) + (row, flat, col, row, col, flat, col) * 2,
        check_vma=False,
    )
```

```python
import jax
import jax.numpy as jnp
from jax import lax
from jax.experimental import pallas as pl
from jax.experimental.pallas import tpu as pltpu
from jax.sharding import PartitionSpec as P

MESH = pl.DeviceIdType.MESH
LOG2E = 1.4426950408889634
C2 = 0.125 * LOG2E
SEQ = 2048
QC = 256
KT = 256
NKT = SEQ // KT
MIB = 1 << 20


def dot(a, b):
    return jnp.dot(a, b, preferred_element_type=jnp.float32)


def place():
    b = lax.axis_index("blk")
    r = lax.rem(lax.rem(b, 4) - b // 4 + 7, 4)
    return b, 3 * (b // 4) + r, r < 3


def owner_of(hh):
    y = hh // 3
    return 4 * y + lax.rem(y + lax.rem(hh, 3) + 1, 4)


def copy_to(src, dst, send_sem, recv_sem, d):
    return pltpu.make_async_remote_copy(
        src_ref=src,
        dst_ref=dst,
        send_sem=send_sem,
        recv_sem=recv_sem,
        device_id={"blk": d},
        device_id_type=MESH,
    )


def start_to(src, dst, send_sem, recv_sem, d, b):
    @pl.when(d != b)
    def _():
        copy_to(src, dst, send_sem, recv_sem, d).start()

    @pl.when(d == b)
    def _():
        pltpu.make_async_copy(src, dst, recv_sem).start()


def sent_to(src, dst, send_sem, recv_sem, d, b):
    @pl.when(d != b)
    def _():
        copy_to(src, dst, send_sem, recv_sem, d).wait_send()


def got(dst, recv_sem):
    pltpu.make_async_copy(dst, dst, recv_sem).wait()


def lanes(start, size):
    return pl.ds(pl.multiple_of(start, 128), size)


def fold(v):
    return jnp.sum(v.reshape(v.shape[0] // 8, 8, v.shape[1]), axis=0)


def key_ok(length):
    rows = lax.broadcasted_iota(jnp.int32, (KT, QC), 0) + (SEQ - KT)
    return rows < length


def natural(x):
    return x.astype(jnp.float32).T.astype(jnp.bfloat16)


def weight_row(len_ref, flag_ref, head, first, use):
    q = lax.broadcasted_iota(jnp.int32, (1, QC), 1) + first
    factor = jnp.where(use, flag_ref[head].astype(jnp.float32) * (2.0 * SEQ), 0.0)
    return jnp.where(q < len_ref[0], factor, 0.0)


SMEM = pl.BlockSpec(memory_space=pltpu.SMEM)
VMEM = pl.BlockSpec(memory_space=pltpu.VMEM)
DMA = pltpu.SemaphoreType.DMA
BF = jnp.bfloat16
F32 = jnp.float32


SQRT_HALF = 0.7071067811865476
INV_SQRT_2PI = 0.3989422804014327


def dot_t(a, b):
    return lax.dot_general(a, b, (((1,), (1,)), ((), ())), preferred_element_type=F32)


def norm_forward(v, gain, shift):
    center = v - jnp.mean(v, axis=-1, keepdims=True)
    scale = lax.rsqrt(jnp.mean(center * center, axis=-1, keepdims=True) + 1e-06)
    unit = center * scale
    return unit * gain + shift, unit, scale


def norm_backward(grad, gain, unit, scale):
    scaled = grad * gain
    mean_one = jnp.mean(scaled, axis=-1, keepdims=True)
    mean_two = jnp.mean(scaled * unit, axis=-1, keepdims=True)
    return (
        (scaled - mean_one - unit * mean_two) * scale,
        jnp.sum(grad * unit, axis=0, keepdims=True),
        jnp.sum(grad, axis=0, keepdims=True),
    )


def qkv_blocks(low, w, bias, src, heads):
    span = heads * 64
    for part in range(3):
        joint = dot(low, w[:, part * span : (part + 1) * span])
        if part != 1:
            first = 0 if part == 0 else span
            joint = joint + bias[:, first : first + span]
        src[:, part * 64 : (part + 1) * 64, :] = joint.T.astype(BF).reshape(heads, 64, 128)


def dense_up(residual, attended, w_out, w_up, w_down, up_bias, vec, act, slope, unit1, scale1, normed_low):
    ff = up_bias.shape[1]
    first = residual + dot(attended, w_out) + vec[0:1, :]
    normed, unit, scale = norm_forward(first, vec[1:2, :], vec[2:3, :])
    unit1[...] = unit
    scale1[...] = jnp.broadcast_to(scale, (128, 128))
    low = normed.astype(BF)
    normed_low[...] = low
    step = 512
    for j in range(ff // step):
        cols = slice(j * step, (j + 1) * step)
        u = dot(low, w_up[:, cols]) + up_bias[:, cols]
        cdf = 0.5 + 0.5 * lax.erf(u * SQRT_HALF)
        act[:, cols] = (u * cdf).astype(BF)
        slope[:, cols] = (cdf + u * (jnp.exp(-0.5 * u * u) * INV_SQRT_2PI)).astype(slope.dtype)
    second = normed + dot(act[...], w_down) + vec[3:4, :]
    return norm_forward(second, vec[4:5, :], vec[5:6, :])


def dense_down(grad, unit2, scale2, unit1, scale1, w_out, w_up, w_down, vec, slope, gu, g2r, g1r, sums, row):
    ff = w_up.shape[1]
    g2, gain_two, shift_two = norm_backward(grad, vec[4:5, :], unit2, scale2)
    low2 = g2.astype(BF)
    g2r[...] = low2
    step = 512
    for j in range(ff // step):
        cols = slice(j * step, (j + 1) * step)
        g = dot_t(low2, w_down[cols, :]) * slope[:, cols].astype(F32)
        gu[:, cols] = g.astype(BF)
        total = jnp.sum(g, axis=0, keepdims=True)
        done = 0
        while done < step:
            at = j * step + done
            size = min(step - done, 768 - at % 768)
            sums[row + 6 + at // 768 : row + 7 + at // 768, at % 768 : at % 768 + size] = total[:, done : done + size]
            done += size
    g1, gain_one, shift_one = norm_backward(g2 + dot_t(gu[...], w_up[...]), vec[1:2, :], unit1, scale1)
    low1 = g1.astype(BF)
    g1r[...] = low1
    rows = (
        jnp.sum(g1, axis=0, keepdims=True), gain_one, shift_one,
        jnp.sum(g2, axis=0, keepdims=True), gain_two, shift_two,
    )
    for i, value in enumerate(rows):
        sums[row + i : row + i + 1, :] = value
    return g1, dot_t(low1, w_out[...])


def load_all(pairs, sem):
    copies = [pltpu.make_async_copy(a, b, sem.at[i]) for i, (a, b) in enumerate(pairs)]
    for copy in copies:
        copy.start()
    return copies


def forward_stage(c_score, c_exp, c_out, do, par, q_at, kn, v_ref, s_ref, p_ref, st, put, length):
    if do[0]:
        q = q_at(c_score)
    m8 = jnp.full((8, QC), -3e38, F32)
    l8 = jnp.zeros((8, QC), F32)
    out = jnp.zeros((64, QC), F32)
    top = st[1 - par, 0:1, :]
    for t in range(NKT):
        rows = slice(t * KT, (t + 1) * KT)
        if do[0]:
            s = dot(kn[rows, :], q)
            if t == NKT - 1:
                s = jnp.where(key_ok(length), s, -1e30)
            s_ref[par, rows, :] = s
            m8 = jnp.maximum(m8, jnp.max(s.reshape(KT // 8, 8, QC), axis=0))
        if do[1]:
            p = jnp.exp2(s_ref[1 - par, rows, :] * C2 - top)
            l8 = l8 + fold(p)
            p_ref[1 - par, rows, :] = p.astype(BF)
        if do[2]:
            out = out + dot(v_ref[128:192, rows], p_ref[par, rows, :])
    if do[2]:
        put(c_out, out / st[2 + par, 0:1, :], st[4 + par, 0:1, :])
    if do[1]:
        total = jnp.sum(l8, axis=0, keepdims=True)
        st[3 - par] = jnp.broadcast_to(total, (8, QC))
        st[5 - par] = jnp.broadcast_to(top + jnp.log2(total), (8, QC))
    if do[0]:
        st[par] = jnp.broadcast_to(jnp.max(m8, axis=0, keepdims=True) * C2, (8, QC))


def forward_chunks(n, *rest):
    forward_stage(0, 0, 0, (1, 0, 0), 0, *rest)
    forward_stage(1, 0, 0, (1, 1, 0), 1, *rest)

    def body(i, carry):
        forward_stage(2 * i, 2 * i - 1, 2 * i - 2, (1, 1, 1), 0, *rest)
        forward_stage(2 * i + 1, 2 * i, 2 * i - 1, (1, 1, 1), 1, *rest)
        return carry

    lax.fori_loop(1, n // 2, body, 0)
    forward_stage(0, n - 1, n - 2, (0, 1, 1), 0, *rest)
    forward_stage(0, 0, n - 1, (0, 0, 1), 1, *rest)


def backward_chunk(c, prev, par, at, kn, k2n, vn, kt_ref, length, pf, gf, x_ref, acc, put):
    q, q2, do, lse, lse2, weight = at(c)
    pq, _, pdo, _, _, _ = at(prev)
    both = jnp.concatenate([pq, pdo], axis=0).astype(F32).T
    col = lax.broadcasted_iota(jnp.int32, (QC, 128), 1)
    rhs = jnp.concatenate(
        [jnp.where(col < 64, both, 0.0), jnp.where(col < 64, 0.0, both)], axis=0
    ).astype(BF)
    d8 = jnp.zeros((8, QC), F32)
    dq = jnp.zeros((64, QC), F32)
    for t in range(NKT):
        rows = slice(t * KT, (t + 1) * KT)
        p = jnp.exp2(dot(kn[rows, :], q) * C2 - lse)
        p2 = jnp.exp2(dot(k2n[rows, :], q2) * C2 - lse2)
        if t == NKT - 1:
            ok = key_ok(length)
            p = jnp.where(ok, p, 0.0)
            p2 = jnp.where(ok, p2, 0.0)
        g = dot(vn[rows, :], do) + weight * (p - p2)
        d8 = d8 + fold(p * g)
        pf[rows, :] = p
        gf[rows, :] = g
        x_ref[par, rows, QC:] = p.astype(BF)
        acc[rows, :] += dot(x_ref[1 - par, rows, :], rhs)
        dq = dq + dot(kt_ref[64:128, rows], x_ref[1 - par, rows, :QC])
    put(prev, dq * 0.125)
    delta = jnp.sum(d8, axis=0, keepdims=True)
    for t in range(NKT):
        rows = slice(t * KT, (t + 1) * KT)
        x_ref[par, rows, :QC] = (pf[rows, :] * (gf[rows, :] - delta)).astype(BF)


def backward_last(prev, par, at, kt_ref, x_ref, acc, put):
    pq, _, pdo, _, _, _ = at(prev)
    both = jnp.concatenate([pq, pdo], axis=0).astype(F32).T
    col = lax.broadcasted_iota(jnp.int32, (QC, 128), 1)
    rhs = jnp.concatenate(
        [jnp.where(col < 64, both, 0.0), jnp.where(col < 64, 0.0, both)], axis=0
    ).astype(BF)
    dq = jnp.zeros((64, QC), F32)
    for t in range(NKT):
        rows = slice(t * KT, (t + 1) * KT)
        acc[rows, :] += dot(x_ref[par, rows, :], rhs)
        dq = dq + dot(kt_ref[64:128, rows], x_ref[par, rows, :QC])
    put(prev, dq * 0.125)


def back_blocks(acc, dkv_buf):
    row = lax.broadcasted_iota(jnp.int32, (128, SEQ), 0)
    total = acc[...].T
    dkv_buf[...] = jnp.where(row < 64, total * 0.125, total).astype(BF)


def natural_wide(blocks):
    return blocks.astype(F32).T.astype(BF)


def loop(n, body):
    def step(i, carry):
        body(i)
        return carry

    lax.fori_loop(0, n, step, 0)


def greet_start():
    b = lax.axis_index("blk")
    sem = pltpu.get_barrier_semaphore()
    loop(15, lambda i: pl.semaphore_signal(
        sem, inc=1, device_id={"blk": lax.rem(b + 1 + i, 16)}, device_id_type=MESH
    ))


def greet_end():
    pl.semaphore_wait(pltpu.get_barrier_semaphore(), 15)


def forward_kernel(
    len_ref, x_in, source, flags, cot,
    w_qkv_t, w_out_t, w_up_t, w_down_t, w_qkv_s, w_out_s, w_up_s, w_down_s,
    bias_t, upb_t, vec_t, bias_s, upb_s, vec_s,
    output, buf_t, dist, buf_s, lse_t, lse_d, lse_s,
    x0_low, normed_low_t, hidden_low, normed_low_s, g1r_s, g2r_s,
    att_t, act_t, att_s, act_s, gu_s,
    slope_t, unit1_t, scale1_t, unit2_t, scale2_t, g1_s, datt_s, sums,
    v_qkv_t, v_out_t, v_up_t, v_down_t, v_qkv_s, v_out_s, v_up_s, v_down_s,
    x0_ref, src_t, src_s, land_t, land_s, o_t, o_s, kn, s_ref, p_ref, st,
    slope_s, unit1_s, scale1_s,
    w_sem, t_send, t_recv, d_send, d_recv, a_send, a_recv, lse_sem,
    s_send, s_recv, b_send, b_recv, local_sem,
):
    b, hh, owner = place()
    half, head = hh // 6, lax.rem(hh, 6)
    greet_start()
    weights = load_all(
        [
            (w_qkv_t, v_qkv_t), (w_out_t, v_out_t), (w_up_t, v_up_t), (w_down_t, v_down_t),
            (w_qkv_s, v_qkv_s), (w_out_s, v_out_s), (w_up_s, v_up_s), (w_down_s, v_down_s),
        ],
        w_sem,
    )
    length = len_ref[0]
    replaced = flags[...] == 1
    place_of = lax.broadcasted_iota(jnp.int32, (128, 128), 0)
    turned = jnp.where((place_of == source[...]) & replaced, 1.0, 0.0)
    chooser = turned.T
    taken = dot(chooser.astype(BF), x_in[...])
    x0 = jnp.where(jnp.sum(chooser, axis=1, keepdims=True) > 0.5, taken, x_in[...].astype(F32))
    x0_ref[...] = x0
    low = x0.astype(BF)
    x0_low[...] = low
    weights[0].wait()
    qkv_blocks(low, v_qkv_t, bias_t, src_t, 12)
    greet_end()

    mine = lanes(b * 128, 128)

    def t_copy(h):
        return src_t.at[h], buf_t.at[:, mine], t_send.at[h], t_recv.at[b], owner_of(h), b

    def d_copy(h):
        return src_t.at[h, 0:128], dist.at[:, mine], d_send.at[h], d_recv.at[b], owner_of(h + 6), b

    loop(12, lambda j: start_to(*t_copy(lax.rem(j + b, 12))))
    loop(6, lambda j: start_to(*d_copy(lax.rem(j + b, 6))))

    def a_copy(d):
        return o_t.at[:, lanes(d * 128, 128)], land_t.at[hh], a_send.at[d], a_recv.at[hh], d, b

    @pl.when(owner)
    def _():
        loop(16, lambda i: got(buf_t.at[:, lanes(i * 128, 128)], t_recv.at[i]))
        kn[...] = natural(buf_t[64:128, :])

        def put(c, o, stat):
            here = lanes(c * QC, QC)
            o_t[:, here] = o.astype(BF)
            lse_t[:, here] = jnp.broadcast_to(stat, (8, QC))
            for i in range(2):
                start_to(*a_copy(2 * c + i))

        forward_chunks(
            SEQ // QC, lambda c: buf_t[0:64, lanes(c * QC, QC)], kn, buf_t, s_ref, p_ref, st, put, length
        )

    @pl.when(owner & (hh < 6))
    def _():
        lse_d[:, 0:1024] = lse_t[:, 0:1024]
        copy_to(
            lse_t.at[:, 1024:2048], lse_d.at[:, 1024:2048], lse_sem.at[0], lse_sem.at[1], owner_of(hh + 6)
        ).start()
        pltpu.make_async_copy(buf_t.at[0:128], dist, local_sem.at[0]).start()

    loop(12, lambda h: got(land_t.at[h], a_recv.at[h]))
    att_t[...] = natural_wide(land_t[...].reshape(768, 128))
    for i in (1, 2, 3):
        weights[i].wait()
    hidden, unit, scale = dense_up(
        x0_ref[...], att_t[...], v_out_t[...], v_up_t, v_down_t[...], upb_t, vec_t,
        act_t, slope_t, unit1_t, scale1_t, normed_low_t,
    )
    unit2_t[...] = unit
    scale2_t[...] = jnp.broadcast_to(scale, (128, 128))
    x0_ref[...] = hidden
    low = hidden.astype(BF)
    hidden_low[...] = low
    weights[4].wait()
    qkv_blocks(low, v_qkv_s, bias_s, src_s, 6)

    def s_copy(h):
        return src_s.at[lax.rem(h, 6)], buf_s.at[:, mine], s_send.at[h], s_recv.at[b], owner_of(h), b

    loop(12, lambda j: start_to(*s_copy(lax.rem(j + b, 12))))

    def b_copy(j):
        return o_s.at[:, lanes(j * 128, 128)], land_s.at[head], b_send.at[j], b_recv.at[head], 8 * half + j, b

    @pl.when(owner)
    def _():
        lse_s[:, 0:1024] = jnp.full((8, 1024), 1e30, F32)
        loop(16, lambda i: got(buf_s.at[:, lanes(i * 128, 128)], s_recv.at[i]))
        kn[...] = natural(buf_s[64:128, :])

        def put(c, o, stat):
            o_s[:, lanes(c * QC, QC)] = o.astype(BF)
            lse_s[:, lanes(half * 1024 + c * QC, QC)] = jnp.broadcast_to(stat, (8, QC))
            for i in range(2):
                start_to(*b_copy(2 * c + i))

        forward_chunks(
            1024 // QC, lambda c: buf_s[0:64, lanes(half * 1024 + c * QC, QC)],
            kn, buf_s, s_ref, p_ref, st, put, length,
        )

    @pl.when(owner & (hh >= 6))
    def _():
        copy_to(
            lse_s.at[:, 1024:2048], lse_s.at[:, 1024:2048], lse_sem.at[2], lse_sem.at[3], owner_of(hh - 6)
        ).start()

    loop(6, lambda h: got(land_s.at[h], b_recv.at[h]))
    att_s[...] = natural_wide(land_s[...].reshape(384, 128))
    for i in (5, 6, 7):
        weights[i].wait()
    result, unit, scale = dense_up(
        x0_ref[...], att_s[...], v_out_s[...], v_up_s, v_down_s[...], upb_s, vec_s,
        act_s, slope_s, unit1_s, scale1_s, normed_low_s,
    )
    output[...] = result
    sums[...] = jnp.zeros((24, 768), F32)
    g1, datt = dense_down(
        cot[...].astype(F32), unit, scale, unit1_s[...], scale1_s[:, 0:1],
        v_out_s, v_up_s, v_down_s, vec_s, slope_s, gu_s, g2r_s, g1r_s, sums, 12,
    )
    g1_s[...] = g1
    datt_s[...] = datt.T.astype(BF).reshape(6, 64, 128)

    @pl.when(owner)
    def _():
        loop(16, lambda d: sent_to(*a_copy(d)))
        loop(8, lambda j: sent_to(*b_copy(j)))

    @pl.when(owner & (hh < 6))
    def _():
        copy_to(
            lse_t.at[:, 1024:2048], lse_d.at[:, 1024:2048], lse_sem.at[0], lse_sem.at[1], owner_of(hh + 6)
        ).wait_send()
        pltpu.make_async_copy(buf_t.at[0:128], dist, local_sem.at[0]).wait()
        got(lse_s.at[:, 1024:2048], lse_sem.at[3])

    @pl.when(owner & (hh >= 6))
    def _():
        loop(16, lambda i: got(dist.at[:, lanes(i * 128, 128)], d_recv.at[i]))
        got(lse_d.at[:, 1024:2048], lse_sem.at[1])
        copy_to(
            lse_s.at[:, 1024:2048], lse_s.at[:, 1024:2048], lse_sem.at[2], lse_sem.at[3], owner_of(hh - 6)
        ).wait_send()

    loop(12, lambda h: sent_to(*t_copy(h)))
    loop(6, lambda h: sent_to(*d_copy(h)))
    loop(12, lambda h: sent_to(*s_copy(h)))


def backward_kernel(
    len_ref, flag_ref, source, flags,
    w_qkv_s, w_down_t, w_up_t, w_out_t, w_qkv_t, vec_t,
    buf_t, dist, buf_s, lse_t, lse_d, lse_s,
    slope_t, unit1_t, scale1_t, unit2_t, scale2_t, g1_s, datt_s, sums_s,
    grad_in, joined_t, joined_s, gu_t, g1r_t, g2r_t, sums,
    v_qkv_s, v_down_t, v_up_t, v_out_t, v_qkv_t,
    src_t, do_s, do_t, dq_s, dkv_s, dqkv_t, dq_buf, dq_buf2, dkv_buf, dkv_buf2,
    kn, k2n, vn, pf, gf, x_ref, acc, g1_ref,
    w_sem, s1, r1, s2, r2, s3, r3, s4, r4, s5, r5, s6, r6,
):
    b, hh, owner = place()
    half, head = hh // 6, lax.rem(hh, 6)
    greet_start()
    weights = load_all(
        [(w_qkv_s, v_qkv_s), (w_down_t, v_down_t), (w_up_t, v_up_t), (w_out_t, v_out_t), (w_qkv_t, v_qkv_t)],
        w_sem,
    )
    length = len_ref[0]
    greet_end()

    def c1(h):
        return (
            datt_s.at[h], do_s.at[:, lanes(lax.rem(b, 8) * 128, 128)],
            s1.at[h], r1.at[lax.rem(b, 8)], owner_of(h + 6 * (b // 8)), b,
        )

    def c2(j):
        return dq_buf.at[:, lanes(j * 128, 128)], dq_s.at[head], s2.at[j], r2.at[head], 8 * half + j, b

    def c3(d):
        return dkv_buf.at[:, lanes(d * 128, 128)], dkv_s.at[hh], s3.at[d], r3.at[hh], d, b

    def c4(h):
        return src_t.at[h], do_t.at[:, lanes(b * 128, 128)], s4.at[h], r4.at[b], owner_of(h), b

    def c5(d):
        return dq_buf2.at[:, lanes(d * 128, 128)], dqkv_t.at[hh, 0:64], s5.at[d], r5.at[hh], d, b

    def c6(d):
        return dkv_buf2.at[:, lanes(d * 128, 128)], dqkv_t.at[hh, 64:192], s6.at[d], r6.at[hh], d, b

    def run_chunks(n, at, kt_ref, put):
        acc[...] = jnp.zeros_like(acc)
        x_ref[1] = jnp.zeros((SEQ, 2 * QC), BF)
        rest = (at, kn, k2n, vn, kt_ref, length, pf, gf, x_ref, acc)

        def pair(i):
            backward_chunk(
                2 * i, jnp.maximum(2 * i - 1, 0), 0, *rest, lambda c, g: put(c, g, i > 0)
            )
            backward_chunk(2 * i + 1, 2 * i, 1, *rest, lambda c, g: put(c, g, True))

        loop(n // 2, pair)
        backward_last(n - 1, 1, at, kt_ref, x_ref, acc, lambda c, g: put(c, g, True))

    def send_pair(copy, c, real):
        if real is True:
            for i in range(2):
                start_to(*copy(2 * c + i))
        else:
            @pl.when(real)
            def _():
                for i in range(2):
                    start_to(*copy(2 * c + i))

    loop(6, lambda j: start_to(*c1(lax.rem(j + b, 6))))

    @pl.when(owner)
    def _():
        kn[...] = natural(buf_s[64:128, :])
        vn[...] = natural(buf_s[128:192, :])
        k2n[...] = natural(dist[64:128, :])
        loop(8, lambda i: got(do_s.at[:, lanes(i * 128, 128)], r1.at[i]))

        def at(c):
            first = half * 1024 + c * QC
            here = lanes(first, QC)
            return (
                buf_s[0:64, here], dist[0:64, here], do_s[:, lanes(c * QC, QC)],
                lse_s[0:1, here], lse_d[0:1, here], weight_row(len_ref, flag_ref, head, first, True),
            )

        def put(c, g, real):
            dq_buf[:, lanes(c * QC, QC)] = g.astype(BF)
            send_pair(c2, c, real)

        run_chunks(1024 // QC, at, buf_s, put)
        back_blocks(acc, dkv_buf)
        loop(16, lambda i: start_to(*c3(lax.rem(b + i, 16))))

    loop(6, lambda h: got(dq_s.at[h], r2.at[h]))
    loop(12, lambda h: got(dkv_s.at[h], r3.at[h]))
    joined_s[:, 0:384] = natural_wide(dq_s[...].reshape(384, 128))
    for part in range(2):
        rows = slice(64 * part, 64 * part + 64)
        both = dkv_s[0:6, rows, :].astype(F32) + dkv_s[6:12, rows, :].astype(F32)
        joined_s[:, 384 * (part + 1) : 384 * (part + 2)] = both.reshape(384, 128).T.astype(BF)
    sums[...] = sums_s[...]
    low_sums = jnp.sum(joined_s[...].astype(F32), axis=0, keepdims=True)
    sums[20:21, 0:384] = low_sums[:, 0:384]
    sums[20:21, 384:768] = low_sums[:, 768:1152]
    weights[0].wait()
    grad_hidden = g1_s[...] + dot_t(joined_s[...], v_qkv_s[...])
    for i in (1, 2, 3):
        weights[i].wait()
    g1, datt = dense_down(
        grad_hidden, unit2_t[...], scale2_t[:, 0:1], unit1_t[...], scale1_t[:, 0:1],
        v_out_t, v_up_t, v_down_t, vec_t, slope_t, gu_t, g2r_t, g1r_t, sums, 0,
    )
    g1_ref[...] = g1
    src_t[...] = datt.T.astype(BF).reshape(12, 64, 128)
    loop(12, lambda j: start_to(*c4(lax.rem(j + b, 12))))

    @pl.when(owner)
    def _():
        kn[...] = natural(buf_t[64:128, :])
        vn[...] = natural(buf_t[128:192, :])
        k2n[...] = natural(buf_s[64:128, :])
        loop(16, lambda i: got(do_t.at[:, lanes(i * 128, 128)], r4.at[i]))

        def at(c):
            here = lanes(c * QC, QC)
            return (
                buf_t[0:64, here], buf_s[0:64, here], do_t[:, here],
                lse_t[0:1, here], lse_s[0:1, here], weight_row(len_ref, flag_ref, head, c * QC, hh < 6),
            )

        def put(c, g, real):
            dq_buf2[:, lanes(c * QC, QC)] = g.astype(BF)
            send_pair(c5, c, real)

        run_chunks(SEQ // QC, at, buf_t, put)
        back_blocks(acc, dkv_buf2)
        loop(16, lambda i: start_to(*c6(lax.rem(b + i, 16))))

    loop(12, lambda h: got(dqkv_t.at[h, 0:64], r5.at[h]))
    loop(12, lambda h: got(dqkv_t.at[h, 64:192], r6.at[h]))
    for part in range(3):
        joined_t[:, 768 * part : 768 * (part + 1)] = natural_wide(
            dqkv_t[:, 64 * part : 64 * (part + 1), :].reshape(768, 128)
        )
    for row, part in ((10, 0), (11, 2)):
        sums[row : row + 1, :] = jnp.sum(
            joined_t[:, 768 * part : 768 * (part + 1)].astype(F32), axis=0, keepdims=True
        )
    weights[4].wait()
    grad = g1_ref[...] + dot_t(joined_t[...], v_qkv_t[...])
    place_of = lax.broadcasted_iota(jnp.int32, (128, 128), 0)
    turned = jnp.where((place_of == source[...]) & (flags[...] == 1), 1.0, 0.0)
    back = turned.astype(BF)
    one = grad.astype(BF)
    rest = grad - one.astype(F32)
    two = rest.astype(BF)
    three = (rest - two.astype(F32)).astype(BF)
    copied = dot(back, one) + dot(back, two) + dot(back, three)
    kept = jnp.sum(turned.T, axis=1, keepdims=True) < 0.5
    grad_in[...] = jnp.where(kept, grad, 0.0) + copied

    @pl.when(owner)
    def _():
        loop(8, lambda j: sent_to(*c2(j)))
        loop(16, lambda d: sent_to(*c3(d)))
        loop(16, lambda d: sent_to(*c5(d)))
        loop(16, lambda d: sent_to(*c6(d)))

    loop(6, lambda h: sent_to(*c1(h)))
    loop(12, lambda h: sent_to(*c4(h)))


ANY = pl.BlockSpec(memory_space=pl.ANY)


def mega_call(kernel, ident, specs, outs, scratch, args, name):
    return pl.pallas_call(
        kernel,
        name=name,
        out_shape=tuple(jax.ShapeDtypeStruct(s, t) for s, t in outs),
        in_specs=specs,
        out_specs=tuple(VMEM for _ in outs),
        scratch_shapes=scratch,
        compiler_params=pltpu.CompilerParams(
            collective_id=ident, has_side_effects=True, vmem_limit_bytes=60 * MIB
        ),
    )(*args)


def vb(*shape):
    return pltpu.VMEM(shape, BF)


def vf(*shape):
    return pltpu.VMEM(shape, F32)


def run_forward(lengths, x_in, source, flags, cot, weights, smalls):
    outs = [
        ((128, 768), F32), ((192, SEQ), BF), ((128, SEQ), BF), ((192, SEQ), BF),
        ((8, SEQ), F32), ((8, SEQ), F32), ((8, SEQ), F32),
        ((128, 768), BF), ((128, 768), BF), ((128, 768), BF), ((128, 768), BF), ((128, 768), BF), ((128, 768), BF),
        ((128, 768), BF), ((128, 3072), BF), ((128, 384), BF), ((128, 1536), BF), ((128, 1536), BF),
        ((128, 3072), BF), ((128, 768), F32), ((128, 128), F32), ((128, 768), F32), ((128, 128), F32),
        ((128, 768), F32), ((6, 64, 128), BF), ((24, 768), F32),
    ]
    scratch = [
        vb(768, 2304), vb(768, 768), vb(768, 3072), vb(3072, 768),
        vb(768, 1152), vb(384, 768), vb(768, 1536), vb(1536, 768),
        vf(128, 768), vb(12, 192, 128), vb(6, 192, 128), vb(12, 64, 128), vb(6, 64, 128),
        vb(64, SEQ), vb(64, 1024), vb(SEQ, 64), vf(2, SEQ, QC), vb(2, SEQ, QC), vf(6, 8, QC),
        vb(128, 1536), vf(128, 768), vf(128, 128),
        DMA((8,)), DMA((12,)), DMA((16,)), DMA((6,)), DMA((16,)), DMA((16,)), DMA((12,)), DMA((4,)),
        DMA((12,)), DMA((16,)), DMA((8,)), DMA((6,)), DMA((1,)),
    ]
    specs = [SMEM] + [VMEM] * 4 + [ANY] * 8 + [VMEM] * 6
    return mega_call(
        forward_kernel, 1, specs, outs, scratch, (lengths, x_in, source, flags, cot, *weights, *smalls), "forward"
    )


def run_backward(lengths, head_flags, source, flags, weights, vec_t, kept):
    outs = [
        ((128, 768), F32), ((128, 2304), BF), ((128, 1152), BF), ((128, 3072), BF),
        ((128, 768), BF), ((128, 768), BF), ((24, 768), F32),
    ]
    scratch = [
        vb(768, 1152), vb(3072, 768), vb(768, 3072), vb(768, 768), vb(768, 2304),
        vb(12, 64, 128), vb(64, 1024), vb(64, SEQ), vb(6, 64, 128), vb(12, 128, 128), vb(12, 192, 128),
        vb(64, 1024), vb(64, SEQ), vb(128, SEQ), vb(128, SEQ),
        vb(SEQ, 64), vb(SEQ, 64), vb(SEQ, 64), vf(SEQ, QC), vf(SEQ, QC), vb(2, SEQ, 2 * QC), vf(SEQ, 128),
        vf(128, 768),
        DMA((5,)), DMA((6,)), DMA((8,)), DMA((8,)), DMA((6,)), DMA((16,)), DMA((12,)),
        DMA((12,)), DMA((16,)), DMA((16,)), DMA((12,)), DMA((16,)), DMA((12,)),
    ]
    specs = [SMEM] * 2 + [VMEM] * 2 + [ANY] * 5 + [VMEM] * (1 + len(kept))
    return mega_call(
        backward_kernel, 2, specs, outs, scratch,
        (lengths, head_flags, source, flags, *weights, vec_t, *kept), "backward",
    )

CUTS = ((0, 12, 12), (12, 6, 6), (18, 2, 1), (20, 12, 12), (32, 5, 4), (37, 3, 3), (40, 9, 9), (49, 6, 6))
PARTS = ((0, 20), (20, 20), (40, 16))
MEMBERS = ((0, 1, 2), (3, 4, 5), (6, 7))
TILES = 56
WIDE = TILES * 128


def where_am_i():
    dp, blk = lax.axis_index("dp"), lax.axis_index("blk")
    return dp // 2, lax.rem(dp, 2), blk // 4, lax.rem(blk, 4)


def at_axis(axis, v):
    x, c, y, z = where_am_i()
    if axis == "x":
        return {"dp": 2 * v + c, "blk": 4 * y + z}
    if axis == "y":
        return {"dp": 2 * x + c, "blk": 4 * v + z}
    return {"dp": 2 * x + c, "blk": 4 * y + v}


def send_to(src, dst, send_sem, recv_sem, device):
    return pltpu.make_async_remote_copy(
        src_ref=src, dst_ref=dst, send_sem=send_sem, recv_sem=recv_sem,
        device_id=device, device_id_type=MESH,
    )


ORDERS = ("xyz", "yzx", "zxy")


def reduce_kernel(*refs):
    narrow, wide, small = refs[0:8], refs[8:16], refs[16]
    out, sums = refs[17:19]
    (nt, cf, sml, sma, pb, l1, a1, l2, a2, l3, a3,
     own_sem, n_send, n_recv, c_send, c_recv, s_send, s_recv,
     st_send, st_recv, f_send, f_recv) = refs[19:]
    x, c, y, z = where_am_i()
    here = {"x": x, "y": y, "z": z}
    dp, blk = 2 * x + c, 4 * y + z
    me = 16 * dp + blk
    partner = {"dp": 2 * x + 1 - c, "blk": blk}

    def holder(p, q, core):
        first, second = me // 32, lax.rem(me // 8, 4)
        at = dict(zip(ORDERS[p], (first, second, q)))
        return 2 * at["x"] + core, 4 * at["y"] + at["z"]

    def owner(p, k):
        i = 32 * here[ORDERS[p][0]] + 8 * here[ORDERS[p][1]] + k
        return i, {"dp": i // 16, "blk": lax.rem(i, 16)}

    barrier = pltpu.get_barrier_semaphore()
    pl.semaphore_signal(barrier, inc=1, device_id=partner, device_id_type=MESH)
    for axis in "xyz":
        for j in range(1, 4):
            pl.semaphore_signal(
                barrier, inc=1, device_id=at_axis(axis, lax.rem(here[axis] + j, 4)), device_id_type=MESH
            )
    for p in range(3):
        for q in range(4):
            for core in range(2):
                hd, hb = holder(p, q, core)

                pl.semaphore_signal(
                    barrier, inc=1, device_id={"dp": hd, "blk": hb}, device_id_type=MESH
                )
    pl.semaphore_wait(barrier, 34)

    small_copies = [send_to(small, sml.at[0], s_send.at[0], s_recv.at[0], partner)]
    small_copies[0].start()

    def small_step(axis, n):
        src = sma.at[n // 3]
        for j in range(1, 4):
            slot = n + j
            copy = send_to(
                src, sml.at[slot], s_send.at[slot], s_recv.at[slot],
                at_axis(axis, lax.rem(here[axis] + j, 4)),
            )
            copy.start()
            small_copies.append(copy)

    def small_sum(n):
        for j in range(1, 4):
            small_copies[n + j].wait_recv()
        return sma[n // 3] + sml[n + 1] + sml[n + 2] + sml[n + 3]

    n_copies, c_copies, own_copies = [], [], []
    for m, (first, count, step) in enumerate(CUTS):
        cols = slice(first * 128, (first + count) * 128)
        keep = pltpu.make_async_copy(
            wide[m].at[:, lanes(c * step * 128, count * 128)], cf.at[0:128, cols], own_sem.at[m]
        )
        keep.start()
        own_copies.append(keep)
        give = send_to(
            wide[m].at[:, lanes((1 - c) * step * 128, count * 128)], cf.at[128:256, cols],
            c_send.at[m], c_recv.at[m], partner,
        )
        give.start()
        c_copies.append(give)
        nt[m, :, 0:128] = narrow[m][...].T
        give = send_to(
            nt.at[m, :, 0:128], nt.at[m, :, 128:256], n_send.at[m], n_recv.at[m], partner
        )
        give.start()
        n_copies.append(give)

    def part_cols(p):
        return slice(PARTS[p][0] * 128, (PARTS[p][0] + PARTS[p][1]) * 128)

    def stage_copies(p, stage):
        axis = ORDERS[p][stage]
        copies = []
        for j in range(1, 4):
            v = lax.rem(here[axis] + j, 4)
            if stage == 0:
                src = pb.at[pl.ds(pl.multiple_of(192 * v, 16), 192), part_cols(p)]
                dst = l1.at[j - 1, :, part_cols(p)]
            elif stage == 1:
                src = a1.at[pl.ds(pl.multiple_of(48 * v, 16), 48), part_cols(p)]
                dst = l2.at[j - 1, :, part_cols(p)]
            else:
                q = PARTS[p][1] * 32
                src = a2.at[:, lanes(PARTS[p][0] * 128 + v * q, q)]
                dst = l3.at[j - 1, :, slice(PARTS[p][0] * 32, PARTS[p][0] * 32 + q)]
            n = 9 * stage + 3 * p + j - 1
            copies.append(send_to(src, dst, st_send.at[n], st_recv.at[n], at_axis(axis, v)))
        return copies

    copies = {}
    for p in range(3):
        for m in MEMBERS[p]:
            first, count, _ = CUTS[m]
            own_copies[m].wait()
            c_copies[m].wait_recv()
            n_copies[m].wait_recv()
            size = 3 if count % 3 == 0 else count

            def piece(i, carry, m=m, first=first, size=size):
                cols = lanes((first + i * size) * 128, size * 128)
                pb[:, cols] = dot(nt[m], cf[:, cols]).astype(BF)
                return carry

            lax.fori_loop(0, count // size, piece, 0)
        copies[p, 0] = stage_copies(p, 0)
        for copy in copies[p, 0]:
            copy.start()

    small_copies[0].wait_recv()
    sma[0] = small[...] + sml[0]
    small_step("x", 0)

    for p in range(3):
        cols = part_cols(p)
        base = 192 * here[ORDERS[p][0]]
        for copy in copies[p, 0]:
            copy.wait_recv()

        def add1(r, carry, cols=cols, base=base):
            rows = pl.ds(pl.multiple_of(16 * r, 16), 16)
            own = pl.ds(pl.multiple_of(base + 16 * r, 16), 16)
            total = pb[own, cols].astype(F32)
            for j in range(3):
                total = total + l1[j, rows, cols].astype(F32)
            a1[rows, cols] = total.astype(BF)
            return carry

        lax.fori_loop(0, 12, add1, 0)
        copies[p, 1] = stage_copies(p, 1)
        for copy in copies[p, 1]:
            copy.start()

    sma[1] = small_sum(0)
    small_step("y", 3)

    for p in range(3):
        cols = part_cols(p)
        base = 48 * here[ORDERS[p][1]]
        for copy in copies[p, 1]:
            copy.wait_recv()

        def add2(r, carry, cols=cols, base=base):
            rows = pl.ds(pl.multiple_of(16 * r, 16), 16)
            own = pl.ds(pl.multiple_of(base + 16 * r, 16), 16)
            total = a1[own, cols].astype(F32)
            for j in range(3):
                total = total + l2[j, rows, cols].astype(F32)
            a2[rows, cols] = total.astype(BF)
            return carry

        lax.fori_loop(0, 3, add2, 0)
        copies[p, 2] = stage_copies(p, 2)
        for copy in copies[p, 2]:
            copy.start()

    sma[2] = small_sum(3)
    small_step("z", 6)

    for p in range(3):
        q = PARTS[p][1] * 32
        off = PARTS[p][0] * 32
        third = here[ORDERS[p][2]]
        for copy in copies[p, 2]:
            copy.wait_recv()
        total = a2[:, lanes(PARTS[p][0] * 128 + third * q, q)].astype(F32)
        for j in range(3):
            total = total + l3[j, :, off : off + q].astype(F32)
        for k in range(8):
            a3[k, 0:6, off : off + q] = total[6 * k : 6 * k + 6, :]

    def final(p, k):
        q = PARTS[p][1] * 32
        off = PARTS[p][0] * 32
        third = here[ORDERS[p][2]]
        i, device = owner(p, k)
        src = a3.at[k, :, slice(off, off + q)]
        dst = out.at[:, lanes((c * TILES + PARTS[p][0]) * 128 + third * q, q)]
        slot = f_recv.at[(c * 3 + p) * 4 + third]
        return i, src, dst, slot, send_to(src, dst, f_send.at[8 * p + k], slot, device)

    for p in range(3):
        for k in range(8):
            i, src, dst, slot, copy = final(p, k)

            @pl.when(i != me)
            def _():
                copy.start()

            @pl.when(i == me)
            def _():
                pltpu.make_async_copy(src, dst, slot).start()

    for core in range(2):
        for p in range(3):
            q = PARTS[p][1] * 32
            for third in range(4):
                start = (core * TILES + PARTS[p][0]) * 128 + third * q
                got(out.at[:, start : start + q], f_recv.at[(core * 3 + p) * 4 + third])
    for p in range(3):
        for k in range(8):
            i, src, dst, slot, copy = final(p, k)

            @pl.when(i != me)
            def _():
                copy.wait_send()
    sums[...] = small_sum(6)
    for copy in small_copies + n_copies + c_copies + sum(copies.values(), []):
        copy.wait_send()


def reduce_all(narrow, wide, small):
    return pl.pallas_call(
        reduce_kernel,
        name="reduce",
        out_shape=(jax.ShapeDtypeStruct((8, 2 * WIDE), F32), jax.ShapeDtypeStruct((24, 768), F32)),
        in_specs=[VMEM] * 17,
        out_specs=(VMEM, VMEM),
        scratch_shapes=[
            pltpu.VMEM((8, 768, 256), BF), pltpu.VMEM((256, WIDE), BF), pltpu.VMEM((10, 24, 768), F32), pltpu.VMEM((3, 24, 768), F32),
            pltpu.VMEM((768, WIDE), BF), pltpu.VMEM((3, 192, WIDE), BF), pltpu.VMEM((192, WIDE), BF),
            pltpu.VMEM((3, 48, WIDE), BF), pltpu.VMEM((48, WIDE), BF),
            pltpu.VMEM((3, 48, WIDE // 4), BF), pltpu.VMEM((8, 8, WIDE // 4), F32),
            DMA((8,)), DMA((8,)), DMA((8,)), DMA((8,)), DMA((8,)), DMA((10,)), DMA((10,)),
            DMA((27,)), DMA((27,)), DMA((24,)), DMA((24,)),
        ],
        compiler_params=pltpu.CompilerParams(
            collective_id=5, has_side_effects=True, vmem_limit_bytes=56 * MIB
        ),
    )(*narrow, *wide, small)


def unpack_kernel(whole, sums, *outs):
    def columns(m):
        first, count, step = CUTS[m]
        both = [whole[:, first * 128 : (first + count) * 128]]
        skip = count - step
        start = TILES + first + skip
        both.append(whole[:, start * 128 : (start + count - skip) * 128])
        return jnp.concatenate(both, axis=1)

    for m, o in ((6, 0), (5, 2), (0, 3), (3, 4), (4, 7), (2, 9), (1, 10), (7, 11)):
        outs[o][...] = columns(m)[0:6]
    i = 16 * lax.axis_index("dp") + lax.axis_index("blk")

    def turn(rows, by):
        return pltpu.roll(rows, lax.rem(768 - by, 768), 1)

    def pick(first, count, per):
        row = first + (i * per) // 768
        wide = jnp.broadcast_to(sums[pl.ds(row, 1), :], (8, 768))
        return turn(wide, lax.rem(i * per, 768))[0:1, 0:per]

    outs[1][...] = pick(10, 2, 12)
    outs[5][...] = pick(6, 4, 24)
    outs[8][...] = pick(20, 1, 6)
    outs[12][...] = pick(18, 2, 12)
    outs[6][...] = turn(sums[0:8, :], i * 6)[0:6, 0:6]
    outs[13][...] = turn(sums[8:24, :], i * 6)[4:10, 0:6]


def unpack(whole, sums):
    shapes = (
        (6, 2304), (1, 12), (6, 768), (6, 3072), (6, 3072), (1, 24), (6, 6),
        (6, 1152), (1, 6), (6, 384), (6, 1536), (6, 1536), (1, 12), (6, 6),
    )
    outs = list(
        pl.pallas_call(
            unpack_kernel,
            name="unpack",
            out_shape=tuple(jax.ShapeDtypeStruct(s, F32) for s in shapes),
            in_specs=[VMEM] * 2,
            out_specs=tuple(VMEM for _ in shapes),
            compiler_params=pltpu.CompilerParams(vmem_limit_bytes=40 * MIB),
        )(whole, sums)
    )
    for i in (1, 5, 8, 12):
        outs[i] = outs[i].reshape(-1)
    for i in (2, 4, 9, 11):
        outs[i] = outs[i].T
    return tuple(outs)


def per_device(
    inputs, aug_source, aug_flags, lengths, head_flags, cotangent,
    qkv_teacher, qv_bias_teacher, out_teacher, up_teacher, down_teacher, up_bias_teacher, vectors_teacher,
    qkv_student, qv_bias_student, out_student, up_student, down_student, up_bias_student, vectors_student,
):
    (
        output, buf_t, dist, buf_s, lse_t, lse_d, lse_s,
        x0_low, normed_low_t, hidden_low, normed_low_s, g1r_s, g2r_s,
        att_t, act_t, att_s, act_s, gu_s,
        slope_t, unit1_t, scale1_t, unit2_t, scale2_t, g1_s, datt_s, sums_s,
    ) = run_forward(
        lengths, inputs[0], aug_source, aug_flags, cotangent[0],
        (qkv_teacher, out_teacher, up_teacher, down_teacher, qkv_student, out_student, up_student, down_student),
        (
            qv_bias_teacher[None], up_bias_teacher[None], vectors_teacher,
            qv_bias_student[None], up_bias_student[None], vectors_student,
        ),
    )
    grad_in, joined_t, joined_s, gu_t, g1r_t, g2r_t, sums = run_backward(
        lengths, head_flags, aug_source, aug_flags,
        (qkv_student, down_teacher, up_teacher, out_teacher, qkv_teacher), vectors_teacher,
        (
            buf_t, dist, buf_s, lse_t, lse_d, lse_s,
            slope_t, unit1_t, scale1_t, unit2_t, scale2_t, g1_s, datt_s, sums_s,
        ),
    )
    pairs = (
        (normed_low_t, gu_t), (normed_low_s, gu_s), (g1r_s, att_s), (g2r_t, act_t),
        (hidden_low, joined_s), (g1r_t, att_t), (x0_low, joined_t), (g2r_s, act_s),
    )
    whole, total = reduce_all([n for n, _ in pairs], [w for _, w in pairs], sums)
    return (output[None], grad_in[None]) + unpack(whole, total)


def solution(mesh):
    both = ("dp", "blk")
    row, flat, col = P(both, None), P(both), P(None, both)
    tokens, marks = P("dp", "blk", None), P("dp", "blk")
    return jax.shard_map(
        per_device,
        mesh=mesh,
        in_specs=(tokens, marks, marks, P("dp"), P(), tokens) + (P(),) * 14,
        out_specs=(tokens, tokens) + (row, flat, col, row, col, flat, col) * 2,
        check_vma=False,
    )
```

```python
import jax
import jax.numpy as jnp
from jax import lax
from jax.experimental import pallas as pl
from jax.experimental.pallas import tpu as pltpu
from jax.sharding import PartitionSpec as P

MESH = pl.DeviceIdType.MESH
LOG2E = 1.4426950408889634
C2 = 0.125 * LOG2E
SEQ = 2048
QC = 256
KT = 256
NKT = SEQ // KT
MIB = 1 << 20


def dot(a, b):
    return jnp.dot(a, b, preferred_element_type=jnp.float32)


def place():
    b = lax.axis_index("blk")
    r = lax.rem(lax.rem(b, 4) - b // 4 + 7, 4)
    return b, 3 * (b // 4) + r, r < 3


def owner_of(hh):
    y = hh // 3
    return 4 * y + lax.rem(y + lax.rem(hh, 3) + 1, 4)


def copy_to(src, dst, send_sem, recv_sem, d):
    return pltpu.make_async_remote_copy(
        src_ref=src,
        dst_ref=dst,
        send_sem=send_sem,
        recv_sem=recv_sem,
        device_id={"blk": d},
        device_id_type=MESH,
    )


def start_to(src, dst, send_sem, recv_sem, d, b):
    @pl.when(d != b)
    def _():
        copy_to(src, dst, send_sem, recv_sem, d).start()

    @pl.when(d == b)
    def _():
        pltpu.make_async_copy(src, dst, recv_sem).start()


def sent_to(src, dst, send_sem, recv_sem, d, b):
    @pl.when(d != b)
    def _():
        copy_to(src, dst, send_sem, recv_sem, d).wait_send()


def got(dst, recv_sem):
    pltpu.make_async_copy(dst, dst, recv_sem).wait()


def lanes(start, size):
    return pl.ds(pl.multiple_of(start, 128), size)


def fold(v):
    return jnp.sum(v.reshape(v.shape[0] // 8, 8, v.shape[1]), axis=0)


def key_ok(length):
    rows = lax.broadcasted_iota(jnp.int32, (KT, QC), 0) + (SEQ - KT)
    return rows < length


def natural(x):
    return x.astype(jnp.float32).T.astype(jnp.bfloat16)


def weight_row(len_ref, flag_ref, head, first, use):
    q = lax.broadcasted_iota(jnp.int32, (1, QC), 1) + first
    factor = jnp.where(use, flag_ref[head].astype(jnp.float32) * (2.0 * SEQ), 0.0)
    return jnp.where(q < len_ref[0], factor, 0.0)


SMEM = pl.BlockSpec(memory_space=pltpu.SMEM)
VMEM = pl.BlockSpec(memory_space=pltpu.VMEM)
DMA = pltpu.SemaphoreType.DMA
BF = jnp.bfloat16
F32 = jnp.float32


SQRT_HALF = 0.7071067811865476
INV_SQRT_2PI = 0.3989422804014327


def dot_t(a, b):
    return lax.dot_general(a, b, (((1,), (1,)), ((), ())), preferred_element_type=F32)


def norm_forward(v, gain, shift):
    center = v - jnp.mean(v, axis=-1, keepdims=True)
    scale = lax.rsqrt(jnp.mean(center * center, axis=-1, keepdims=True) + 1e-06)
    unit = center * scale
    return unit * gain + shift, unit, scale


def norm_backward(grad, gain, unit, scale):
    scaled = grad * gain
    mean_one = jnp.mean(scaled, axis=-1, keepdims=True)
    mean_two = jnp.mean(scaled * unit, axis=-1, keepdims=True)
    return (
        (scaled - mean_one - unit * mean_two) * scale,
        jnp.sum(grad * unit, axis=0, keepdims=True),
        jnp.sum(grad, axis=0, keepdims=True),
    )


def qkv_blocks(low, w, bias, src, heads):
    span = heads * 64
    for part in range(3):
        joint = dot(low, w[:, part * span : (part + 1) * span])
        if part != 1:
            first = 0 if part == 0 else span
            joint = joint + bias[:, first : first + span]
        src[:, part * 64 : (part + 1) * 64, :] = joint.T.astype(BF).reshape(heads, 64, 128)


def dense_up(residual, attended, w_out, w_up, w_down, up_bias, vec, act, slope, unit1, scale1, normed_turned):
    ff = up_bias.shape[1]
    first = residual + dot(attended, w_out) + vec[0:1, :]
    normed, unit, scale = norm_forward(first, vec[1:2, :], vec[2:3, :])
    unit1[...] = unit
    scale1[...] = jnp.broadcast_to(scale, (128, 128))
    low = normed.astype(BF)
    normed_turned[...] = normed.T.astype(BF)
    step = 512
    for j in range(ff // step):
        cols = slice(j * step, (j + 1) * step)
        u = dot(low, w_up[:, cols]) + up_bias[:, cols]
        cdf = 0.5 + 0.5 * lax.erf(u * SQRT_HALF)
        act[:, cols] = (u * cdf).astype(BF)
        slope[:, cols] = (cdf + u * (jnp.exp(-0.5 * u * u) * INV_SQRT_2PI)).astype(slope.dtype)
    second = normed + dot(act[...], w_down) + vec[3:4, :]
    return norm_forward(second, vec[4:5, :], vec[5:6, :])


def dense_down(grad, unit2, scale2, unit1, scale1, w_out, w_up, w_down, vec, slope, gu, g2r, g1r, sums, row):
    ff = w_up.shape[1]
    g2, gain_two, shift_two = norm_backward(grad, vec[4:5, :], unit2, scale2)
    low2 = g2.astype(BF)
    g2r[...] = g2.T.astype(BF)
    step = 512
    for j in range(ff // step):
        cols = slice(j * step, (j + 1) * step)
        g = dot_t(low2, w_down[cols, :]) * slope[:, cols].astype(F32)
        gu[:, cols] = g.astype(BF)
        total = jnp.sum(g, axis=0, keepdims=True)
        done = 0
        while done < step:
            at = j * step + done
            size = min(step - done, 768 - at % 768)
            sums[row + 6 + at // 768 : row + 7 + at // 768, at % 768 : at % 768 + size] = total[:, done : done + size]
            done += size
    g1, gain_one, shift_one = norm_backward(g2 + dot_t(gu[...], w_up[...]), vec[1:2, :], unit1, scale1)
    low1 = g1.astype(BF)
    g1r[...] = g1.T.astype(BF)
    rows = (
        jnp.sum(g1, axis=0, keepdims=True), gain_one, shift_one,
        jnp.sum(g2, axis=0, keepdims=True), gain_two, shift_two,
    )
    for i, value in enumerate(rows):
        sums[row + i : row + i + 1, :] = value
    return g1, dot_t(low1, w_out[...])


def load_all(pairs, sem):
    copies = [pltpu.make_async_copy(a, b, sem.at[i]) for i, (a, b) in enumerate(pairs)]
    for copy in copies:
        copy.start()
    return copies


def forward_stage(c_score, c_exp, c_out, do, par, q_at, kn, v_ref, s_ref, p_ref, st, put, length):
    if do[0]:
        q = q_at(c_score)
    m8 = jnp.full((8, QC), -3e38, F32)
    l8 = jnp.zeros((8, QC), F32)
    out = jnp.zeros((64, QC), F32)
    top = st[1 - par, 0:1, :]
    for t in range(NKT):
        rows = slice(t * KT, (t + 1) * KT)
        if do[0]:
            s = dot(kn[rows, :], q)
            if t == NKT - 1:
                s = jnp.where(key_ok(length), s, -1e30)
            s_ref[par, rows, :] = s
            m8 = jnp.maximum(m8, jnp.max(s.reshape(KT // 8, 8, QC), axis=0))
        if do[1]:
            p = jnp.exp2(s_ref[1 - par, rows, :] * C2 - top)
            l8 = l8 + fold(p)
            p_ref[1 - par, rows, :] = p.astype(BF)
        if do[2]:
            out = out + dot(v_ref[128:192, rows], p_ref[par, rows, :])
    if do[2]:
        put(c_out, out / st[2 + par, 0:1, :], st[4 + par, 0:1, :])
    if do[1]:
        total = jnp.sum(l8, axis=0, keepdims=True)
        st[3 - par] = jnp.broadcast_to(total, (8, QC))
        st[5 - par] = jnp.broadcast_to(top + jnp.log2(total), (8, QC))
    if do[0]:
        st[par] = jnp.broadcast_to(jnp.max(m8, axis=0, keepdims=True) * C2, (8, QC))


def forward_chunks(n, *rest):
    forward_stage(0, 0, 0, (1, 0, 0), 0, *rest)
    forward_stage(1, 0, 0, (1, 1, 0), 1, *rest)

    def body(i, carry):
        forward_stage(2 * i, 2 * i - 1, 2 * i - 2, (1, 1, 1), 0, *rest)
        forward_stage(2 * i + 1, 2 * i, 2 * i - 1, (1, 1, 1), 1, *rest)
        return carry

    lax.fori_loop(1, n // 2, body, 0)
    forward_stage(0, n - 1, n - 2, (0, 1, 1), 0, *rest)
    forward_stage(0, 0, n - 1, (0, 0, 1), 1, *rest)


def backward_chunk(c, prev, par, at, kn, k2n, vn, kt_ref, length, gf, x_ref, acc, put):
    q, q2, do, lse, lse2, weight = at(c)
    pq, _, pdo, _, _, _ = at(prev)
    both = jnp.concatenate([pq, pdo], axis=0).astype(F32).T
    col = lax.broadcasted_iota(jnp.int32, (QC, 128), 1)
    rhs = jnp.concatenate(
        [jnp.where(col < 64, both, 0.0), jnp.where(col < 64, 0.0, both)], axis=0
    ).astype(BF)
    d8 = jnp.zeros((8, QC), F32)
    dq = jnp.zeros((64, QC), F32)
    for t in range(NKT):
        rows = slice(t * KT, (t + 1) * KT)
        p = jnp.exp2(dot(kn[rows, :], q) * C2 - lse)
        p2 = jnp.exp2(dot(k2n[rows, :], q2) * C2 - lse2)
        if t == NKT - 1:
            ok = key_ok(length)
            p = jnp.where(ok, p, 0.0)
            p2 = jnp.where(ok, p2, 0.0)
        g = dot(vn[rows, :], do) + weight * (p - p2)
        d8 = d8 + fold(p * g)
        gf[rows, :] = g
        x_ref[par, rows, QC:] = p.astype(BF)
        acc[rows, :] += dot(x_ref[1 - par, rows, :], rhs)
        dq = dq + dot(kt_ref[64:128, rows], x_ref[1 - par, rows, :QC])
    put(prev, dq * 0.125)
    delta = jnp.sum(d8, axis=0, keepdims=True)
    for t in range(NKT):
        rows = slice(t * KT, (t + 1) * KT)
        x_ref[par, rows, :QC] = (x_ref[par, rows, QC:].astype(F32) * (gf[rows, :] - delta)).astype(BF)


def backward_last(prev, par, at, kt_ref, x_ref, acc, put):
    pq, _, pdo, _, _, _ = at(prev)
    both = jnp.concatenate([pq, pdo], axis=0).astype(F32).T
    col = lax.broadcasted_iota(jnp.int32, (QC, 128), 1)
    rhs = jnp.concatenate(
        [jnp.where(col < 64, both, 0.0), jnp.where(col < 64, 0.0, both)], axis=0
    ).astype(BF)
    dq = jnp.zeros((64, QC), F32)
    for t in range(NKT):
        rows = slice(t * KT, (t + 1) * KT)
        acc[rows, :] += dot(x_ref[par, rows, :], rhs)
        dq = dq + dot(kt_ref[64:128, rows], x_ref[par, rows, :QC])
    put(prev, dq * 0.125)


def back_blocks(acc, dkv_buf):
    row = lax.broadcasted_iota(jnp.int32, (128, SEQ), 0)
    total = acc[...].T
    dkv_buf[...] = jnp.where(row < 64, total * 0.125, total).astype(BF)


def natural_wide(blocks):
    return blocks.astype(F32).T.astype(BF)


def loop(n, body):
    def step(i, carry):
        body(i)
        return carry

    lax.fori_loop(0, n, step, 0)


def greet_start():
    b = lax.axis_index("blk")
    sem = pltpu.get_barrier_semaphore()
    loop(15, lambda i: pl.semaphore_signal(
        sem, inc=1, device_id={"blk": lax.rem(b + 1 + i, 16)}, device_id_type=MESH
    ))


def greet_end():
    pl.semaphore_wait(pltpu.get_barrier_semaphore(), 15)


def forward_kernel(
    len_ref, x_in, source, flags, cot,
    w_qkv_t, w_out_t, w_up_t, w_down_t, w_qkv_s, w_out_s, w_up_s, w_down_s,
    bias_t, upb_t, vec_t, bias_s, upb_s, vec_s,
    *refs,
):
    kept_out, refs = refs[0:26], refs[26:]
    kept, refs = refs[0:26], refs[26:]
    (
        output, buf_t, dist, buf_s, lse_t, lse_d, lse_s,
        x0_turn, normed_turn_t, hidden_turn, normed_turn_s, g1r_s, g2r_s,
        att_t, act_t, att_s, act_s, gu_s,
        slope_t, unit1_t, scale1_t, unit2_t, scale2_t, g1_s, datt_s, sums,
    ) = kept
    (
    v_qkv_t, v_out_t, v_up_t, v_down_t, v_qkv_s, v_out_s, v_up_s, v_down_s,
    x0_ref, src_t, src_s, land_t, land_s, o_t, o_s, kn, s_ref, p_ref, st,
    slope_s, unit1_s, scale1_s,
    w_sem, t_send, t_recv, d_send, d_recv, a_send, a_recv, lse_sem,
    s_send, s_recv, b_send, b_recv, local_sem, keep_sem,
    ) = refs

    def keep(*which):
        for i in which:
            pltpu.make_async_copy(kept[i], kept_out[i], keep_sem.at[i]).start()

    b, hh, owner = place()
    half, head = hh // 6, lax.rem(hh, 6)
    greet_start()
    weights = load_all(
        [
            (w_qkv_t, v_qkv_t), (w_out_t, v_out_t), (w_up_t, v_up_t), (w_down_t, v_down_t),
            (w_qkv_s, v_qkv_s), (w_out_s, v_out_s), (w_up_s, v_up_s), (w_down_s, v_down_s),
        ],
        w_sem,
    )
    length = len_ref[0]
    replaced = flags[...] == 1
    place_of = lax.broadcasted_iota(jnp.int32, (128, 128), 0)
    turned = jnp.where((place_of == source[...]) & replaced, 1.0, 0.0)
    chooser = turned.T
    taken = dot(chooser.astype(BF), x_in[...])
    x0 = jnp.where(jnp.sum(chooser, axis=1, keepdims=True) > 0.5, taken, x_in[...].astype(F32))
    x0_ref[...] = x0
    low = x0.astype(BF)
    x0_turn[...] = x0.T.astype(BF)
    keep(7)
    weights[0].wait()
    qkv_blocks(low, v_qkv_t, bias_t, src_t, 12)
    greet_end()

    mine = lanes(b * 128, 128)

    def t_copy(h):
        return src_t.at[h], buf_t.at[:, mine], t_send.at[h], t_recv.at[b], owner_of(h), b

    def d_copy(h):
        return src_t.at[h, 0:128], dist.at[:, mine], d_send.at[h], d_recv.at[b], owner_of(h + 6), b

    loop(12, lambda j: start_to(*t_copy(lax.rem(j + b, 12))))
    loop(6, lambda j: start_to(*d_copy(lax.rem(j + b, 6))))

    def a_copy(d):
        return o_t.at[:, lanes(d * 128, 128)], land_t.at[hh], a_send.at[d], a_recv.at[hh], d, b

    @pl.when(owner)
    def _():
        loop(16, lambda i: got(buf_t.at[:, lanes(i * 128, 128)], t_recv.at[i]))
        kn[...] = natural(buf_t[64:128, :])

        def put(c, o, stat):
            here = lanes(c * QC, QC)
            o_t[:, here] = o.astype(BF)
            lse_t[:, here] = jnp.broadcast_to(stat, (8, QC))
            for i in range(2):
                start_to(*a_copy(2 * c + i))

        forward_chunks(
            SEQ // QC, lambda c: buf_t[0:64, lanes(c * QC, QC)], kn, buf_t, s_ref, p_ref, st, put, length
        )

    @pl.when(owner & (hh < 6))
    def _():
        lse_d[:, 0:1024] = lse_t[:, 0:1024]
        copy_to(
            lse_t.at[:, 1024:2048], lse_d.at[:, 1024:2048], lse_sem.at[0], lse_sem.at[1], owner_of(hh + 6)
        ).start()
        pltpu.make_async_copy(buf_t.at[0:128], dist, local_sem.at[0]).start()

    loop(12, lambda h: got(land_t.at[h], a_recv.at[h]))
    att_t[...] = natural_wide(land_t[...].reshape(768, 128))
    keep(1, 4, 13)
    for i in (1, 2, 3):
        weights[i].wait()
    hidden, unit, scale = dense_up(
        x0_ref[...], att_t[...], v_out_t[...], v_up_t, v_down_t[...], upb_t, vec_t,
        act_t, slope_t, unit1_t, scale1_t, normed_turn_t,
    )
    unit2_t[...] = unit
    scale2_t[...] = jnp.broadcast_to(scale, (128, 128))
    x0_ref[...] = hidden
    low = hidden.astype(BF)
    hidden_turn[...] = hidden.T.astype(BF)
    keep(8, 9, 14, 18, 19, 20, 21, 22)
    weights[4].wait()
    qkv_blocks(low, v_qkv_s, bias_s, src_s, 6)

    def s_copy(h):
        return src_s.at[lax.rem(h, 6)], buf_s.at[:, mine], s_send.at[h], s_recv.at[b], owner_of(h), b

    loop(12, lambda j: start_to(*s_copy(lax.rem(j + b, 12))))

    def b_copy(j):
        return o_s.at[:, lanes(j * 128, 128)], land_s.at[head], b_send.at[j], b_recv.at[head], 8 * half + j, b

    @pl.when(owner)
    def _():
        lse_s[:, 0:1024] = jnp.full((8, 1024), 1e30, F32)
        loop(16, lambda i: got(buf_s.at[:, lanes(i * 128, 128)], s_recv.at[i]))
        kn[...] = natural(buf_s[64:128, :])

        def put(c, o, stat):
            o_s[:, lanes(c * QC, QC)] = o.astype(BF)
            lse_s[:, lanes(half * 1024 + c * QC, QC)] = jnp.broadcast_to(stat, (8, QC))
            for i in range(2):
                start_to(*b_copy(2 * c + i))

        forward_chunks(
            1024 // QC, lambda c: buf_s[0:64, lanes(half * 1024 + c * QC, QC)],
            kn, buf_s, s_ref, p_ref, st, put, length,
        )

    @pl.when(owner & (hh >= 6))
    def _():
        copy_to(
            lse_s.at[:, 1024:2048], lse_s.at[:, 1024:2048], lse_sem.at[2], lse_sem.at[3], owner_of(hh - 6)
        ).start()

    loop(6, lambda h: got(land_s.at[h], b_recv.at[h]))
    att_s[...] = natural_wide(land_s[...].reshape(384, 128))
    keep(3, 15)
    for i in (5, 6, 7):
        weights[i].wait()
    result, unit, scale = dense_up(
        x0_ref[...], att_s[...], v_out_s[...], v_up_s, v_down_s[...], upb_s, vec_s,
        act_s, slope_s, unit1_s, scale1_s, normed_turn_s,
    )
    output[...] = result
    keep(0, 10, 16)
    sums[...] = jnp.zeros((24, 768), F32)
    g1, datt = dense_down(
        cot[...].astype(F32), unit, scale, unit1_s[...], scale1_s[:, 0:1],
        v_out_s, v_up_s, v_down_s, vec_s, slope_s, gu_s, g2r_s, g1r_s, sums, 12,
    )
    g1_s[...] = g1
    datt_s[...] = datt.T.astype(BF).reshape(6, 64, 128)
    keep(11, 12, 17, 23, 24, 25)

    @pl.when(owner)
    def _():
        loop(16, lambda d: sent_to(*a_copy(d)))
        loop(8, lambda j: sent_to(*b_copy(j)))

    @pl.when(owner & (hh < 6))
    def _():
        copy_to(
            lse_t.at[:, 1024:2048], lse_d.at[:, 1024:2048], lse_sem.at[0], lse_sem.at[1], owner_of(hh + 6)
        ).wait_send()
        pltpu.make_async_copy(buf_t.at[0:128], dist, local_sem.at[0]).wait()
        got(lse_s.at[:, 1024:2048], lse_sem.at[3])

    @pl.when(owner & (hh >= 6))
    def _():
        loop(16, lambda i: got(dist.at[:, lanes(i * 128, 128)], d_recv.at[i]))
        got(lse_d.at[:, 1024:2048], lse_sem.at[1])
        copy_to(
            lse_s.at[:, 1024:2048], lse_s.at[:, 1024:2048], lse_sem.at[2], lse_sem.at[3], owner_of(hh - 6)
        ).wait_send()

    keep(2, 5, 6)
    loop(12, lambda h: sent_to(*t_copy(h)))
    loop(6, lambda h: sent_to(*d_copy(h)))
    loop(12, lambda h: sent_to(*s_copy(h)))
    for i in range(26):
        pltpu.make_async_copy(kept[i], kept_out[i], keep_sem.at[i]).wait()


def where_am_i():
    dp, blk = lax.axis_index("dp"), lax.axis_index("blk")
    return dp // 2, lax.rem(dp, 2), blk // 4, lax.rem(blk, 4)


def at_axis(axis, v):
    x, c, y, z = where_am_i()
    if axis == "x":
        return {"dp": 2 * v + c, "blk": 4 * y + z}
    if axis == "y":
        return {"dp": 2 * x + c, "blk": 4 * v + z}
    return {"dp": 2 * x + c, "blk": 4 * y + v}


def send_to(src, dst, send_sem, recv_sem, device):
    return pltpu.make_async_remote_copy(
        src_ref=src, dst_ref=dst, send_sem=send_sem, recv_sem=recv_sem,
        device_id=device, device_id_type=MESH,
    )


ORDERS = ("xyz", "yzx", "zxy")
CUTS = (
    (12, 12, ((16, 12),)), (6, 6, ((0, 6),)), (2, 1, ((6, 2),)), (12, 12, ((28, 12),)),
    (5, 4, ((43, 5),)), (3, 3, ((40, 3),)), (9, 9, ((48, 3), (52, 3), (56, 3))), (6, 6, ((8, 3), (12, 3))),
)
TILES = 60
WIDE = TILES * 128
BATCHES = (
    (0, 16, (1, 2, 7), ((0, 8, 8), (8, 4, 3), (12, 4, 3))),
    (16, 32, (0, 3, 5, 4), ((16, 16, 16), (32, 8, 8), (40, 8, 8))),
    (48, 12, (6,), ((48, 4, 3), (52, 4, 3), (56, 4, 3))),
)
PB_TILES = 32
TURN = 2


def drain(ref, sem):
    pltpu.make_async_copy(ref, ref, sem).wait()


def backward_kernel(
    len_ref, flag_ref, source, flags,
    w_qkv_s, w_down_t, w_up_t, w_out_t, w_qkv_t,
    in_buf_s, in_dist, in_lse_s, in_lse_d, in_g1_s, in_buf_t, in_lse_t,
    in_unit2_t, in_scale2_t, in_slope_t, in_unit1_t, in_scale1_t, datt_s,
    vec_t, sums_s,
    x0_turn, normed_turn_t, hidden_turn, normed_turn_s, g1r_s, g2r_s,
    att_t, act_t, att_s, act_s, gu_s,
    grad_in, out, sums,
    v_qkv_s, v_down_t, v_up_t, v_out_t,
    buf_s, dist, lse_s, lse_d, g1_s, buf_t, lse_t, unit2_t, scale2_t, slope_t, unit1_t, scale1_t,
    joined_t, joined_s, gu_t,
    src_t, do_s, do_t, dq_s, dkv_s, dqkv_t, dq_buf, dkv_buf,
    kn, k2n, vn, gf, x_ref, acc,
    nt, cf, pb, rl, l1, a1, l2, a2, l3, a3, sml, sma,
    w_sem, k_sem, s1, r1, s2, r2, s3, r3, s4, r4, s5, r5, s6, r6,
    own_n, own_c, n_send, n_recv, c_send, c_recv, st_send, st_recv, f_send, f_recv, m_send, m_recv,
):
    b, hh, owner = place()
    half, head = hh // 6, lax.rem(hh, 6)
    x, c, y, z = where_am_i()
    here_at = {"x": x, "y": y, "z": z}
    dp = 2 * x + c
    me = 16 * dp + b
    partner = {"dp": 2 * x + 1 - c, "blk": b}

    barrier = pltpu.get_barrier_semaphore()
    loop(15, lambda i: pl.semaphore_signal(
        barrier, inc=1, device_id={"blk": lax.rem(b + 1 + i, 16)}, device_id_type=MESH
    ))
    pl.semaphore_signal(barrier, inc=1, device_id=partner, device_id_type=MESH)
    for axis in "xyz":
        for j in range(1, 4):
            pl.semaphore_signal(
                barrier, inc=1, device_id=at_axis(axis, lax.rem(here_at[axis] + j, 4)), device_id_type=MESH
            )
    for p in range(3):
        for q in range(4):
            for core in range(2):
                at = dict(zip(ORDERS[p], (me // 32, lax.rem(me // 8, 4), q)))
                pl.semaphore_signal(
                    barrier, inc=1, device_id={"dp": 2 * at["x"] + core, "blk": 4 * at["y"] + at["z"]},
                    device_id_type=MESH,
                )
    kept = load_all(
        [
            (in_buf_s, buf_s), (in_dist, dist), (in_lse_s, lse_s), (in_lse_d, lse_d),
            (in_g1_s, g1_s), (in_buf_t, buf_t), (in_lse_t, lse_t), (in_unit2_t, unit2_t),
            (in_scale2_t, scale2_t), (in_slope_t, slope_t), (in_unit1_t, unit1_t), (in_scale1_t, scale1_t),
        ],
        k_sem,
    )
    weights = load_all(
        [(w_qkv_s, v_qkv_s), (w_down_t, v_down_t), (w_up_t, v_up_t), (w_out_t, v_out_t)], w_sem
    )
    length = len_ref[0]
    for copy in kept[0:4]:
        copy.wait()

    @pl.when(owner)
    def _():
        kn[...] = natural(buf_s[64:128, :])
        vn[...] = natural(buf_s[128:192, :])
        k2n[...] = natural(dist[64:128, :])

    pl.semaphore_wait(barrier, 49)

    def pool_wide(m, ref):
        _, step, segments = CUTS[m]
        done = 0
        for n, (first, count) in enumerate(segments):
            cols = slice(first * 128, (first + count) * 128)
            pltpu.make_async_copy(
                ref.at[:, lanes((c * step + done) * 128, count * 128)], cf.at[0:128, cols], own_c.at[m + 8 * n]
            ).start()
            send_to(
                ref.at[:, lanes(((1 - c) * step + done) * 128, count * 128)], cf.at[128:256, cols],
                c_send.at[m + 8 * n], c_recv.at[m + 8 * n], partner,
            ).start()
            done += count

    def pool_narrow(m, ref):
        if ref is None:
            ref = nt.at[m, :, 0:128]
        else:
            pltpu.make_async_copy(ref, nt.at[m, :, 0:128], own_n.at[m]).start()
        send_to(ref, nt.at[m, :, 128:256], n_send.at[m], n_recv.at[m], partner).start()

    def products(k):
        begin, _, members, _ = BATCHES[k]
        for m in members:
            if m not in (3, 5):
                drain(nt.at[m, :, 0:128], own_n.at[m])
            drain(nt.at[m, :, 128:256], n_recv.at[m])
            for n, (first, count) in enumerate(CUTS[m][2]):
                cols = slice(first * 128, (first + count) * 128)
                drain(cf.at[0:128, cols], own_c.at[m + 8 * n])
                drain(cf.at[128:256, cols], c_recv.at[m + 8 * n])
                size = 3 if count % 3 == 0 else count

                def piece(i, m=m, first=first, size=size):
                    from_cols = lanes((first + i * size) * 128, size * 128)
                    to_cols = lanes((first - begin + i * size) * 128, size * 128)
                    pb[:, to_cols] = dot(nt[m], cf[:, from_cols]).astype(BF)

                loop(count // size, piece)

    def sem_of(k, p, kind):
        return 18 * k + 6 * p + kind

    def tiles(first, count):
        return slice(first * 128, (first + count) * 128)

    def rows_of(height, v):
        return pl.ds(pl.multiple_of(height * v, 16), height)

    def ring(p, stage):
        axis = ORDERS[p][stage]
        u = here_at[axis]
        around = [lax.rem(u + j, 4) for j in range(4)]
        return around, [at_axis(axis, v) for v in around]

    def stage_start(k, stage):
        begin, _, _, parts = BATCHES[k]
        for p, (first, count, used) in enumerate(parts):
            around, devices = ring(p, stage)
            if stage == 0:
                first_half = (used + 1) // 2
                one, two = (0, first_half), (first_half, used - first_half)
                for j, (start, size), to, dst, kind in (
                    (2, one, 1, rl, 0), (2, two, 3, rl, 1), (1, two, 1, l1.at[0], 2), (3, one, 3, l1.at[1], 3),
                ):
                    send_to(
                        pb.at[rows_of(192, around[j]), tiles(first - begin + start, size)],
                        dst.at[:, tiles(first + start, size)],
                        st_send.at[sem_of(k, p, 0)], st_recv.at[sem_of(k, p, kind)], devices[to],
                    ).start()
                continue
            for j in range(1, 4):
                if stage == 1:
                    src = a1.at[rows_of(48, around[j]), tiles(first, used)]
                    dst = l2.at[j - 1, :, tiles(first, used)]
                else:
                    src = a2.at[:, lanes(first * 128 + around[j] * count * 32, count * 32)]
                    dst = l3.at[j - 1, :, slice(first * 32, (first + count) * 32)]
                kind = 3 + stage
                send_to(
                    src, dst, st_send.at[sem_of(k, p, kind)], st_recv.at[sem_of(k, p, kind)], devices[j]
                ).start()

    def relay(k):
        begin, _, _, parts = BATCHES[k]
        for p, (first, count, used) in enumerate(parts):
            around, devices = ring(p, 0)
            first_half = (used + 1) // 2
            for start, size, to, slot in ((0, first_half, 1, 0), (first_half, used - first_half, 3, 1)):
                land = rl.at[:, tiles(first + start, size)]
                drain(land, st_recv.at[sem_of(k, p, slot)])
                own_cols = tiles(first - begin + start, size)

                def add(r, own_cols=own_cols, start=start, size=size, to=to, first=first, around=around):
                    own = pl.ds(pl.multiple_of(192 * around[to] + 16 * r, 16), 16)
                    rows = pl.ds(pl.multiple_of(16 * r, 16), 16)
                    total = pb[own, own_cols].astype(F32) + rl[rows, tiles(first + start, size)].astype(F32)
                    pb[own, own_cols] = total.astype(BF)

                loop(12, add)
                send_to(
                    pb.at[rows_of(192, around[to]), own_cols], l1.at[slot, :, tiles(first + start, size)],
                    st_send.at[sem_of(k, p, 1)], st_recv.at[sem_of(k, p, 2 + slot)], devices[to],
                ).start()

    def stage_sent(k, stage):
        for p, (first, count, used) in enumerate(BATCHES[k][3]):
            if stage == 0:
                drain(l1.at[:, :, tiles(first, used)], st_send.at[sem_of(k, p, 0)])
                drain(rl.at[:, tiles(first, used)], st_send.at[sem_of(k, p, 1)])
            elif stage == 1:
                drain(l2.at[:, :, tiles(first, used)], st_send.at[sem_of(k, p, 4)])
            else:
                drain(l3.at[:, :, slice(first * 32, (first + count) * 32)], st_send.at[sem_of(k, p, 5)])

    def stage_sum(k, stage):
        begin, _, _, parts = BATCHES[k]
        for p, (first, count, used) in enumerate(parts):
            at = here_at[ORDERS[p][stage]]
            cols = tiles(first, used)
            if stage == 0:
                for slot in range(2):
                    drain(l1.at[slot, :, cols], st_recv.at[sem_of(k, p, 2 + slot)])
                src, land, dst, height, peers, scols = pb, l1, a1, 192, 2, tiles(first - begin, used)
            elif stage == 1:
                drain(l2.at[:, :, cols], st_recv.at[sem_of(k, p, 4)])
                src, land, dst, height, peers, scols = a1, l2, a2, 48, 3, cols
            else:
                quarter = slice(first * 32, (first + count) * 32)
                drain(l3.at[:, :, quarter], st_recv.at[sem_of(k, p, 5)])
                total = a2[:, lanes(first * 128 + at * count * 32, count * 32)].astype(F32)
                for j in range(3):
                    total = total + l3[j, :, quarter].astype(F32)
                for i in range(8):
                    a3[i, 0:6, quarter] = total[6 * i : 6 * i + 6, :]
                continue

            def add(r, src=src, land=land, dst=dst, height=height, peers=peers, at=at, cols=cols, scols=scols):
                rows = pl.ds(pl.multiple_of(16 * r, 16), 16)
                own = pl.ds(pl.multiple_of(height * at + 16 * r, 16), 16)
                total = src[own, scols].astype(F32)
                for j in range(peers):
                    total = total + land[j, rows, cols].astype(F32)
                dst[rows, cols] = total.astype(BF)

            loop(height // 16, add)

    def final_each(k, act):
        for p, (first, count, _) in enumerate(BATCHES[k][3]):
            third = here_at[ORDERS[p][2]]
            for i in range(8):
                to = 32 * here_at[ORDERS[p][0]] + 8 * here_at[ORDERS[p][1]] + i
                src = a3.at[i, :, slice(first * 32, (first + count) * 32)]
                dst = out.at[:, lanes((c * TILES + first) * 128 + third * count * 32, count * 32)]
                act(to, src, dst, f_send.at[24 * k + 8 * p + i], f_recv.at[2 * k + c])

    def final_start(k):
        def act(to, src, dst, send_sem, recv_sem):
            @pl.when(to != me)
            def _():
                send_to(src, dst, send_sem, recv_sem, {"dp": to // 16, "blk": lax.rem(to, 16)}).start()

            @pl.when(to == me)
            def _():
                pltpu.make_async_copy(src, dst, recv_sem).start()

        final_each(k, act)

    def final_wait(k):
        begin, count, _, _ = BATCHES[k]
        for core in range(2):
            start = (core * TILES + begin) * 128
            drain(out.at[:, start : start + count * 128], f_recv.at[2 * k + core])

        def act(to, src, dst, send_sem, recv_sem):
            @pl.when(to != me)
            def _():
                send_to(src, dst, send_sem, recv_sem, {"dp": to // 16, "blk": lax.rem(to, 16)}).wait_send()

        final_each(k, act)

    def small_copy(slot):
        if slot == 0:
            return send_to(sma.at[0], sml.at[0], m_send.at[0], m_recv.at[0], partner)
        n, j = (slot - 1) // 3, (slot - 1) % 3 + 1
        axis = "xyz"[n]
        return send_to(
            sma.at[n + 1], sml.at[slot], m_send.at[slot], m_recv.at[slot],
            at_axis(axis, lax.rem(here_at[axis] + j, 4)),
        )

    def small_step(n):
        if n > 0:
            slots = (0,) if n == 1 else tuple(range(3 * n - 5, 3 * n - 2))
            total = sma[n - 1]
            for slot in slots:
                small_copy(slot).wait_recv()
                total = total + sml[slot]
            if n == 4:
                return total
            sma[n] = total
        for slot in (0,) if n == 0 else range(3 * n - 2, 3 * n + 1):
            small_copy(slot).start()
        return None

    def c1(h):
        return (
            datt_s.at[h], do_s.at[:, lanes(lax.rem(b, 8) * 128, 128)],
            s1.at[h], r1.at[lax.rem(b, 8)], owner_of(h + 6 * (b // 8)), b,
        )

    def c2(j):
        return dq_buf.at[:, lanes(j * 128, 128)], dq_s.at[head], s2.at[j], r2.at[head], 8 * half + j, b

    def c3(d):
        return dkv_buf.at[:, lanes(d * 128, 128)], dkv_s.at[hh], s3.at[d], r3.at[hh], d, b

    def c4(h):
        return src_t.at[h], do_t.at[:, lanes(b * 128, 128)], s4.at[h], r4.at[b], owner_of(h), b

    def c5(d):
        return dq_buf.at[:, lanes(d * 128, 128)], dqkv_t.at[hh, 0:64], s5.at[d], r5.at[hh], d, b

    def c6(d):
        return dkv_buf.at[:, lanes(d * 128, 128)], dqkv_t.at[hh, 64:192], s6.at[d], r6.at[hh], d, b

    def run_chunks(n, at, kt_ref, put, low, high):
        if low == 0:
            acc[...] = jnp.zeros_like(acc)
            x_ref[1] = jnp.zeros((SEQ, 2 * QC), BF)
        rest = (at, kn, k2n, vn, kt_ref, length, gf, x_ref, acc)

        def pair(i):
            backward_chunk(
                2 * i, jnp.maximum(2 * i - 1, 0), 0, *rest, lambda ch, g: put(ch, g, i > 0)
            )
            backward_chunk(2 * i + 1, 2 * i, 1, *rest, lambda ch, g: put(ch, g, True))

        loop(high - low, lambda i: pair(i + low))
        if 2 * high == n:
            backward_last(n - 1, 1, at, kt_ref, x_ref, acc, lambda ch, g: put(ch, g, True))

    def send_pair(copy, ch, real):
        if real is True:
            for i in range(2):
                start_to(*copy(2 * ch + i))
        else:
            @pl.when(real)
            def _():
                for i in range(2):
                    start_to(*copy(2 * ch + i))

    def teacher_at(ch):
        here = lanes(ch * QC, QC)
        return (
            buf_t[0:64, here], buf_s[0:64, here], do_t[:, here],
            lse_t[0:1, here], lse_s[0:1, here], weight_row(len_ref, flag_ref, head, ch * QC, hh < 6),
        )

    def teacher_put(ch, g, real):
        dq_buf[:, lanes(ch * QC, QC)] = g.astype(BF)
        send_pair(c5, ch, real)

    loop(6, lambda j: start_to(*c1(lax.rem(j + b, 6))))
    for m, ref in ((1, normed_turn_s), (2, g1r_s), (7, g2r_s)):
        pool_narrow(m, ref)
    for m, ref in ((1, gu_s), (2, att_s), (7, act_s)):
        pool_wide(m, ref)
    for m, ref in ((0, normed_turn_t), (4, hidden_turn), (6, x0_turn)):
        pool_narrow(m, ref)
    for m, ref in ((3, act_t), (5, att_t)):
        pool_wide(m, ref)

    products(0)
    stage_start(0, 0)

    @pl.when(owner)
    def _():
        loop(8, lambda i: got(do_s.at[:, lanes(i * 128, 128)], r1.at[i]))

        def at(ch):
            first = half * 1024 + ch * QC
            here = lanes(first, QC)
            return (
                buf_s[0:64, here], dist[0:64, here], do_s[:, lanes(ch * QC, QC)],
                lse_s[0:1, here], lse_d[0:1, here], weight_row(len_ref, flag_ref, head, first, True),
            )

        def put(ch, g, real):
            dq_buf[:, lanes(ch * QC, QC)] = g.astype(BF)
            send_pair(c2, ch, real)

        run_chunks(1024 // QC, at, buf_s, put, 0, 2)
        back_blocks(acc, dkv_buf)
        loop(16, lambda i: start_to(*c3(lax.rem(b + i, 16))))

    relay(0)
    loop(6, lambda h: got(dq_s.at[h], r2.at[h]))
    loop(12, lambda h: got(dkv_s.at[h], r3.at[h]))
    joined_s[:, 0:384] = natural_wide(dq_s[...].reshape(384, 128))
    for part in range(2):
        rows = slice(64 * part, 64 * part + 64)
        both = dkv_s[0:6, rows, :].astype(F32) + dkv_s[6:12, rows, :].astype(F32)
        joined_s[:, 384 * (part + 1) : 384 * (part + 2)] = both.reshape(384, 128).T.astype(BF)
    pool_wide(4, joined_s)
    sma[0] = sums_s[...]
    low_sums = jnp.sum(joined_s[...].astype(F32), axis=0, keepdims=True)
    sma[0, 20:21, 0:384] = low_sums[:, 0:384]
    sma[0, 20:21, 384:768] = low_sums[:, 768:1152]
    for copy in kept[4:]:
        copy.wait()
    weights[0].wait()
    grad_hidden = g1_s[...] + dot_t(joined_s[...], v_qkv_s[...])
    for i in (1, 2, 3):
        weights[i].wait()
    g1, datt = dense_down(
        grad_hidden, unit2_t[...], scale2_t[:, 0:1], unit1_t[...], scale1_t[:, 0:1],
        v_out_t, v_up_t, v_down_t, vec_t, slope_t, gu_t, nt.at[3, :, 0:128], nt.at[5, :, 0:128], sma.at[0], 0,
    )
    grad_in[...] = g1
    src_t[...] = datt.T.astype(BF).reshape(12, 64, 128)
    loop(12, lambda j: start_to(*c4(lax.rem(j + b, 12))))
    pool_wide(0, gu_t)
    pool_narrow(3, None)
    pool_narrow(5, None)
    late = load_all(
        [(w_qkv_t.at[:, 768 * p : 768 * (p + 1)], v_down_t.at[768 * p : 768 * (p + 1), :]) for p in range(3)],
        w_sem.at[pl.ds(4, 3)],
    )
    stage_sum(0, 0)
    stage_start(0, 1)

    @pl.when(owner)
    def _():
        kn[...] = natural(buf_t[64:128, :])
        vn[...] = natural(buf_t[128:192, :])
        k2n[...] = natural(buf_s[64:128, :])

    stage_sent(0, 0)
    products(1)
    stage_start(1, 0)

    @pl.when(owner)
    def _():
        loop(8, lambda j: sent_to(*c2(j)))
        loop(16, lambda d: sent_to(*c3(d)))
        loop(16, lambda i: got(do_t.at[:, lanes(i * 128, 128)], r4.at[i]))

        run_chunks(SEQ // QC, teacher_at, buf_t, teacher_put, 0, TURN)

    relay(1)

    @pl.when(owner)
    def _():
        run_chunks(SEQ // QC, teacher_at, buf_t, teacher_put, TURN, SEQ // QC // 2)
        back_blocks(acc, dkv_buf)
        loop(16, lambda i: start_to(*c6(lax.rem(b + i, 16))))

    stage_sum(0, 1)
    stage_start(0, 2)
    loop(12, lambda h: got(dqkv_t.at[h, 0:64], r5.at[h]))
    loop(12, lambda h: got(dqkv_t.at[h, 64:192], r6.at[h]))
    for part in range(3):
        joined_t[:, 768 * part : 768 * (part + 1)] = natural_wide(
            dqkv_t[:, 64 * part : 64 * (part + 1), :].reshape(768, 128)
        )
    pool_wide(6, joined_t)
    for row, part in ((10, 0), (11, 2)):
        sma[0, row : row + 1, :] = jnp.sum(
            joined_t[:, 768 * part : 768 * (part + 1)].astype(F32), axis=0, keepdims=True
        )
    small_step(0)
    stage_sum(1, 0)
    stage_start(1, 1)
    stage_sent(1, 0)
    products(2)
    stage_start(2, 0)
    small_step(1)
    stage_sum(0, 2)
    final_start(0)
    for copy in late:
        copy.wait()
    grad = grad_in[...]
    for p in range(3):
        grad = grad + dot_t(joined_t[:, 768 * p : 768 * (p + 1)], v_down_t[768 * p : 768 * (p + 1), :])
    place_of = lax.broadcasted_iota(jnp.int32, (128, 128), 0)
    turned = jnp.where((place_of == source[...]) & (flags[...] == 1), 1.0, 0.0)
    back = turned.astype(BF)
    one = grad.astype(BF)
    rest = grad - one.astype(F32)
    two = rest.astype(BF)
    three = (rest - two.astype(F32)).astype(BF)
    copied = dot(back, one) + dot(back, two) + dot(back, three)
    kept = jnp.sum(turned.T, axis=1, keepdims=True) < 0.5
    grad_in[...] = jnp.where(kept, grad, 0.0) + copied
    relay(2)
    small_step(2)
    stage_sum(1, 1)
    stage_start(1, 2)
    stage_sum(2, 0)
    stage_start(2, 1)
    small_step(3)
    stage_sum(1, 2)
    final_start(1)
    stage_sum(2, 1)
    stage_start(2, 2)
    sums[...] = small_step(4)
    stage_sum(2, 2)
    final_start(2)

    @pl.when(owner)
    def _():
        loop(16, lambda d: sent_to(*c5(d)))
        loop(16, lambda d: sent_to(*c6(d)))

    loop(6, lambda h: sent_to(*c1(h)))
    loop(12, lambda h: sent_to(*c4(h)))
    for m, (_, _, segments) in enumerate(CUTS):
        for n, (first, count) in enumerate(segments):
            drain(cf.at[128:256, slice(first * 128, (first + count) * 128)], c_send.at[m + 8 * n])
        drain(nt.at[m, :, 128:256], n_send.at[m])
    for slot in range(10):
        small_copy(slot).wait_send()
    for k, stage in ((0, 1), (0, 2), (1, 1), (1, 2), (2, 0), (2, 1), (2, 2)):
        stage_sent(k, stage)
    for k in range(3):
        final_wait(k)


ANY = pl.BlockSpec(memory_space=pl.ANY)


def mega_call(kernel, ident, specs, outs, scratch, args, name, out_spec):
    return pl.pallas_call(
        kernel,
        name=name,
        out_shape=tuple(jax.ShapeDtypeStruct(s, t) for s, t in outs),
        in_specs=specs,
        out_specs=tuple(out_spec for _ in outs),
        scratch_shapes=scratch,
        compiler_params=pltpu.CompilerParams(
            collective_id=ident, has_side_effects=True, vmem_limit_bytes=62 * MIB
        ),
    )(*args)


def vb(*shape):
    return pltpu.VMEM(shape, BF)


def vf(*shape):
    return pltpu.VMEM(shape, F32)


def run_forward(lengths, x_in, source, flags, cot, weights, smalls):
    outs = [
        ((128, 768), F32), ((192, SEQ), BF), ((128, SEQ), BF), ((192, SEQ), BF),
        ((8, SEQ), F32), ((8, SEQ), F32), ((8, SEQ), F32),
        *[((768, 128), BF)] * 6,
        ((128, 768), BF), ((128, 3072), BF), ((128, 384), BF), ((128, 1536), BF), ((128, 1536), BF),
        ((128, 3072), BF), ((128, 768), F32), ((128, 128), F32), ((128, 768), F32), ((128, 128), F32),
        ((128, 768), F32), ((6, 64, 128), BF), ((24, 768), F32),
    ]
    scratch = [pltpu.VMEM(shape, kind) for shape, kind in outs] + [
        vb(768, 2304), vb(768, 768), vb(768, 3072), vb(3072, 768),
        vb(768, 1152), vb(384, 768), vb(768, 1536), vb(1536, 768),
        vf(128, 768), vb(12, 192, 128), vb(6, 192, 128), vb(12, 64, 128), vb(6, 64, 128),
        vb(64, SEQ), vb(64, 1024), vb(SEQ, 64), vf(2, SEQ, QC), vb(2, SEQ, QC), vf(6, 8, QC),
        vb(128, 1536), vf(128, 768), vf(128, 128),
        DMA((8,)), DMA((12,)), DMA((16,)), DMA((6,)), DMA((16,)), DMA((16,)), DMA((12,)), DMA((4,)),
        DMA((12,)), DMA((16,)), DMA((8,)), DMA((6,)), DMA((1,)), DMA((26,)),
    ]
    specs = [SMEM] + [VMEM] * 4 + [ANY] * 8 + [VMEM] * 6
    return mega_call(
        forward_kernel, 1, specs, outs, scratch, (lengths, x_in, source, flags, cot, *weights, *smalls), "forward", ANY
    )


def run_backward(lengths, head_flags, source, flags, weights, kept, held, pooled):
    outs = [((128, 768), F32), ((8, 2 * WIDE), F32), ((24, 768), F32)]
    scratch = [
        vb(768, 1152), vb(3072, 768), vb(768, 3072), vb(768, 768),
        vb(192, SEQ), vb(128, SEQ), vf(8, SEQ), vf(8, SEQ), vf(128, 768), vb(192, SEQ), vf(8, SEQ),
        vf(128, 768), vf(128, 128), vb(128, 3072), vf(128, 768), vf(128, 128),
        vb(128, 2304), vb(128, 1152), vb(128, 3072),
        vb(12, 64, 128), vb(64, 1024), vb(64, SEQ), vb(6, 64, 128), vb(12, 128, 128), vb(12, 192, 128),
        vb(64, SEQ), vb(128, SEQ),
        vb(SEQ, 64), vb(SEQ, 64), vb(SEQ, 64), vf(SEQ, QC), vb(2, SEQ, 2 * QC), vf(SEQ, 128),
        vb(8, 768, 256), vb(256, WIDE), vb(768, PB_TILES * 128),
        vb(192, WIDE), vb(2, 192, WIDE), vb(192, WIDE), vb(3, 48, WIDE), vb(48, WIDE), vb(3, 48, WIDE // 4), vf(8, 8, WIDE // 4),
        vf(10, 24, 768), vf(4, 24, 768),
        DMA((7,)), DMA((12,)), DMA((6,)), DMA((8,)), DMA((8,)), DMA((6,)), DMA((16,)), DMA((12,)),
        DMA((12,)), DMA((16,)), DMA((16,)), DMA((12,)), DMA((16,)), DMA((12,)),
        DMA((8,)), DMA((24,)), DMA((8,)), DMA((8,)), DMA((24,)), DMA((24,)),
        DMA((54,)), DMA((54,)), DMA((72,)), DMA((6,)), DMA((10,)), DMA((10,)),
    ]
    specs = [SMEM] * 2 + [VMEM] * 2 + [ANY] * (5 + len(kept)) + [VMEM] * len(held) + [ANY] * len(pooled)
    return mega_call(
        backward_kernel, 2, specs, outs, scratch,
        (lengths, head_flags, source, flags, *weights, *kept, *held, *pooled), "backward", VMEM,
    )


def unpack_kernel(whole, sums, first_in, second_in, *outs):
    first_out, second_out, outs, copy_sem = outs[0], outs[1], outs[2:16], outs[16]
    copies = load_all([(first_in, first_out), (second_in, second_out)], copy_sem)

    def columns(m):
        count, step, segments = CUTS[m]
        skip = count - step
        pieces = [whole[:, first * 128 : (first + size) * 128] for first, size in segments]
        for first, size in segments:
            start = TILES + first + skip
            pieces.append(whole[:, start * 128 : (start + size - skip) * 128])
            skip = 0
        return jnp.concatenate(pieces, axis=1)

    for m, o in ((6, 0), (5, 2), (0, 3), (3, 4), (4, 7), (2, 9), (1, 10), (7, 11)):
        outs[o][...] = columns(m)[0:6]
    i = 16 * lax.axis_index("dp") + lax.axis_index("blk")

    def turn(rows, by):
        return pltpu.roll(rows, lax.rem(768 - by, 768), 1)

    def pick(first, count, per):
        row = first + (i * per) // 768
        wide = jnp.broadcast_to(sums[pl.ds(row, 1), :], (8, 768))
        return turn(wide, lax.rem(i * per, 768))[0:1, 0:per]

    outs[1][...] = pick(10, 2, 12)
    outs[5][...] = pick(6, 4, 24)
    outs[8][...] = pick(20, 1, 6)
    outs[12][...] = pick(18, 2, 12)
    outs[6][...] = turn(sums[0:8, :], i * 6)[0:6, 0:6]
    outs[13][...] = turn(sums[8:24, :], i * 6)[4:10, 0:6]
    for copy in copies:
        copy.wait()


def unpack(whole, sums, output, grad_in):
    shapes = (
        (6, 2304), (1, 12), (6, 768), (6, 3072), (6, 3072), (1, 24), (6, 6),
        (6, 1152), (1, 6), (6, 384), (6, 1536), (6, 1536), (1, 12), (6, 6),
    )
    outs = list(
        pl.pallas_call(
            unpack_kernel,
            name="unpack",
            out_shape=tuple(jax.ShapeDtypeStruct(s, F32) for s in ((128, 768), (128, 768)) + shapes),
            in_specs=[VMEM] * 2 + [ANY] * 2,
            out_specs=(ANY, ANY) + tuple(VMEM for _ in shapes),
            scratch_shapes=[DMA((2,))],
            compiler_params=pltpu.CompilerParams(vmem_limit_bytes=40 * MIB),
        )(whole, sums, output, grad_in)
    )
    for i in (3, 7, 10, 14):
        outs[i] = outs[i].reshape(-1)
    for i in (4, 6, 11, 13):
        outs[i] = outs[i].T
    outs[0], outs[1] = outs[0][None], outs[1][None]
    return tuple(outs)


def per_device(
    inputs, aug_source, aug_flags, lengths, head_flags, cotangent,
    qkv_teacher, qv_bias_teacher, out_teacher, up_teacher, down_teacher, up_bias_teacher, vectors_teacher,
    qkv_student, qv_bias_student, out_student, up_student, down_student, up_bias_student, vectors_student,
):
    (
        output, buf_t, dist, buf_s, lse_t, lse_d, lse_s,
        x0_turn, normed_turn_t, hidden_turn, normed_turn_s, g1r_s, g2r_s,
        att_t, act_t, att_s, act_s, gu_s,
        slope_t, unit1_t, scale1_t, unit2_t, scale2_t, g1_s, datt_s, sums_s,
    ) = run_forward(
        lengths, inputs[0], aug_source, aug_flags, cotangent[0],
        (qkv_teacher, out_teacher, up_teacher, down_teacher, qkv_student, out_student, up_student, down_student),
        (
            qv_bias_teacher[None], up_bias_teacher[None], vectors_teacher,
            qv_bias_student[None], up_bias_student[None], vectors_student,
        ),
    )
    grad_in, whole, total = run_backward(
        lengths, head_flags, aug_source, aug_flags,
        (qkv_student, down_teacher, up_teacher, out_teacher, qkv_teacher),
        (
            buf_s, dist, lse_s, lse_d, g1_s, buf_t, lse_t,
            unit2_t, scale2_t, slope_t, unit1_t, scale1_t, datt_s,
        ),
        (vectors_teacher, sums_s),
        (
            x0_turn, normed_turn_t, hidden_turn, normed_turn_s, g1r_s, g2r_s,
            att_t, act_t, att_s, act_s, gu_s,
        ),
    )
    return unpack(whole, total, output, grad_in)


def solution(mesh):
    both = ("dp", "blk")
    row, flat, col = P(both, None), P(both), P(None, both)
    tokens, marks = P("dp", "blk", None), P("dp", "blk")
    return jax.shard_map(
        per_device,
        mesh=mesh,
        in_specs=(tokens, marks, marks, P("dp"), P(), tokens) + (P(),) * 14,
        out_specs=(tokens, tokens) + (row, flat, col, row, col, flat, col) * 2,
        check_vma=False,
    )
```

```python
import jax
import jax.numpy as jnp
from jax import lax
from jax.experimental import pallas as pl
from jax.experimental.pallas import tpu as pltpu
from jax.sharding import PartitionSpec as P

MESH = pl.DeviceIdType.MESH
LOG2E = 1.4426950408889634
C2 = 0.125 * LOG2E
SEQ = 2048
QC = 256
KT = 256
NKT = SEQ // KT
MIB = 1 << 20


def dot(a, b):
    return jnp.dot(a, b, preferred_element_type=jnp.float32)


def place():
    b = lax.axis_index("blk")
    r = lax.rem(lax.rem(b, 4) - b // 4 + 7, 4)
    return b, 3 * (b // 4) + r, r < 3


def owner_of(hh):
    y = hh // 3
    return 4 * y + lax.rem(y + lax.rem(hh, 3) + 1, 4)


def copy_to(src, dst, send_sem, recv_sem, d):
    return pltpu.make_async_remote_copy(
        src_ref=src,
        dst_ref=dst,
        send_sem=send_sem,
        recv_sem=recv_sem,
        device_id={"blk": d},
        device_id_type=MESH,
    )


def start_to(src, dst, sems, d, b):
    send_sem, recv_sem, own_sem = sems

    @pl.when(d != b)
    def _():
        copy_to(src, dst, send_sem, recv_sem, d).start()

    @pl.when(d == b)
    def _():
        pltpu.make_async_copy(src, dst, own_sem).start()


def arrive(own, blocks, count, sems):
    @pl.when(own)
    def _():
        got(blocks(count - 1), sems[1])
        got(blocks(1), sems[2])

    @pl.when(jnp.logical_not(own))
    def _():
        got(blocks(count), sems[1])


def leave(own, blocks, count, sems):
    @pl.when(own)
    def _():
        got(blocks(count - 1), sems[0])

    @pl.when(jnp.logical_not(own))
    def _():
        got(blocks(count), sems[0])


def got(dst, recv_sem):
    pltpu.make_async_copy(dst, dst, recv_sem).wait()


def lanes(start, size):
    return pl.ds(pl.multiple_of(start, 128), size)


def fold(v):
    return jnp.sum(v.reshape(v.shape[0] // 8, 8, v.shape[1]), axis=0)


def key_ok(length):
    rows = lax.broadcasted_iota(jnp.int32, (KT, QC), 0) + (SEQ - KT)
    return rows < length


def natural(x):
    return x.astype(jnp.float32).T.astype(jnp.bfloat16)


def weight_row(len_ref, flag_ref, head, first, use):
    q = lax.broadcasted_iota(jnp.int32, (1, QC), 1) + first
    factor = jnp.where(use, flag_ref[head].astype(jnp.float32) * (2.0 * SEQ), 0.0)
    return jnp.where(q < len_ref[0], factor, 0.0)


SMEM = pl.BlockSpec(memory_space=pltpu.SMEM)
VMEM = pl.BlockSpec(memory_space=pltpu.VMEM)
DMA = pltpu.SemaphoreType.DMA
BF = jnp.bfloat16
F32 = jnp.float32


SQRT_HALF = 0.7071067811865476
INV_SQRT_2PI = 0.3989422804014327


def dot_t(a, b):
    return lax.dot_general(a, b, (((1,), (1,)), ((), ())), preferred_element_type=F32)


def norm_forward(v, gain, shift):
    center = v - jnp.mean(v, axis=-1, keepdims=True)
    scale = lax.rsqrt(jnp.mean(center * center, axis=-1, keepdims=True) + 1e-06)
    unit = center * scale
    return unit * gain + shift, unit, scale


def norm_backward(grad, gain, unit, scale):
    scaled = grad * gain
    mean_one = jnp.mean(scaled, axis=-1, keepdims=True)
    mean_two = jnp.mean(scaled * unit, axis=-1, keepdims=True)
    return (
        (scaled - mean_one - unit * mean_two) * scale,
        jnp.sum(grad * unit, axis=0, keepdims=True),
        jnp.sum(grad, axis=0, keepdims=True),
    )


def qkv_blocks(low, w, bias, src, heads):
    span = heads * 64
    for part in range(3):
        joint = dot(low, w[:, part * span : (part + 1) * span])
        if part != 1:
            first = 0 if part == 0 else span
            joint = joint + bias[first : first + span].reshape(1, span)
        src[:, part * 64 : (part + 1) * 64, :] = joint.T.astype(BF).reshape(heads, 64, 128)


def dense_up(residual, attended, w_out, w_up, w_down, up_bias, vec, act, slope, unit1, scale1, normed_turned):
    ff = up_bias.shape[0]
    first = residual + dot(attended, w_out) + vec[0:1, :]
    normed, unit, scale = norm_forward(first, vec[1:2, :], vec[2:3, :])
    unit1[...] = unit
    scale1[...] = jnp.broadcast_to(scale, (128, 128))
    low = normed.astype(BF)
    normed_turned[...] = normed.T.astype(BF)
    step = 512
    for j in range(ff // step):
        cols = slice(j * step, (j + 1) * step)
        u = dot(low, w_up[:, cols]) + up_bias[cols].reshape(1, step)
        cdf = 0.5 + 0.5 * lax.erf(u * SQRT_HALF)
        act[:, cols] = (u * cdf).astype(BF)
        slope[:, cols] = (cdf + u * (jnp.exp(-0.5 * u * u) * INV_SQRT_2PI)).astype(slope.dtype)
    second = normed + dot(act[...], w_down) + vec[3:4, :]
    return norm_forward(second, vec[4:5, :], vec[5:6, :])


def dense_down(grad, unit2, scale2, unit1, scale1, w_out, w_up, w_down, vec, slope, gu, g2r, g1r, sums, row, hooks=(None,) * 3):
    ff = w_up.shape[1]
    g2, gain_two, shift_two = norm_backward(grad, vec[4:5, :], unit2, scale2)
    low2 = g2.astype(BF)
    g2r[...] = g2.T.astype(BF)
    if hooks[0]:
        hooks[0]()
    step = 512
    for j in range(ff // step):
        cols = slice(j * step, (j + 1) * step)
        g = dot_t(low2, w_down[cols, :]) * slope[:, cols].astype(F32)
        gu[:, cols] = g.astype(BF)
        total = jnp.sum(g, axis=0, keepdims=True)
        done = 0
        while done < step:
            at = j * step + done
            size = min(step - done, 768 - at % 768)
            sums[row + 6 + at // 768 : row + 7 + at // 768, at % 768 : at % 768 + size] = total[:, done : done + size]
            done += size
    if hooks[1]:
        hooks[1]()
    g1, gain_one, shift_one = norm_backward(g2 + dot_t(gu[...], w_up[...]), vec[1:2, :], unit1, scale1)
    low1 = g1.astype(BF)
    g1r[...] = g1.T.astype(BF)
    if hooks[2]:
        hooks[2]()
    rows = (
        jnp.sum(g1, axis=0, keepdims=True), gain_one, shift_one,
        jnp.sum(g2, axis=0, keepdims=True), gain_two, shift_two,
    )
    for i, value in enumerate(rows):
        sums[row + i : row + i + 1, :] = value
    return g1, dot_t(low1, w_out[...])


def load_all(pairs, sem):
    copies = [pltpu.make_async_copy(a, b, sem.at[i]) for i, (a, b) in enumerate(pairs)]
    for copy in copies:
        copy.start()
    return copies


def forward_stage(c_score, c_exp, c_out, do, par, q_at, kn, v_ref, s_ref, p_ref, st, put, length):
    if do[0]:
        q = q_at(c_score)
    m8 = jnp.full((8, QC), -3e38, F32)
    l8 = jnp.zeros((8, QC), F32)
    out = jnp.zeros((64, QC), F32)
    top = st[1 - par, 0:1, :]
    for t in range(NKT):
        rows = slice(t * KT, (t + 1) * KT)
        if do[0]:
            s = dot(kn[rows, :], q)
            if t == NKT - 1:
                s = jnp.where(key_ok(length), s, -1e30)
            s_ref[par, rows, :] = s
            m8 = jnp.maximum(m8, jnp.max(s.reshape(KT // 8, 8, QC), axis=0))
        if do[1]:
            p = jnp.exp2(s_ref[1 - par, rows, :] * C2 - top)
            l8 = l8 + fold(p)
            p_ref[1 - par, rows, :] = p.astype(BF)
        if do[2]:
            out = out + dot(v_ref[128:192, rows], p_ref[par, rows, :])
    if do[2]:
        put(c_out, out / st[2 + par, 0:1, :], st[4 + par, 0:1, :])
    if do[1]:
        total = jnp.sum(l8, axis=0, keepdims=True)
        st[3 - par] = jnp.broadcast_to(total, (8, QC))
        st[5 - par] = jnp.broadcast_to(top + jnp.log2(total), (8, QC))
    if do[0]:
        st[par] = jnp.broadcast_to(jnp.max(m8, axis=0, keepdims=True) * C2, (8, QC))


def forward_chunks(n, values_here, *rest):
    forward_stage(0, 0, 0, (1, 0, 0), 0, *rest)
    forward_stage(1, 0, 0, (1, 1, 0), 1, *rest)
    values_here()

    def body(i, carry):
        forward_stage(2 * i, 2 * i - 1, 2 * i - 2, (1, 1, 1), 0, *rest)
        forward_stage(2 * i + 1, 2 * i, 2 * i - 1, (1, 1, 1), 1, *rest)
        return carry

    lax.fori_loop(1, n // 2, body, 0)
    forward_stage(0, n - 1, n - 2, (0, 1, 1), 0, *rest)
    forward_stage(0, 0, n - 1, (0, 0, 1), 1, *rest)


def backward_chunk(c, prev, par, at, kn, k2n, vn, kt_ref, length, gf, x_ref, acc, put):
    q, q2, do, lse, lse2, weight = at(c)
    pq, _, pdo, _, _, _ = at(prev)
    both = jnp.concatenate([pq, pdo], axis=0).astype(F32).T
    col = lax.broadcasted_iota(jnp.int32, (QC, 128), 1)
    rhs = jnp.concatenate(
        [jnp.where(col < 64, both, 0.0), jnp.where(col < 64, 0.0, both)], axis=0
    ).astype(BF)
    d8 = jnp.zeros((8, QC), F32)
    dq = jnp.zeros((64, QC), F32)
    for t in range(NKT):
        rows = slice(t * KT, (t + 1) * KT)
        p = jnp.exp2(dot(kn[rows, :], q) * C2 - lse)
        p2 = jnp.exp2(dot(k2n[rows, :], q2) * C2 - lse2)
        if t == NKT - 1:
            ok = key_ok(length)
            p = jnp.where(ok, p, 0.0)
            p2 = jnp.where(ok, p2, 0.0)
        g = dot(vn[rows, :], do) + weight * (p - p2)
        d8 = d8 + fold(p * g)
        gf[rows, :] = g
        x_ref[par, rows, QC:] = p.astype(BF)
        acc[rows, :] += dot(x_ref[1 - par, rows, :], rhs)
        dq = dq + dot(kt_ref[64:128, rows], x_ref[1 - par, rows, :QC])
    put(prev, dq * 0.125)
    delta = jnp.sum(d8, axis=0, keepdims=True)
    for t in range(NKT):
        rows = slice(t * KT, (t + 1) * KT)
        x_ref[par, rows, :QC] = (x_ref[par, rows, QC:].astype(F32) * (gf[rows, :] - delta)).astype(BF)


def backward_last(prev, par, at, kt_ref, x_ref, acc, put, put_keys):
    pq, _, pdo, _, _, _ = at(prev)
    both = jnp.concatenate([pq, pdo], axis=0).astype(F32).T
    col = lax.broadcasted_iota(jnp.int32, (QC, 128), 1)
    rhs = jnp.concatenate(
        [jnp.where(col < 64, both, 0.0), jnp.where(col < 64, 0.0, both)], axis=0
    ).astype(BF)
    dq = jnp.zeros((64, QC), F32)
    row = lax.broadcasted_iota(jnp.int32, (128, KT), 0)
    for t in range(NKT):
        rows = slice(t * KT, (t + 1) * KT)
        dq = dq + dot(kt_ref[64:128, rows], x_ref[par, rows, :QC])
    put(prev, dq * 0.125)
    for t in range(NKT):
        rows = slice(t * KT, (t + 1) * KT)
        total = (acc[rows, :] + dot(x_ref[par, rows, :], rhs)).T
        put_keys(t, jnp.where(row < 64, total * 0.125, total).astype(BF))


def natural_wide(blocks):
    return blocks.astype(F32).T.astype(BF)


def loop(n, body):
    def step(i, carry):
        body(i)
        return carry

    lax.fori_loop(0, n, step, 0)


def greet_start():
    b = lax.axis_index("blk")
    sem = pltpu.get_barrier_semaphore()
    loop(15, lambda i: pl.semaphore_signal(
        sem, inc=1, device_id={"blk": lax.rem(b + 1 + i, 16)}, device_id_type=MESH
    ))


def greet_end():
    pl.semaphore_wait(pltpu.get_barrier_semaphore(), 15)


def forward_kernel(
    len_ref, x_in, source, flags, cot,
    w_qkv_t, w_out_t, w_up_t, w_down_t, w_qkv_s, w_out_s, w_up_s, w_down_s,
    bias_t, upb_t, vec_t, bias_s, upb_s, vec_s,
    *refs,
):
    kept_out, refs = refs[0:26], refs[26:]
    kept, refs = refs[0:26], refs[26:]
    (
        output, buf_t, dist, buf_s, lse_t, lse_d, lse_s,
        x0_turn, normed_turn_t, hidden_turn, normed_turn_s, g1r_s, g2r_s,
        att_t, act_t, att_s, act_s, gu_s,
        slope_t, unit1_t, scale1_t, unit2_t, scale2_t, g1_s, datt_s, sums,
    ) = kept
    (
    v_qkv_t, v_out_t, v_up_t, v_down_t, v_qkv_s, v_out_s, v_up_s, v_down_s,
    x0_ref, src_t, src_s, land_t, land_s, o_t, o_s, kn, s_ref, p_ref, st,
    slope_s, unit1_s, scale1_s,
    w_sem, x_sem, lse_sem, local_sem, keep_sem,
    ) = refs

    def keep(*which):
        for i in which:
            pltpu.make_async_copy(kept[i], kept_out[i], keep_sem.at[i]).start()

    b, hh, owner = place()
    half, head = hh // 6, lax.rem(hh, 6)
    t_sems, tv_sems, d_sems, a_sems, s_sems, sv_sems, b_sems = [
        tuple(x_sem.at[3 * i + j] for j in range(3)) for i in range(7)
    ]
    mine_half = owner & (half == b // 8)
    greet_start()
    weights = load_all(
        [
            (w_qkv_t, v_qkv_t), (w_out_t, v_out_t), (w_up_t, v_up_t), (w_down_t, v_down_t),
            (w_qkv_s, v_qkv_s), (w_out_s, v_out_s), (w_up_s, v_up_s), (w_down_s, v_down_s),
        ],
        w_sem,
    )
    length = len_ref[0]
    replaced = flags[...] == 1
    place_of = lax.broadcasted_iota(jnp.int32, (128, 128), 0)
    turned = jnp.where((place_of == source[...]) & replaced, 1.0, 0.0)
    chooser = turned.T
    taken = dot(chooser.astype(BF), x_in[...])
    x0 = jnp.where(jnp.sum(chooser, axis=1, keepdims=True) > 0.5, taken, x_in[...].astype(F32))
    x0_ref[...] = x0
    low = x0.astype(BF)
    x0_turn[...] = x0.T.astype(BF)
    keep(7)
    weights[0].wait()
    qkv_blocks(low, v_qkv_t, bias_t, src_t, 12)
    greet_end()

    mine = lanes(b * 128, 128)

    def t_copy(h):
        return src_t.at[h, 0:128], buf_t.at[0:128, mine], t_sems, owner_of(h), b

    def tv_copy(h):
        return src_t.at[h, 128:192], buf_t.at[128:192, mine], tv_sems, owner_of(h), b

    def d_copy(h):
        return src_t.at[h, 0:128], dist.at[:, mine], d_sems, owner_of(h + 6), b

    loop(12, lambda j: start_to(*t_copy(lax.rem(j + b, 12))))
    loop(12, lambda j: start_to(*tv_copy(lax.rem(j + b, 12))))

    def a_copy(d):
        return o_t.at[:, lanes(d * 128, 128)], land_t.at[hh], a_sems, d, b

    @pl.when(owner)
    def _():
        arrive(owner, lambda n: buf_t.at[0:128, 0 : n * 128], 16, t_sems)
        kn[...] = natural(buf_t[64:128, :])

        def put(c, o, stat):
            here = lanes(c * QC, QC)
            o_t[:, here] = o.astype(BF)
            lse_t[:, here] = jnp.broadcast_to(stat, (8, QC))
            for i in range(2):
                start_to(*a_copy(2 * c + i))

        forward_chunks(
            SEQ // QC,
            lambda: arrive(owner, lambda n: buf_t.at[128:192, 0 : n * 128], 16, tv_sems),
            lambda c: buf_t[0:64, lanes(c * QC, QC)], kn, buf_t, s_ref, p_ref, st, put, length,
        )

    @pl.when(owner & (hh < 6))
    def _():
        lse_d[:, 0:1024] = lse_t[:, 0:1024]
        copy_to(
            lse_t.at[:, 1024:2048], lse_d.at[:, 1024:2048], lse_sem.at[0], lse_sem.at[1], owner_of(hh + 6)
        ).start()
        pltpu.make_async_copy(buf_t.at[0:128], dist, local_sem.at[0]).start()

    arrive(owner, lambda n: land_t.at[0:n], 12, a_sems)
    loop(6, lambda j: start_to(*d_copy(lax.rem(j + b, 6))))
    att_t[...] = natural_wide(land_t[...].reshape(768, 128))
    keep(1, 4, 13)
    for i in (1, 2, 3):
        weights[i].wait()
    hidden, unit, scale = dense_up(
        x0_ref[...], att_t[...], v_out_t[...], v_up_t, v_down_t[...], upb_t, vec_t,
        act_t, slope_t, unit1_t, scale1_t, normed_turn_t,
    )
    unit2_t[...] = unit
    scale2_t[...] = jnp.broadcast_to(scale, (128, 128))
    x0_ref[...] = hidden
    low = hidden.astype(BF)
    hidden_turn[...] = hidden.T.astype(BF)
    keep(8, 9, 14, 18, 19, 20, 21, 22)
    weights[4].wait()
    qkv_blocks(low, v_qkv_s, bias_s, src_s, 6)

    def s_copy(h):
        return (
            src_s.at[lax.rem(h, 6), 0:128], buf_s.at[0:128, mine], s_sems, owner_of(h), b
        )

    def sv_copy(h):
        return (
            src_s.at[lax.rem(h, 6), 128:192], buf_s.at[128:192, mine],
            sv_sems, owner_of(h), b,
        )

    loop(12, lambda j: start_to(*s_copy(lax.rem(j + b, 12))))
    loop(12, lambda j: start_to(*sv_copy(lax.rem(j + b, 12))))

    def b_copy(j):
        return o_s.at[:, lanes(j * 128, 128)], land_s.at[head], b_sems, 8 * half + j, b

    @pl.when(owner)
    def _():
        lse_s[:, 0:1024] = jnp.full((8, 1024), 1e30, F32)
        arrive(owner, lambda n: buf_s.at[0:128, 0 : n * 128], 16, s_sems)
        kn[...] = natural(buf_s[64:128, :])

        def put(c, o, stat):
            o_s[:, lanes(c * QC, QC)] = o.astype(BF)
            lse_s[:, lanes(half * 1024 + c * QC, QC)] = jnp.broadcast_to(stat, (8, QC))
            for i in range(2):
                start_to(*b_copy(2 * c + i))

        forward_chunks(
            1024 // QC,
            lambda: arrive(owner, lambda n: buf_s.at[128:192, 0 : n * 128], 16, sv_sems),
            lambda c: buf_s[0:64, lanes(half * 1024 + c * QC, QC)],
            kn, buf_s, s_ref, p_ref, st, put, length,
        )

    @pl.when(owner & (hh >= 6))
    def _():
        copy_to(
            lse_s.at[:, 1024:2048], lse_s.at[:, 1024:2048], lse_sem.at[2], lse_sem.at[3], owner_of(hh - 6)
        ).start()

    arrive(mine_half, lambda n: land_s.at[0:n], 6, b_sems)
    att_s[...] = natural_wide(land_s[...].reshape(384, 128))
    keep(3, 15)
    for i in (5, 6, 7):
        weights[i].wait()
    result, unit, scale = dense_up(
        x0_ref[...], att_s[...], v_out_s[...], v_up_s, v_down_s[...], upb_s, vec_s,
        act_s, slope_s, unit1_s, scale1_s, normed_turn_s,
    )
    output[...] = result
    keep(0, 10, 16)
    sums[...] = jnp.zeros((24, 768), F32)
    g1, datt = dense_down(
        cot[...].astype(F32), unit, scale, unit1_s[...], scale1_s[:, 0:1],
        v_out_s, v_up_s, v_down_s, vec_s, slope_s, gu_s, g2r_s, g1r_s, sums, 12,
    )
    g1_s[...] = g1
    datt_s[...] = datt.T.astype(BF).reshape(6, 64, 128)
    keep(11, 12, 17, 23, 24, 25)

    @pl.when(owner)
    def _():
        got(o_t.at[:, 0 : 15 * 128], a_sems[0])
        leave(mine_half, lambda n: o_s.at[:, 0 : n * 128], 8, b_sems)

    @pl.when(owner & (hh < 6))
    def _():
        copy_to(
            lse_t.at[:, 1024:2048], lse_d.at[:, 1024:2048], lse_sem.at[0], lse_sem.at[1], owner_of(hh + 6)
        ).wait_send()
        pltpu.make_async_copy(buf_t.at[0:128], dist, local_sem.at[0]).wait()
        got(lse_s.at[:, 1024:2048], lse_sem.at[3])

    @pl.when(owner & (hh >= 6))
    def _():
        arrive(hh >= 6, lambda n: dist.at[:, 0 : n * 128], 16, d_sems)
        got(lse_d.at[:, 1024:2048], lse_sem.at[1])
        copy_to(
            lse_s.at[:, 1024:2048], lse_s.at[:, 1024:2048], lse_sem.at[2], lse_sem.at[3], owner_of(hh - 6)
        ).wait_send()

    keep(2, 5, 6)
    leave(owner, lambda n: src_t.at[0:n, 0:128], 12, t_sems)
    leave(owner, lambda n: src_t.at[0:n, 128:192], 12, tv_sems)
    leave(owner & (hh >= 6), lambda n: src_t.at[0:n, 0:128], 6, d_sems)
    leave(owner, lambda n: src_t.at[0:n, 0:128], 12, s_sems)
    leave(owner, lambda n: src_t.at[0:n, 128:192], 12, sv_sems)
    for i in range(26):
        pltpu.make_async_copy(kept[i], kept_out[i], keep_sem.at[i]).wait()


def where_am_i():
    dp, blk = lax.axis_index("dp"), lax.axis_index("blk")
    return dp // 2, lax.rem(dp, 2), blk // 4, lax.rem(blk, 4)


def at_axis(axis, v):
    x, c, y, z = where_am_i()
    if axis == "x":
        return {"dp": 2 * v + c, "blk": 4 * y + z}
    if axis == "y":
        return {"dp": 2 * x + c, "blk": 4 * v + z}
    return {"dp": 2 * x + c, "blk": 4 * y + v}


def send_to(src, dst, send_sem, recv_sem, device):
    return pltpu.make_async_remote_copy(
        src_ref=src, dst_ref=dst, send_sem=send_sem, recv_sem=recv_sem,
        device_id=device, device_id_type=MESH,
    )


ORDERS = ("xyz", "yzx", "zxy")
CUTS = (
    (12, 12, ((16, 12),)), (6, 6, ((0, 6),)), (2, 1, ((6, 2),)), (12, 12, ((28, 12),)),
    (5, 4, ((43, 5),)), (3, 3, ((40, 3),)), (9, 9, ((48, 3), (52, 3), (56, 3))), (6, 6, ((8, 3), (12, 3))),
)
TILES = 60
WIDE = TILES * 128
BATCHES = (
    (0, 16, (1, 2, 7), ((0, 8, 8), (8, 4, 3), (12, 4, 3))),
    (16, 32, (0, 3, 5, 4), ((16, 12, 12), (28, 12, 12), (40, 8, 8))),
    (48, 12, (6,), ((48, 4, 3), (52, 4, 3), (56, 4, 3))),
)
PB_TILES = 32
PIECES = ((3, 0, (0, 2, 5)), (3, 3, (0, 1, 4)), (2, 6, (0, 1, 3)))
PIECE_TILES = 8


def piece_place(k, p, tile):
    half, first, starts = PIECES[p]
    at = starts[k] + tile
    return 8 * (at // half), first + at % half
TURN = 3


def drain(ref, sem):
    pltpu.make_async_copy(ref, ref, sem).wait()


def backward_kernel(
    len_ref, flag_ref, source, flags,
    w_qkv_s, w_down_t, w_up_t, w_out_t, w_qkv_t,
    in_buf_s, in_dist, in_lse_s, in_lse_d, in_g1_s, in_buf_t, in_lse_t,
    in_unit2_t, in_scale2_t, in_slope_t, in_unit1_t, in_scale1_t, datt_s,
    vec_t, sums_s,
    x0_turn, normed_turn_t, hidden_turn, normed_turn_s, g1r_s, g2r_s,
    att_t, act_t, att_s, act_s, gu_s,
    grad_in, out, sums,
    v_qkv_s, v_down_t, v_up_t, v_out_t,
    buf_s, dist, lse_s, lse_d, g1_s, buf_t, lse_t, unit2_t, scale2_t, slope_t, unit1_t, scale1_t,
    joined_t, joined_s, gu_t,
    src_t, do_s, do_t, dq_s, dkv_s, dqkv_t, dq_buf, dkv_buf,
    kn, k2n, vn, gf, x_ref, acc,
    nt, cf, pb, rl, l1, a1, l2, a2, l3, a3, a4, sml, sma,
    w_sem, k_sem, x_sem,
    own_n, own_c, n_send, n_recv, c_send, c_recv, st_send, st_recv, f_send, f_recv, m_send, m_recv,
):
    b, hh, owner = place()
    half, head = hh // 6, lax.rem(hh, 6)
    mine_half = owner & (half == b // 8)
    e1, e2, e3, e4, e5, e6 = [tuple(x_sem.at[3 * i + j] for j in range(3)) for i in range(6)]
    x, c, y, z = where_am_i()
    here_at = {"x": x, "y": y, "z": z}
    dp = 2 * x + c
    me = 16 * dp + b
    partner = {"dp": 2 * x + 1 - c, "blk": b}

    barrier = pltpu.get_barrier_semaphore()
    loop(15, lambda i: pl.semaphore_signal(
        barrier, inc=1, device_id={"blk": lax.rem(b + 1 + i, 16)}, device_id_type=MESH
    ))
    pl.semaphore_signal(barrier, inc=1, device_id=partner, device_id_type=MESH)
    for axis in "xyz":
        for j in range(1, 4):
            pl.semaphore_signal(
                barrier, inc=1, device_id=at_axis(axis, lax.rem(here_at[axis] + j, 4)), device_id_type=MESH
            )
    for p in range(3):
        for q in range(4):
            for core in range(2):
                at = dict(zip(ORDERS[p], (me // 32, lax.rem(me // 8, 4), q)))
                pl.semaphore_signal(
                    barrier, inc=1, device_id={"dp": 2 * at["x"] + core, "blk": 4 * at["y"] + at["z"]},
                    device_id_type=MESH,
                )
    kept = load_all(
        [
            (in_buf_s, buf_s), (in_dist, dist), (in_lse_s, lse_s), (in_lse_d, lse_d),
            (in_g1_s, g1_s), (in_buf_t, buf_t), (in_lse_t, lse_t), (in_unit2_t, unit2_t),
            (in_scale2_t, scale2_t), (in_slope_t, slope_t), (in_unit1_t, unit1_t), (in_scale1_t, scale1_t),
        ],
        k_sem,
    )
    weights = load_all(
        [(w_qkv_s, v_qkv_s), (w_down_t, v_down_t), (w_up_t, v_up_t), (w_out_t, v_out_t)], w_sem
    )
    length = len_ref[0]
    for copy in kept[0:4]:
        copy.wait()

    @pl.when(owner)
    def _():
        kn[...] = natural(buf_s[64:128, :])
        vn[...] = natural(buf_s[128:192, :])
        k2n[...] = natural(dist[64:128, :])

    pl.semaphore_wait(barrier, 49)

    def pool_wide(m, ref):
        _, step, segments = CUTS[m]
        done = 0
        for n, (first, count) in enumerate(segments):
            cols = slice(first * 128, (first + count) * 128)
            pltpu.make_async_copy(
                ref.at[:, lanes((c * step + done) * 128, count * 128)], cf.at[0:128, cols], own_c.at[m + 8 * n]
            ).start()
            send_to(
                ref.at[:, lanes(((1 - c) * step + done) * 128, count * 128)], cf.at[128:256, cols],
                c_send.at[m + 8 * n], c_recv.at[m + 8 * n], partner,
            ).start()
            done += count

    def pool_narrow(m, ref):
        if ref is None:
            ref = nt.at[m, :, 0:128]
        else:
            pltpu.make_async_copy(ref, nt.at[m, :, 0:128], own_n.at[m]).start()
        send_to(ref, nt.at[m, :, 128:256], n_send.at[m], n_recv.at[m], partner).start()

    def products(k):
        begin, _, members, _ = BATCHES[k]
        for m in members:
            if m not in (3, 5):
                drain(nt.at[m, :, 0:128], own_n.at[m])
            drain(nt.at[m, :, 128:256], n_recv.at[m])
            for n, (first, count) in enumerate(CUTS[m][2]):
                cols = slice(first * 128, (first + count) * 128)
                drain(cf.at[0:128, cols], own_c.at[m + 8 * n])
                drain(cf.at[128:256, cols], c_recv.at[m + 8 * n])
                size = 3 if count % 3 == 0 else count

                def piece(i, m=m, first=first, size=size):
                    from_cols = lanes((first + i * size) * 128, size * 128)
                    to_cols = lanes((first - begin + i * size) * 128, size * 128)
                    pb[:, to_cols] = dot(nt[m], cf[:, from_cols]).astype(BF)

                loop(count // size, piece)

    def sem_of(k, p, kind):
        return 18 * k + 6 * p + kind

    def tiles(first, count):
        return slice(first * 128, (first + count) * 128)

    def rows_of(height, v):
        return pl.ds(pl.multiple_of(height * v, 16), height)

    def ring(p, stage):
        axis = ORDERS[p][stage]
        u = here_at[axis]
        around = [lax.rem(u + j, 4) for j in range(4)]
        return around, [at_axis(axis, v) for v in around]

    def stage_start(k, stage):
        begin, _, _, parts = BATCHES[k]
        for p, (first, count, used) in enumerate(parts):
            around, devices = ring(p, stage)
            if stage == 0:
                first_half = (used + 1) // 2
                one, two = (0, first_half), (first_half, used - first_half)
                for j, (start, size), to, dst, kind in (
                    (2, one, 1, rl, 0), (2, two, 3, rl, 1), (1, two, 1, l1.at[0], 2), (3, one, 3, l1.at[1], 3),
                ):
                    send_to(
                        pb.at[rows_of(192, around[j]), tiles(first - begin + start, size)],
                        dst.at[:, tiles(first + start, size)],
                        st_send.at[sem_of(k, p, 0)], st_recv.at[sem_of(k, p, kind)], devices[to],
                    ).start()
                continue
            for j in range(1, 4):
                if stage == 1:
                    src = a1.at[rows_of(48, around[j]), tiles(first, used)]
                    dst = l2.at[j - 1, :, tiles(first, used)]
                else:
                    src = a2.at[:, lanes(first * 128 + around[j] * count * 32, count * 32)]
                    dst = l3.at[j - 1, :, slice(first * 32, (first + count) * 32)]
                kind = 3 + stage
                send_to(
                    src, dst, st_send.at[sem_of(k, p, kind)], st_recv.at[sem_of(k, p, kind)], devices[j]
                ).start()

    def relay(k):
        begin, _, _, parts = BATCHES[k]
        for p, (first, count, used) in enumerate(parts):
            around, devices = ring(p, 0)
            first_half = (used + 1) // 2
            for start, size, to, slot in ((0, first_half, 1, 0), (first_half, used - first_half, 3, 1)):
                land = rl.at[:, tiles(first + start, size)]
                drain(land, st_recv.at[sem_of(k, p, slot)])
                own_cols = tiles(first - begin + start, size)

                def add(r, own_cols=own_cols, start=start, size=size, to=to, first=first, around=around):
                    own = pl.ds(pl.multiple_of(192 * around[to] + 16 * r, 16), 16)
                    rows = pl.ds(pl.multiple_of(16 * r, 16), 16)
                    total = pb[own, own_cols].astype(F32) + rl[rows, tiles(first + start, size)].astype(F32)
                    pb[own, own_cols] = total.astype(BF)

                loop(12, add)
                send_to(
                    pb.at[rows_of(192, around[to]), own_cols], l1.at[slot, :, tiles(first + start, size)],
                    st_send.at[sem_of(k, p, 1)], st_recv.at[sem_of(k, p, 2 + slot)], devices[to],
                ).start()

    def stage_sent(k, stage):
        for p, (first, count, used) in enumerate(BATCHES[k][3]):
            if stage == 0:
                drain(l1.at[:, :, tiles(first, used)], st_send.at[sem_of(k, p, 0)])
                drain(rl.at[:, tiles(first, used)], st_send.at[sem_of(k, p, 1)])
            elif stage == 1:
                drain(l2.at[:, :, tiles(first, used)], st_send.at[sem_of(k, p, 4)])
            else:
                drain(l3.at[:, :, slice(first * 32, (first + count) * 32)], st_send.at[sem_of(k, p, 5)])

    def stage_sum(k, stage):
        begin, _, _, parts = BATCHES[k]
        for p, (first, count, used) in enumerate(parts):
            at = here_at[ORDERS[p][stage]]
            cols = tiles(first, used)
            if stage == 0:
                for slot in range(2):
                    drain(l1.at[slot, :, cols], st_recv.at[sem_of(k, p, 2 + slot)])
                src, land, dst, height, peers, scols = pb, l1, a1, 192, 2, tiles(first - begin, used)
            elif stage == 1:
                drain(l2.at[:, :, cols], st_recv.at[sem_of(k, p, 4)])
                src, land, dst, height, peers, scols = a1, l2, a2, 48, 3, cols
            else:
                quarter = slice(first * 32, (first + count) * 32)
                drain(l3.at[:, :, quarter], st_recv.at[sem_of(k, p, 5)])
                total = a2[:, lanes(first * 128 + at * count * 32, count * 32)].astype(F32)
                for j in range(3):
                    total = total + l3[j, :, quarter].astype(F32)
                for tile in range(count // 4):
                    row, at_tile = piece_place(k, p, tile)
                    for i in range(8):
                        a3[i, row : row + 6, tiles(at_tile, 1)] = total[6 * i : 6 * i + 6, tiles(tile, 1)]
                continue

            def add(r, src=src, land=land, dst=dst, height=height, peers=peers, at=at, cols=cols, scols=scols):
                rows = pl.ds(pl.multiple_of(16 * r, 16), 16)
                own = pl.ds(pl.multiple_of(height * at + 16 * r, 16), 16)
                total = src[own, scols].astype(F32)
                for j in range(peers):
                    total = total + land[j, rows, cols].astype(F32)
                dst[rows, cols] = total.astype(BF)

            loop(height // 16, add)

    def final_part(p):
        half, first, _ = PIECES[p]
        begin = 32 * here_at[ORDERS[p][0]] + 8 * here_at[ORDERS[p][1]]
        return begin, half, first, here_at[ORDERS[p][2]]

    def final_start():
        a4[...] = a3[...].astype(BF)
        for p in range(3):
            begin, half, first, third = final_part(p)
            for i in range(8):
                to = begin + i
                src = a4.at[i, :, tiles(first, half)]
                dst = out.at[:, lanes(((4 * c + third) * PIECE_TILES + first) * 128, half * 128)]

                @pl.when(to != me)
                def _():
                    send_to(
                        src, dst, f_send.at[p], f_recv.at[0], {"dp": to // 16, "blk": lax.rem(to, 16)}
                    ).start()

                @pl.when(to == me)
                def _():
                    pltpu.make_async_copy(src, dst, f_recv.at[0]).start()

    def final_wait():
        drain(out, f_recv.at[0])
        for p in range(3):
            begin, half, first, _ = final_part(p)
            own = (me >= begin) & (me < begin + 8)
            leave(own, lambda n, first=first, half=half: a4.at[0:n, :, tiles(first, half)], 8, (f_send.at[p],))

    def small_copy(slot):
        if slot == 0:
            return send_to(sma.at[0], sml.at[0], m_send.at[0], m_recv.at[0], partner)
        n, j = (slot - 1) // 3, (slot - 1) % 3 + 1
        axis = "xyz"[n]
        return send_to(
            sma.at[n + 1], sml.at[slot], m_send.at[slot], m_recv.at[slot],
            at_axis(axis, lax.rem(here_at[axis] + j, 4)),
        )

    def small_step(n):
        if n > 0:
            slots = (0,) if n == 1 else tuple(range(3 * n - 5, 3 * n - 2))
            total = sma[n - 1]
            for slot in slots:
                small_copy(slot).wait_recv()
                total = total + sml[slot]
            if n == 4:
                return total
            sma[n] = total
        for slot in (0,) if n == 0 else range(3 * n - 2, 3 * n + 1):
            small_copy(slot).start()
        return None

    def c1(h):
        return (
            datt_s.at[h], do_s.at[:, lanes(lax.rem(b, 8) * 128, 128)],
            e1, owner_of(h + 6 * (b // 8)), b,
        )

    def c2(j):
        return dq_buf.at[:, lanes(j * 128, 128)], dq_s.at[head], e2, 8 * half + j, b

    def c3(d):
        return dkv_buf.at[:, lanes(d * 128, 128)], dkv_s.at[hh], e3, d, b

    def c4(h):
        return src_t.at[h], do_t.at[:, lanes(b * 128, 128)], e4, owner_of(h), b

    def c5(d):
        return dq_buf.at[:, lanes(d * 128, 128)], dqkv_t.at[hh, 0:64], e5, d, b

    def c6(d):
        return dkv_buf.at[:, lanes(d * 128, 128)], dqkv_t.at[hh, 64:192], e6, d, b

    def run_chunks(n, at, kt_ref, put, low, high, put_keys=None):
        if low == 0:
            acc[...] = jnp.zeros_like(acc)
            x_ref[1] = jnp.zeros((SEQ, 2 * QC), BF)
        rest = (at, kn, k2n, vn, kt_ref, length, gf, x_ref, acc)

        def pair(i):
            backward_chunk(
                2 * i, jnp.maximum(2 * i - 1, 0), 0, *rest, lambda ch, g: put(ch, g, i > 0)
            )
            backward_chunk(2 * i + 1, 2 * i, 1, *rest, lambda ch, g: put(ch, g, True))

        loop(high - low, lambda i: pair(i + low))
        if 2 * high == n:
            backward_last(n - 1, 1, at, kt_ref, x_ref, acc, lambda ch, g: put(ch, g, True), put_keys)

    def keys_out(copy):
        def put_keys(t, block):
            dkv_buf[:, t * KT : (t + 1) * KT] = block
            for i in range(2):
                start_to(*copy(2 * t + i))

        return put_keys

    def send_pair(copy, ch, real):
        if real is True:
            for i in range(2):
                start_to(*copy(2 * ch + i))
        else:
            @pl.when(real)
            def _():
                for i in range(2):
                    start_to(*copy(2 * ch + i))

    def teacher_at(ch):
        here = lanes(ch * QC, QC)
        return (
            buf_t[0:64, here], buf_s[0:64, here], do_t[:, here],
            lse_t[0:1, here], lse_s[0:1, here], weight_row(len_ref, flag_ref, head, ch * QC, hh < 6),
        )

    def teacher_put(ch, g, real):
        dq_buf[:, lanes(ch * QC, QC)] = g.astype(BF)
        send_pair(c5, ch, real)

    loop(6, lambda j: start_to(*c1(lax.rem(j + b, 6))))
    for m, ref in ((1, normed_turn_s), (2, g1r_s), (7, g2r_s)):
        pool_narrow(m, ref)
    for m, ref in ((1, gu_s), (2, att_s), (7, act_s)):
        pool_wide(m, ref)
    for m, ref in ((0, normed_turn_t), (4, hidden_turn), (6, x0_turn)):
        pool_narrow(m, ref)
    for m, ref in ((3, act_t), (5, att_t)):
        pool_wide(m, ref)

    products(0)
    stage_start(0, 0)

    @pl.when(owner)
    def _():
        arrive(mine_half, lambda n: do_s.at[:, 0 : n * 128], 8, e1)

        def at(ch):
            first = half * 1024 + ch * QC
            here = lanes(first, QC)
            return (
                buf_s[0:64, here], dist[0:64, here], do_s[:, lanes(ch * QC, QC)],
                lse_s[0:1, here], lse_d[0:1, here], weight_row(len_ref, flag_ref, head, first, True),
            )

        def put(ch, g, real):
            dq_buf[:, lanes(ch * QC, QC)] = g.astype(BF)
            send_pair(c2, ch, real)

        run_chunks(1024 // QC, at, buf_s, put, 0, 2, keys_out(c3))

    relay(0)
    arrive(mine_half, lambda n: dq_s.at[0:n], 6, e2)
    arrive(owner, lambda n: dkv_s.at[0:n], 12, e3)
    joined_s[:, 0:384] = natural_wide(dq_s[...].reshape(384, 128))
    for part in range(2):
        rows = slice(64 * part, 64 * part + 64)
        both = dkv_s[0:6, rows, :].astype(F32) + dkv_s[6:12, rows, :].astype(F32)
        joined_s[:, 384 * (part + 1) : 384 * (part + 2)] = both.reshape(384, 128).T.astype(BF)
    pool_wide(4, joined_s)
    sma[0] = sums_s[...]
    low_sums = jnp.sum(joined_s[...].astype(F32), axis=0, keepdims=True)
    sma[0, 20:21, 0:384] = low_sums[:, 0:384]
    sma[0, 20:21, 384:768] = low_sums[:, 768:1152]
    for copy in kept[4:]:
        copy.wait()
    weights[0].wait()
    grad_hidden = g1_s[...] + dot_t(joined_s[...], v_qkv_s[...])
    for i in (1, 2, 3):
        weights[i].wait()
    g1, datt = dense_down(
        grad_hidden, unit2_t[...], scale2_t[:, 0:1], unit1_t[...], scale1_t[:, 0:1],
        v_out_t, v_up_t, v_down_t, vec_t, slope_t, gu_t, nt.at[3, :, 0:128], nt.at[5, :, 0:128], sma.at[0], 0,
        (lambda: pool_narrow(3, None), lambda: pool_wide(0, gu_t), lambda: pool_narrow(5, None)),
    )
    grad_in[...] = g1
    src_t[...] = datt.T.astype(BF).reshape(12, 64, 128)
    loop(12, lambda j: start_to(*c4(lax.rem(j + b, 12))))
    late = load_all(
        [(w_qkv_t.at[:, 768 * p : 768 * (p + 1)], v_down_t.at[768 * p : 768 * (p + 1), :]) for p in range(3)],
        w_sem.at[pl.ds(4, 3)],
    )
    stage_sum(0, 0)
    stage_start(0, 1)

    @pl.when(owner)
    def _():
        kn[...] = natural(buf_t[64:128, :])
        vn[...] = natural(buf_t[128:192, :])
        k2n[...] = natural(buf_s[64:128, :])

    stage_sent(0, 0)
    products(1)
    stage_start(1, 0)

    @pl.when(owner)
    def _():
        leave(mine_half, lambda n: dq_buf.at[:, 0 : n * 128], 8, e2)
        got(dkv_buf.at[:, 0 : 15 * 128], e3[0])
        arrive(owner, lambda n: do_t.at[:, 0 : n * 128], 16, e4)

        run_chunks(SEQ // QC, teacher_at, buf_t, teacher_put, 0, TURN)

    relay(1)
    stage_sum(0, 1)
    stage_start(0, 2)

    @pl.when(owner)
    def _():
        run_chunks(SEQ // QC, teacher_at, buf_t, teacher_put, TURN, SEQ // QC // 2, keys_out(c6))

    stage_sum(0, 2)
    stage_sum(1, 0)
    stage_start(1, 1)
    arrive(owner, lambda n: dqkv_t.at[0:n, 0:64], 12, e5)
    arrive(owner, lambda n: dqkv_t.at[0:n, 64:192], 12, e6)
    for part in range(3):
        joined_t[:, 768 * part : 768 * (part + 1)] = natural_wide(
            dqkv_t[:, 64 * part : 64 * (part + 1), :].reshape(768, 128)
        )
    pool_wide(6, joined_t)
    for row, part in ((10, 0), (11, 2)):
        sma[0, row : row + 1, :] = jnp.sum(
            joined_t[:, 768 * part : 768 * (part + 1)].astype(F32), axis=0, keepdims=True
        )
    small_step(0)
    stage_sent(1, 0)
    products(2)
    stage_start(2, 0)
    small_step(1)
    stage_sum(1, 1)
    stage_start(1, 2)
    for copy in late:
        copy.wait()
    grad = grad_in[...]
    for p in range(3):
        grad = grad + dot_t(joined_t[:, 768 * p : 768 * (p + 1)], v_down_t[768 * p : 768 * (p + 1), :])
    place_of = lax.broadcasted_iota(jnp.int32, (128, 128), 0)
    turned = jnp.where((place_of == source[...]) & (flags[...] == 1), 1.0, 0.0)
    back = turned.astype(BF)
    one = grad.astype(BF)
    rest = grad - one.astype(F32)
    two = rest.astype(BF)
    three = (rest - two.astype(F32)).astype(BF)
    copied = dot(back, one) + dot(back, two) + dot(back, three)
    kept = jnp.sum(turned.T, axis=1, keepdims=True) < 0.5
    grad_in[...] = jnp.where(kept, grad, 0.0) + copied
    relay(2)
    small_step(2)
    stage_sum(2, 0)
    stage_start(2, 1)
    small_step(3)
    stage_sum(1, 2)
    stage_sum(2, 1)
    stage_start(2, 2)
    sums[...] = small_step(4)
    stage_sum(2, 2)
    final_start()

    @pl.when(owner)
    def _():
        got(dq_buf.at[:, 0 : 15 * 128], e5[0])
        got(dkv_buf.at[:, 0 : 15 * 128], e6[0])

    leave(mine_half, lambda n: dq_s.at[0:n], 6, e1)
    leave(owner, lambda n: src_t.at[0:n], 12, e4)
    for m, (_, _, segments) in enumerate(CUTS):
        for n, (first, count) in enumerate(segments):
            drain(cf.at[128:256, slice(first * 128, (first + count) * 128)], c_send.at[m + 8 * n])
        drain(nt.at[m, :, 128:256], n_send.at[m])
    for slot in range(10):
        small_copy(slot).wait_send()
    for k, stage in ((0, 1), (0, 2), (1, 1), (1, 2), (2, 0), (2, 1), (2, 2)):
        stage_sent(k, stage)
    final_wait()


ANY = pl.BlockSpec(memory_space=pl.ANY)


def mega_call(kernel, ident, specs, outs, scratch, args, name, out_spec):
    return pl.pallas_call(
        kernel,
        name=name,
        out_shape=tuple(jax.ShapeDtypeStruct(s, t) for s, t in outs),
        in_specs=specs,
        out_specs=tuple(out_spec for _ in outs),
        scratch_shapes=scratch,
        compiler_params=pltpu.CompilerParams(
            collective_id=ident, has_side_effects=True, vmem_limit_bytes=62 * MIB
        ),
    )(*args)


def vb(*shape):
    return pltpu.VMEM(shape, BF)


def vf(*shape):
    return pltpu.VMEM(shape, F32)


def run_forward(lengths, x_in, source, flags, cot, weights, smalls):
    outs = [
        ((128, 768), F32), ((192, SEQ), BF), ((128, SEQ), BF), ((192, SEQ), BF),
        ((8, SEQ), F32), ((8, SEQ), F32), ((8, SEQ), F32),
        *[((768, 128), BF)] * 6,
        ((128, 768), BF), ((128, 3072), BF), ((128, 384), BF), ((128, 1536), BF), ((128, 1536), BF),
        ((128, 3072), BF), ((128, 768), F32), ((128, 128), F32), ((128, 768), F32), ((128, 128), F32),
        ((128, 768), F32), ((6, 64, 128), BF), ((24, 768), F32),
    ]
    scratch = [pltpu.VMEM(shape, kind) for shape, kind in outs] + [
        vb(768, 2304), vb(768, 768), vb(768, 3072), vb(3072, 768),
        vb(768, 1152), vb(384, 768), vb(768, 1536), vb(1536, 768),
        vf(128, 768), vb(12, 192, 128), vb(6, 192, 128), vb(12, 64, 128), vb(6, 64, 128),
        vb(64, SEQ), vb(64, 1024), vb(SEQ, 64), vf(2, SEQ, QC), vb(2, SEQ, QC), vf(6, 8, QC),
        vb(128, 1536), vf(128, 768), vf(128, 128),
        DMA((8,)), DMA((21,)), DMA((4,)), DMA((1,)), DMA((26,)),
    ]
    specs = [SMEM] + [VMEM] * 4 + [ANY] * 8 + [VMEM] * 6
    return mega_call(
        forward_kernel, 1, specs, outs, scratch, (lengths, x_in, source, flags, cot, *weights, *smalls), "forward", ANY
    )


def run_backward(lengths, head_flags, source, flags, weights, kept, held, pooled):
    outs = [((128, 768), F32), ((16, 8 * PIECE_TILES * 128), BF), ((24, 768), F32)]
    scratch = [
        vb(768, 1152), vb(3072, 768), vb(768, 3072), vb(768, 768),
        vb(192, SEQ), vb(128, SEQ), vf(8, SEQ), vf(8, SEQ), vf(128, 768), vb(192, SEQ), vf(8, SEQ),
        vf(128, 768), vf(128, 128), vb(128, 3072), vf(128, 768), vf(128, 128),
        vb(128, 2304), vb(128, 1152), vb(128, 3072),
        vb(12, 64, 128), vb(64, 1024), vb(64, SEQ), vb(6, 64, 128), vb(12, 128, 128), vb(12, 192, 128),
        vb(64, SEQ), vb(128, SEQ),
        vb(SEQ, 64), vb(SEQ, 64), vb(SEQ, 64), vf(SEQ, QC), vb(2, SEQ, 2 * QC), vf(SEQ, 128),
        vb(8, 768, 256), vb(256, WIDE), vb(768, PB_TILES * 128),
        vb(192, WIDE), vb(2, 192, WIDE), vb(192, WIDE), vb(3, 48, WIDE), vb(48, WIDE), vb(3, 48, WIDE // 4), vf(8, 16, PIECE_TILES * 128), vb(8, 16, PIECE_TILES * 128),
        vf(10, 24, 768), vf(4, 24, 768),
        DMA((7,)), DMA((12,)), DMA((18,)),
        DMA((8,)), DMA((24,)), DMA((8,)), DMA((8,)), DMA((24,)), DMA((24,)),
        DMA((54,)), DMA((54,)), DMA((3,)), DMA((1,)), DMA((10,)), DMA((10,)),
    ]
    specs = [SMEM] * 2 + [VMEM] * 2 + [ANY] * (5 + len(kept)) + [VMEM] * len(held) + [ANY] * len(pooled)
    return mega_call(
        backward_kernel, 2, specs, outs, scratch,
        (lengths, head_flags, source, flags, *weights, *kept, *held, *pooled), "backward", VMEM,
    )


def unpack_kernel(whole, sums, first_in, second_in, *outs):
    first_out, second_out, outs = outs[0], outs[1], outs[2:16]
    first_out[...] = first_in[...]
    second_out[...] = second_in[...]

    def tile_at(core, tile):
        for k, (_, _, _, parts) in enumerate(BATCHES):
            for p, (first, count, _) in enumerate(parts):
                if first <= tile < first + count:
                    third, rest = (tile - first) // (count // 4), (tile - first) % (count // 4)
                    row, at = piece_place(k, p, rest)
                    start = ((4 * core + third) * PIECE_TILES + at) * 128
                    return wide[row : row + 8, start : start + 128]

    wide = whole[...].astype(F32)

    def columns(m):
        count, step, segments = CUTS[m]
        spots = [first + i for first, size in segments for i in range(size)]
        pieces = [tile_at(0, tile) for tile in spots] + [tile_at(1, tile) for tile in spots[count - step :]]
        return jnp.concatenate(pieces, axis=1)

    for m, o in ((6, 0), (5, 2), (0, 3), (3, 4), (4, 7), (2, 9), (1, 10), (7, 11)):
        outs[o][...] = columns(m)[0:6]
    i = 16 * lax.axis_index("dp") + lax.axis_index("blk")

    def turn(rows, by):
        return pltpu.roll(rows, lax.rem(768 - by, 768), 1)

    def pick(first, count, per):
        row = first + (i * per) // 768
        wide = jnp.broadcast_to(sums[pl.ds(row, 1), :], (8, 768))
        return turn(wide, lax.rem(i * per, 768))[0:1, 0:per]

    outs[1][...] = pick(10, 2, 12)
    outs[5][...] = pick(6, 4, 24)
    outs[8][...] = pick(20, 1, 6)
    outs[12][...] = pick(18, 2, 12)
    outs[6][...] = turn(sums[0:8, :], i * 6)[0:6, 0:6]
    outs[13][...] = turn(sums[8:24, :], i * 6)[4:10, 0:6]


def unpack(whole, sums, output, grad_in):
    shapes = (
        (6, 2304), (1, 12), (6, 768), (6, 3072), (6, 3072), (1, 24), (6, 6),
        (6, 1152), (1, 6), (6, 384), (6, 1536), (6, 1536), (1, 12), (6, 6),
    )
    outs = list(
        pl.pallas_call(
            unpack_kernel,
            name="unpack",
            out_shape=tuple(jax.ShapeDtypeStruct(s, F32) for s in ((128, 768), (128, 768)) + shapes),
            in_specs=[VMEM] * 4,
            out_specs=(VMEM, VMEM) + tuple(VMEM for _ in shapes),
            compiler_params=pltpu.CompilerParams(vmem_limit_bytes=62 * MIB),
        )(whole, sums, output, grad_in)
    )
    for i in (3, 7, 10, 14):
        outs[i] = outs[i].reshape(-1)
    for i in (4, 6, 11, 13):
        outs[i] = outs[i].T
    outs[0], outs[1] = outs[0][None], outs[1][None]
    return tuple(outs)


def per_device(
    inputs, aug_source, aug_flags, lengths, head_flags, cotangent,
    qkv_teacher, qv_bias_teacher, out_teacher, up_teacher, down_teacher, up_bias_teacher, vectors_teacher,
    qkv_student, qv_bias_student, out_student, up_student, down_student, up_bias_student, vectors_student,
):
    (
        output, buf_t, dist, buf_s, lse_t, lse_d, lse_s,
        x0_turn, normed_turn_t, hidden_turn, normed_turn_s, g1r_s, g2r_s,
        att_t, act_t, att_s, act_s, gu_s,
        slope_t, unit1_t, scale1_t, unit2_t, scale2_t, g1_s, datt_s, sums_s,
    ) = run_forward(
        lengths, inputs[0], aug_source, aug_flags, cotangent[0],
        (qkv_teacher, out_teacher, up_teacher, down_teacher, qkv_student, out_student, up_student, down_student),
        (
            qv_bias_teacher, up_bias_teacher, vectors_teacher,
            qv_bias_student, up_bias_student, vectors_student,
        ),
    )
    grad_in, whole, total = run_backward(
        lengths, head_flags, aug_source, aug_flags,
        (qkv_student, down_teacher, up_teacher, out_teacher, qkv_teacher),
        (
            buf_s, dist, lse_s, lse_d, g1_s, buf_t, lse_t,
            unit2_t, scale2_t, slope_t, unit1_t, scale1_t, datt_s,
        ),
        (vectors_teacher, sums_s),
        (
            x0_turn, normed_turn_t, hidden_turn, normed_turn_s, g1r_s, g2r_s,
            att_t, act_t, att_s, act_s, gu_s,
        ),
    )
    return unpack(whole, total, output, grad_in)


def solution(mesh):
    both = ("dp", "blk")
    row, flat, col = P(both, None), P(both), P(None, both)
    tokens, marks = P("dp", "blk", None), P("dp", "blk")
    return jax.shard_map(
        per_device,
        mesh=mesh,
        in_specs=(tokens, marks, marks, P("dp"), P(), tokens) + (P(),) * 14,
        out_specs=(tokens, tokens) + (row, flat, col, row, col, flat, col) * 2,
        check_vma=False,
    )
```

```python
import jax
import jax.numpy as jnp
from jax import lax
from jax.experimental import pallas as pl
from jax.experimental.pallas import tpu as pltpu
from jax.sharding import PartitionSpec as P

MESH = pl.DeviceIdType.MESH
LOG2E = 1.4426950408889634
C2 = 0.125 * LOG2E
SEQ = 2048
QC = 256
KT = 256
NKT = SEQ // KT
MIB = 1 << 20


def dot(a, b):
    return jnp.dot(a, b, preferred_element_type=jnp.float32)


def place():
    b = lax.axis_index("blk")
    r = lax.rem(lax.rem(b, 4) - b // 4 + 7, 4)
    return b, 3 * (b // 4) + r, r < 3


def owner_of(hh):
    y = hh // 3
    return 4 * y + lax.rem(y + lax.rem(hh, 3) + 1, 4)


def copy_to(src, dst, send_sem, recv_sem, d):
    return pltpu.make_async_remote_copy(
        src_ref=src,
        dst_ref=dst,
        send_sem=send_sem,
        recv_sem=recv_sem,
        device_id={"blk": d},
        device_id_type=MESH,
    )


def start_to(src, dst, sems, d, b):
    send_sem, recv_sem, own_sem = sems

    @pl.when(d != b)
    def _():
        copy_to(src, dst, send_sem, recv_sem, d).start()

    @pl.when(d == b)
    def _():
        pltpu.make_async_copy(src, dst, own_sem).start()


def arrive(own, blocks, count, sems):
    @pl.when(own)
    def _():
        got(blocks(count - 1), sems[1])
        got(blocks(1), sems[2])

    @pl.when(jnp.logical_not(own))
    def _():
        got(blocks(count), sems[1])


def leave(own, blocks, count, sems):
    @pl.when(own)
    def _():
        got(blocks(count - 1), sems[0])

    @pl.when(jnp.logical_not(own))
    def _():
        got(blocks(count), sems[0])


def got(dst, recv_sem):
    pltpu.make_async_copy(dst, dst, recv_sem).wait()


def lanes(start, size):
    return pl.ds(pl.multiple_of(start, 128), size)


def fold(v):
    return jnp.sum(v.reshape(v.shape[0] // 8, 8, v.shape[1]), axis=0)


def key_ok(length):
    rows = lax.broadcasted_iota(jnp.int32, (KT, QC), 0) + (SEQ - KT)
    return rows < length


def natural(x):
    return x.astype(jnp.float32).T.astype(jnp.bfloat16)


def weight_row(len_ref, flag_ref, head, first, use):
    q = lax.broadcasted_iota(jnp.int32, (1, QC), 1) + first
    factor = jnp.where(use, flag_ref[head].astype(jnp.float32) * (2.0 * SEQ), 0.0)
    return jnp.where(q < len_ref[0], factor, 0.0)


SMEM = pl.BlockSpec(memory_space=pltpu.SMEM)
VMEM = pl.BlockSpec(memory_space=pltpu.VMEM)
DMA = pltpu.SemaphoreType.DMA
BF = jnp.bfloat16
F32 = jnp.float32


SQRT_HALF = 0.7071067811865476
INV_SQRT_2PI = 0.3989422804014327


def dot_t(a, b):
    return lax.dot_general(a, b, (((1,), (1,)), ((), ())), preferred_element_type=F32)


def norm_forward(v, gain, shift):
    center = v - jnp.mean(v, axis=-1, keepdims=True)
    scale = lax.rsqrt(jnp.mean(center * center, axis=-1, keepdims=True) + 1e-06)
    unit = center * scale
    return unit * gain + shift, unit, scale


def norm_backward(grad, gain, unit, scale):
    scaled = grad * gain
    mean_one = jnp.mean(scaled, axis=-1, keepdims=True)
    mean_two = jnp.mean(scaled * unit, axis=-1, keepdims=True)
    return (
        (scaled - mean_one - unit * mean_two) * scale,
        jnp.sum(grad * unit, axis=0, keepdims=True),
        jnp.sum(grad, axis=0, keepdims=True),
    )


def qkv_blocks(low, w, bias, src, heads):
    span = heads * 64
    for part in range(3):
        joint = dot(low, w[:, part * span : (part + 1) * span])
        if part != 1:
            first = 0 if part == 0 else span
            joint = joint + bias[first : first + span].reshape(1, span)
        src[:, part * 64 : (part + 1) * 64, :] = joint.T.astype(BF).reshape(heads, 64, 128)


def dense_up(residual, attended, w_out, w_up, w_down, up_bias, vec, act, slope, unit1, scale1, normed_turned):
    ff = up_bias.shape[0]
    first = residual + dot(attended, w_out) + vec[0:1, :]
    normed, unit, scale = norm_forward(first, vec[1:2, :], vec[2:3, :])
    unit1[...] = unit
    scale1[...] = jnp.broadcast_to(scale, (128, 128))
    low = normed.astype(BF)
    normed_turned[...] = normed.T.astype(BF)
    step = 512
    for j in range(ff // step):
        cols = slice(j * step, (j + 1) * step)
        u = dot(low, w_up[:, cols]) + up_bias[cols].reshape(1, step)
        cdf = 0.5 + 0.5 * lax.erf(u * SQRT_HALF)
        act[:, cols] = (u * cdf).astype(BF)
        slope[:, cols] = (cdf + u * (jnp.exp(-0.5 * u * u) * INV_SQRT_2PI)).astype(slope.dtype)
    second = normed + dot(act[...], w_down) + vec[3:4, :]
    return norm_forward(second, vec[4:5, :], vec[5:6, :])


def dense_down(grad, unit2, scale2, unit1, scale1, w_out, w_up, w_down, vec, slope, gu, g2r, g1r, sums, row, hooks=(None,) * 3):
    ff = w_up.shape[1]
    g2, gain_two, shift_two = norm_backward(grad, vec[4:5, :], unit2, scale2)
    low2 = g2.astype(BF)
    g2r[...] = g2.T.astype(BF)
    if hooks[0]:
        hooks[0]()
    step = 512
    for j in range(ff // step):
        cols = slice(j * step, (j + 1) * step)
        g = dot_t(low2, w_down[cols, :]) * slope[:, cols].astype(F32)
        gu[:, cols] = g.astype(BF)
        total = jnp.sum(g, axis=0, keepdims=True)
        done = 0
        while done < step:
            at = j * step + done
            size = min(step - done, 768 - at % 768)
            sums[row + 6 + at // 768 : row + 7 + at // 768, at % 768 : at % 768 + size] = total[:, done : done + size]
            done += size
    if hooks[1]:
        hooks[1]()
    g1, gain_one, shift_one = norm_backward(g2 + dot_t(gu[...], w_up[...]), vec[1:2, :], unit1, scale1)
    low1 = g1.astype(BF)
    g1r[...] = g1.T.astype(BF)
    if hooks[2]:
        hooks[2]()
    rows = (
        jnp.sum(g1, axis=0, keepdims=True), gain_one, shift_one,
        jnp.sum(g2, axis=0, keepdims=True), gain_two, shift_two,
    )
    for i, value in enumerate(rows):
        sums[row + i : row + i + 1, :] = value
    return g1, dot_t(low1, w_out[...])


def load_all(pairs, sem):
    copies = [pltpu.make_async_copy(a, b, sem.at[i]) for i, (a, b) in enumerate(pairs)]
    for copy in copies:
        copy.start()
    return copies


def forward_stage(c_score, c_exp, c_out, do, par, q_at, kn, v_ref, s_ref, p_ref, st, put, length):
    if do[0]:
        q = q_at(c_score)
    m8 = jnp.full((8, QC), -3e38, F32)
    l8 = jnp.zeros((8, QC), F32)
    out = jnp.zeros((64, QC), F32)
    top = st[1 - par, 0:1, :]
    for t in range(NKT):
        rows = slice(t * KT, (t + 1) * KT)
        if do[0]:
            s = dot(kn[rows, :], q)
            if t == NKT - 1:
                s = jnp.where(key_ok(length), s, -1e30)
            s_ref[par, rows, :] = s
            m8 = jnp.maximum(m8, jnp.max(s.reshape(KT // 8, 8, QC), axis=0))
        if do[1]:
            p = jnp.exp2(s_ref[1 - par, rows, :] * C2 - top)
            l8 = l8 + fold(p)
            p_ref[1 - par, rows, :] = p.astype(BF)
        if do[2]:
            out = out + dot(v_ref[128:192, rows], p_ref[par, rows, :])
    if do[2]:
        put(c_out, out / st[2 + par, 0:1, :], st[4 + par, 0:1, :])
    if do[1]:
        total = jnp.sum(l8, axis=0, keepdims=True)
        st[3 - par] = jnp.broadcast_to(total, (8, QC))
        st[5 - par] = jnp.broadcast_to(top + jnp.log2(total), (8, QC))
    if do[0]:
        st[par] = jnp.broadcast_to(jnp.max(m8, axis=0, keepdims=True) * C2, (8, QC))


def forward_chunks(n, values_here, *rest):
    forward_stage(0, 0, 0, (1, 0, 0), 0, *rest)
    forward_stage(1, 0, 0, (1, 1, 0), 1, *rest)
    values_here()

    def body(i, carry):
        forward_stage(2 * i, 2 * i - 1, 2 * i - 2, (1, 1, 1), 0, *rest)
        forward_stage(2 * i + 1, 2 * i, 2 * i - 1, (1, 1, 1), 1, *rest)
        return carry

    lax.fori_loop(1, n // 2, body, 0)
    forward_stage(0, n - 1, n - 2, (0, 1, 1), 0, *rest)
    forward_stage(0, 0, n - 1, (0, 0, 1), 1, *rest)


def backward_chunk(c, prev, par, at, kn, k2n, vn, kt_ref, length, gf, x_ref, acc, put):
    q, q2, do, lse, lse2, weight = at(c)
    pq, _, pdo, _, _, _ = at(prev)
    both = jnp.concatenate([pq, pdo], axis=0).astype(F32).T
    col = lax.broadcasted_iota(jnp.int32, (QC, 128), 1)
    rhs = jnp.concatenate(
        [jnp.where(col < 64, both, 0.0), jnp.where(col < 64, 0.0, both)], axis=0
    ).astype(BF)
    d8 = jnp.zeros((8, QC), F32)
    dq = jnp.zeros((64, QC), F32)
    for t in range(NKT):
        rows = slice(t * KT, (t + 1) * KT)
        p = jnp.exp2(dot(kn[rows, :], q) * C2 - lse)
        p2 = jnp.exp2(dot(k2n[rows, :], q2) * C2 - lse2)
        if t == NKT - 1:
            ok = key_ok(length)
            p = jnp.where(ok, p, 0.0)
            p2 = jnp.where(ok, p2, 0.0)
        g = dot(vn[rows, :], do) + weight * (p - p2)
        d8 = d8 + fold(p * g)
        gf[rows, :] = g
        x_ref[par, rows, QC:] = p.astype(BF)
        acc[rows, :] += dot(x_ref[1 - par, rows, :], rhs)
        dq = dq + dot(kt_ref[64:128, rows], x_ref[1 - par, rows, :QC])
    put(prev, dq * 0.125)
    delta = jnp.sum(d8, axis=0, keepdims=True)
    for t in range(NKT):
        rows = slice(t * KT, (t + 1) * KT)
        x_ref[par, rows, :QC] = (x_ref[par, rows, QC:].astype(F32) * (gf[rows, :] - delta)).astype(BF)


def backward_last(prev, par, at, kt_ref, x_ref, acc, put, put_keys):
    pq, _, pdo, _, _, _ = at(prev)
    both = jnp.concatenate([pq, pdo], axis=0).astype(F32).T
    col = lax.broadcasted_iota(jnp.int32, (QC, 128), 1)
    rhs = jnp.concatenate(
        [jnp.where(col < 64, both, 0.0), jnp.where(col < 64, 0.0, both)], axis=0
    ).astype(BF)
    dq = jnp.zeros((64, QC), F32)
    row = lax.broadcasted_iota(jnp.int32, (128, KT), 0)
    for t in range(NKT):
        rows = slice(t * KT, (t + 1) * KT)
        dq = dq + dot(kt_ref[64:128, rows], x_ref[par, rows, :QC])
    put(prev, dq * 0.125)
    for t in range(NKT):
        rows = slice(t * KT, (t + 1) * KT)
        total = (acc[rows, :] + dot(x_ref[par, rows, :], rhs)).T
        put_keys(t, jnp.where(row < 64, total * 0.125, total).astype(BF))


def natural_wide(blocks):
    return blocks.astype(F32).T.astype(BF)


def loop(n, body):
    def step(i, carry):
        body(i)
        return carry

    lax.fori_loop(0, n, step, 0)


def greet_start():
    b = lax.axis_index("blk")
    sem = pltpu.get_barrier_semaphore()
    loop(15, lambda i: pl.semaphore_signal(
        sem, inc=1, device_id={"blk": lax.rem(b + 1 + i, 16)}, device_id_type=MESH
    ))


def greet_end():
    pl.semaphore_wait(pltpu.get_barrier_semaphore(), 15)


def forward_kernel(
    len_ref, x_in, source, flags, cot,
    w_qkv_t, w_out_t, w_up_t, w_down_t, w_qkv_s, w_out_s, w_up_s, w_down_s,
    bias_t, upb_t, vec_t, bias_s, upb_s, vec_s,
    *refs,
):
    kept_out, refs = refs[0:26], refs[26:]
    kept, refs = refs[0:26], refs[26:]
    (
        output, buf_t, dist, buf_s, lse_t, lse_d, lse_s,
        x0_turn, normed_turn_t, hidden_turn, normed_turn_s, g1r_s, g2r_s,
        att_t, act_t, att_s, act_s, gu_s,
        slope_t, unit1_t, scale1_t, unit2_t, scale2_t, g1_s, datt_s, sums,
    ) = kept
    (
    v_qkv_t, v_out_t, v_up_t, v_down_t, v_qkv_s, v_out_s, v_up_s, v_down_s,
    x0_ref, src_t, src_s, land_t, land_s, o_t, o_s, kn, s_ref, p_ref, st,
    slope_s, unit1_s, scale1_s,
    w_sem, x_sem, lse_sem, local_sem, keep_sem,
    ) = refs

    def keep(*which):
        for i in which:
            pltpu.make_async_copy(kept[i], kept_out[i], keep_sem.at[i]).start()

    b, hh, owner = place()
    half, head = hh // 6, lax.rem(hh, 6)
    t_sems, tv_sems, d_sems, a_sems, s_sems, sv_sems, b_sems = [
        tuple(x_sem.at[3 * i + j] for j in range(3)) for i in range(7)
    ]
    mine_half = owner & (half == b // 8)
    greet_start()
    weights = load_all(
        [
            (w_qkv_t, v_qkv_t), (w_out_t, v_out_t), (w_up_t, v_up_t), (w_down_t, v_down_t),
            (w_qkv_s, v_qkv_s), (w_out_s, v_out_s), (w_up_s, v_up_s), (w_down_s, v_down_s),
        ],
        w_sem,
    )
    length = len_ref[0]
    replaced = flags[...] == 1
    place_of = lax.broadcasted_iota(jnp.int32, (128, 128), 0)
    turned = jnp.where((place_of == source[...]) & replaced, 1.0, 0.0)
    chooser = turned.T
    taken = dot(chooser.astype(BF), x_in[...])
    x0 = jnp.where(jnp.sum(chooser, axis=1, keepdims=True) > 0.5, taken, x_in[...].astype(F32))
    x0_ref[...] = x0
    low = x0.astype(BF)
    x0_turn[...] = x0.T.astype(BF)
    keep(7)
    weights[0].wait()
    qkv_blocks(low, v_qkv_t, bias_t, src_t, 12)
    greet_end()

    mine = lanes(b * 128, 128)

    def t_copy(h):
        return src_t.at[h, 0:128], buf_t.at[0:128, mine], t_sems, owner_of(h), b

    def tv_copy(h):
        return src_t.at[h, 128:192], buf_t.at[128:192, mine], tv_sems, owner_of(h), b

    def d_copy(h):
        return src_t.at[h, 0:128], dist.at[:, mine], d_sems, owner_of(h + 6), b

    loop(12, lambda j: start_to(*t_copy(lax.rem(j + b, 12))))
    loop(12, lambda j: start_to(*tv_copy(lax.rem(j + b, 12))))

    def a_copy(d):
        return o_t.at[:, lanes(d * 128, 128)], land_t.at[hh], a_sems, d, b

    @pl.when(owner)
    def _():
        arrive(owner, lambda n: buf_t.at[0:128, 0 : n * 128], 16, t_sems)
        kn[...] = natural(buf_t[64:128, :])

        def put(c, o, stat):
            here = lanes(c * QC, QC)
            o_t[:, here] = o.astype(BF)
            lse_t[:, here] = jnp.broadcast_to(stat, (8, QC))
            for i in range(2):
                start_to(*a_copy(2 * c + i))

        forward_chunks(
            SEQ // QC,
            lambda: arrive(owner, lambda n: buf_t.at[128:192, 0 : n * 128], 16, tv_sems),
            lambda c: buf_t[0:64, lanes(c * QC, QC)], kn, buf_t, s_ref, p_ref, st, put, length,
        )

    @pl.when(owner & (hh < 6))
    def _():
        lse_d[:, 0:1024] = lse_t[:, 0:1024]
        copy_to(
            lse_t.at[:, 1024:2048], lse_d.at[:, 1024:2048], lse_sem.at[0], lse_sem.at[1], owner_of(hh + 6)
        ).start()
        pltpu.make_async_copy(buf_t.at[0:128], dist, local_sem.at[0]).start()

    arrive(owner, lambda n: land_t.at[0:n], 12, a_sems)
    loop(6, lambda j: start_to(*d_copy(lax.rem(j + b, 6))))
    att_t[...] = natural_wide(land_t[...].reshape(768, 128))
    keep(1, 4, 13)
    for i in (1, 2, 3):
        weights[i].wait()
    hidden, unit, scale = dense_up(
        x0_ref[...], att_t[...], v_out_t[...], v_up_t, v_down_t[...], upb_t, vec_t,
        act_t, slope_t, unit1_t, scale1_t, normed_turn_t,
    )
    unit2_t[...] = unit
    scale2_t[...] = jnp.broadcast_to(scale, (128, 128))
    x0_ref[...] = hidden
    low = hidden.astype(BF)
    hidden_turn[...] = hidden.T.astype(BF)
    keep(8, 9, 14, 18, 19, 20, 21, 22)
    weights[4].wait()
    qkv_blocks(low, v_qkv_s, bias_s, src_s, 6)

    def s_copy(h):
        return (
            src_s.at[lax.rem(h, 6), 0:128], buf_s.at[0:128, mine], s_sems, owner_of(h), b
        )

    def sv_copy(h):
        return (
            src_s.at[lax.rem(h, 6), 128:192], buf_s.at[128:192, mine],
            sv_sems, owner_of(h), b,
        )

    loop(12, lambda j: start_to(*s_copy(lax.rem(j + b, 12))))
    loop(12, lambda j: start_to(*sv_copy(lax.rem(j + b, 12))))

    def b_copy(j):
        return o_s.at[:, lanes(j * 128, 128)], land_s.at[head], b_sems, 8 * half + j, b

    @pl.when(owner)
    def _():
        lse_s[:, 0:1024] = jnp.full((8, 1024), 1e30, F32)
        arrive(owner, lambda n: buf_s.at[0:128, 0 : n * 128], 16, s_sems)
        kn[...] = natural(buf_s[64:128, :])

        def put(c, o, stat):
            o_s[:, lanes(c * QC, QC)] = o.astype(BF)
            lse_s[:, lanes(half * 1024 + c * QC, QC)] = jnp.broadcast_to(stat, (8, QC))
            for i in range(2):
                start_to(*b_copy(2 * c + i))

        forward_chunks(
            1024 // QC,
            lambda: arrive(owner, lambda n: buf_s.at[128:192, 0 : n * 128], 16, sv_sems),
            lambda c: buf_s[0:64, lanes(half * 1024 + c * QC, QC)],
            kn, buf_s, s_ref, p_ref, st, put, length,
        )

    @pl.when(owner & (hh >= 6))
    def _():
        copy_to(
            lse_s.at[:, 1024:2048], lse_s.at[:, 1024:2048], lse_sem.at[2], lse_sem.at[3], owner_of(hh - 6)
        ).start()

    @pl.when(owner & (hh < 6))
    def _():
        pltpu.make_async_copy(buf_t.at[0:128], dist, local_sem.at[0]).wait()

    @pl.when(owner & (hh >= 6))
    def _():
        arrive(hh >= 6, lambda n: dist.at[:, 0 : n * 128], 16, d_sems)
        got(lse_d.at[:, 1024:2048], lse_sem.at[1])

    keep(2, 5)
    arrive(mine_half, lambda n: land_s.at[0:n], 6, b_sems)
    att_s[...] = natural_wide(land_s[...].reshape(384, 128))
    keep(3, 15)
    for i in (5, 6, 7):
        weights[i].wait()
    result, unit, scale = dense_up(
        x0_ref[...], att_s[...], v_out_s[...], v_up_s, v_down_s[...], upb_s, vec_s,
        act_s, slope_s, unit1_s, scale1_s, normed_turn_s,
    )
    output[...] = result
    keep(0, 10, 16)
    sums[...] = jnp.zeros((24, 768), F32)
    g1, datt = dense_down(
        cot[...].astype(F32), unit, scale, unit1_s[...], scale1_s[:, 0:1],
        v_out_s, v_up_s, v_down_s, vec_s, slope_s, gu_s, g2r_s, g1r_s, sums, 12,
    )
    g1_s[...] = g1
    datt_s[...] = datt.T.astype(BF).reshape(6, 64, 128)
    keep(11, 12, 17, 23, 24, 25)

    @pl.when(owner)
    def _():
        got(o_t.at[:, 0 : 15 * 128], a_sems[0])
        leave(mine_half, lambda n: o_s.at[:, 0 : n * 128], 8, b_sems)

    @pl.when(owner & (hh < 6))
    def _():
        copy_to(
            lse_t.at[:, 1024:2048], lse_d.at[:, 1024:2048], lse_sem.at[0], lse_sem.at[1], owner_of(hh + 6)
        ).wait_send()
        got(lse_s.at[:, 1024:2048], lse_sem.at[3])

    @pl.when(owner & (hh >= 6))
    def _():
        copy_to(
            lse_s.at[:, 1024:2048], lse_s.at[:, 1024:2048], lse_sem.at[2], lse_sem.at[3], owner_of(hh - 6)
        ).wait_send()

    keep(6)
    leave(owner, lambda n: src_t.at[0:n, 0:128], 12, t_sems)
    leave(owner, lambda n: src_t.at[0:n, 128:192], 12, tv_sems)
    leave(owner & (hh >= 6), lambda n: src_t.at[0:n, 0:128], 6, d_sems)
    leave(owner, lambda n: src_t.at[0:n, 0:128], 12, s_sems)
    leave(owner, lambda n: src_t.at[0:n, 128:192], 12, sv_sems)
    for i in range(26):
        pltpu.make_async_copy(kept[i], kept_out[i], keep_sem.at[i]).wait()


def where_am_i():
    dp, blk = lax.axis_index("dp"), lax.axis_index("blk")
    return dp // 2, lax.rem(dp, 2), blk // 4, lax.rem(blk, 4)


def at_axis(axis, v):
    x, c, y, z = where_am_i()
    if axis == "x":
        return {"dp": 2 * v + c, "blk": 4 * y + z}
    if axis == "y":
        return {"dp": 2 * x + c, "blk": 4 * v + z}
    return {"dp": 2 * x + c, "blk": 4 * y + v}


def send_to(src, dst, send_sem, recv_sem, device):
    return pltpu.make_async_remote_copy(
        src_ref=src, dst_ref=dst, send_sem=send_sem, recv_sem=recv_sem,
        device_id=device, device_id_type=MESH,
    )


ORDERS = ("xyz", "yzx", "zxy")
CUTS = (
    (12, 12, ((16, 12),)), (6, 6, ((0, 6),)), (2, 1, ((6, 2),)), (12, 12, ((28, 12),)),
    (5, 4, ((43, 5),)), (3, 3, ((40, 3),)), (9, 9, ((48, 3), (52, 3), (56, 3))), (6, 6, ((8, 3), (12, 3))),
)
TILES = 60
WIDE = TILES * 128
BATCHES = (
    (0, 16, (1, 2, 7), ((0, 8, 8), (8, 4, 3), (12, 4, 3))),
    (16, 32, (0, 3, 5, 4), ((16, 16, 16), (32, 8, 8), (40, 8, 8))),
    (48, 12, (6,), ((48, 4, 3), (52, 4, 3), (56, 4, 3))),
)
PB_TILES = 32
PIECES = ((4, 0, (0, 2, 6)), (2, 4, (0, 1, 3)), (2, 6, (0, 1, 3)))
PIECE_TILES = 8


def piece_place(k, p, tile):
    half, first, starts = PIECES[p]
    at = starts[k] + tile
    return 8 * (at // half), first + at % half
TURN = 3


def drain(ref, sem):
    pltpu.make_async_copy(ref, ref, sem).wait()


def backward_kernel(
    len_ref, flag_ref, source, flags,
    w_qkv_s, w_down_t, w_up_t, w_out_t, w_qkv_t,
    in_buf_s, in_dist, in_lse_s, in_lse_d, in_g1_s, in_buf_t, in_lse_t,
    in_unit2_t, in_scale2_t, in_slope_t, in_unit1_t, in_scale1_t, datt_s,
    vec_t, sums_s,
    x0_turn, normed_turn_t, hidden_turn, normed_turn_s, g1r_s, g2r_s,
    att_t, act_t, att_s, act_s, gu_s,
    grad_in, out, sums,
    v_qkv_s, v_down_t, v_up_t, v_out_t,
    buf_s, dist, lse_s, lse_d, g1_s, buf_t, lse_t, unit2_t, scale2_t, slope_t, unit1_t, scale1_t,
    joined_t, joined_s, gu_t,
    src_t, do_s, do_t, dq_s, dkv_s, dqkv_t, dq_buf, dkv_buf,
    kn, k2n, vn, gf, x_ref, acc,
    nt, cf, cft, pb, rl, l1, a1, l2, a2, l3, a3, a4, sml, sma, smh,
    w_sem, k_sem, x_sem,
    own_n, own_c, n_send, n_recv, c_send, c_recv, st_send, st_recv, f_send, f_recv, m_send, m_recv,
):
    b, hh, owner = place()
    half, head = hh // 6, lax.rem(hh, 6)
    mine_half = owner & (half == b // 8)
    e1, e2, e3, e4, e5, e6 = [tuple(x_sem.at[3 * i + j] for j in range(3)) for i in range(6)]
    x, c, y, z = where_am_i()
    here_at = {"x": x, "y": y, "z": z}
    dp = 2 * x + c
    me = 16 * dp + b
    partner = {"dp": 2 * x + 1 - c, "blk": b}

    barrier = pltpu.get_barrier_semaphore()
    loop(15, lambda i: pl.semaphore_signal(
        barrier, inc=1, device_id={"blk": lax.rem(b + 1 + i, 16)}, device_id_type=MESH
    ))
    pl.semaphore_signal(barrier, inc=1, device_id=partner, device_id_type=MESH)
    for axis in "xyz":
        for j in range(1, 4):
            pl.semaphore_signal(
                barrier, inc=1, device_id=at_axis(axis, lax.rem(here_at[axis] + j, 4)), device_id_type=MESH
            )
    for p in range(3):
        for q in range(4):
            for core in range(2):
                at = dict(zip(ORDERS[p], (me // 32, lax.rem(me // 8, 4), q)))
                pl.semaphore_signal(
                    barrier, inc=1, device_id={"dp": 2 * at["x"] + core, "blk": 4 * at["y"] + at["z"]},
                    device_id_type=MESH,
                )
    kept = load_all(
        [
            (in_buf_s, buf_s), (in_dist, dist), (in_lse_s, lse_s), (in_lse_d, lse_d),
            (in_g1_s, g1_s), (in_buf_t, buf_t), (in_lse_t, lse_t), (in_unit2_t, unit2_t),
            (in_scale2_t, scale2_t), (in_slope_t, slope_t), (in_unit1_t, unit1_t), (in_scale1_t, scale1_t),
        ],
        k_sem,
    )
    weights = load_all(
        [(w_qkv_s, v_qkv_s), (w_down_t, v_down_t), (w_up_t, v_up_t), (w_out_t, v_out_t)], w_sem
    )
    length = len_ref[0]
    for copy in kept[0:4]:
        copy.wait()

    @pl.when(owner)
    def _():
        kn[...] = natural(buf_s[64:128, :])
        vn[...] = natural(buf_s[128:192, :])
        k2n[...] = natural(dist[64:128, :])
        acc[...] = jnp.zeros_like(acc)
        x_ref[1] = jnp.zeros((SEQ, 2 * QC), BF)

    pl.semaphore_wait(barrier, 49)

    def tiles(first, count):
        return slice(first * 128, (first + count) * 128)

    def pool_wide(m, ref):
        _, step, segments = CUTS[m]
        done = 0
        for n, (first, count) in enumerate(segments):
            cols = slice(first * 128, (first + count) * 128)
            pltpu.make_async_copy(
                ref.at[:, lanes((c * step + done) * 128, count * 128)], cf.at[0:128, cols], own_c.at[m + 8 * n]
            ).start()
            send_to(
                ref.at[:, lanes(((1 - c) * step + done) * 128, count * 128)], cf.at[128:256, cols],
                c_send.at[m + 8 * n], c_recv.at[m + 8 * n], partner,
            ).start()
            done += count

    def pool_heads():
        pltpu.make_async_copy(dqkv_t.at[pl.ds(6 * c, 6)], cft.at[:, :, 0:128], own_c.at[6]).start()
        send_to(
            dqkv_t.at[pl.ds(6 * (1 - c), 6)], cft.at[:, :, 128:256], c_send.at[6], c_recv.at[6], partner
        ).start()

    def pool_narrow(m, ref):
        if ref is None:
            ref = nt.at[m, :, 0:128]
        else:
            pltpu.make_async_copy(ref, nt.at[m, :, 0:128], own_n.at[m]).start()
        send_to(ref, nt.at[m, :, 128:256], n_send.at[m], n_recv.at[m], partner).start()

    def products(k, members=None):
        begin = BATCHES[k][0]
        for m in members or BATCHES[k][2]:
            if m not in (3, 5):
                drain(nt.at[m, :, 0:128], own_n.at[m])
            drain(nt.at[m, :, 128:256], n_recv.at[m])
            if m == 6:
                drain(cft.at[:, :, 0:128], own_c.at[6])
                drain(cft.at[:, :, 128:256], c_recv.at[6])
                for n, (first, count) in enumerate(CUTS[m][2]):
                    pb[:, tiles(first - begin, count)] = dot_t(
                        nt[m], cft[2 * n : 2 * n + 2].reshape(384, 256)
                    ).astype(BF)
                continue
            for n, (first, count) in enumerate(CUTS[m][2]):
                cols = slice(first * 128, (first + count) * 128)
                drain(cf.at[0:128, cols], own_c.at[m + 8 * n])
                drain(cf.at[128:256, cols], c_recv.at[m + 8 * n])
                size = 3 if count % 3 == 0 else count

                def piece(i, m=m, first=first, size=size):
                    from_cols = lanes((first + i * size) * 128, size * 128)
                    to_cols = lanes((first - begin + i * size) * 128, size * 128)
                    pb[:, to_cols] = dot(nt[m], cf[:, from_cols]).astype(BF)

                loop(count // size, piece)

    def sem_of(k, p, kind):
        return 18 * k + 6 * p + kind

    def rows_of(height, v):
        return pl.ds(pl.multiple_of(height * v, 16), height)

    def ring(p, stage):
        axis = ORDERS[p][stage]
        u = here_at[axis]
        around = [lax.rem(u + j, 4) for j in range(4)]
        return around, [at_axis(axis, v) for v in around]

    def stage_start(k, stage, only=(0, 1, 2)):
        begin, _, _, parts = BATCHES[k]
        for p in only:
            first, count, used = parts[p]
            around, devices = ring(p, stage)
            if stage == 0:
                first_half = (used + 1) // 2
                one, two = (0, first_half), (first_half, used - first_half)
                for j, (start, size), to, dst, kind in (
                    (2, one, 1, rl, 0), (2, two, 3, rl, 1), (1, two, 1, l1.at[0], 2), (3, one, 3, l1.at[1], 3),
                ):
                    send_to(
                        pb.at[rows_of(192, around[j]), tiles(first - begin + start, size)],
                        dst.at[:, tiles(first + start, size)],
                        st_send.at[sem_of(k, p, 0)], st_recv.at[sem_of(k, p, kind)], devices[to],
                    ).start()
                continue
            for j in range(1, 4):
                if stage == 1:
                    src = a1.at[rows_of(48, around[j]), tiles(first, used)]
                    dst = l2.at[j - 1, :, tiles(first, used)]
                else:
                    src = a2.at[:, lanes(first * 128 + around[j] * count * 32, count * 32)]
                    dst = l3.at[j - 1, :, slice(first * 32, (first + count) * 32)]
                kind = 3 + stage
                send_to(
                    src, dst, st_send.at[sem_of(k, p, kind)], st_recv.at[sem_of(k, p, kind)], devices[j]
                ).start()

    def relay(k):
        begin, _, _, parts = BATCHES[k]
        for p, (first, count, used) in enumerate(parts):
            around, devices = ring(p, 0)
            first_half = (used + 1) // 2
            for start, size, to, slot in ((0, first_half, 1, 0), (first_half, used - first_half, 3, 1)):
                land = rl.at[:, tiles(first + start, size)]
                drain(land, st_recv.at[sem_of(k, p, slot)])
                own_cols = tiles(first - begin + start, size)

                def add(r, own_cols=own_cols, start=start, size=size, to=to, first=first, around=around):
                    own = pl.ds(pl.multiple_of(192 * around[to] + 16 * r, 16), 16)
                    rows = pl.ds(pl.multiple_of(16 * r, 16), 16)
                    total = pb[own, own_cols].astype(F32) + rl[rows, tiles(first + start, size)].astype(F32)
                    pb[own, own_cols] = total.astype(BF)

                loop(12, add)
                send_to(
                    pb.at[rows_of(192, around[to]), own_cols], l1.at[slot, :, tiles(first + start, size)],
                    st_send.at[sem_of(k, p, 1)], st_recv.at[sem_of(k, p, 2 + slot)], devices[to],
                ).start()

    def stage_sent(k, stage):
        for p, (first, count, used) in enumerate(BATCHES[k][3]):
            if stage == 0:
                drain(l1.at[:, :, tiles(first, used)], st_send.at[sem_of(k, p, 0)])
                drain(rl.at[:, tiles(first, used)], st_send.at[sem_of(k, p, 1)])
            elif stage == 1:
                drain(l2.at[:, :, tiles(first, used)], st_send.at[sem_of(k, p, 4)])
            else:
                drain(l3.at[:, :, slice(first * 32, (first + count) * 32)], st_send.at[sem_of(k, p, 5)])

    def stage_sum(k, stage):
        begin, _, _, parts = BATCHES[k]
        for p, (first, count, used) in enumerate(parts):
            at = here_at[ORDERS[p][stage]]
            cols = tiles(first, used)
            if stage == 0:
                for slot in range(2):
                    drain(l1.at[slot, :, cols], st_recv.at[sem_of(k, p, 2 + slot)])
                src, land, dst, height, peers, scols = pb, l1, a1, 192, 2, tiles(first - begin, used)
            elif stage == 1:
                drain(l2.at[:, :, cols], st_recv.at[sem_of(k, p, 4)])
                src, land, dst, height, peers, scols = a1, l2, a2, 48, 3, cols
            else:
                quarter = slice(first * 32, (first + count) * 32)
                drain(l3.at[:, :, quarter], st_recv.at[sem_of(k, p, 5)])
                total = a2[:, lanes(first * 128 + at * count * 32, count * 32)].astype(F32)
                for j in range(3):
                    total = total + l3[j, :, quarter].astype(F32)
                for tile in range(count // 4):
                    row, at_tile = piece_place(k, p, tile)
                    for i in range(8):
                        a3[i, row : row + 6, tiles(at_tile, 1)] = total[6 * i : 6 * i + 6, tiles(tile, 1)]
                continue

            def add(r, src=src, land=land, dst=dst, height=height, peers=peers, at=at, cols=cols, scols=scols):
                rows = pl.ds(pl.multiple_of(16 * r, 16), 16)
                own = pl.ds(pl.multiple_of(height * at + 16 * r, 16), 16)
                total = src[own, scols].astype(F32)
                for j in range(peers):
                    total = total + land[j, rows, cols].astype(F32)
                dst[rows, cols] = total.astype(BF)

            loop(height // 16, add)

    def final_part(p):
        half, first, _ = PIECES[p]
        begin = 32 * here_at[ORDERS[p][0]] + 8 * here_at[ORDERS[p][1]]
        return begin, half, first, here_at[ORDERS[p][2]]

    def final_start():
        a4[...] = a3[...].astype(BF)
        for p in range(3):
            begin, half, first, third = final_part(p)
            for i in range(8):
                to = begin + i
                src = a4.at[i, :, tiles(first, half)]
                dst = out.at[:, lanes(((4 * c + third) * PIECE_TILES + first) * 128, half * 128)]

                @pl.when(to != me)
                def _():
                    send_to(
                        src, dst, f_send.at[p], f_recv.at[0], {"dp": to // 16, "blk": lax.rem(to, 16)}
                    ).start()

                @pl.when(to == me)
                def _():
                    pltpu.make_async_copy(src, dst, f_recv.at[0]).start()

    def final_wait():
        drain(out, f_recv.at[0])
        for p in range(3):
            begin, half, first, _ = final_part(p)
            own = (me >= begin) & (me < begin + 8)
            leave(own, lambda n, first=first, half=half: a4.at[0:n, :, tiles(first, half)], 8, (f_send.at[p],))

    half_lanes = lanes(c * 384, 384)

    def small_copy(slot):
        if slot in (0, 10):
            src = sma.at[0, :, lanes((1 - c) * 384, 384)] if slot == 0 else sums.at[:, half_lanes]
            dst = sml.at[0] if slot == 0 else sums.at[:, half_lanes]
            return send_to(src, dst, m_send.at[slot], m_recv.at[slot], partner)
        n, j = (slot - 1) // 3, (slot - 1) % 3 + 1
        axis = "xyz"[n]
        return send_to(
            smh.at[n], sml.at[slot], m_send.at[slot], m_recv.at[slot],
            at_axis(axis, lax.rem(here_at[axis] + j, 4)),
        )

    def small_step(n):
        if n == 0:
            small_copy(0).start()
            return
        total = sma[0, :, half_lanes] if n == 1 else smh[n - 2]
        for slot in (0,) if n == 1 else range(3 * n - 5, 3 * n - 2):
            small_copy(slot).wait_recv()
            total = total + sml[slot]
        if n == 4:
            sums[:, half_lanes] = total
            small_copy(10).start()
            return
        smh[n - 1] = total
        for slot in range(3 * n - 2, 3 * n + 1):
            small_copy(slot).start()

    def c1(h):
        return (
            datt_s.at[h], do_s.at[:, lanes(lax.rem(b, 8) * 128, 128)],
            e1, owner_of(h + 6 * (b // 8)), b,
        )

    def c2(j):
        return dq_buf.at[:, lanes(j * 128, 128)], dq_s.at[head], e2, 8 * half + j, b

    def c3(d):
        return dkv_buf.at[:, lanes(d * 128, 128)], dkv_s.at[hh], e3, d, b

    def c4(h):
        return src_t.at[h], do_t.at[:, lanes(b * 128, 128)], e4, owner_of(h), b

    def c5(d):
        return dq_buf.at[:, lanes(d * 128, 128)], dqkv_t.at[hh, 0:64], e5, d, b

    def c6(d):
        return dkv_buf.at[:, lanes(d * 128, 128)], dqkv_t.at[hh, 64:192], e6, d, b

    def run_chunks(n, at, kt_ref, put, low, high, put_keys=None):
        rest = (at, kn, k2n, vn, kt_ref, length, gf, x_ref, acc)

        def pair(i):
            backward_chunk(
                2 * i, jnp.maximum(2 * i - 1, 0), 0, *rest, lambda ch, g: put(ch, g, i > 0)
            )
            backward_chunk(2 * i + 1, 2 * i, 1, *rest, lambda ch, g: put(ch, g, True))

        loop(high - low, lambda i: pair(i + low))
        if 2 * high == n:
            backward_last(n - 1, 1, at, kt_ref, x_ref, acc, lambda ch, g: put(ch, g, True), put_keys)

    def keys_out(copy):
        def put_keys(t, block):
            dkv_buf[:, t * KT : (t + 1) * KT] = block
            for i in range(2):
                start_to(*copy(2 * t + i))

        return put_keys

    def send_pair(copy, ch, real):
        if real is True:
            for i in range(2):
                start_to(*copy(2 * ch + i))
        else:
            @pl.when(real)
            def _():
                for i in range(2):
                    start_to(*copy(2 * ch + i))

    def teacher_at(ch):
        here = lanes(ch * QC, QC)
        return (
            buf_t[0:64, here], buf_s[0:64, here], do_t[:, here],
            lse_t[0:1, here], lse_s[0:1, here], weight_row(len_ref, flag_ref, head, ch * QC, hh < 6),
        )

    def teacher_put(ch, g, real):
        dq_buf[:, lanes(ch * QC, QC)] = g.astype(BF)
        send_pair(c5, ch, real)

    loop(6, lambda j: start_to(*c1(lax.rem(j + b, 6))))
    for m, ref in ((1, normed_turn_s), (2, g1r_s), (7, g2r_s)):
        pool_narrow(m, ref)
    for m, ref in ((1, gu_s), (2, att_s), (7, act_s)):
        pool_wide(m, ref)
    for m, ref in ((0, normed_turn_t), (4, hidden_turn), (6, x0_turn)):
        pool_narrow(m, ref)
    for m, ref in ((3, act_t), (5, att_t)):
        pool_wide(m, ref)

    products(0)
    stage_start(0, 0)

    @pl.when(owner)
    def _():
        arrive(mine_half, lambda n: do_s.at[:, 0 : n * 128], 8, e1)

        def at(ch):
            first = half * 1024 + ch * QC
            here = lanes(first, QC)
            return (
                buf_s[0:64, here], dist[0:64, here], do_s[:, lanes(ch * QC, QC)],
                lse_s[0:1, here], lse_d[0:1, here], weight_row(len_ref, flag_ref, head, first, True),
            )

        def put(ch, g, real):
            dq_buf[:, lanes(ch * QC, QC)] = g.astype(BF)
            send_pair(c2, ch, real)

        run_chunks(1024 // QC, at, buf_s, put, 0, 2, keys_out(c3))

    relay(0)
    arrive(mine_half, lambda n: dq_s.at[0:n], 6, e2)
    arrive(owner, lambda n: dkv_s.at[0:n], 12, e3)
    joined_s[:, 0:384] = natural_wide(dq_s[...].reshape(384, 128))
    for part in range(2):
        rows = slice(64 * part, 64 * part + 64)
        both = dkv_s[0:6, rows, :].astype(F32) + dkv_s[6:12, rows, :].astype(F32)
        joined_s[:, 384 * (part + 1) : 384 * (part + 2)] = both.reshape(384, 128).T.astype(BF)
    pool_wide(4, joined_s)
    sma[0] = sums_s[...]
    low_sums = jnp.sum(joined_s[...].astype(F32), axis=0, keepdims=True)
    sma[0, 20:21, 0:384] = low_sums[:, 0:384]
    sma[0, 20:21, 384:768] = low_sums[:, 768:1152]
    for copy in kept[4:]:
        copy.wait()
    weights[0].wait()
    grad_hidden = g1_s[...] + dot_t(joined_s[...], v_qkv_s[...])
    for i in (1, 2, 3):
        weights[i].wait()
    g1, datt = dense_down(
        grad_hidden, unit2_t[...], scale2_t[:, 0:1], unit1_t[...], scale1_t[:, 0:1],
        v_out_t, v_up_t, v_down_t, vec_t, slope_t, gu_t, nt.at[3, :, 0:128], nt.at[5, :, 0:128], sma.at[0], 0,
        (lambda: pool_narrow(3, None), lambda: pool_wide(0, gu_t), lambda: pool_narrow(5, None)),
    )
    grad_in[...] = g1
    src_t[...] = datt.T.astype(BF).reshape(12, 64, 128)
    loop(12, lambda j: start_to(*c4(lax.rem(j + b, 12))))
    late = load_all(
        [(w_qkv_t.at[:, 768 * p : 768 * (p + 1)], v_down_t.at[768 * p : 768 * (p + 1), :]) for p in range(3)],
        w_sem.at[pl.ds(4, 3)],
    )
    stage_sum(0, 0)
    stage_sent(0, 0)
    products(1, (0, 3))
    stage_start(1, 0, (0, 1))
    products(1, (5, 4))
    stage_start(1, 0, (2,))

    @pl.when(owner)
    def _():
        kn[...] = natural(buf_t[64:128, :])
        vn[...] = natural(buf_t[128:192, :])
        k2n[...] = natural(buf_s[64:128, :])
        acc[...] = jnp.zeros_like(acc)
        x_ref[1] = jnp.zeros((SEQ, 2 * QC), BF)

    @pl.when(owner)
    def _():
        leave(mine_half, lambda n: dq_buf.at[:, 0 : n * 128], 8, e2)
        got(dkv_buf.at[:, 0 : 15 * 128], e3[0])
        arrive(owner, lambda n: do_t.at[:, 0 : n * 128], 16, e4)

        run_chunks(SEQ // QC, teacher_at, buf_t, teacher_put, 0, TURN)

    relay(1)
    stage_start(0, 1)

    @pl.when(owner)
    def _():
        run_chunks(SEQ // QC, teacher_at, buf_t, teacher_put, TURN, SEQ // QC // 2, keys_out(c6))

    stage_sum(0, 1)
    stage_start(0, 2)
    stage_sum(1, 0)
    stage_start(1, 1)
    arrive(owner, lambda n: dqkv_t.at[0:n, 0:64], 12, e5)
    arrive(owner, lambda n: dqkv_t.at[0:n, 64:192], 12, e6)
    pool_heads()
    stage_sent(1, 0)
    for part in range(3):
        joined_t[:, 768 * part : 768 * (part + 1)] = natural_wide(
            dqkv_t[:, 64 * part : 64 * (part + 1), :].reshape(768, 128)
        )
    for row, part in ((10, 0), (11, 2)):
        sma[0, row : row + 1, :] = jnp.sum(
            joined_t[:, 768 * part : 768 * (part + 1)].astype(F32), axis=0, keepdims=True
        )
    small_step(0)
    products(2)
    stage_start(2, 0)
    small_step(1)
    stage_sum(1, 1)
    stage_start(1, 2)
    for copy in late:
        copy.wait()
    grad = grad_in[...]
    for p in range(3):
        grad = grad + dot_t(joined_t[:, 768 * p : 768 * (p + 1)], v_down_t[768 * p : 768 * (p + 1), :])
    place_of = lax.broadcasted_iota(jnp.int32, (128, 128), 0)
    turned = jnp.where((place_of == source[...]) & (flags[...] == 1), 1.0, 0.0)
    back = turned.astype(BF)
    one = grad.astype(BF)
    rest = grad - one.astype(F32)
    two = rest.astype(BF)
    three = (rest - two.astype(F32)).astype(BF)
    copied = dot(back, one) + dot(back, two) + dot(back, three)
    kept = jnp.sum(turned.T, axis=1, keepdims=True) < 0.5
    grad_in[...] = jnp.where(kept, grad, 0.0) + copied
    relay(2)
    small_step(2)
    stage_sum(2, 0)
    stage_start(2, 1)
    small_step(3)
    stage_sum(0, 2)
    stage_sum(1, 2)
    stage_sum(2, 1)
    stage_start(2, 2)
    small_step(4)
    stage_sum(2, 2)
    final_start()

    @pl.when(owner)
    def _():
        got(dq_buf.at[:, 0 : 15 * 128], e5[0])
        got(dkv_buf.at[:, 0 : 15 * 128], e6[0])

    leave(mine_half, lambda n: dq_s.at[0:n], 6, e1)
    leave(owner, lambda n: src_t.at[0:n], 12, e4)
    for m, (_, _, segments) in enumerate(CUTS):
        if m == 6:
            drain(cft.at[:, :, 128:256], c_send.at[6])
            segments = ()
        for n, (first, count) in enumerate(segments):
            drain(cf.at[128:256, slice(first * 128, (first + count) * 128)], c_send.at[m + 8 * n])
        drain(nt.at[m, :, 128:256], n_send.at[m])
    for slot in range(11):
        small_copy(slot).wait_send()
    small_copy(10).wait_recv()
    for k, stage in ((0, 1), (0, 2), (1, 1), (1, 2), (2, 0), (2, 1), (2, 2)):
        stage_sent(k, stage)
    final_wait()


ANY = pl.BlockSpec(memory_space=pl.ANY)


def mega_call(kernel, ident, specs, outs, scratch, args, name, out_spec):
    return pl.pallas_call(
        kernel,
        name=name,
        out_shape=tuple(jax.ShapeDtypeStruct(s, t) for s, t in outs),
        in_specs=specs,
        out_specs=tuple(out_spec for _ in outs),
        scratch_shapes=scratch,
        compiler_params=pltpu.CompilerParams(
            collective_id=ident, has_side_effects=True, vmem_limit_bytes=62 * MIB
        ),
    )(*args)


def vb(*shape):
    return pltpu.VMEM(shape, BF)


def vf(*shape):
    return pltpu.VMEM(shape, F32)


def run_forward(lengths, x_in, source, flags, cot, weights, smalls):
    outs = [
        ((128, 768), F32), ((192, SEQ), BF), ((128, SEQ), BF), ((192, SEQ), BF),
        ((8, SEQ), F32), ((8, SEQ), F32), ((8, SEQ), F32),
        *[((768, 128), BF)] * 6,
        ((128, 768), BF), ((128, 3072), BF), ((128, 384), BF), ((128, 1536), BF), ((128, 1536), BF),
        ((128, 3072), BF), ((128, 768), F32), ((128, 128), F32), ((128, 768), F32), ((128, 128), F32),
        ((128, 768), F32), ((6, 64, 128), BF), ((24, 768), F32),
    ]
    scratch = [pltpu.VMEM(shape, kind) for shape, kind in outs] + [
        vb(768, 2304), vb(768, 768), vb(768, 3072), vb(3072, 768),
        vb(768, 1152), vb(384, 768), vb(768, 1536), vb(1536, 768),
        vf(128, 768), vb(12, 192, 128), vb(6, 192, 128), vb(12, 64, 128), vb(6, 64, 128),
        vb(64, SEQ), vb(64, 1024), vb(SEQ, 64), vf(2, SEQ, QC), vb(2, SEQ, QC), vf(6, 8, QC),
        vb(128, 1536), vf(128, 768), vf(128, 128),
        DMA((8,)), DMA((21,)), DMA((4,)), DMA((1,)), DMA((26,)),
    ]
    specs = [SMEM] + [VMEM] * 4 + [ANY] * 8 + [VMEM] * 6
    return mega_call(
        forward_kernel, 1, specs, outs, scratch, (lengths, x_in, source, flags, cot, *weights, *smalls), "forward", ANY
    )


def run_backward(lengths, head_flags, source, flags, weights, kept, held, pooled):
    outs = [((128, 768), F32), ((16, 8 * PIECE_TILES * 128), BF), ((24, 768), F32)]
    scratch = [
        vb(768, 1152), vb(3072, 768), vb(768, 3072), vb(768, 768),
        vb(192, SEQ), vb(128, SEQ), vf(8, SEQ), vf(8, SEQ), vf(128, 768), vb(192, SEQ), vf(8, SEQ),
        vf(128, 768), vf(128, 128), vb(128, 3072), vf(128, 768), vf(128, 128),
        vb(128, 2304), vb(128, 1152), vb(128, 3072),
        vb(12, 64, 128), vb(64, 1024), vb(64, SEQ), vb(6, 64, 128), vb(12, 128, 128), vb(12, 192, 128),
        vb(64, SEQ), vb(128, SEQ),
        vb(SEQ, 64), vb(SEQ, 64), vb(SEQ, 64), vf(SEQ, QC), vb(2, SEQ, 2 * QC), vf(SEQ, 128),
        vb(8, 768, 256), vb(256, 48 * 128), vb(6, 192, 256), vb(768, PB_TILES * 128),
        vb(192, WIDE), vb(2, 192, WIDE), vb(192, WIDE), vb(3, 48, WIDE), vb(48, WIDE), vb(3, 48, WIDE // 4), vf(8, 16, PIECE_TILES * 128), vb(8, 16, PIECE_TILES * 128),
        vf(10, 24, 384), vf(1, 24, 768), vf(3, 24, 384),
        DMA((7,)), DMA((12,)), DMA((18,)),
        DMA((8,)), DMA((24,)), DMA((8,)), DMA((8,)), DMA((24,)), DMA((24,)),
        DMA((54,)), DMA((54,)), DMA((3,)), DMA((1,)), DMA((11,)), DMA((11,)),
    ]
    specs = [SMEM] * 2 + [VMEM] * 2 + [ANY] * (5 + len(kept)) + [VMEM] * len(held) + [ANY] * len(pooled)
    return mega_call(
        backward_kernel, 2, specs, outs, scratch,
        (lengths, head_flags, source, flags, *weights, *kept, *held, *pooled), "backward", VMEM,
    )


def unpack_kernel(whole, sums, first_in, second_in, *outs):
    first_out, second_out, outs = outs[0], outs[1], outs[2:16]
    first_out[...] = first_in[...]
    second_out[...] = second_in[...]

    def tile_at(core, tile):
        for k, (_, _, _, parts) in enumerate(BATCHES):
            for p, (first, count, _) in enumerate(parts):
                if first <= tile < first + count:
                    third, rest = (tile - first) // (count // 4), (tile - first) % (count // 4)
                    row, at = piece_place(k, p, rest)
                    start = ((4 * core + third) * PIECE_TILES + at) * 128
                    return wide[row : row + 8, start : start + 128]

    wide = whole[...].astype(F32)

    def columns(m):
        count, step, segments = CUTS[m]
        if m == 6:
            tiles_of = [[tile_at(core, first + i) for first, size in segments for i in range(size)] for core in range(2)]
            pieces = []
            for part in range(3):
                for head in range(12):
                    lane = 192 * (head % 6) + 64 * part
                    pieces.append(tiles_of[head // 6][lane // 128][:, lane % 128 : lane % 128 + 64])
            return jnp.concatenate(pieces, axis=1)
        spots = [first + i for first, size in segments for i in range(size)]
        pieces = [tile_at(0, tile) for tile in spots] + [tile_at(1, tile) for tile in spots[count - step :]]
        return jnp.concatenate(pieces, axis=1)

    for m, o in ((6, 0), (5, 2), (0, 3), (3, 4), (4, 7), (2, 9), (1, 10), (7, 11)):
        outs[o][...] = columns(m)[0:6]
    i = 16 * lax.axis_index("dp") + lax.axis_index("blk")

    def turn(rows, by):
        return pltpu.roll(rows, lax.rem(768 - by, 768), 1)

    def pick(first, count, per):
        row = first + (i * per) // 768
        wide = jnp.broadcast_to(sums[pl.ds(row, 1), :], (8, 768))
        return turn(wide, lax.rem(i * per, 768))[0:1, 0:per]

    outs[1][...] = pick(10, 2, 12)
    outs[5][...] = pick(6, 4, 24)
    outs[8][...] = pick(20, 1, 6)
    outs[12][...] = pick(18, 2, 12)
    outs[6][...] = turn(sums[0:8, :], i * 6)[0:6, 0:6]
    outs[13][...] = turn(sums[8:24, :], i * 6)[4:10, 0:6]


def unpack(whole, sums, output, grad_in):
    shapes = (
        (6, 2304), (1, 12), (6, 768), (6, 3072), (6, 3072), (1, 24), (6, 6),
        (6, 1152), (1, 6), (6, 384), (6, 1536), (6, 1536), (1, 12), (6, 6),
    )
    outs = list(
        pl.pallas_call(
            unpack_kernel,
            name="unpack",
            out_shape=tuple(jax.ShapeDtypeStruct(s, F32) for s in ((128, 768), (128, 768)) + shapes),
            in_specs=[VMEM] * 4,
            out_specs=(VMEM, VMEM) + tuple(VMEM for _ in shapes),
            compiler_params=pltpu.CompilerParams(vmem_limit_bytes=62 * MIB),
        )(whole, sums, output, grad_in)
    )
    for i in (3, 7, 10, 14):
        outs[i] = outs[i].reshape(-1)
    for i in (4, 6, 11, 13):
        outs[i] = outs[i].T
    outs[0], outs[1] = outs[0][None], outs[1][None]
    return tuple(outs)


def per_device(
    inputs, aug_source, aug_flags, lengths, head_flags, cotangent,
    qkv_teacher, qv_bias_teacher, out_teacher, up_teacher, down_teacher, up_bias_teacher, vectors_teacher,
    qkv_student, qv_bias_student, out_student, up_student, down_student, up_bias_student, vectors_student,
):
    (
        output, buf_t, dist, buf_s, lse_t, lse_d, lse_s,
        x0_turn, normed_turn_t, hidden_turn, normed_turn_s, g1r_s, g2r_s,
        att_t, act_t, att_s, act_s, gu_s,
        slope_t, unit1_t, scale1_t, unit2_t, scale2_t, g1_s, datt_s, sums_s,
    ) = run_forward(
        lengths, inputs[0], aug_source, aug_flags, cotangent[0],
        (qkv_teacher, out_teacher, up_teacher, down_teacher, qkv_student, out_student, up_student, down_student),
        (
            qv_bias_teacher, up_bias_teacher, vectors_teacher,
            qv_bias_student, up_bias_student, vectors_student,
        ),
    )
    grad_in, whole, total = run_backward(
        lengths, head_flags, aug_source, aug_flags,
        (qkv_student, down_teacher, up_teacher, out_teacher, qkv_teacher),
        (
            buf_s, dist, lse_s, lse_d, g1_s, buf_t, lse_t,
            unit2_t, scale2_t, slope_t, unit1_t, scale1_t, datt_s,
        ),
        (vectors_teacher, sums_s),
        (
            x0_turn, normed_turn_t, hidden_turn, normed_turn_s, g1r_s, g2r_s,
            att_t, act_t, att_s, act_s, gu_s,
        ),
    )
    return unpack(whole, total, output, grad_in)


def solution(mesh):
    both = ("dp", "blk")
    row, flat, col = P(both, None), P(both), P(None, both)
    tokens, marks = P("dp", "blk", None), P("dp", "blk")
    return jax.shard_map(
        per_device,
        mesh=mesh,
        in_specs=(tokens, marks, marks, P("dp"), P(), tokens) + (P(),) * 14,
        out_specs=(tokens, tokens) + (row, flat, col, row, col, flat, col) * 2,
        check_vma=False,
    )
```

```python
import jax
import jax.numpy as jnp
from jax import lax
from jax.experimental import pallas as pl
from jax.experimental.pallas import tpu as pltpu
from jax.sharding import PartitionSpec as P

MESH = pl.DeviceIdType.MESH
LOG2E = 1.4426950408889634
C2 = 0.125 * LOG2E
SEQ = 2048
QC = 256
KT = 256
NKT = SEQ // KT
MIB = 1 << 20


def dot(a, b):
    return jnp.dot(a, b, preferred_element_type=jnp.float32)


def place():
    b = lax.axis_index("blk")
    r = lax.rem(lax.rem(b, 4) - b // 4 + 7, 4)
    return b, 3 * (b // 4) + r, r < 3


def owner_of(hh):
    y = hh // 3
    return 4 * y + lax.rem(y + lax.rem(hh, 3) + 1, 4)


def copy_to(src, dst, send_sem, recv_sem, d):
    return pltpu.make_async_remote_copy(
        src_ref=src,
        dst_ref=dst,
        send_sem=send_sem,
        recv_sem=recv_sem,
        device_id={"blk": d},
        device_id_type=MESH,
    )


def start_to(src, dst, sems, d, b):
    send_sem, recv_sem, own_sem = sems

    @pl.when(d != b)
    def _():
        copy_to(src, dst, send_sem, recv_sem, d).start()

    @pl.when(d == b)
    def _():
        pltpu.make_async_copy(src, dst, own_sem).start()


def arrive(own, blocks, count, sems):
    @pl.when(own)
    def _():
        got(blocks(count - 1), sems[1])
        got(blocks(1), sems[2])

    @pl.when(jnp.logical_not(own))
    def _():
        got(blocks(count), sems[1])


def leave(own, blocks, count, sems):
    @pl.when(own)
    def _():
        got(blocks(count - 1), sems[0])

    @pl.when(jnp.logical_not(own))
    def _():
        got(blocks(count), sems[0])


def got(dst, recv_sem):
    pltpu.make_async_copy(dst, dst, recv_sem).wait()


def lanes(start, size):
    return pl.ds(pl.multiple_of(start, 128), size)


def fold(v):
    return jnp.sum(v.reshape(v.shape[0] // 8, 8, v.shape[1]), axis=0)


def key_ok(length):
    rows = lax.broadcasted_iota(jnp.int32, (KT, QC), 0) + (SEQ - KT)
    return rows < length


def natural(x):
    return x.astype(jnp.float32).T.astype(jnp.bfloat16)


def weight_row(len_ref, flag_ref, head, first, use):
    q = lax.broadcasted_iota(jnp.int32, (1, QC), 1) + first
    factor = jnp.where(use, flag_ref[head].astype(jnp.float32) * (2.0 * SEQ), 0.0)
    return jnp.where(q < len_ref[0], factor, 0.0)


SMEM = pl.BlockSpec(memory_space=pltpu.SMEM)
VMEM = pl.BlockSpec(memory_space=pltpu.VMEM)
DMA = pltpu.SemaphoreType.DMA
BF = jnp.bfloat16
F32 = jnp.float32


SQRT_HALF = 0.7071067811865476
INV_SQRT_2PI = 0.3989422804014327


def dot_t(a, b):
    return lax.dot_general(a, b, (((1,), (1,)), ((), ())), preferred_element_type=F32)


def norm_forward(v, gain, shift):
    center = v - jnp.mean(v, axis=-1, keepdims=True)
    scale = lax.rsqrt(jnp.mean(center * center, axis=-1, keepdims=True) + 1e-06)
    unit = center * scale
    return unit * gain + shift, unit, scale


def norm_backward(grad, gain, unit, scale):
    scaled = grad * gain
    mean_one = jnp.mean(scaled, axis=-1, keepdims=True)
    mean_two = jnp.mean(scaled * unit, axis=-1, keepdims=True)
    return (
        (scaled - mean_one - unit * mean_two) * scale,
        jnp.sum(grad * unit, axis=0, keepdims=True),
        jnp.sum(grad, axis=0, keepdims=True),
    )


def qkv_blocks(low, w, bias, src, heads):
    span = heads * 64
    for part in range(3):
        joint = dot(low, w[:, part * span : (part + 1) * span])
        if part != 1:
            first = 0 if part == 0 else span
            joint = joint + bias[first : first + span].reshape(1, span)
        src[:, part * 64 : (part + 1) * 64, :] = joint.T.astype(BF).reshape(heads, 64, 128)


def dense_up(residual, attended, w_out, w_up, w_down, up_bias, vec, act, slope, unit1, scale1, normed_turned):
    ff = up_bias.shape[0]
    first = residual + dot(attended, w_out) + vec[0:1, :]
    normed, unit, scale = norm_forward(first, vec[1:2, :], vec[2:3, :])
    unit1[...] = unit
    scale1[...] = jnp.broadcast_to(scale, (128, 128))
    low = normed.astype(BF)
    normed_turned[...] = normed.T.astype(BF)
    step = 512
    for j in range(ff // step):
        cols = slice(j * step, (j + 1) * step)
        u = dot(low, w_up[:, cols]) + up_bias[cols].reshape(1, step)
        cdf = 0.5 + 0.5 * lax.erf(u * SQRT_HALF)
        act[:, cols] = (u * cdf).astype(BF)
        slope[:, cols] = (cdf + u * (jnp.exp(-0.5 * u * u) * INV_SQRT_2PI)).astype(slope.dtype)
    second = normed + dot(act[...], w_down) + vec[3:4, :]
    return norm_forward(second, vec[4:5, :], vec[5:6, :])


def dense_down(grad, unit2, scale2, unit1, scale1, w_out, w_up, w_down, vec, slope, gu, g2r, g1r, sums, row, hooks=(None,) * 3):
    ff = w_up.shape[1]
    g2, gain_two, shift_two = norm_backward(grad, vec[4:5, :], unit2, scale2)
    low2 = g2.astype(BF)
    g2r[...] = g2.T.astype(BF)
    if hooks[0]:
        hooks[0]()
    step = 512
    for j in range(ff // step):
        cols = slice(j * step, (j + 1) * step)
        g = dot_t(low2, w_down[cols, :]) * slope[:, cols].astype(F32)
        gu[:, cols] = g.astype(BF)
        total = jnp.sum(g, axis=0, keepdims=True)
        done = 0
        while done < step:
            at = j * step + done
            size = min(step - done, 768 - at % 768)
            sums[row + 6 + at // 768 : row + 7 + at // 768, at % 768 : at % 768 + size] = total[:, done : done + size]
            done += size
    if hooks[1]:
        hooks[1]()
    g1, gain_one, shift_one = norm_backward(g2 + dot_t(gu[...], w_up[...]), vec[1:2, :], unit1, scale1)
    low1 = g1.astype(BF)
    g1r[...] = g1.T.astype(BF)
    if hooks[2]:
        hooks[2]()
    rows = (
        jnp.sum(g1, axis=0, keepdims=True), gain_one, shift_one,
        jnp.sum(g2, axis=0, keepdims=True), gain_two, shift_two,
    )
    for i, value in enumerate(rows):
        sums[row + i : row + i + 1, :] = value
    return g1, dot_t(low1, w_out[...])


def load_all(pairs, sem):
    copies = [pltpu.make_async_copy(a, b, sem.at[i]) for i, (a, b) in enumerate(pairs)]
    for copy in copies:
        copy.start()
    return copies


def forward_stage(c_score, c_exp, c_out, do, par, q_at, kn, v_ref, s_ref, p_ref, st, put, length):
    if do[0]:
        q = q_at(c_score)
    m8 = jnp.full((8, QC), -3e38, F32)
    l8 = jnp.zeros((8, QC), F32)
    out = jnp.zeros((64, QC), F32)
    top = st[1 - par, 0:1, :]
    for t in range(NKT):
        rows = slice(t * KT, (t + 1) * KT)
        if do[0]:
            s = dot(kn[rows, :], q)
            if t == NKT - 1:
                s = jnp.where(key_ok(length), s, -1e30)
            s_ref[par, rows, :] = s
            m8 = jnp.maximum(m8, jnp.max(s.reshape(KT // 8, 8, QC), axis=0))
        if do[1]:
            p = jnp.exp2(s_ref[1 - par, rows, :] * C2 - top)
            l8 = l8 + fold(p)
            p_ref[1 - par, rows, :] = p.astype(BF)
        if do[2]:
            out = out + dot(v_ref[128:192, rows], p_ref[par, rows, :])
    if do[2]:
        put(c_out, out / st[2 + par, 0:1, :], st[4 + par, 0:1, :])
    if do[1]:
        total = jnp.sum(l8, axis=0, keepdims=True)
        st[3 - par] = jnp.broadcast_to(total, (8, QC))
        st[5 - par] = jnp.broadcast_to(top + jnp.log2(total), (8, QC))
    if do[0]:
        st[par] = jnp.broadcast_to(jnp.max(m8, axis=0, keepdims=True) * C2, (8, QC))


def forward_chunks(n, values_here, *rest):
    forward_stage(0, 0, 0, (1, 0, 0), 0, *rest)
    forward_stage(1, 0, 0, (1, 1, 0), 1, *rest)
    values_here()

    def body(i, carry):
        forward_stage(2 * i, 2 * i - 1, 2 * i - 2, (1, 1, 1), 0, *rest)
        forward_stage(2 * i + 1, 2 * i, 2 * i - 1, (1, 1, 1), 1, *rest)
        return carry

    lax.fori_loop(1, n // 2, body, 0)
    forward_stage(0, n - 1, n - 2, (0, 1, 1), 0, *rest)
    forward_stage(0, 0, n - 1, (0, 0, 1), 1, *rest)


def backward_chunk(c, prev, par, at, kn, k2n, vn, kt_ref, length, gf, x_ref, acc, put):
    q, q2, do, lse, lse2, weight = at(c)
    pq, _, pdo, _, _, _ = at(prev)
    both = jnp.concatenate([pq, pdo], axis=0).astype(F32).T
    col = lax.broadcasted_iota(jnp.int32, (QC, 128), 1)
    rhs = jnp.concatenate(
        [jnp.where(col < 64, both, 0.0), jnp.where(col < 64, 0.0, both)], axis=0
    ).astype(BF)
    d8 = jnp.zeros((8, QC), F32)
    dq = jnp.zeros((64, QC), F32)
    for t in range(NKT):
        rows = slice(t * KT, (t + 1) * KT)
        p = jnp.exp2(dot(kn[rows, :], q) * C2 - lse)
        p2 = jnp.exp2(dot(k2n[rows, :], q2) * C2 - lse2)
        if t == NKT - 1:
            ok = key_ok(length)
            p = jnp.where(ok, p, 0.0)
            p2 = jnp.where(ok, p2, 0.0)
        g = dot(vn[rows, :], do) + weight * (p - p2)
        d8 = d8 + fold(p * g)
        gf[rows, :] = g
        x_ref[par, rows, QC:] = p.astype(BF)
        acc[rows, :] += dot(x_ref[1 - par, rows, :], rhs)
        dq = dq + dot(kt_ref[64:128, rows], x_ref[1 - par, rows, :QC])
    put(prev, dq * 0.125)
    delta = jnp.sum(d8, axis=0, keepdims=True)
    for t in range(NKT):
        rows = slice(t * KT, (t + 1) * KT)
        x_ref[par, rows, :QC] = (x_ref[par, rows, QC:].astype(F32) * (gf[rows, :] - delta)).astype(BF)


def backward_last(prev, par, at, kt_ref, x_ref, acc, put, put_keys):
    pq, _, pdo, _, _, _ = at(prev)
    both = jnp.concatenate([pq, pdo], axis=0).astype(F32).T
    col = lax.broadcasted_iota(jnp.int32, (QC, 128), 1)
    rhs = jnp.concatenate(
        [jnp.where(col < 64, both, 0.0), jnp.where(col < 64, 0.0, both)], axis=0
    ).astype(BF)
    dq = jnp.zeros((64, QC), F32)
    row = lax.broadcasted_iota(jnp.int32, (128, KT), 0)
    for t in range(NKT):
        rows = slice(t * KT, (t + 1) * KT)
        dq = dq + dot(kt_ref[64:128, rows], x_ref[par, rows, :QC])
    put(prev, dq * 0.125)
    for t in range(NKT):
        rows = slice(t * KT, (t + 1) * KT)
        total = (acc[rows, :] + dot(x_ref[par, rows, :], rhs)).T
        put_keys(t, jnp.where(row < 64, total * 0.125, total).astype(BF))


def natural_wide(blocks):
    return blocks.astype(F32).T.astype(BF)


def loop(n, body):
    def step(i, carry):
        body(i)
        return carry

    lax.fori_loop(0, n, step, 0)


def greet_start():
    b = lax.axis_index("blk")
    sem = pltpu.get_barrier_semaphore()
    loop(15, lambda i: pl.semaphore_signal(
        sem, inc=1, device_id={"blk": lax.rem(b + 1 + i, 16)}, device_id_type=MESH
    ))


def greet_end():
    pl.semaphore_wait(pltpu.get_barrier_semaphore(), 15)


def forward_kernel(
    len_ref, x_in, source, flags, cot,
    w_qkv_t, w_out_t, w_up_t, w_down_t, w_qkv_s, w_out_s, w_up_s, w_down_s,
    bias_t, upb_t, vec_t, bias_s, upb_s, vec_s,
    *refs,
):
    kept_out, refs = refs[0:26], refs[26:]
    kept, refs = refs[0:26], refs[26:]
    (
        output, buf_t, dist, buf_s, lse_t, lse_d, lse_s,
        x0_turn, normed_turn_t, hidden_turn, normed_turn_s, g1r_s, g2r_s,
        att_t, act_t, att_s, act_s, gu_s,
        slope_t, unit1_t, scale1_t, unit2_t, scale2_t, g1_s, datt_s, sums,
    ) = kept
    (
    v_qkv_t, v_out_t, v_up_t, v_down_t, v_qkv_s, v_out_s, v_up_s, v_down_s,
    x0_ref, src_t, src_s, land_t, land_s, o_t, o_s, kn, s_ref, p_ref, st,
    slope_s, unit1_s, scale1_s,
    w_sem, x_sem, lse_sem, local_sem, keep_sem,
    ) = refs

    def keep(*which):
        for i in which:
            pltpu.make_async_copy(kept[i], kept_out[i], keep_sem.at[i]).start()

    b, hh, owner = place()
    half, head = hh // 6, lax.rem(hh, 6)
    t_sems, tv_sems, d_sems, a_sems, s_sems, sv_sems, b_sems = [
        tuple(x_sem.at[3 * i + j] for j in range(3)) for i in range(7)
    ]
    mine_half = owner & (half == b // 8)
    greet_start()
    weights = load_all(
        [
            (w_qkv_t, v_qkv_t), (w_out_t, v_out_t), (w_up_t, v_up_t), (w_down_t, v_down_t),
            (w_qkv_s, v_qkv_s), (w_out_s, v_out_s), (w_up_s, v_up_s), (w_down_s, v_down_s),
        ],
        w_sem,
    )
    length = len_ref[0]
    replaced = flags[...] == 1
    place_of = lax.broadcasted_iota(jnp.int32, (128, 128), 0)
    turned = jnp.where((place_of == source[...]) & replaced, 1.0, 0.0)
    chooser = turned.T
    taken = dot(chooser.astype(BF), x_in[...])
    x0 = jnp.where(jnp.sum(chooser, axis=1, keepdims=True) > 0.5, taken, x_in[...].astype(F32))
    x0_ref[...] = x0
    low = x0.astype(BF)
    x0_turn[...] = x0.T.astype(BF)
    keep(7)
    weights[0].wait()
    qkv_blocks(low, v_qkv_t, bias_t, src_t, 12)
    greet_end()

    mine = lanes(b * 128, 128)

    def t_copy(h):
        return src_t.at[h, 0:128], buf_t.at[0:128, mine], t_sems, owner_of(h), b

    def tv_copy(h):
        return src_t.at[h, 128:192], buf_t.at[128:192, mine], tv_sems, owner_of(h), b

    def d_copy(h):
        return src_t.at[h, 0:128], dist.at[:, mine], d_sems, owner_of(h + 6), b

    loop(12, lambda j: start_to(*t_copy(lax.rem(j + b, 12))))
    loop(12, lambda j: start_to(*tv_copy(lax.rem(j + b, 12))))

    def a_copy(d):
        return o_t.at[:, lanes(d * 128, 128)], land_t.at[hh], a_sems, d, b

    @pl.when(owner)
    def _():
        arrive(owner, lambda n: buf_t.at[0:128, 0 : n * 128], 16, t_sems)
        kn[...] = natural(buf_t[64:128, :])

        def put(c, o, stat):
            here = lanes(c * QC, QC)
            o_t[:, here] = o.astype(BF)
            lse_t[:, here] = jnp.broadcast_to(stat, (8, QC))
            for i in range(2):
                start_to(*a_copy(2 * c + i))

        forward_chunks(
            SEQ // QC,
            lambda: arrive(owner, lambda n: buf_t.at[128:192, 0 : n * 128], 16, tv_sems),
            lambda c: buf_t[0:64, lanes(c * QC, QC)], kn, buf_t, s_ref, p_ref, st, put, length,
        )

    @pl.when(owner & (hh < 6))
    def _():
        lse_d[:, 0:1024] = lse_t[:, 0:1024]
        copy_to(
            lse_t.at[:, 1024:2048], lse_d.at[:, 1024:2048], lse_sem.at[0], lse_sem.at[1], owner_of(hh + 6)
        ).start()
        pltpu.make_async_copy(buf_t.at[0:128], dist, local_sem.at[0]).start()

    arrive(owner, lambda n: land_t.at[0:n], 12, a_sems)
    loop(6, lambda j: start_to(*d_copy(lax.rem(j + b, 6))))
    att_t[...] = natural_wide(land_t[...].reshape(768, 128))
    keep(1, 4, 13)
    for i in (1, 2, 3):
        weights[i].wait()
    hidden, unit, scale = dense_up(
        x0_ref[...], att_t[...], v_out_t[...], v_up_t, v_down_t[...], upb_t, vec_t,
        act_t, slope_t, unit1_t, scale1_t, normed_turn_t,
    )
    unit2_t[...] = unit
    scale2_t[...] = jnp.broadcast_to(scale, (128, 128))
    x0_ref[...] = hidden
    low = hidden.astype(BF)
    hidden_turn[...] = hidden.T.astype(BF)
    keep(8, 9, 14, 18, 19, 20, 21, 22)
    weights[4].wait()
    qkv_blocks(low, v_qkv_s, bias_s, src_s, 6)

    def s_copy(h):
        return (
            src_s.at[lax.rem(h, 6), 0:128], buf_s.at[0:128, mine], s_sems, owner_of(h), b
        )

    def sv_copy(h):
        return (
            src_s.at[lax.rem(h, 6), 128:192], buf_s.at[128:192, mine],
            sv_sems, owner_of(h), b,
        )

    loop(12, lambda j: start_to(*s_copy(lax.rem(j + b, 12))))
    loop(12, lambda j: start_to(*sv_copy(lax.rem(j + b, 12))))

    def b_copy(j):
        return o_s.at[:, lanes(j * 128, 128)], land_s.at[head], b_sems, 8 * half + j, b

    @pl.when(owner)
    def _():
        lse_s[:, 0:1024] = jnp.full((8, 1024), 1e30, F32)
        arrive(owner, lambda n: buf_s.at[0:128, 0 : n * 128], 16, s_sems)
        kn[...] = natural(buf_s[64:128, :])

        def put(c, o, stat):
            o_s[:, lanes(c * QC, QC)] = o.astype(BF)
            lse_s[:, lanes(half * 1024 + c * QC, QC)] = jnp.broadcast_to(stat, (8, QC))
            for i in range(2):
                start_to(*b_copy(2 * c + i))

        forward_chunks(
            1024 // QC,
            lambda: arrive(owner, lambda n: buf_s.at[128:192, 0 : n * 128], 16, sv_sems),
            lambda c: buf_s[0:64, lanes(half * 1024 + c * QC, QC)],
            kn, buf_s, s_ref, p_ref, st, put, length,
        )

    @pl.when(owner & (hh >= 6))
    def _():
        copy_to(
            lse_s.at[:, 1024:2048], lse_s.at[:, 1024:2048], lse_sem.at[2], lse_sem.at[3], owner_of(hh - 6)
        ).start()

    @pl.when(owner & (hh < 6))
    def _():
        pltpu.make_async_copy(buf_t.at[0:128], dist, local_sem.at[0]).wait()

    @pl.when(owner & (hh >= 6))
    def _():
        arrive(hh >= 6, lambda n: dist.at[:, 0 : n * 128], 16, d_sems)
        got(lse_d.at[:, 1024:2048], lse_sem.at[1])

    keep(2, 5)
    arrive(mine_half, lambda n: land_s.at[0:n], 6, b_sems)
    att_s[...] = natural_wide(land_s[...].reshape(384, 128))
    keep(3, 15)
    for i in (5, 6, 7):
        weights[i].wait()
    result, unit, scale = dense_up(
        x0_ref[...], att_s[...], v_out_s[...], v_up_s, v_down_s[...], upb_s, vec_s,
        act_s, slope_s, unit1_s, scale1_s, normed_turn_s,
    )
    output[...] = result
    keep(0, 10, 16)
    sums[...] = jnp.zeros((24, 768), F32)
    g1, datt = dense_down(
        cot[...].astype(F32), unit, scale, unit1_s[...], scale1_s[:, 0:1],
        v_out_s, v_up_s, v_down_s, vec_s, slope_s, gu_s, g2r_s, g1r_s, sums, 12,
    )
    g1_s[...] = g1
    datt_s[...] = datt.T.astype(BF).reshape(6, 64, 128)
    keep(11, 12, 17, 23, 24, 25)

    @pl.when(owner)
    def _():
        got(o_t.at[:, 0 : 15 * 128], a_sems[0])
        leave(mine_half, lambda n: o_s.at[:, 0 : n * 128], 8, b_sems)

    @pl.when(owner & (hh < 6))
    def _():
        copy_to(
            lse_t.at[:, 1024:2048], lse_d.at[:, 1024:2048], lse_sem.at[0], lse_sem.at[1], owner_of(hh + 6)
        ).wait_send()
        got(lse_s.at[:, 1024:2048], lse_sem.at[3])

    @pl.when(owner & (hh >= 6))
    def _():
        copy_to(
            lse_s.at[:, 1024:2048], lse_s.at[:, 1024:2048], lse_sem.at[2], lse_sem.at[3], owner_of(hh - 6)
        ).wait_send()

    keep(6)
    leave(owner, lambda n: src_t.at[0:n, 0:128], 12, t_sems)
    leave(owner, lambda n: src_t.at[0:n, 128:192], 12, tv_sems)
    leave(owner & (hh >= 6), lambda n: src_t.at[0:n, 0:128], 6, d_sems)
    leave(owner, lambda n: src_t.at[0:n, 0:128], 12, s_sems)
    leave(owner, lambda n: src_t.at[0:n, 128:192], 12, sv_sems)
    for i in range(26):
        pltpu.make_async_copy(kept[i], kept_out[i], keep_sem.at[i]).wait()


def where_am_i():
    dp, blk = lax.axis_index("dp"), lax.axis_index("blk")
    return dp // 2, lax.rem(dp, 2), blk // 4, lax.rem(blk, 4)


def at_axis(axis, v):
    x, c, y, z = where_am_i()
    if axis == "x":
        return {"dp": 2 * v + c, "blk": 4 * y + z}
    if axis == "y":
        return {"dp": 2 * x + c, "blk": 4 * v + z}
    return {"dp": 2 * x + c, "blk": 4 * y + v}


def send_to(src, dst, send_sem, recv_sem, device):
    return pltpu.make_async_remote_copy(
        src_ref=src, dst_ref=dst, send_sem=send_sem, recv_sem=recv_sem,
        device_id=device, device_id_type=MESH,
    )


ORDERS = ("xyz", "yzx", "zxy")
CUTS = (
    (12, 12, ((16, 12),)), (6, 6, ((0, 6),)), (2, 1, ((6, 2),)), (12, 12, ((28, 12),)),
    (5, 4, ((43, 5),)), (3, 3, ((40, 3),)), (9, 9, ((48, 3), (52, 3), (56, 3))), (6, 6, ((8, 3), (12, 3))),
)
TILES = 60
WIDE = TILES * 128
BATCHES = (
    (0, 16, (1, 2, 7), ((0, 8, 8), (8, 4, 3), (12, 4, 3))),
    (16, 32, (0, 3, 5, 4), ((16, 16, 16), (32, 8, 8), (40, 8, 8))),
    (48, 12, (6,), ((48, 4, 3), (52, 4, 3), (56, 4, 3))),
)
PB_TILES = 32
PIECES = ((4, 0, (0, 2, 6)), (2, 4, (0, 1, 3)), (2, 6, (0, 1, 3)))
PIECE_TILES = 8


def piece_place(k, p, tile):
    half, first, starts = PIECES[p]
    at = starts[k] + tile
    return 8 * (at // half), first + at % half
TURN = 3


def drain(ref, sem):
    pltpu.make_async_copy(ref, ref, sem).wait()


def backward_kernel(
    len_ref, flag_ref, source, flags,
    w_qkv_s, w_down_t, w_up_t, w_out_t, w_qkv_t,
    in_buf_s, in_dist, in_lse_s, in_lse_d, in_g1_s, in_buf_t, in_lse_t,
    in_unit2_t, in_scale2_t, in_slope_t, in_unit1_t, in_scale1_t, datt_s,
    vec_t, sums_s,
    x0_turn, normed_turn_t, hidden_turn, normed_turn_s, g1r_s, g2r_s,
    att_t, act_t, att_s, act_s, gu_s,
    grad_in, out, sums,
    v_qkv_s, v_down_t, v_up_t, v_out_t,
    buf_s, dist, lse_s, lse_d, g1_s, buf_t, lse_t, unit2_t, scale2_t, slope_t, unit1_t, scale1_t,
    joined_t, joined_s, gu_t,
    src_t, do_s, do_t, dq_s, dkv_s, dqkv_t, dq_buf, dkv_buf,
    kn, k2n, vn, gf, x_ref, acc,
    nt, cf, cft, pb, rl, l1, a1, l2, a2, l3, a3, a4, sml, sma, smh,
    w_sem, k_sem, x_sem,
    own_n, own_c, n_send, n_recv, c_send, c_recv, st_send, st_recv, f_send, f_recv, m_send, m_recv,
):
    b, hh, owner = place()
    half, head = hh // 6, lax.rem(hh, 6)
    mine_half = owner & (half == b // 8)
    e1, e2, e3, e4, e5, e6 = [tuple(x_sem.at[3 * i + j] for j in range(3)) for i in range(6)]
    x, c, y, z = where_am_i()
    here_at = {"x": x, "y": y, "z": z}
    dp = 2 * x + c
    me = 16 * dp + b
    partner = {"dp": 2 * x + 1 - c, "blk": b}

    barrier = pltpu.get_barrier_semaphore()
    loop(15, lambda i: pl.semaphore_signal(
        barrier, inc=1, device_id={"blk": lax.rem(b + 1 + i, 16)}, device_id_type=MESH
    ))
    pl.semaphore_signal(barrier, inc=1, device_id=partner, device_id_type=MESH)
    for axis in "xyz":
        for j in range(1, 4):
            pl.semaphore_signal(
                barrier, inc=1, device_id=at_axis(axis, lax.rem(here_at[axis] + j, 4)), device_id_type=MESH
            )
    for p in range(3):
        for q in range(4):
            for core in range(2):
                at = dict(zip(ORDERS[p], (me // 32, lax.rem(me // 8, 4), q)))
                pl.semaphore_signal(
                    barrier, inc=1, device_id={"dp": 2 * at["x"] + core, "blk": 4 * at["y"] + at["z"]},
                    device_id_type=MESH,
                )
    kept = load_all(
        [
            (in_buf_s, buf_s), (in_dist, dist), (in_lse_s, lse_s), (in_lse_d, lse_d),
            (in_g1_s, g1_s), (in_buf_t, buf_t), (in_lse_t, lse_t), (in_unit2_t, unit2_t),
            (in_scale2_t, scale2_t), (in_slope_t, slope_t), (in_unit1_t, unit1_t), (in_scale1_t, scale1_t),
        ],
        k_sem,
    )
    weights = load_all(
        [(w_qkv_s, v_qkv_s), (w_down_t, v_down_t), (w_up_t, v_up_t), (w_out_t, v_out_t)], w_sem
    )
    length = len_ref[0]
    for copy in kept[0:4]:
        copy.wait()

    @pl.when(owner)
    def _():
        kn[...] = natural(buf_s[64:128, :])
        vn[...] = natural(buf_s[128:192, :])
        k2n[...] = natural(dist[64:128, :])
        acc[...] = jnp.zeros_like(acc)
        x_ref[1] = jnp.zeros((SEQ, 2 * QC), BF)

    pl.semaphore_wait(barrier, 49)

    def tiles(first, count):
        return slice(first * 128, (first + count) * 128)

    def pool_wide(m, ref):
        _, step, segments = CUTS[m]
        done = 0
        for n, (first, count) in enumerate(segments):
            cols = slice(first * 128, (first + count) * 128)
            pltpu.make_async_copy(
                ref.at[:, lanes((c * step + done) * 128, count * 128)], cf.at[0:128, cols], own_c.at[m + 8 * n]
            ).start()
            send_to(
                ref.at[:, lanes(((1 - c) * step + done) * 128, count * 128)], cf.at[128:256, cols],
                c_send.at[m + 8 * n], c_recv.at[m + 8 * n], partner,
            ).start()
            done += count

    def pool_heads():
        pltpu.make_async_copy(dqkv_t.at[pl.ds(6 * c, 6)], cft.at[:, :, 0:128], own_c.at[6]).start()
        send_to(
            dqkv_t.at[pl.ds(6 * (1 - c), 6)], cft.at[:, :, 128:256], c_send.at[6], c_recv.at[6], partner
        ).start()

    def pool_narrow(m, ref):
        if ref is None:
            ref = nt.at[m, :, 0:128]
        else:
            pltpu.make_async_copy(ref, nt.at[m, :, 0:128], own_n.at[m]).start()
        send_to(ref, nt.at[m, :, 128:256], n_send.at[m], n_recv.at[m], partner).start()

    def products(k, members=None):
        begin = BATCHES[k][0]
        for m in members or BATCHES[k][2]:
            if m not in (3, 5):
                drain(nt.at[m, :, 0:128], own_n.at[m])
            drain(nt.at[m, :, 128:256], n_recv.at[m])
            if m == 6:
                drain(cft.at[:, :, 0:128], own_c.at[6])
                drain(cft.at[:, :, 128:256], c_recv.at[6])
                for n, (first, count) in enumerate(CUTS[m][2]):
                    pb[:, tiles(first - begin, count)] = dot_t(
                        nt[m], cft[2 * n : 2 * n + 2].reshape(384, 256)
                    ).astype(BF)
                continue
            for n, (first, count) in enumerate(CUTS[m][2]):
                cols = slice(first * 128, (first + count) * 128)
                drain(cf.at[0:128, cols], own_c.at[m + 8 * n])
                drain(cf.at[128:256, cols], c_recv.at[m + 8 * n])
                size = 3 if count % 3 == 0 else count

                def piece(i, m=m, first=first, size=size):
                    from_cols = lanes((first + i * size) * 128, size * 128)
                    to_cols = lanes((first - begin + i * size) * 128, size * 128)
                    pb[:, to_cols] = dot(nt[m], cf[:, from_cols]).astype(BF)

                loop(count // size, piece)

    def sem_of(k, p, kind):
        return 18 * k + 6 * p + kind

    def rows_of(height, v):
        return pl.ds(pl.multiple_of(height * v, 16), height)

    def ring(p, stage):
        axis = ORDERS[p][stage]
        u = here_at[axis]
        around = [lax.rem(u + j, 4) for j in range(4)]
        return around, [at_axis(axis, v) for v in around]

    def stage_start(k, stage, only=(0, 1, 2)):
        begin, _, _, parts = BATCHES[k]
        for p in only:
            first, count, used = parts[p]
            around, devices = ring(p, stage)
            if stage == 0:
                first_half = (used + 1) // 2
                one, two = (0, first_half), (first_half, used - first_half)
                for j, (start, size), to, dst, kind in (
                    (2, one, 1, rl, 0), (2, two, 3, rl, 1), (1, two, 1, l1.at[0], 2), (3, one, 3, l1.at[1], 3),
                ):
                    send_to(
                        pb.at[rows_of(192, around[j]), tiles(first - begin + start, size)],
                        dst.at[:, tiles(first + start, size)],
                        st_send.at[sem_of(k, p, 0)], st_recv.at[sem_of(k, p, kind)], devices[to],
                    ).start()
                continue
            for j in range(1, 4):
                if stage == 1:
                    src = a1.at[rows_of(48, around[j]), tiles(first, used)]
                    dst = l2.at[j - 1, :, tiles(first, used)]
                else:
                    src = a2.at[:, lanes(first * 128 + around[j] * count * 32, count * 32)]
                    dst = l3.at[j - 1, :, slice(first * 32, (first + count) * 32)]
                kind = 3 + stage
                send_to(
                    src, dst, st_send.at[sem_of(k, p, kind)], st_recv.at[sem_of(k, p, kind)], devices[j]
                ).start()

    def relay(k):
        begin, _, _, parts = BATCHES[k]
        for p, (first, count, used) in enumerate(parts):
            around, devices = ring(p, 0)
            first_half = (used + 1) // 2
            for start, size, to, slot in ((0, first_half, 1, 0), (first_half, used - first_half, 3, 1)):
                land = rl.at[:, tiles(first + start, size)]
                drain(land, st_recv.at[sem_of(k, p, slot)])
                own_cols = tiles(first - begin + start, size)

                def add(r, own_cols=own_cols, start=start, size=size, to=to, first=first, around=around):
                    own = pl.ds(pl.multiple_of(192 * around[to] + 16 * r, 16), 16)
                    rows = pl.ds(pl.multiple_of(16 * r, 16), 16)
                    total = pb[own, own_cols].astype(F32) + rl[rows, tiles(first + start, size)].astype(F32)
                    pb[own, own_cols] = total.astype(BF)

                loop(12, add)
                send_to(
                    pb.at[rows_of(192, around[to]), own_cols], l1.at[slot, :, tiles(first + start, size)],
                    st_send.at[sem_of(k, p, 1)], st_recv.at[sem_of(k, p, 2 + slot)], devices[to],
                ).start()

    def stage_sent(k, stage):
        for p, (first, count, used) in enumerate(BATCHES[k][3]):
            if stage == 0:
                drain(l1.at[:, :, tiles(first, used)], st_send.at[sem_of(k, p, 0)])
                drain(rl.at[:, tiles(first, used)], st_send.at[sem_of(k, p, 1)])
            elif stage == 1:
                drain(l2.at[:, :, tiles(first, used)], st_send.at[sem_of(k, p, 4)])
            else:
                drain(l3.at[:, :, slice(first * 32, (first + count) * 32)], st_send.at[sem_of(k, p, 5)])

    def stage_sum(k, stage):
        begin, _, _, parts = BATCHES[k]
        for p, (first, count, used) in enumerate(parts):
            at = here_at[ORDERS[p][stage]]
            cols = tiles(first, used)
            if stage == 0:
                for slot in range(2):
                    drain(l1.at[slot, :, cols], st_recv.at[sem_of(k, p, 2 + slot)])
                src, land, dst, height, peers, scols = pb, l1, a1, 192, 2, tiles(first - begin, used)
            elif stage == 1:
                drain(l2.at[:, :, cols], st_recv.at[sem_of(k, p, 4)])
                src, land, dst, height, peers, scols = a1, l2, a2, 48, 3, cols
            else:
                quarter = slice(first * 32, (first + count) * 32)
                drain(l3.at[:, :, quarter], st_recv.at[sem_of(k, p, 5)])
                total = a2[:, lanes(first * 128 + at * count * 32, count * 32)].astype(F32)
                for j in range(3):
                    total = total + l3[j, :, quarter].astype(F32)
                for tile in range(count // 4):
                    row, at_tile = piece_place(k, p, tile)
                    for i in range(8):
                        a3[i, row : row + 6, tiles(at_tile, 1)] = total[6 * i : 6 * i + 6, tiles(tile, 1)]
                continue

            def add(r, src=src, land=land, dst=dst, height=height, peers=peers, at=at, cols=cols, scols=scols):
                rows = pl.ds(pl.multiple_of(16 * r, 16), 16)
                own = pl.ds(pl.multiple_of(height * at + 16 * r, 16), 16)
                total = src[own, scols].astype(F32)
                for j in range(peers):
                    total = total + land[j, rows, cols].astype(F32)
                dst[rows, cols] = total.astype(BF)

            loop(height // 16, add)

    def final_part(p):
        half, first, _ = PIECES[p]
        begin = 32 * here_at[ORDERS[p][0]] + 8 * here_at[ORDERS[p][1]]
        return begin, half, first, here_at[ORDERS[p][2]]

    def final_start():
        a4[...] = a3[...].astype(BF)
        for p in range(3):
            begin, half, first, third = final_part(p)
            for i in range(8):
                to = begin + i
                src = a4.at[i, :, tiles(first, half)]
                dst = out.at[:, lanes(((4 * c + third) * PIECE_TILES + first) * 128, half * 128)]

                @pl.when(to != me)
                def _():
                    send_to(
                        src, dst, f_send.at[p], f_recv.at[0], {"dp": to // 16, "blk": lax.rem(to, 16)}
                    ).start()

                @pl.when(to == me)
                def _():
                    pltpu.make_async_copy(src, dst, f_recv.at[0]).start()

    def final_wait():
        drain(out, f_recv.at[0])
        for p in range(3):
            begin, half, first, _ = final_part(p)
            own = (me >= begin) & (me < begin + 8)
            leave(own, lambda n, first=first, half=half: a4.at[0:n, :, tiles(first, half)], 8, (f_send.at[p],))

    half_lanes = lanes(c * 384, 384)

    def small_copy(slot):
        if slot in (0, 10):
            src = sma.at[0, :, lanes((1 - c) * 384, 384)] if slot == 0 else sums.at[:, half_lanes]
            dst = sml.at[0] if slot == 0 else sums.at[:, half_lanes]
            return send_to(src, dst, m_send.at[slot], m_recv.at[slot], partner)
        n, j = (slot - 1) // 3, (slot - 1) % 3 + 1
        axis = "xyz"[n]
        return send_to(
            smh.at[n], sml.at[slot], m_send.at[slot], m_recv.at[slot],
            at_axis(axis, lax.rem(here_at[axis] + j, 4)),
        )

    def small_step(n):
        if n == 0:
            small_copy(0).start()
            return
        total = sma[0, :, half_lanes] if n == 1 else smh[n - 2]
        for slot in (0,) if n == 1 else range(3 * n - 5, 3 * n - 2):
            small_copy(slot).wait_recv()
            total = total + sml[slot]
        if n == 4:
            sums[:, half_lanes] = total
            small_copy(10).start()
            return
        smh[n - 1] = total
        for slot in range(3 * n - 2, 3 * n + 1):
            small_copy(slot).start()

    def c1(h):
        return (
            datt_s.at[h], do_s.at[:, lanes(lax.rem(b, 8) * 128, 128)],
            e1, owner_of(h + 6 * (b // 8)), b,
        )

    def c2(j):
        return dq_buf.at[:, lanes(j * 128, 128)], dq_s.at[head], e2, 8 * half + j, b

    def c3(d):
        return dkv_buf.at[:, lanes(d * 128, 128)], dkv_s.at[hh], e3, d, b

    def c4(h):
        return src_t.at[h], do_t.at[:, lanes(b * 128, 128)], e4, owner_of(h), b

    def c5(d):
        return dq_buf.at[:, lanes(d * 128, 128)], dqkv_t.at[hh, 0:64], e5, d, b

    def c6(d):
        return dkv_buf.at[:, lanes(d * 128, 128)], dqkv_t.at[hh, 64:192], e6, d, b

    def run_chunks(n, at, kt_ref, put, low, high, put_keys=None):
        rest = (at, kn, k2n, vn, kt_ref, length, gf, x_ref, acc)

        def pair(i):
            backward_chunk(
                2 * i, jnp.maximum(2 * i - 1, 0), 0, *rest, lambda ch, g: put(ch, g, i > 0)
            )
            backward_chunk(2 * i + 1, 2 * i, 1, *rest, lambda ch, g: put(ch, g, True))

        loop(high - low, lambda i: pair(i + low))
        if 2 * high == n:
            backward_last(n - 1, 1, at, kt_ref, x_ref, acc, lambda ch, g: put(ch, g, True), put_keys)

    def keys_out(copy):
        def put_keys(t, block):
            dkv_buf[:, t * KT : (t + 1) * KT] = block
            for i in range(2):
                start_to(*copy(2 * t + i))

        return put_keys

    def send_pair(copy, ch, real):
        if real is True:
            for i in range(2):
                start_to(*copy(2 * ch + i))
        else:
            @pl.when(real)
            def _():
                for i in range(2):
                    start_to(*copy(2 * ch + i))

    def teacher_at(ch):
        here = lanes(ch * QC, QC)
        return (
            buf_t[0:64, here], buf_s[0:64, here], do_t[:, here],
            lse_t[0:1, here], lse_s[0:1, here], weight_row(len_ref, flag_ref, head, ch * QC, hh < 6),
        )

    def teacher_put(ch, g, real):
        dq_buf[:, lanes(ch * QC, QC)] = g.astype(BF)
        send_pair(c5, ch, real)

    loop(6, lambda j: start_to(*c1(lax.rem(j + b, 6))))
    for m, ref in ((1, normed_turn_s), (2, g1r_s), (7, g2r_s)):
        pool_narrow(m, ref)
    for m, ref in ((1, gu_s), (2, att_s), (7, act_s)):
        pool_wide(m, ref)
    for m, ref in ((0, normed_turn_t), (4, hidden_turn), (6, x0_turn)):
        pool_narrow(m, ref)
    for m, ref in ((3, act_t), (5, att_t)):
        pool_wide(m, ref)

    products(0)
    stage_start(0, 0)

    @pl.when(owner)
    def _():
        arrive(mine_half, lambda n: do_s.at[:, 0 : n * 128], 8, e1)

        def at(ch):
            first = half * 1024 + ch * QC
            here = lanes(first, QC)
            return (
                buf_s[0:64, here], dist[0:64, here], do_s[:, lanes(ch * QC, QC)],
                lse_s[0:1, here], lse_d[0:1, here], weight_row(len_ref, flag_ref, head, first, True),
            )

        def put(ch, g, real):
            dq_buf[:, lanes(ch * QC, QC)] = g.astype(BF)
            send_pair(c2, ch, real)

        run_chunks(1024 // QC, at, buf_s, put, 0, 2, keys_out(c3))

    relay(0)
    arrive(mine_half, lambda n: dq_s.at[0:n], 6, e2)
    arrive(owner, lambda n: dkv_s.at[0:n], 12, e3)
    joined_s[:, 0:384] = natural_wide(dq_s[...].reshape(384, 128))
    for part in range(2):
        rows = slice(64 * part, 64 * part + 64)
        both = dkv_s[0:6, rows, :].astype(F32) + dkv_s[6:12, rows, :].astype(F32)
        joined_s[:, 384 * (part + 1) : 384 * (part + 2)] = both.reshape(384, 128).T.astype(BF)
    pool_wide(4, joined_s)
    sma[0] = sums_s[...]
    low_sums = jnp.sum(joined_s[...].astype(F32), axis=0, keepdims=True)
    sma[0, 20:21, 0:384] = low_sums[:, 0:384]
    sma[0, 20:21, 384:768] = low_sums[:, 768:1152]
    for copy in kept[4:]:
        copy.wait()
    weights[0].wait()
    grad_hidden = g1_s[...] + dot_t(joined_s[...], v_qkv_s[...])
    for i in (1, 2, 3):
        weights[i].wait()
    g1, datt = dense_down(
        grad_hidden, unit2_t[...], scale2_t[:, 0:1], unit1_t[...], scale1_t[:, 0:1],
        v_out_t, v_up_t, v_down_t, vec_t, slope_t, gu_t, nt.at[3, :, 0:128], nt.at[5, :, 0:128], sma.at[0], 0,
        (lambda: pool_narrow(3, None), lambda: pool_wide(0, gu_t), lambda: pool_narrow(5, None)),
    )
    grad_in[...] = g1
    src_t[...] = datt.T.astype(BF).reshape(12, 64, 128)
    loop(12, lambda j: start_to(*c4(lax.rem(j + b, 12))))
    late = load_all(
        [(w_qkv_t.at[:, 768 * p : 768 * (p + 1)], v_down_t.at[768 * p : 768 * (p + 1), :]) for p in range(3)],
        w_sem.at[pl.ds(4, 3)],
    )
    stage_sum(0, 0)
    stage_sent(0, 0)
    products(1, (0, 3))
    stage_start(1, 0, (0, 1))
    products(1, (5, 4))
    stage_start(1, 0, (2,))

    @pl.when(owner)
    def _():
        kn[...] = natural(buf_t[64:128, :])
        vn[...] = natural(buf_t[128:192, :])
        k2n[...] = natural(buf_s[64:128, :])
        acc[...] = jnp.zeros_like(acc)
        x_ref[1] = jnp.zeros((SEQ, 2 * QC), BF)

    @pl.when(owner)
    def _():
        leave(mine_half, lambda n: dq_buf.at[:, 0 : n * 128], 8, e2)
        got(dkv_buf.at[:, 0 : 15 * 128], e3[0])
        arrive(owner, lambda n: do_t.at[:, 0 : n * 128], 16, e4)

        run_chunks(SEQ // QC, teacher_at, buf_t, teacher_put, 0, TURN)

    relay(1)
    stage_start(0, 1)

    @pl.when(owner)
    def _():
        run_chunks(SEQ // QC, teacher_at, buf_t, teacher_put, TURN, SEQ // QC // 2, keys_out(c6))

    stage_sum(0, 1)
    stage_start(0, 2)
    stage_sum(1, 0)
    stage_start(1, 1)
    arrive(owner, lambda n: dqkv_t.at[0:n, 0:64], 12, e5)
    arrive(owner, lambda n: dqkv_t.at[0:n, 64:192], 12, e6)
    pool_heads()
    stage_sent(1, 0)
    for part in range(3):
        joined_t[:, 768 * part : 768 * (part + 1)] = natural_wide(
            dqkv_t[:, 64 * part : 64 * (part + 1), :].reshape(768, 128)
        )
    for row, part in ((10, 0), (11, 2)):
        sma[0, row : row + 1, :] = jnp.sum(
            joined_t[:, 768 * part : 768 * (part + 1)].astype(F32), axis=0, keepdims=True
        )
    small_step(0)
    products(2)
    stage_start(2, 0)
    small_step(1)
    stage_sum(1, 1)
    stage_start(1, 2)
    for copy in late:
        copy.wait()
    grad = grad_in[...]
    for p in range(3):
        grad = grad + dot_t(joined_t[:, 768 * p : 768 * (p + 1)], v_down_t[768 * p : 768 * (p + 1), :])
    place_of = lax.broadcasted_iota(jnp.int32, (128, 128), 0)
    turned = jnp.where((place_of == source[...]) & (flags[...] == 1), 1.0, 0.0)
    back = turned.astype(BF)
    one = grad.astype(BF)
    rest = grad - one.astype(F32)
    two = rest.astype(BF)
    three = (rest - two.astype(F32)).astype(BF)
    copied = dot(back, one) + dot(back, two) + dot(back, three)
    kept = jnp.sum(turned.T, axis=1, keepdims=True) < 0.5
    grad_in[...] = jnp.where(kept, grad, 0.0) + copied
    relay(2)
    small_step(2)
    stage_sum(2, 0)
    stage_start(2, 1)
    small_step(3)
    stage_sum(0, 2)
    stage_sum(1, 2)
    stage_sum(2, 1)
    stage_start(2, 2)
    small_step(4)
    stage_sum(2, 2)
    final_start()

    @pl.when(owner)
    def _():
        got(dq_buf.at[:, 0 : 15 * 128], e5[0])
        got(dkv_buf.at[:, 0 : 15 * 128], e6[0])

    leave(mine_half, lambda n: dq_s.at[0:n], 6, e1)
    leave(owner, lambda n: src_t.at[0:n], 12, e4)
    for m, (_, _, segments) in enumerate(CUTS):
        if m == 6:
            drain(cft.at[:, :, 128:256], c_send.at[6])
            segments = ()
        for n, (first, count) in enumerate(segments):
            drain(cf.at[128:256, slice(first * 128, (first + count) * 128)], c_send.at[m + 8 * n])
        drain(nt.at[m, :, 128:256], n_send.at[m])
    for slot in range(11):
        small_copy(slot).wait_send()
    small_copy(10).wait_recv()
    for k, stage in ((0, 1), (0, 2), (1, 1), (1, 2), (2, 0), (2, 1), (2, 2)):
        stage_sent(k, stage)
    final_wait()


ANY = pl.BlockSpec(memory_space=pl.ANY)


def mega_call(kernel, ident, specs, outs, scratch, args, name, out_spec):
    return pl.pallas_call(
        kernel,
        name=name,
        out_shape=tuple(jax.ShapeDtypeStruct(s, t) for s, t in outs),
        in_specs=specs,
        out_specs=tuple(out_spec for _ in outs),
        scratch_shapes=scratch,
        compiler_params=pltpu.CompilerParams(
            collective_id=ident, has_side_effects=True, vmem_limit_bytes=62 * MIB
        ),
    )(*args)


def vb(*shape):
    return pltpu.VMEM(shape, BF)


def vf(*shape):
    return pltpu.VMEM(shape, F32)


def run_forward(lengths, x_in, source, flags, cot, weights, smalls):
    outs = [
        ((128, 768), F32), ((192, SEQ), BF), ((128, SEQ), BF), ((192, SEQ), BF),
        ((8, SEQ), F32), ((8, SEQ), F32), ((8, SEQ), F32),
        *[((768, 128), BF)] * 6,
        ((128, 768), BF), ((128, 3072), BF), ((128, 384), BF), ((128, 1536), BF), ((128, 1536), BF),
        ((128, 3072), BF), ((128, 768), F32), ((128, 128), F32), ((128, 768), F32), ((128, 128), F32),
        ((128, 768), F32), ((6, 64, 128), BF), ((24, 768), F32),
    ]
    scratch = [pltpu.VMEM(shape, kind) for shape, kind in outs] + [
        vb(768, 2304), vb(768, 768), vb(768, 3072), vb(3072, 768),
        vb(768, 1152), vb(384, 768), vb(768, 1536), vb(1536, 768),
        vf(128, 768), vb(12, 192, 128), vb(6, 192, 128), vb(12, 64, 128), vb(6, 64, 128),
        vb(64, SEQ), vb(64, 1024), vb(SEQ, 64), vf(2, SEQ, QC), vb(2, SEQ, QC), vf(6, 8, QC),
        vb(128, 1536), vf(128, 768), vf(128, 128),
        DMA((8,)), DMA((21,)), DMA((4,)), DMA((1,)), DMA((26,)),
    ]
    specs = [SMEM] + [VMEM] * 4 + [ANY] * 8 + [VMEM] * 6
    return mega_call(
        forward_kernel, 1, specs, outs, scratch, (lengths, x_in, source, flags, cot, *weights, *smalls), "forward", ANY
    )


def run_backward(lengths, head_flags, source, flags, weights, kept, held, pooled):
    outs = [((128, 768), F32), ((16, 8 * PIECE_TILES * 128), BF), ((24, 768), F32)]
    scratch = [
        vb(768, 1152), vb(3072, 768), vb(768, 3072), vb(768, 768),
        vb(192, SEQ), vb(128, SEQ), vf(8, SEQ), vf(8, SEQ), vf(128, 768), vb(192, SEQ), vf(8, SEQ),
        vf(128, 768), vf(128, 128), vb(128, 3072), vf(128, 768), vf(128, 128),
        vb(128, 2304), vb(128, 1152), vb(128, 3072),
        vb(12, 64, 128), vb(64, 1024), vb(64, SEQ), vb(6, 64, 128), vb(12, 128, 128), vb(12, 192, 128),
        vb(64, SEQ), vb(128, SEQ),
        vb(SEQ, 64), vb(SEQ, 64), vb(SEQ, 64), vf(SEQ, QC), vb(2, SEQ, 2 * QC), vf(SEQ, 128),
        vb(8, 768, 256), vb(256, 48 * 128), vb(6, 192, 256), vb(768, PB_TILES * 128),
        vb(192, WIDE), vb(2, 192, WIDE), vb(192, WIDE), vb(3, 48, WIDE), vb(48, WIDE), vb(3, 48, WIDE // 4), vf(8, 16, PIECE_TILES * 128), vb(8, 16, PIECE_TILES * 128),
        vf(10, 24, 384), vf(1, 24, 768), vf(3, 24, 384),
        DMA((7,)), DMA((12,)), DMA((18,)),
        DMA((8,)), DMA((24,)), DMA((8,)), DMA((8,)), DMA((24,)), DMA((24,)),
        DMA((54,)), DMA((54,)), DMA((3,)), DMA((1,)), DMA((11,)), DMA((11,)),
    ]
    specs = [SMEM] * 2 + [VMEM] * 2 + [ANY] * (5 + len(kept)) + [VMEM] * len(held) + [ANY] * len(pooled)
    return mega_call(
        backward_kernel, 2, specs, outs, scratch,
        (lengths, head_flags, source, flags, *weights, *kept, *held, *pooled), "backward", VMEM,
    )


def unpack_kernel(whole, sums, *outs):
    def tile_at(core, tile):
        for k, (_, _, _, parts) in enumerate(BATCHES):
            for p, (first, count, _) in enumerate(parts):
                if first <= tile < first + count:
                    third, rest = (tile - first) // (count // 4), (tile - first) % (count // 4)
                    row, at = piece_place(k, p, rest)
                    start = ((4 * core + third) * PIECE_TILES + at) * 128
                    return wide[row : row + 8, start : start + 128]

    wide = whole[...].astype(F32)

    def columns(m):
        count, step, segments = CUTS[m]
        if m == 6:
            tiles_of = [[tile_at(core, first + i) for first, size in segments for i in range(size)] for core in range(2)]
            pieces = []
            for part in range(3):
                for head in range(12):
                    lane = 192 * (head % 6) + 64 * part
                    pieces.append(tiles_of[head // 6][lane // 128][:, lane % 128 : lane % 128 + 64])
            return jnp.concatenate(pieces, axis=1)
        spots = [first + i for first, size in segments for i in range(size)]
        pieces = [tile_at(0, tile) for tile in spots] + [tile_at(1, tile) for tile in spots[count - step :]]
        return jnp.concatenate(pieces, axis=1)

    for m, o in ((6, 0), (5, 2), (0, 3), (3, 4), (4, 7), (2, 9), (1, 10), (7, 11)):
        outs[o][...] = columns(m)[0:6]
    i = 16 * lax.axis_index("dp") + lax.axis_index("blk")

    def turn(rows, by):
        return pltpu.roll(rows, lax.rem(768 - by, 768), 1)

    def pick(first, count, per):
        row = first + (i * per) // 768
        wide = jnp.broadcast_to(sums[pl.ds(row, 1), :], (8, 768))
        return turn(wide, lax.rem(i * per, 768))[0:1, 0:per]

    outs[1][...] = pick(10, 2, 12)
    outs[5][...] = pick(6, 4, 24)
    outs[8][...] = pick(20, 1, 6)
    outs[12][...] = pick(18, 2, 12)
    outs[6][...] = turn(sums[0:8, :], i * 6)[0:6, 0:6]
    outs[13][...] = turn(sums[8:24, :], i * 6)[4:10, 0:6]


def unpack(whole, sums):
    shapes = (
        (6, 2304), (1, 12), (6, 768), (6, 3072), (6, 3072), (1, 24), (6, 6),
        (6, 1152), (1, 6), (6, 384), (6, 1536), (6, 1536), (1, 12), (6, 6),
    )
    outs = list(
        pl.pallas_call(
            unpack_kernel,
            name="unpack",
            out_shape=tuple(jax.ShapeDtypeStruct(s, F32) for s in shapes),
            in_specs=[VMEM] * 2,
            out_specs=tuple(VMEM for _ in shapes),
            compiler_params=pltpu.CompilerParams(vmem_limit_bytes=62 * MIB),
        )(whole, sums)
    )
    for i in (1, 5, 8, 12):
        outs[i] = outs[i].reshape(-1)
    for i in (2, 4, 9, 11):
        outs[i] = outs[i].T
    return tuple(outs)


def per_device(
    inputs, aug_source, aug_flags, lengths, head_flags, cotangent,
    qkv_teacher, qv_bias_teacher, out_teacher, up_teacher, down_teacher, up_bias_teacher, vectors_teacher,
    qkv_student, qv_bias_student, out_student, up_student, down_student, up_bias_student, vectors_student,
):
    (
        output, buf_t, dist, buf_s, lse_t, lse_d, lse_s,
        x0_turn, normed_turn_t, hidden_turn, normed_turn_s, g1r_s, g2r_s,
        att_t, act_t, att_s, act_s, gu_s,
        slope_t, unit1_t, scale1_t, unit2_t, scale2_t, g1_s, datt_s, sums_s,
    ) = run_forward(
        lengths, inputs[0], aug_source, aug_flags, cotangent[0],
        (qkv_teacher, out_teacher, up_teacher, down_teacher, qkv_student, out_student, up_student, down_student),
        (
            qv_bias_teacher, up_bias_teacher, vectors_teacher,
            qv_bias_student, up_bias_student, vectors_student,
        ),
    )
    grad_in, whole, total = run_backward(
        lengths, head_flags, aug_source, aug_flags,
        (qkv_student, down_teacher, up_teacher, out_teacher, qkv_teacher),
        (
            buf_s, dist, lse_s, lse_d, g1_s, buf_t, lse_t,
            unit2_t, scale2_t, slope_t, unit1_t, scale1_t, datt_s,
        ),
        (vectors_teacher, sums_s),
        (
            x0_turn, normed_turn_t, hidden_turn, normed_turn_s, g1r_s, g2r_s,
            att_t, act_t, att_s, act_s, gu_s,
        ),
    )
    return (output[None], grad_in[None]) + unpack(whole, total)


def solution(mesh):
    both = ("dp", "blk")
    row, flat, col = P(both, None), P(both), P(None, both)
    tokens, marks = P("dp", "blk", None), P("dp", "blk")
    return jax.shard_map(
        per_device,
        mesh=mesh,
        in_specs=(tokens, marks, marks, P("dp"), P(), tokens) + (P(),) * 14,
        out_specs=(tokens, tokens) + (row, flat, col, row, col, flat, col) * 2,
        check_vma=False,
    )
```

```python
import jax
import jax.numpy as jnp
from jax import lax
from jax.experimental import pallas as pl
from jax.experimental.pallas import tpu as pltpu
from jax.sharding import PartitionSpec as P

MESH = pl.DeviceIdType.MESH
LOG2E = 1.4426950408889634
C2 = 0.125 * LOG2E
SEQ = 2048
QC = 256
KT = 256
NKT = SEQ // KT
MIB = 1 << 20


def dot(a, b):
    return jnp.dot(a, b, preferred_element_type=jnp.float32)


def place():
    b = lax.axis_index("blk")
    r = lax.rem(lax.rem(b, 4) - b // 4 + 7, 4)
    return b, 3 * (b // 4) + r, r < 3


def owner_of(hh):
    y = hh // 3
    return 4 * y + lax.rem(y + lax.rem(hh, 3) + 1, 4)


def copy_to(src, dst, send_sem, recv_sem, d):
    return pltpu.make_async_remote_copy(
        src_ref=src,
        dst_ref=dst,
        send_sem=send_sem,
        recv_sem=recv_sem,
        device_id={"blk": d},
        device_id_type=MESH,
    )


def start_to(src, dst, sems, d, b):
    send_sem, recv_sem, own_sem = sems

    @pl.when(d != b)
    def _():
        copy_to(src, dst, send_sem, recv_sem, d).start()

    @pl.when(d == b)
    def _():
        pltpu.make_async_copy(src, dst, own_sem).start()


def arrive(own, blocks, count, sems):
    @pl.when(own)
    def _():
        got(blocks(count - 1), sems[1])
        got(blocks(1), sems[2])

    @pl.when(jnp.logical_not(own))
    def _():
        got(blocks(count), sems[1])


def leave(own, blocks, count, sems):
    @pl.when(own)
    def _():
        got(blocks(count - 1), sems[0])

    @pl.when(jnp.logical_not(own))
    def _():
        got(blocks(count), sems[0])


def got(dst, recv_sem):
    pltpu.make_async_copy(dst, dst, recv_sem).wait()


def lanes(start, size):
    return pl.ds(pl.multiple_of(start, 128), size)


def fold(v):
    return jnp.sum(v.reshape(v.shape[0] // 8, 8, v.shape[1]), axis=0)


def key_ok(length):
    rows = lax.broadcasted_iota(jnp.int32, (KT, QC), 0) + (SEQ - KT)
    return rows < length


def natural(x):
    return x.astype(jnp.float32).T.astype(jnp.bfloat16)


def weight_row(len_ref, flag_ref, head, first, use):
    q = lax.broadcasted_iota(jnp.int32, (1, QC), 1) + first
    factor = jnp.where(use, flag_ref[head].astype(jnp.float32) * (2.0 * SEQ), 0.0)
    return jnp.where(q < len_ref[0], factor, 0.0)


SMEM = pl.BlockSpec(memory_space=pltpu.SMEM)
VMEM = pl.BlockSpec(memory_space=pltpu.VMEM)
DMA = pltpu.SemaphoreType.DMA
BF = jnp.bfloat16
F32 = jnp.float32


SQRT_HALF = 0.7071067811865476
INV_SQRT_2PI = 0.3989422804014327


def dot_t(a, b):
    return lax.dot_general(a, b, (((1,), (1,)), ((), ())), preferred_element_type=F32)


def norm_forward(v, gain, shift):
    center = v - jnp.mean(v, axis=-1, keepdims=True)
    scale = lax.rsqrt(jnp.mean(center * center, axis=-1, keepdims=True) + 1e-06)
    unit = center * scale
    return unit * gain + shift, unit, scale


def norm_backward(grad, gain, unit, scale):
    scaled = grad * gain
    mean_one = jnp.mean(scaled, axis=-1, keepdims=True)
    mean_two = jnp.mean(scaled * unit, axis=-1, keepdims=True)
    return (
        (scaled - mean_one - unit * mean_two) * scale,
        jnp.sum(grad * unit, axis=0, keepdims=True),
        jnp.sum(grad, axis=0, keepdims=True),
    )


def qkv_blocks(low, w, bias, src, heads, parts):
    span = heads * 64
    for part in parts:
        joint = dot(low, w[:, part * span : (part + 1) * span])
        if part != 1:
            first = 0 if part == 0 else span
            joint = joint + bias[first : first + span].reshape(1, span)
        src[:, part * 64 : (part + 1) * 64, :] = joint.T.astype(BF).reshape(heads, 64, 128)


def dense_up(residual, attended, w_out, w_up, w_down, up_bias, vec, act, slope, unit1, scale1, normed_turned):
    ff = up_bias.shape[0]
    first = residual + dot(attended, w_out) + vec[0:1, :]
    normed, unit, scale = norm_forward(first, vec[1:2, :], vec[2:3, :])
    unit1[...] = unit
    scale1[...] = jnp.broadcast_to(scale, (128, 128))
    low = normed.astype(BF)
    normed_turned[...] = normed.T.astype(BF)
    step = 512
    for j in range(ff // step):
        cols = slice(j * step, (j + 1) * step)
        u = dot(low, w_up[:, cols]) + up_bias[cols].reshape(1, step)
        cdf = 0.5 + 0.5 * lax.erf(u * SQRT_HALF)
        act[:, cols] = (u * cdf).astype(BF)
        slope[:, cols] = (cdf + u * (jnp.exp(-0.5 * u * u) * INV_SQRT_2PI)).astype(slope.dtype)
    second = normed + dot(act[...], w_down) + vec[3:4, :]
    return norm_forward(second, vec[4:5, :], vec[5:6, :])


def dense_down(grad, unit2, scale2, unit1, scale1, w_out, w_up, w_down, vec, slope, gu, g2r, g1r, sums, row, hooks=(None,) * 3):
    ff = w_up.shape[1]
    g2, gain_two, shift_two = norm_backward(grad, vec[4:5, :], unit2, scale2)
    low2 = g2.astype(BF)
    g2r[...] = g2.T.astype(BF)
    if hooks[0]:
        hooks[0]()
    step = 512
    for j in range(ff // step):
        cols = slice(j * step, (j + 1) * step)
        g = dot_t(low2, w_down[cols, :]) * slope[:, cols].astype(F32)
        gu[:, cols] = g.astype(BF)
        total = jnp.sum(g, axis=0, keepdims=True)
        done = 0
        while done < step:
            at = j * step + done
            size = min(step - done, 768 - at % 768)
            sums[row + 6 + at // 768 : row + 7 + at // 768, at % 768 : at % 768 + size] = total[:, done : done + size]
            done += size
    if hooks[1]:
        hooks[1]()
    g1, gain_one, shift_one = norm_backward(g2 + dot_t(gu[...], w_up[...]), vec[1:2, :], unit1, scale1)
    low1 = g1.astype(BF)
    g1r[...] = g1.T.astype(BF)
    if hooks[2]:
        hooks[2]()
    rows = (
        jnp.sum(g1, axis=0, keepdims=True), gain_one, shift_one,
        jnp.sum(g2, axis=0, keepdims=True), gain_two, shift_two,
    )
    for i, value in enumerate(rows):
        sums[row + i : row + i + 1, :] = value
    return g1, dot_t(low1, w_out[...])


def load_all(pairs, sem):
    copies = [pltpu.make_async_copy(a, b, sem.at[i]) for i, (a, b) in enumerate(pairs)]
    for copy in copies:
        copy.start()
    return copies


def forward_stage(c_score, c_exp, c_out, do, par, q_at, kn, v_ref, s_ref, p_ref, st, put, length):
    if do[0]:
        q = q_at(c_score)
    m8 = jnp.full((8, QC), -3e38, F32)
    l8 = jnp.zeros((8, QC), F32)
    out = jnp.zeros((64, QC), F32)
    top = st[1 - par, 0:1, :]
    for t in range(NKT):
        rows = slice(t * KT, (t + 1) * KT)
        if do[0]:
            s = dot(kn[rows, :], q)
            if t == NKT - 1:
                s = jnp.where(key_ok(length), s, -1e30)
            s_ref[par, rows, :] = s
            m8 = jnp.maximum(m8, jnp.max(s.reshape(KT // 8, 8, QC), axis=0))
        if do[1]:
            p = jnp.exp2(s_ref[1 - par, rows, :] * C2 - top)
            l8 = l8 + fold(p)
            p_ref[1 - par, rows, :] = p.astype(BF)
        if do[2]:
            out = out + dot(v_ref[128:192, rows], p_ref[par, rows, :])
    if do[2]:
        put(c_out, out / st[2 + par, 0:1, :], st[4 + par, 0:1, :])
    if do[1]:
        total = jnp.sum(l8, axis=0, keepdims=True)
        st[3 - par] = jnp.broadcast_to(total, (8, QC))
        st[5 - par] = jnp.broadcast_to(top + jnp.log2(total), (8, QC))
    if do[0]:
        st[par] = jnp.broadcast_to(jnp.max(m8, axis=0, keepdims=True) * C2, (8, QC))


def forward_chunks(n, values_here, *rest):
    forward_stage(0, 0, 0, (1, 0, 0), 0, *rest)
    forward_stage(1, 0, 0, (1, 1, 0), 1, *rest)
    values_here()

    def body(i, carry):
        forward_stage(2 * i, 2 * i - 1, 2 * i - 2, (1, 1, 1), 0, *rest)
        forward_stage(2 * i + 1, 2 * i, 2 * i - 1, (1, 1, 1), 1, *rest)
        return carry

    lax.fori_loop(1, n // 2, body, 0)
    forward_stage(0, n - 1, n - 2, (0, 1, 1), 0, *rest)
    forward_stage(0, 0, n - 1, (0, 0, 1), 1, *rest)


def backward_chunk(c, prev, par, at, kn, k2n, vn, kt_ref, length, gf, x_ref, acc, put):
    q, q2, do, lse, lse2, weight = at(c)
    pq, _, pdo, _, _, _ = at(prev)
    both = jnp.concatenate([pq, pdo], axis=0).astype(F32).T
    col = lax.broadcasted_iota(jnp.int32, (QC, 128), 1)
    rhs = jnp.concatenate(
        [jnp.where(col < 64, both, 0.0), jnp.where(col < 64, 0.0, both)], axis=0
    ).astype(BF)
    d8 = jnp.zeros((8, QC), F32)
    dq = jnp.zeros((64, QC), F32)
    for t in range(NKT):
        rows = slice(t * KT, (t + 1) * KT)
        p = jnp.exp2(dot(kn[rows, :], q) * C2 - lse)
        p2 = jnp.exp2(dot(k2n[rows, :], q2) * C2 - lse2)
        if t == NKT - 1:
            ok = key_ok(length)
            p = jnp.where(ok, p, 0.0)
            p2 = jnp.where(ok, p2, 0.0)
        g = dot(vn[rows, :], do) + weight * (p - p2)
        d8 = d8 + fold(p * g)
        gf[rows, :] = g
        x_ref[par, rows, QC:] = p.astype(BF)
        acc[rows, :] += dot(x_ref[1 - par, rows, :], rhs)
        dq = dq + dot(kt_ref[64:128, rows], x_ref[1 - par, rows, :QC])
    put(prev, dq * 0.125)
    delta = jnp.sum(d8, axis=0, keepdims=True)
    for t in range(NKT):
        rows = slice(t * KT, (t + 1) * KT)
        x_ref[par, rows, :QC] = (x_ref[par, rows, QC:].astype(F32) * (gf[rows, :] - delta)).astype(BF)


def backward_last(prev, par, at, kt_ref, x_ref, acc, put, put_keys):
    pq, _, pdo, _, _, _ = at(prev)
    both = jnp.concatenate([pq, pdo], axis=0).astype(F32).T
    col = lax.broadcasted_iota(jnp.int32, (QC, 128), 1)
    rhs = jnp.concatenate(
        [jnp.where(col < 64, both, 0.0), jnp.where(col < 64, 0.0, both)], axis=0
    ).astype(BF)
    dq = jnp.zeros((64, QC), F32)
    row = lax.broadcasted_iota(jnp.int32, (128, KT), 0)
    for t in range(NKT):
        rows = slice(t * KT, (t + 1) * KT)
        dq = dq + dot(kt_ref[64:128, rows], x_ref[par, rows, :QC])
    put(prev, dq * 0.125)
    for t in range(NKT):
        rows = slice(t * KT, (t + 1) * KT)
        total = (acc[rows, :] + dot(x_ref[par, rows, :], rhs)).T
        put_keys(t, jnp.where(row < 64, total * 0.125, total).astype(BF))


def natural_wide(blocks):
    return blocks.astype(F32).T.astype(BF)


def loop(n, body):
    def step(i, carry):
        body(i)
        return carry

    lax.fori_loop(0, n, step, 0)


def greet_start():
    b = lax.axis_index("blk")
    sem = pltpu.get_barrier_semaphore()
    loop(15, lambda i: pl.semaphore_signal(
        sem, inc=1, device_id={"blk": lax.rem(b + 1 + i, 16)}, device_id_type=MESH
    ))


def greet_end():
    pl.semaphore_wait(pltpu.get_barrier_semaphore(), 15)


def forward_kernel(
    len_ref, x_in, source, flags, cot,
    w_qkv_t, w_out_t, w_up_t, w_down_t, w_qkv_s, w_out_s, w_up_s, w_down_s,
    bias_t, upb_t, vec_t, bias_s, upb_s, vec_s,
    *refs,
):
    kept_out, refs = refs[0:26], refs[26:]
    kept, refs = refs[0:26], refs[26:]
    (
        output, buf_t, dist, buf_s, lse_t, lse_d, lse_s,
        x0_turn, normed_turn_t, hidden_turn, normed_turn_s, g1r_s, g2r_s,
        att_t, act_t, att_s, act_s, gu_s,
        slope_t, unit1_t, scale1_t, unit2_t, scale2_t, g1_s, datt_s, sums,
    ) = kept
    (
    v_qkv_t, v_out_t, v_up_t, v_down_t, v_qkv_s, v_out_s, v_up_s, v_down_s,
    x0_ref, src_t, src_s, land_t, land_s, o_t, o_s, kn, s_ref, p_ref, st,
    slope_s, unit1_s, scale1_s,
    w_sem, x_sem, lse_sem, local_sem, keep_sem,
    ) = refs

    def keep(*which):
        for i in which:
            pltpu.make_async_copy(kept[i], kept_out[i], keep_sem.at[i]).start()

    b, hh, owner = place()
    half, head = hh // 6, lax.rem(hh, 6)
    t_sems, tv_sems, d_sems, a_sems, s_sems, sv_sems, b_sems = [
        tuple(x_sem.at[3 * i + j] for j in range(3)) for i in range(7)
    ]
    mine_half = owner & (half == b // 8)
    greet_start()
    weights = load_all(
        [
            (w_qkv_t, v_qkv_t), (w_out_t, v_out_t), (w_up_t, v_up_t), (w_down_t, v_down_t),
            (w_qkv_s, v_qkv_s), (w_out_s, v_out_s), (w_up_s, v_up_s), (w_down_s, v_down_s),
        ],
        w_sem,
    )
    length = len_ref[0]
    replaced = flags[...] == 1
    place_of = lax.broadcasted_iota(jnp.int32, (128, 128), 0)
    turned = jnp.where((place_of == source[...]) & replaced, 1.0, 0.0)
    chooser = turned.T
    taken = dot(chooser.astype(BF), x_in[...])
    x0 = jnp.where(jnp.sum(chooser, axis=1, keepdims=True) > 0.5, taken, x_in[...].astype(F32))
    x0_ref[...] = x0
    low = x0.astype(BF)
    x0_turn[...] = x0.T.astype(BF)
    keep(7)
    weights[0].wait()
    qkv_blocks(low, v_qkv_t, bias_t, src_t, 12, (0, 1))
    greet_end()

    mine = lanes(b * 128, 128)

    def t_copy(h):
        return src_t.at[h, 0:128], buf_t.at[0:128, mine], t_sems, owner_of(h), b

    def tv_copy(h):
        return src_t.at[h, 128:192], buf_t.at[128:192, mine], tv_sems, owner_of(h), b

    def d_copy(h):
        return src_t.at[h, 0:128], dist.at[:, mine], d_sems, owner_of(h + 6), b

    loop(12, lambda j: start_to(*t_copy(lax.rem(j + b, 12))))
    qkv_blocks(low, v_qkv_t, bias_t, src_t, 12, (2,))
    loop(12, lambda j: start_to(*tv_copy(lax.rem(j + b, 12))))

    def a_copy(d):
        return o_t.at[:, lanes(d * 128, 128)], land_t.at[hh], a_sems, d, b

    @pl.when(owner)
    def _():
        arrive(owner, lambda n: buf_t.at[0:128, 0 : n * 128], 16, t_sems)
        kn[...] = natural(buf_t[64:128, :])

        def put(c, o, stat):
            here = lanes(c * QC, QC)
            o_t[:, here] = o.astype(BF)
            lse_t[:, here] = jnp.broadcast_to(stat, (8, QC))
            for i in range(2):
                start_to(*a_copy(2 * c + i))

        forward_chunks(
            SEQ // QC,
            lambda: arrive(owner, lambda n: buf_t.at[128:192, 0 : n * 128], 16, tv_sems),
            lambda c: buf_t[0:64, lanes(c * QC, QC)], kn, buf_t, s_ref, p_ref, st, put, length,
        )

    @pl.when(owner & (hh < 6))
    def _():
        lse_d[:, 0:1024] = lse_t[:, 0:1024]
        copy_to(
            lse_t.at[:, 1024:2048], lse_d.at[:, 1024:2048], lse_sem.at[0], lse_sem.at[1], owner_of(hh + 6)
        ).start()
        pltpu.make_async_copy(buf_t.at[0:128], dist, local_sem.at[0]).start()

    arrive(owner, lambda n: land_t.at[0:n], 12, a_sems)
    loop(6, lambda j: start_to(*d_copy(lax.rem(j + b, 6))))
    att_t[...] = natural_wide(land_t[...].reshape(768, 128))
    keep(1, 4, 13)
    for i in (1, 2, 3):
        weights[i].wait()
    hidden, unit, scale = dense_up(
        x0_ref[...], att_t[...], v_out_t[...], v_up_t, v_down_t[...], upb_t, vec_t,
        act_t, slope_t, unit1_t, scale1_t, normed_turn_t,
    )
    unit2_t[...] = unit
    scale2_t[...] = jnp.broadcast_to(scale, (128, 128))
    x0_ref[...] = hidden
    low = hidden.astype(BF)
    hidden_turn[...] = hidden.T.astype(BF)
    keep(8, 9, 14, 18, 19, 20, 21, 22)
    weights[4].wait()
    qkv_blocks(low, v_qkv_s, bias_s, src_s, 6, (0, 1))

    def s_copy(h):
        return (
            src_s.at[lax.rem(h, 6), 0:128], buf_s.at[0:128, mine], s_sems, owner_of(h), b
        )

    def sv_copy(h):
        return (
            src_s.at[lax.rem(h, 6), 128:192], buf_s.at[128:192, mine],
            sv_sems, owner_of(h), b,
        )

    loop(12, lambda j: start_to(*s_copy(lax.rem(j + b, 12))))
    qkv_blocks(low, v_qkv_s, bias_s, src_s, 6, (2,))
    loop(12, lambda j: start_to(*sv_copy(lax.rem(j + b, 12))))

    def b_copy(j):
        return o_s.at[:, lanes(j * 128, 128)], land_s.at[head], b_sems, 8 * half + j, b

    @pl.when(owner)
    def _():
        lse_s[:, 0:1024] = jnp.full((8, 1024), 1e30, F32)
        arrive(owner, lambda n: buf_s.at[0:128, 0 : n * 128], 16, s_sems)
        kn[...] = natural(buf_s[64:128, :])

        def put(c, o, stat):
            o_s[:, lanes(c * QC, QC)] = o.astype(BF)
            lse_s[:, lanes(half * 1024 + c * QC, QC)] = jnp.broadcast_to(stat, (8, QC))
            for i in range(2):
                start_to(*b_copy(2 * c + i))

        forward_chunks(
            1024 // QC,
            lambda: arrive(owner, lambda n: buf_s.at[128:192, 0 : n * 128], 16, sv_sems),
            lambda c: buf_s[0:64, lanes(half * 1024 + c * QC, QC)],
            kn, buf_s, s_ref, p_ref, st, put, length,
        )

    @pl.when(owner & (hh >= 6))
    def _():
        copy_to(
            lse_s.at[:, 1024:2048], lse_s.at[:, 1024:2048], lse_sem.at[2], lse_sem.at[3], owner_of(hh - 6)
        ).start()

    @pl.when(owner & (hh < 6))
    def _():
        pltpu.make_async_copy(buf_t.at[0:128], dist, local_sem.at[0]).wait()

    @pl.when(owner & (hh >= 6))
    def _():
        arrive(hh >= 6, lambda n: dist.at[:, 0 : n * 128], 16, d_sems)
        got(lse_d.at[:, 1024:2048], lse_sem.at[1])

    keep(2, 5)
    arrive(mine_half, lambda n: land_s.at[0:n], 6, b_sems)
    att_s[...] = natural_wide(land_s[...].reshape(384, 128))
    keep(3, 15)
    for i in (5, 6, 7):
        weights[i].wait()
    result, unit, scale = dense_up(
        x0_ref[...], att_s[...], v_out_s[...], v_up_s, v_down_s[...], upb_s, vec_s,
        act_s, slope_s, unit1_s, scale1_s, normed_turn_s,
    )
    output[...] = result
    keep(0, 10, 16)
    sums[...] = jnp.zeros((24, 768), F32)
    g1, datt = dense_down(
        cot[...].astype(F32), unit, scale, unit1_s[...], scale1_s[:, 0:1],
        v_out_s, v_up_s, v_down_s, vec_s, slope_s, gu_s, g2r_s, g1r_s, sums, 12,
    )
    g1_s[...] = g1
    datt_s[...] = datt.T.astype(BF).reshape(6, 64, 128)
    keep(11, 12, 17, 23, 24, 25)

    @pl.when(owner)
    def _():
        got(o_t.at[:, 0 : 15 * 128], a_sems[0])
        leave(mine_half, lambda n: o_s.at[:, 0 : n * 128], 8, b_sems)

    @pl.when(owner & (hh < 6))
    def _():
        copy_to(
            lse_t.at[:, 1024:2048], lse_d.at[:, 1024:2048], lse_sem.at[0], lse_sem.at[1], owner_of(hh + 6)
        ).wait_send()
        got(lse_s.at[:, 1024:2048], lse_sem.at[3])

    @pl.when(owner & (hh >= 6))
    def _():
        copy_to(
            lse_s.at[:, 1024:2048], lse_s.at[:, 1024:2048], lse_sem.at[2], lse_sem.at[3], owner_of(hh - 6)
        ).wait_send()

    keep(6)
    leave(owner, lambda n: src_t.at[0:n, 0:128], 12, t_sems)
    leave(owner, lambda n: src_t.at[0:n, 128:192], 12, tv_sems)
    leave(owner & (hh >= 6), lambda n: src_t.at[0:n, 0:128], 6, d_sems)
    leave(owner, lambda n: src_t.at[0:n, 0:128], 12, s_sems)
    leave(owner, lambda n: src_t.at[0:n, 128:192], 12, sv_sems)
    for i in range(26):
        pltpu.make_async_copy(kept[i], kept_out[i], keep_sem.at[i]).wait()


def where_am_i():
    dp, blk = lax.axis_index("dp"), lax.axis_index("blk")
    return dp // 2, lax.rem(dp, 2), blk // 4, lax.rem(blk, 4)


def at_axis(axis, v):
    x, c, y, z = where_am_i()
    if axis == "x":
        return {"dp": 2 * v + c, "blk": 4 * y + z}
    if axis == "y":
        return {"dp": 2 * x + c, "blk": 4 * v + z}
    return {"dp": 2 * x + c, "blk": 4 * y + v}


def send_to(src, dst, send_sem, recv_sem, device):
    return pltpu.make_async_remote_copy(
        src_ref=src, dst_ref=dst, send_sem=send_sem, recv_sem=recv_sem,
        device_id=device, device_id_type=MESH,
    )


ORDERS = ("xyz", "yzx", "zxy")
CUTS = (
    (12, 12, ((16, 12),)), (6, 6, ((0, 6),)), (2, 1, ((6, 2),)), (12, 12, ((28, 12),)),
    (5, 4, ((43, 5),)), (3, 3, ((40, 3),)), (9, 9, ((48, 3), (52, 3), (56, 3))), (6, 6, ((8, 3), (12, 3))),
)
TILES = 60
WIDE = TILES * 128
BATCHES = (
    (0, 16, (1, 2, 7), ((0, 8, 8), (8, 4, 3), (12, 4, 3))),
    (16, 32, (0, 3, 5, 4), ((16, 16, 16), (32, 8, 8), (40, 8, 8))),
    (48, 12, (6,), ((48, 4, 3), (52, 4, 3), (56, 4, 3))),
)
PB_TILES = 32
PIECES = ((4, 0, (0, 2, 6)), (2, 4, (0, 1, 3)), (2, 6, (0, 1, 3)))
PIECE_TILES = 8


def piece_place(k, p, tile):
    half, first, starts = PIECES[p]
    at = starts[k] + tile
    return 8 * (at // half), first + at % half
TURN = 3


def drain(ref, sem):
    pltpu.make_async_copy(ref, ref, sem).wait()


def backward_kernel(
    len_ref, flag_ref, source, flags,
    w_qkv_s, w_down_t, w_up_t, w_out_t, w_qkv_t,
    in_buf_s, in_dist, in_lse_s, in_lse_d, in_g1_s, in_buf_t, in_lse_t,
    in_unit2_t, in_scale2_t, in_slope_t, in_unit1_t, in_scale1_t, datt_s,
    vec_t, sums_s,
    x0_turn, normed_turn_t, hidden_turn, normed_turn_s, g1r_s, g2r_s,
    att_t, act_t, att_s, act_s, gu_s,
    grad_in, out, sums,
    v_qkv_s, v_down_t, v_up_t, v_out_t,
    buf_s, dist, lse_s, lse_d, g1_s, buf_t, lse_t, unit2_t, scale2_t, slope_t, unit1_t, scale1_t,
    joined_t, joined_s, gu_t,
    src_t, do_s, do_t, dq_s, dkv_s, dqkv_t, dq_buf, dkv_buf,
    kn, k2n, vn, gf, x_ref, acc,
    nt, cf, cft, pb, rl, l1, a1, l2, a2, l3, a3, a4, sml, sma, smh,
    w_sem, k_sem, x_sem,
    own_n, own_c, n_send, n_recv, c_send, c_recv, st_send, st_recv, f_send, f_recv, m_send, m_recv,
):
    b, hh, owner = place()
    half, head = hh // 6, lax.rem(hh, 6)
    mine_half = owner & (half == b // 8)
    e1, e2, e3, e4, e5, e6 = [tuple(x_sem.at[3 * i + j] for j in range(3)) for i in range(6)]
    x, c, y, z = where_am_i()
    here_at = {"x": x, "y": y, "z": z}
    dp = 2 * x + c
    me = 16 * dp + b
    partner = {"dp": 2 * x + 1 - c, "blk": b}

    barrier = pltpu.get_barrier_semaphore()
    loop(15, lambda i: pl.semaphore_signal(
        barrier, inc=1, device_id={"blk": lax.rem(b + 1 + i, 16)}, device_id_type=MESH
    ))
    pl.semaphore_signal(barrier, inc=1, device_id=partner, device_id_type=MESH)
    for axis in "xyz":
        for j in range(1, 4):
            pl.semaphore_signal(
                barrier, inc=1, device_id=at_axis(axis, lax.rem(here_at[axis] + j, 4)), device_id_type=MESH
            )
    for p in range(3):
        for q in range(4):
            for core in range(2):
                at = dict(zip(ORDERS[p], (me // 32, lax.rem(me // 8, 4), q)))
                pl.semaphore_signal(
                    barrier, inc=1, device_id={"dp": 2 * at["x"] + core, "blk": 4 * at["y"] + at["z"]},
                    device_id_type=MESH,
                )
    kept = load_all(
        [
            (in_buf_s, buf_s), (in_dist, dist), (in_lse_s, lse_s), (in_lse_d, lse_d),
            (in_g1_s, g1_s), (in_buf_t, buf_t), (in_lse_t, lse_t), (in_unit2_t, unit2_t),
            (in_scale2_t, scale2_t), (in_slope_t, slope_t), (in_unit1_t, unit1_t), (in_scale1_t, scale1_t),
        ],
        k_sem,
    )
    weights = load_all(
        [(w_qkv_s, v_qkv_s), (w_down_t, v_down_t), (w_up_t, v_up_t), (w_out_t, v_out_t)], w_sem
    )
    length = len_ref[0]
    for copy in kept[0:4]:
        copy.wait()

    @pl.when(owner)
    def _():
        kn[...] = natural(buf_s[64:128, :])
        vn[...] = natural(buf_s[128:192, :])
        k2n[...] = natural(dist[64:128, :])
        acc[...] = jnp.zeros_like(acc)
        x_ref[1] = jnp.zeros((SEQ, 2 * QC), BF)

    pl.semaphore_wait(barrier, 49)

    def tiles(first, count):
        return slice(first * 128, (first + count) * 128)

    def pool_wide(m, ref):
        _, step, segments = CUTS[m]
        done = 0
        for n, (first, count) in enumerate(segments):
            cols = slice(first * 128, (first + count) * 128)
            pltpu.make_async_copy(
                ref.at[:, lanes((c * step + done) * 128, count * 128)], cf.at[0:128, cols], own_c.at[m + 8 * n]
            ).start()
            send_to(
                ref.at[:, lanes(((1 - c) * step + done) * 128, count * 128)], cf.at[128:256, cols],
                c_send.at[m + 8 * n], c_recv.at[m + 8 * n], partner,
            ).start()
            done += count

    def pool_heads():
        pltpu.make_async_copy(dqkv_t.at[pl.ds(6 * c, 6)], cft.at[:, :, 0:128], own_c.at[6]).start()
        send_to(
            dqkv_t.at[pl.ds(6 * (1 - c), 6)], cft.at[:, :, 128:256], c_send.at[6], c_recv.at[6], partner
        ).start()

    def pool_narrow(m, ref):
        if ref is None:
            ref = nt.at[m, :, 0:128]
        else:
            pltpu.make_async_copy(ref, nt.at[m, :, 0:128], own_n.at[m]).start()
        send_to(ref, nt.at[m, :, 128:256], n_send.at[m], n_recv.at[m], partner).start()

    def products(k, members=None):
        begin = BATCHES[k][0]
        for m in members or BATCHES[k][2]:
            if m not in (3, 5):
                drain(nt.at[m, :, 0:128], own_n.at[m])
            drain(nt.at[m, :, 128:256], n_recv.at[m])
            if m == 6:
                drain(cft.at[:, :, 0:128], own_c.at[6])
                drain(cft.at[:, :, 128:256], c_recv.at[6])
                for n, (first, count) in enumerate(CUTS[m][2]):
                    pb[:, tiles(first - begin, count)] = dot_t(
                        nt[m], cft[2 * n : 2 * n + 2].reshape(384, 256)
                    ).astype(BF)
                continue
            for n, (first, count) in enumerate(CUTS[m][2]):
                cols = slice(first * 128, (first + count) * 128)
                drain(cf.at[0:128, cols], own_c.at[m + 8 * n])
                drain(cf.at[128:256, cols], c_recv.at[m + 8 * n])
                size = 3 if count % 3 == 0 else count

                def piece(i, m=m, first=first, size=size):
                    from_cols = lanes((first + i * size) * 128, size * 128)
                    to_cols = lanes((first - begin + i * size) * 128, size * 128)
                    pb[:, to_cols] = dot(nt[m], cf[:, from_cols]).astype(BF)

                loop(count // size, piece)

    def sem_of(k, p, kind):
        return 18 * k + 6 * p + kind

    def rows_of(height, v):
        return pl.ds(pl.multiple_of(height * v, 16), height)

    def ring(p, stage):
        axis = ORDERS[p][stage]
        u = here_at[axis]
        around = [lax.rem(u + j, 4) for j in range(4)]
        return around, [at_axis(axis, v) for v in around]

    def stage_start(k, stage, only=(0, 1, 2)):
        begin, _, _, parts = BATCHES[k]
        for p in only:
            first, count, used = parts[p]
            around, devices = ring(p, stage)
            if stage == 0:
                first_half = (used + 1) // 2
                one, two = (0, first_half), (first_half, used - first_half)
                for j, (start, size), to, dst, kind in (
                    (2, one, 1, rl, 0), (2, two, 3, rl, 1), (1, two, 1, l1.at[0], 2), (3, one, 3, l1.at[1], 3),
                ):
                    send_to(
                        pb.at[rows_of(192, around[j]), tiles(first - begin + start, size)],
                        dst.at[:, tiles(first + start, size)],
                        st_send.at[sem_of(k, p, 0)], st_recv.at[sem_of(k, p, kind)], devices[to],
                    ).start()
                continue
            for j in range(1, 4):
                if stage == 1:
                    src = a1.at[rows_of(48, around[j]), tiles(first, used)]
                    dst = l2.at[j - 1, :, tiles(first, used)]
                else:
                    src = a2.at[:, lanes(first * 128 + around[j] * count * 32, count * 32)]
                    dst = l3.at[j - 1, :, slice(first * 32, (first + count) * 32)]
                kind = 3 + stage
                send_to(
                    src, dst, st_send.at[sem_of(k, p, kind)], st_recv.at[sem_of(k, p, kind)], devices[j]
                ).start()

    def relay(k):
        begin, _, _, parts = BATCHES[k]
        for p, (first, count, used) in enumerate(parts):
            around, devices = ring(p, 0)
            first_half = (used + 1) // 2
            for start, size, to, slot in ((0, first_half, 1, 0), (first_half, used - first_half, 3, 1)):
                land = rl.at[:, tiles(first + start, size)]
                drain(land, st_recv.at[sem_of(k, p, slot)])
                own_cols = tiles(first - begin + start, size)

                def add(r, own_cols=own_cols, start=start, size=size, to=to, first=first, around=around):
                    own = pl.ds(pl.multiple_of(192 * around[to] + 16 * r, 16), 16)
                    rows = pl.ds(pl.multiple_of(16 * r, 16), 16)
                    total = pb[own, own_cols].astype(F32) + rl[rows, tiles(first + start, size)].astype(F32)
                    pb[own, own_cols] = total.astype(BF)

                loop(12, add)
                send_to(
                    pb.at[rows_of(192, around[to]), own_cols], l1.at[slot, :, tiles(first + start, size)],
                    st_send.at[sem_of(k, p, 1)], st_recv.at[sem_of(k, p, 2 + slot)], devices[to],
                ).start()

    def stage_sent(k, stage):
        for p, (first, count, used) in enumerate(BATCHES[k][3]):
            if stage == 0:
                drain(l1.at[:, :, tiles(first, used)], st_send.at[sem_of(k, p, 0)])
                drain(rl.at[:, tiles(first, used)], st_send.at[sem_of(k, p, 1)])
            elif stage == 1:
                drain(l2.at[:, :, tiles(first, used)], st_send.at[sem_of(k, p, 4)])
            else:
                drain(l3.at[:, :, slice(first * 32, (first + count) * 32)], st_send.at[sem_of(k, p, 5)])

    def stage_sum(k, stage):
        begin, _, _, parts = BATCHES[k]
        for p, (first, count, used) in enumerate(parts):
            at = here_at[ORDERS[p][stage]]
            cols = tiles(first, used)
            if stage == 0:
                for slot in range(2):
                    drain(l1.at[slot, :, cols], st_recv.at[sem_of(k, p, 2 + slot)])
                src, land, dst, height, peers, scols = pb, l1, a1, 192, 2, tiles(first - begin, used)
            elif stage == 1:
                drain(l2.at[:, :, cols], st_recv.at[sem_of(k, p, 4)])
                src, land, dst, height, peers, scols = a1, l2, a2, 48, 3, cols
            else:
                quarter = slice(first * 32, (first + count) * 32)
                drain(l3.at[:, :, quarter], st_recv.at[sem_of(k, p, 5)])
                total = a2[:, lanes(first * 128 + at * count * 32, count * 32)].astype(F32)
                for j in range(3):
                    total = total + l3[j, :, quarter].astype(F32)
                for tile in range(count // 4):
                    row, at_tile = piece_place(k, p, tile)
                    for i in range(8):
                        a3[i, row : row + 6, tiles(at_tile, 1)] = total[6 * i : 6 * i + 6, tiles(tile, 1)]
                continue

            def add(r, src=src, land=land, dst=dst, height=height, peers=peers, at=at, cols=cols, scols=scols):
                rows = pl.ds(pl.multiple_of(16 * r, 16), 16)
                own = pl.ds(pl.multiple_of(height * at + 16 * r, 16), 16)
                total = src[own, scols].astype(F32)
                for j in range(peers):
                    total = total + land[j, rows, cols].astype(F32)
                dst[rows, cols] = total.astype(BF)

            loop(height // 16, add)

    def final_part(p):
        half, first, _ = PIECES[p]
        begin = 32 * here_at[ORDERS[p][0]] + 8 * here_at[ORDERS[p][1]]
        return begin, half, first, here_at[ORDERS[p][2]]

    def final_start():
        a4[...] = a3[...].astype(BF)
        for p in range(3):
            begin, half, first, third = final_part(p)
            for i in range(8):
                to = begin + i
                src = a4.at[i, :, tiles(first, half)]
                dst = out.at[:, lanes(((4 * c + third) * PIECE_TILES + first) * 128, half * 128)]

                @pl.when(to != me)
                def _():
                    send_to(
                        src, dst, f_send.at[p], f_recv.at[0], {"dp": to // 16, "blk": lax.rem(to, 16)}
                    ).start()

                @pl.when(to == me)
                def _():
                    pltpu.make_async_copy(src, dst, f_recv.at[0]).start()

    def final_wait():
        drain(out, f_recv.at[0])
        for p in range(3):
            begin, half, first, _ = final_part(p)
            own = (me >= begin) & (me < begin + 8)
            leave(own, lambda n, first=first, half=half: a4.at[0:n, :, tiles(first, half)], 8, (f_send.at[p],))

    half_lanes = lanes(c * 384, 384)

    def small_copy(slot):
        if slot in (0, 10):
            src = sma.at[0, :, lanes((1 - c) * 384, 384)] if slot == 0 else sums.at[:, half_lanes]
            dst = sml.at[0] if slot == 0 else sums.at[:, half_lanes]
            return send_to(src, dst, m_send.at[slot], m_recv.at[slot], partner)
        n, j = (slot - 1) // 3, (slot - 1) % 3 + 1
        axis = "xyz"[n]
        return send_to(
            smh.at[n], sml.at[slot], m_send.at[slot], m_recv.at[slot],
            at_axis(axis, lax.rem(here_at[axis] + j, 4)),
        )

    def small_step(n):
        if n == 0:
            small_copy(0).start()
            return
        total = sma[0, :, half_lanes] if n == 1 else smh[n - 2]
        for slot in (0,) if n == 1 else range(3 * n - 5, 3 * n - 2):
            small_copy(slot).wait_recv()
            total = total + sml[slot]
        if n == 4:
            sums[:, half_lanes] = total
            small_copy(10).start()
            return
        smh[n - 1] = total
        for slot in range(3 * n - 2, 3 * n + 1):
            small_copy(slot).start()

    def c1(h):
        return (
            datt_s.at[h], do_s.at[:, lanes(lax.rem(b, 8) * 128, 128)],
            e1, owner_of(h + 6 * (b // 8)), b,
        )

    def c2(j):
        return dq_buf.at[:, lanes(j * 128, 128)], dq_s.at[head], e2, 8 * half + j, b

    def c3(d):
        return dkv_buf.at[:, lanes(d * 128, 128)], dkv_s.at[hh], e3, d, b

    def c4(h):
        return src_t.at[h], do_t.at[:, lanes(b * 128, 128)], e4, owner_of(h), b

    def c5(d):
        return dq_buf.at[:, lanes(d * 128, 128)], dqkv_t.at[hh, 0:64], e5, d, b

    def c6(d):
        return dkv_buf.at[:, lanes(d * 128, 128)], dqkv_t.at[hh, 64:192], e6, d, b

    def run_chunks(n, at, kt_ref, put, low, high, put_keys=None):
        rest = (at, kn, k2n, vn, kt_ref, length, gf, x_ref, acc)

        def pair(i):
            backward_chunk(
                2 * i, jnp.maximum(2 * i - 1, 0), 0, *rest, lambda ch, g: put(ch, g, i > 0)
            )
            backward_chunk(2 * i + 1, 2 * i, 1, *rest, lambda ch, g: put(ch, g, True))

        loop(high - low, lambda i: pair(i + low))
        if 2 * high == n:
            backward_last(n - 1, 1, at, kt_ref, x_ref, acc, lambda ch, g: put(ch, g, True), put_keys)

    def keys_out(copy):
        def put_keys(t, block):
            dkv_buf[:, t * KT : (t + 1) * KT] = block
            for i in range(2):
                start_to(*copy(2 * t + i))

        return put_keys

    def send_pair(copy, ch, real):
        if real is True:
            for i in range(2):
                start_to(*copy(2 * ch + i))
        else:
            @pl.when(real)
            def _():
                for i in range(2):
                    start_to(*copy(2 * ch + i))

    def teacher_at(ch):
        here = lanes(ch * QC, QC)
        return (
            buf_t[0:64, here], buf_s[0:64, here], do_t[:, here],
            lse_t[0:1, here], lse_s[0:1, here], weight_row(len_ref, flag_ref, head, ch * QC, hh < 6),
        )

    def teacher_put(ch, g, real):
        dq_buf[:, lanes(ch * QC, QC)] = g.astype(BF)
        send_pair(c5, ch, real)

    loop(6, lambda j: start_to(*c1(lax.rem(j + b, 6))))
    for m, ref in ((1, normed_turn_s), (2, g1r_s), (7, g2r_s)):
        pool_narrow(m, ref)
    for m, ref in ((1, gu_s), (2, att_s), (7, act_s)):
        pool_wide(m, ref)
    for m, ref in ((0, normed_turn_t), (4, hidden_turn), (6, x0_turn)):
        pool_narrow(m, ref)
    for m, ref in ((3, act_t), (5, att_t)):
        pool_wide(m, ref)

    products(0)
    stage_start(0, 0)

    @pl.when(owner)
    def _():
        arrive(mine_half, lambda n: do_s.at[:, 0 : n * 128], 8, e1)

        def at(ch):
            first = half * 1024 + ch * QC
            here = lanes(first, QC)
            return (
                buf_s[0:64, here], dist[0:64, here], do_s[:, lanes(ch * QC, QC)],
                lse_s[0:1, here], lse_d[0:1, here], weight_row(len_ref, flag_ref, head, first, True),
            )

        def put(ch, g, real):
            dq_buf[:, lanes(ch * QC, QC)] = g.astype(BF)
            send_pair(c2, ch, real)

        run_chunks(1024 // QC, at, buf_s, put, 0, 2, keys_out(c3))

    relay(0)
    arrive(mine_half, lambda n: dq_s.at[0:n], 6, e2)
    arrive(owner, lambda n: dkv_s.at[0:n], 12, e3)
    joined_s[:, 0:384] = natural_wide(dq_s[...].reshape(384, 128))
    for part in range(2):
        rows = slice(64 * part, 64 * part + 64)
        both = dkv_s[0:6, rows, :].astype(F32) + dkv_s[6:12, rows, :].astype(F32)
        joined_s[:, 384 * (part + 1) : 384 * (part + 2)] = both.reshape(384, 128).T.astype(BF)
    pool_wide(4, joined_s)
    sma[0] = sums_s[...]
    low_sums = jnp.sum(joined_s[...].astype(F32), axis=0, keepdims=True)
    sma[0, 20:21, 0:384] = low_sums[:, 0:384]
    sma[0, 20:21, 384:768] = low_sums[:, 768:1152]
    for copy in kept[4:]:
        copy.wait()
    weights[0].wait()
    grad_hidden = g1_s[...] + dot_t(joined_s[...], v_qkv_s[...])
    for i in (1, 2, 3):
        weights[i].wait()
    g1, datt = dense_down(
        grad_hidden, unit2_t[...], scale2_t[:, 0:1], unit1_t[...], scale1_t[:, 0:1],
        v_out_t, v_up_t, v_down_t, vec_t, slope_t, gu_t, nt.at[3, :, 0:128], nt.at[5, :, 0:128], sma.at[0], 0,
        (lambda: pool_narrow(3, None), lambda: pool_wide(0, gu_t), lambda: pool_narrow(5, None)),
    )
    grad_in[...] = g1
    src_t[...] = datt.T.astype(BF).reshape(12, 64, 128)
    loop(12, lambda j: start_to(*c4(lax.rem(j + b, 12))))
    late = load_all(
        [(w_qkv_t.at[:, 768 * p : 768 * (p + 1)], v_down_t.at[768 * p : 768 * (p + 1), :]) for p in range(3)],
        w_sem.at[pl.ds(4, 3)],
    )
    stage_sum(0, 0)
    stage_sent(0, 0)
    products(1, (0, 3))
    stage_start(1, 0, (0, 1))
    products(1, (5, 4))
    stage_start(1, 0, (2,))

    @pl.when(owner)
    def _():
        kn[...] = natural(buf_t[64:128, :])
        vn[...] = natural(buf_t[128:192, :])
        k2n[...] = natural(buf_s[64:128, :])
        acc[...] = jnp.zeros_like(acc)
        x_ref[1] = jnp.zeros((SEQ, 2 * QC), BF)

    @pl.when(owner)
    def _():
        leave(mine_half, lambda n: dq_buf.at[:, 0 : n * 128], 8, e2)
        got(dkv_buf.at[:, 0 : 15 * 128], e3[0])
        arrive(owner, lambda n: do_t.at[:, 0 : n * 128], 16, e4)

        run_chunks(SEQ // QC, teacher_at, buf_t, teacher_put, 0, TURN)

    relay(1)
    stage_start(0, 1)

    @pl.when(owner)
    def _():
        run_chunks(SEQ // QC, teacher_at, buf_t, teacher_put, TURN, SEQ // QC // 2, keys_out(c6))

    stage_sum(0, 1)
    stage_start(0, 2)
    stage_sum(1, 0)
    stage_start(1, 1)
    arrive(owner, lambda n: dqkv_t.at[0:n, 0:64], 12, e5)
    arrive(owner, lambda n: dqkv_t.at[0:n, 64:192], 12, e6)
    pool_heads()
    stage_sent(1, 0)
    for part in range(3):
        joined_t[:, 768 * part : 768 * (part + 1)] = natural_wide(
            dqkv_t[:, 64 * part : 64 * (part + 1), :].reshape(768, 128)
        )
    for row, part in ((10, 0), (11, 2)):
        sma[0, row : row + 1, :] = jnp.sum(
            joined_t[:, 768 * part : 768 * (part + 1)].astype(F32), axis=0, keepdims=True
        )
    small_step(0)
    products(2)
    stage_start(2, 0)
    small_step(1)
    stage_sum(1, 1)
    stage_start(1, 2)
    for copy in late:
        copy.wait()
    grad = grad_in[...]
    for p in range(3):
        grad = grad + dot_t(joined_t[:, 768 * p : 768 * (p + 1)], v_down_t[768 * p : 768 * (p + 1), :])
    place_of = lax.broadcasted_iota(jnp.int32, (128, 128), 0)
    turned = jnp.where((place_of == source[...]) & (flags[...] == 1), 1.0, 0.0)
    back = turned.astype(BF)
    one = grad.astype(BF)
    rest = grad - one.astype(F32)
    two = rest.astype(BF)
    three = (rest - two.astype(F32)).astype(BF)
    copied = dot(back, one) + dot(back, two) + dot(back, three)
    kept = jnp.sum(turned.T, axis=1, keepdims=True) < 0.5
    grad_in[...] = jnp.where(kept, grad, 0.0) + copied
    relay(2)
    small_step(2)
    stage_sum(2, 0)
    stage_start(2, 1)
    small_step(3)
    stage_sum(0, 2)
    stage_sum(1, 2)
    stage_sum(2, 1)
    stage_start(2, 2)
    small_step(4)
    stage_sum(2, 2)
    final_start()

    @pl.when(owner)
    def _():
        got(dq_buf.at[:, 0 : 15 * 128], e5[0])
        got(dkv_buf.at[:, 0 : 15 * 128], e6[0])

    leave(mine_half, lambda n: dq_s.at[0:n], 6, e1)
    leave(owner, lambda n: src_t.at[0:n], 12, e4)
    for m, (_, _, segments) in enumerate(CUTS):
        if m == 6:
            drain(cft.at[:, :, 128:256], c_send.at[6])
            segments = ()
        for n, (first, count) in enumerate(segments):
            drain(cf.at[128:256, slice(first * 128, (first + count) * 128)], c_send.at[m + 8 * n])
        drain(nt.at[m, :, 128:256], n_send.at[m])
    for slot in range(11):
        small_copy(slot).wait_send()
    small_copy(10).wait_recv()
    for k, stage in ((0, 1), (0, 2), (1, 1), (1, 2), (2, 0), (2, 1), (2, 2)):
        stage_sent(k, stage)
    final_wait()


ANY = pl.BlockSpec(memory_space=pl.ANY)


def mega_call(kernel, ident, specs, outs, scratch, args, name, out_spec):
    return pl.pallas_call(
        kernel,
        name=name,
        out_shape=tuple(jax.ShapeDtypeStruct(s, t) for s, t in outs),
        in_specs=specs,
        out_specs=tuple(out_spec for _ in outs),
        scratch_shapes=scratch,
        compiler_params=pltpu.CompilerParams(
            collective_id=ident, has_side_effects=True, vmem_limit_bytes=62 * MIB
        ),
    )(*args)


def vb(*shape):
    return pltpu.VMEM(shape, BF)


def vf(*shape):
    return pltpu.VMEM(shape, F32)


def run_forward(lengths, x_in, source, flags, cot, weights, smalls):
    outs = [
        ((128, 768), F32), ((192, SEQ), BF), ((128, SEQ), BF), ((192, SEQ), BF),
        ((8, SEQ), F32), ((8, SEQ), F32), ((8, SEQ), F32),
        *[((768, 128), BF)] * 6,
        ((128, 768), BF), ((128, 3072), BF), ((128, 384), BF), ((128, 1536), BF), ((128, 1536), BF),
        ((128, 3072), BF), ((128, 768), F32), ((128, 128), F32), ((128, 768), F32), ((128, 128), F32),
        ((128, 768), F32), ((6, 64, 128), BF), ((24, 768), F32),
    ]
    scratch = [pltpu.VMEM(shape, kind) for shape, kind in outs] + [
        vb(768, 2304), vb(768, 768), vb(768, 3072), vb(3072, 768),
        vb(768, 1152), vb(384, 768), vb(768, 1536), vb(1536, 768),
        vf(128, 768), vb(12, 192, 128), vb(6, 192, 128), vb(12, 64, 128), vb(6, 64, 128),
        vb(64, SEQ), vb(64, 1024), vb(SEQ, 64), vf(2, SEQ, QC), vb(2, SEQ, QC), vf(6, 8, QC),
        vb(128, 1536), vf(128, 768), vf(128, 128),
        DMA((8,)), DMA((21,)), DMA((4,)), DMA((1,)), DMA((26,)),
    ]
    specs = [SMEM] + [VMEM] * 4 + [ANY] * 8 + [VMEM] * 6
    return mega_call(
        forward_kernel, 1, specs, outs, scratch, (lengths, x_in, source, flags, cot, *weights, *smalls), "forward", ANY
    )


def run_backward(lengths, head_flags, source, flags, weights, kept, held, pooled):
    outs = [((128, 768), F32), ((16, 8 * PIECE_TILES * 128), BF), ((24, 768), F32)]
    scratch = [
        vb(768, 1152), vb(3072, 768), vb(768, 3072), vb(768, 768),
        vb(192, SEQ), vb(128, SEQ), vf(8, SEQ), vf(8, SEQ), vf(128, 768), vb(192, SEQ), vf(8, SEQ),
        vf(128, 768), vf(128, 128), vb(128, 3072), vf(128, 768), vf(128, 128),
        vb(128, 2304), vb(128, 1152), vb(128, 3072),
        vb(12, 64, 128), vb(64, 1024), vb(64, SEQ), vb(6, 64, 128), vb(12, 128, 128), vb(12, 192, 128),
        vb(64, SEQ), vb(128, SEQ),
        vb(SEQ, 64), vb(SEQ, 64), vb(SEQ, 64), vf(SEQ, QC), vb(2, SEQ, 2 * QC), vf(SEQ, 128),
        vb(8, 768, 256), vb(256, 48 * 128), vb(6, 192, 256), vb(768, PB_TILES * 128),
        vb(192, WIDE), vb(2, 192, WIDE), vb(192, WIDE), vb(3, 48, WIDE), vb(48, WIDE), vb(3, 48, WIDE // 4), vf(8, 16, PIECE_TILES * 128), vb(8, 16, PIECE_TILES * 128),
        vf(10, 24, 384), vf(1, 24, 768), vf(3, 24, 384),
        DMA((7,)), DMA((12,)), DMA((18,)),
        DMA((8,)), DMA((24,)), DMA((8,)), DMA((8,)), DMA((24,)), DMA((24,)),
        DMA((54,)), DMA((54,)), DMA((3,)), DMA((1,)), DMA((11,)), DMA((11,)),
    ]
    specs = [SMEM] * 2 + [VMEM] * 2 + [ANY] * (5 + len(kept)) + [VMEM] * len(held) + [ANY] * len(pooled)
    return mega_call(
        backward_kernel, 2, specs, outs, scratch,
        (lengths, head_flags, source, flags, *weights, *kept, *held, *pooled), "backward", VMEM,
    )


def unpack_kernel(whole, sums, first_in, second_in, *outs):
    first_out, second_out, outs = outs[0], outs[1], outs[2:16]
    first_out[...] = first_in[...]
    second_out[...] = second_in[...]

    def tile_at(core, tile):
        for k, (_, _, _, parts) in enumerate(BATCHES):
            for p, (first, count, _) in enumerate(parts):
                if first <= tile < first + count:
                    third, rest = (tile - first) // (count // 4), (tile - first) % (count // 4)
                    row, at = piece_place(k, p, rest)
                    start = ((4 * core + third) * PIECE_TILES + at) * 128
                    return wide[row : row + 8, start : start + 128]

    wide = whole[...].astype(F32)

    def columns(m):
        count, step, segments = CUTS[m]
        if m == 6:
            tiles_of = [[tile_at(core, first + i) for first, size in segments for i in range(size)] for core in range(2)]
            pieces = []
            for part in range(3):
                for head in range(12):
                    lane = 192 * (head % 6) + 64 * part
                    pieces.append(tiles_of[head // 6][lane // 128][:, lane % 128 : lane % 128 + 64])
            return jnp.concatenate(pieces, axis=1)
        spots = [first + i for first, size in segments for i in range(size)]
        pieces = [tile_at(0, tile) for tile in spots] + [tile_at(1, tile) for tile in spots[count - step :]]
        return jnp.concatenate(pieces, axis=1)

    for m, o in ((6, 0), (5, 2), (0, 3), (3, 4), (4, 7), (2, 9), (1, 10), (7, 11)):
        outs[o][...] = columns(m)[0:6]
    i = 16 * lax.axis_index("dp") + lax.axis_index("blk")

    def turn(rows, by):
        return pltpu.roll(rows, lax.rem(768 - by, 768), 1)

    def pick(first, count, per):
        row = first + (i * per) // 768
        wide = jnp.broadcast_to(sums[pl.ds(row, 1), :], (8, 768))
        return turn(wide, lax.rem(i * per, 768))[0:1, 0:per]

    outs[1][...] = pick(10, 2, 12)
    outs[5][...] = pick(6, 4, 24)
    outs[8][...] = pick(20, 1, 6)
    outs[12][...] = pick(18, 2, 12)
    outs[6][...] = turn(sums[0:8, :], i * 6)[0:6, 0:6]
    outs[13][...] = turn(sums[8:24, :], i * 6)[4:10, 0:6]


def unpack(whole, sums, output, grad_in):
    shapes = (
        (6, 2304), (1, 12), (6, 768), (6, 3072), (6, 3072), (1, 24), (6, 6),
        (6, 1152), (1, 6), (6, 384), (6, 1536), (6, 1536), (1, 12), (6, 6),
    )
    outs = list(
        pl.pallas_call(
            unpack_kernel,
            name="unpack",
            out_shape=tuple(jax.ShapeDtypeStruct(s, F32) for s in ((128, 768), (128, 768)) + shapes),
            in_specs=[VMEM] * 4,
            out_specs=(VMEM, VMEM) + tuple(VMEM for _ in shapes),
            compiler_params=pltpu.CompilerParams(vmem_limit_bytes=62 * MIB),
        )(whole, sums, output, grad_in)
    )
    for i in (3, 7, 10, 14):
        outs[i] = outs[i].reshape(-1)
    for i in (4, 6, 11, 13):
        outs[i] = outs[i].T
    outs[0], outs[1] = outs[0][None], outs[1][None]
    return tuple(outs)


def per_device(
    inputs, aug_source, aug_flags, lengths, head_flags, cotangent,
    qkv_teacher, qv_bias_teacher, out_teacher, up_teacher, down_teacher, up_bias_teacher, vectors_teacher,
    qkv_student, qv_bias_student, out_student, up_student, down_student, up_bias_student, vectors_student,
):
    (
        output, buf_t, dist, buf_s, lse_t, lse_d, lse_s,
        x0_turn, normed_turn_t, hidden_turn, normed_turn_s, g1r_s, g2r_s,
        att_t, act_t, att_s, act_s, gu_s,
        slope_t, unit1_t, scale1_t, unit2_t, scale2_t, g1_s, datt_s, sums_s,
    ) = run_forward(
        lengths, inputs[0], aug_source, aug_flags, cotangent[0],
        (qkv_teacher, out_teacher, up_teacher, down_teacher, qkv_student, out_student, up_student, down_student),
        (
            qv_bias_teacher, up_bias_teacher, vectors_teacher,
            qv_bias_student, up_bias_student, vectors_student,
        ),
    )
    grad_in, whole, total = run_backward(
        lengths, head_flags, aug_source, aug_flags,
        (qkv_student, down_teacher, up_teacher, out_teacher, qkv_teacher),
        (
            buf_s, dist, lse_s, lse_d, g1_s, buf_t, lse_t,
            unit2_t, scale2_t, slope_t, unit1_t, scale1_t, datt_s,
        ),
        (vectors_teacher, sums_s),
        (
            x0_turn, normed_turn_t, hidden_turn, normed_turn_s, g1r_s, g2r_s,
            att_t, act_t, att_s, act_s, gu_s,
        ),
    )
    return unpack(whole, total, output, grad_in)


def solution(mesh):
    both = ("dp", "blk")
    row, flat, col = P(both, None), P(both), P(None, both)
    tokens, marks = P("dp", "blk", None), P("dp", "blk")
    return jax.shard_map(
        per_device,
        mesh=mesh,
        in_specs=(tokens, marks, marks, P("dp"), P(), tokens) + (P(),) * 14,
        out_specs=(tokens, tokens) + (row, flat, col, row, col, flat, col) * 2,
        check_vma=False,
    )
```
